32 devices in a mesh: dp: 8 (over z, y), head: 4 (over x, core).
Axes of the slice: x: 2, y: 2, z: 4, core: 2. Of those that a mesh axis runs over, the one named last changes fastest.
Arguments:
- tokens: bfloat16 [9408, 512], P('dp'), may hold values from -6 to 6
- cotangent: bfloat16 [9408, 512], P('dp'), may hold values from -16 to 16
- crop_image: int32 [32, 6], P('dp'), may hold values from 0 to 2, never falling along the last dimension, each value on 1 to 3 neighbouring positions
- crop_class: int32 [32, 6], P('dp'), may hold values 0 or 1
- weights: float32 [12, 512, 512], P(None, 'dp', 'head'), may hold values from -4 to 4
- row_state: float32 [12, 512], P(None, 'dp'), as said below
- col_state: float32 [12, 512], P(None, 'head'), as said below
- weights_ema: float32 [12, 512, 512], P(None, 'dp', 'head'), may hold values from -4 to 4
- small_params: float32 [71, 512], replicated, may hold values from -4 to 8
- small_state: float32 [71, 512], replicated, as said below
- small_ema: float32 [71, 512], replicated, may hold values from -4 to 8
Outputs:
- block_out: bfloat16 [9408, 512], P('dp')
- input_grad: bfloat16 [9408, 512], P('dp')
- weight_grads: float32 [12, 512, 512], P(None, 'dp', 'head')
- new_row_state: float32 [12, 512], P(None, 'dp')
- new_col_state: float32 [12, 512], P(None, 'head')
- new_weights: float32 [12, 512, 512], P(None, 'dp', 'head')
- weights_copy: bfloat16 [12, 512, 512], P(None, 'dp', 'head')
- new_weights_ema: float32 [12, 512, 512], P(None, 'dp', 'head')
- small_grads: float32 [71, 512], replicated
- new_small_state: float32 [71, 512], replicated
- new_small_params: float32 [71, 512], replicated
- new_small_ema: float32 [71, 512], replicated
- clip_rms: float32 [83], replicated
The draws below stay inside these ranges and needn't reach their ends.
Inputs may be any that keep to these rules, and one draw needn't show every extreme that they name: `crop_image`: along each row the values never fall; each of the 3 images has 1 to 3 crops, and in every group one image has exactly 3 crops. `crop_class`: 1 marks a crop of 3 x 3 cells in the top left corner of its grid, 0 a full crop. `row_state`: entries are positive. `col_state`: entries are positive. `small_state`: entries are positive.
All inputs are finite; a program needn't handle non-finite values. No bound on the sum of `crop_class` on one device may be relied on, other than what follows from the above.
Results may differ from the reference program's by a relative error of at most 0.014.
Values may be sent and summed in bfloat16 or wider, within the bound.
A program may use at most 128 MiB of HBM per device.

```python
import math
import jax
import jax.numpy as jnp
import numpy as np
from jax import lax

D = 512
HEADS = 8
HEAD_DIM = 64
GRID = 7
SMALL_GRID = 3
WINDOW = 7
GROUP_SEQ = 6
IMG_GROUP = 3
GROUPS = 32
TOKENS = 9408
PARAM_ROWS = 71


SECOND_DECAY = 0.999


MATRIX_FACTORS = (1.0, 1.0, 1.0, 2.0, 1.0, 1.0, 1.0, 1.0, 0.5, 0.5, 0.5, 0.5)


GRADIENT_LEVELS = (3.0, 0.05, 3.0, 0.8, 0.25, 0.25, 0.25, 0.25, 1.0, 1.0, 1.0, 1.0)


def rising(col_count, ratio_top):
    columns = jnp.arange(col_count, dtype=jnp.float32) / max(col_count - 1, 1)
    return jnp.exp(columns * math.log(ratio_top))


def draw_cotangent(key, part):
    key = jax.random.fold_in(key, 11)
    noise_key, scale_key = jax.random.split(key)
    rough = jax.random.uniform(scale_key, (D,), jnp.float32, 0.7, 1.4)
    column_scale = rising(D, 3.0) * rough
    noise_vals = jax.random.normal(noise_key, (TOKENS, D), jnp.float32)
    return (noise_vals * column_scale[None, :] * 0.5).astype(jnp.bfloat16)


def matrix_values(key):
    factors = jnp.array(MATRIX_FACTORS, jnp.float32)
    return jax.random.normal(key, (12, D, D), jnp.float32) * factors[:, None, None] / math.sqrt(D)


def draw_weights(key, part):
    key = jax.random.fold_in(key, 21)
    return matrix_values(key)


def draw_weights_ema(key, part):
    key = jax.random.fold_in(key, 22)
    return matrix_values(key)


def state_values(key, row_count, col_count, levels):
    level_key, spread_key = jax.random.split(key)
    level_vals = jnp.exp(jax.random.uniform(level_key, (row_count, 1), jnp.float32, 0.0, math.log(4.0)))
    spread = jnp.exp(jax.random.uniform(spread_key, (row_count, col_count), jnp.float32, math.log(0.5), math.log(2.0)))
    return level_vals * spread * levels[:, None] * (TOKENS * (1.0 - SECOND_DECAY) / SECOND_DECAY)


def draw_row_state(key, part):
    key = jax.random.fold_in(key, 31)
    return state_values(key, 12, D, jnp.array(GRADIENT_LEVELS, jnp.float32))


def draw_col_state(key, part):
    key = jax.random.fold_in(key, 32)
    return state_values(key, 12, D, jnp.array(GRADIENT_LEVELS, jnp.float32))


def draw_small_state(key, part):
    key = jax.random.fold_in(key, 33)
    return state_values(key, PARAM_ROWS, D, jnp.full((PARAM_ROWS,), 2.0, jnp.float32))


def param_values(key, ratio_top, base_gain):
    noise_key, gain_key = jax.random.split(key)
    noise_vals = jax.random.normal(noise_key, (PARAM_ROWS, D), jnp.float32)
    gain_vals = base_gain * rising(D, ratio_top)[None, :] * jnp.exp(0.15 * jax.random.normal(gain_key, (1, D), jnp.float32))
    row_ids = jnp.arange(PARAM_ROWS)[:, None]
    is_gain = (row_ids == 0) | (row_ids == 5)
    return jnp.where(is_gain, gain_vals, jnp.where(row_ids >= 13, 0.15 * noise_vals, 0.3 * noise_vals))


def draw_small_params(key, part):
    key = jax.random.fold_in(key, 41)
    return param_values(key, 3.0, 0.6)


def draw_small_ema(key, part):
    key = jax.random.fold_in(key, 42)
    return param_values(key, 3.0, 0.6)


def plant(values, own_key, least, high):
    longest = values.shape.index(max(values.shape))
    spots = []
    for shift in (0, 1):
        where = [jax.random.randint(jax.random.fold_in(own_key, axis), (), 0, length) for axis, length in enumerate(values.shape)]
        where[longest] = (where[longest] + shift) % values.shape[longest]
        spots.append(tuple(where))
    return values.at[spots[0]].set(least).at[spots[1]].set(high)


def level_of(stream_key, extent, cuts, smallest, high):
    factor_of, own = 1.0, jax.random.fold_in(stream_key, 6)
    for position, shards_of in cuts:
        steps = jnp.exp(jax.random.uniform(jax.random.fold_in(own, position), (shards_of,), jnp.float32, smallest / len(cuts), high / len(cuts)))
        factor_of = factor_of * jnp.repeat(steps, extent[position] // shards_of).reshape([-1 if axis == position else 1 for axis in range(len(extent))])
    return factor_of


def length_profile(amount, total, limit, skew):
    weights = [(1 << 20) // math.isqrt(standing ** skew) + 1 for standing in range(2, amount + 1)]
    rest, holding = total - limit - (amount - 1), [1] * (amount - 1)
    while rest > 0:
        candidates = [i for i in range(amount - 1) if holding[i] < limit]
        pool, budget = sum([weights[i] for i in candidates]), rest
        for i in candidates:
            addition = min(limit - holding[i], max(1, budget * weights[i] // pool), rest)
            holding[i] = holding[i] + addition
            rest = rest - addition
    return np.array([limit] + holding)


def uneven(own_key, count, total, most, lean):
    if count == 2:
        one = jax.random.randint(own_key, (), max(1, total - most), min(most, total - 1) + 1)
        return jnp.stack([one, total - one])
    lengths = jnp.asarray(length_profile(count, total, most, lean), jnp.int32)
    twos = (count - 1) // 2
    source_of, taker = lengths[1:1 + 2 * twos:2], lengths[2:2 + 2 * twos:2]
    margin = jnp.minimum(source_of - 1, most - taker)
    shifted = jax.random.randint(jax.random.fold_in(own_key, 1), (twos,), 0, 1 << 20) % (margin + 1)
    lengths = lengths.at[1:1 + 2 * twos:2].set(source_of - shifted).at[2:2 + 2 * twos:2].set(taker + shifted)
    return lengths[jax.random.permutation(jax.random.fold_in(own_key, 2), count)]


def normal_values(stream_key, dims, deviation, reach, cuts=(), held_as=jnp.bfloat16):
    entries = jax.random.normal(stream_key, dims, jnp.float32) * deviation
    if len(cuts) > 0:
        entries = level_of(stream_key, dims, cuts, -0.22, 0.18) * entries
    return jnp.clip(entries, min=-reach, max=reach).astype(held_as)


def setup_inputs(seed: int = 0) -> dict:
    key_list = jax.random.split(jax.random.key(seed), 12)
    return {
        "tokens": normal_values(key_list[0], (TOKENS, D), 1.0, 6.0, ((0, 8),)),
        "cotangent": draw_cotangent(jax.random.fold_in(key_list[11], 71), 0),
        "crop_image": jax.vmap(lambda own: jnp.searchsorted(jnp.cumsum(uneven(own, IMG_GROUP, GROUP_SEQ, GROUP_SEQ // 2, 0)), jnp.arange(GROUP_SEQ), side="right"))(jax.random.split(key_list[2], GROUPS)).reshape((GROUPS, GROUP_SEQ)).astype(jnp.int32),
        "crop_class": plant((jax.random.randint(key_list[3], (GROUPS, GROUP_SEQ), 0, 10) < 3).astype(jnp.int32), jax.random.fold_in(key_list[3], 1), 0, 1),
        "weights": draw_weights(jax.random.fold_in(key_list[11], 71), 0),
        "row_state": draw_row_state(jax.random.fold_in(key_list[11], 71), 0),
        "col_state": draw_col_state(jax.random.fold_in(key_list[11], 71), 0),
        "weights_ema": draw_weights_ema(jax.random.fold_in(key_list[11], 71), 0),
        "small_params": draw_small_params(jax.random.fold_in(key_list[11], 71), 0),
        "small_state": draw_small_state(jax.random.fold_in(key_list[11], 71), 0),
        "small_ema": draw_small_ema(jax.random.fold_in(key_list[11], 71), 0),
    }


FULL_PRECISION = lax.Precision.HIGHEST
NORM_EPS = 1e-06
SQUARE_FLOOR = 1e-30
SECOND_DECAY = 0.999
STEP_RATE = 0.02
SMALL_RATE = 0.05
AVERAGE_KEEP = 0.9
NEG_LARGE = -1e+30
ROOT_HALF = 0.7071067811865476

@jax.custom_vjp
def low(v):
    return lax.optimization_barrier(v.astype(jnp.bfloat16)).astype(jnp.float32)

@jax.custom_vjp
def low_back(v):
    return v

def low_keep(v):
    return (low(v), None)

def low_pass(kept, grad):
    return (grad,)

def back_keep(v):
    return (v, None)

def back_low(kept, grad):
    return (low(grad),)
low.defvjp(low_keep, low_pass)
low_back.defvjp(back_keep, back_low)

def crop_live(class_row):
    grid_rows = lax.broadcasted_iota(jnp.int32, (GRID, GRID), 0)
    grid_cols = lax.broadcasted_iota(jnp.int32, (GRID, GRID), 1)
    inside = (grid_rows < SMALL_GRID) & (grid_cols < SMALL_GRID)
    return jnp.where((class_row[:, None, None] == 0) | inside[None, :, :], 1.0, 0.0).astype(jnp.float32)

def image_table(image_rows):
    group_count, per_group = image_rows.shape
    labels = (lax.broadcasted_iota(jnp.int32, image_rows.shape, 0) * IMG_GROUP + image_rows).reshape(-1)
    images = lax.broadcasted_iota(jnp.int32, (group_count * IMG_GROUP, group_count * per_group), 0)
    return jnp.where(images == labels[None, :], 1.0, 0.0).astype(jnp.float32)

def window_mask(first_channel, channels):
    shape_taps = (WINDOW * WINDOW, channels)
    head_ids = (first_channel + lax.broadcasted_iota(jnp.int32, shape_taps, 1)) // HEAD_DIM
    reach_cells = jnp.where(head_ids < 2, 1, jnp.where(head_ids < 5, 2, 3))
    tap_ids = lax.broadcasted_iota(jnp.int32, shape_taps, 0)
    centre = WINDOW // 2
    row_off = jnp.abs(tap_ids // WINDOW - centre)
    col_off = jnp.abs(tap_ids % WINDOW - centre)
    return jnp.where((row_off <= reach_cells) & (col_off <= reach_cells), 1.0, 0.0).astype(jnp.float32)

def conv_grid(source, tap_table, window):
    reach_cells = window // 2
    padded = jnp.pad(source, ((0, 0), (reach_cells, reach_cells), (reach_cells, reach_cells), (0, 0)))
    summed = jnp.zeros_like(source)
    for row_tap in range(window):
        for col_tap in range(window):
            summed = summed + tap_table[row_tap * window + col_tap] * padded[:, row_tap:row_tap + GRID, col_tap:col_tap + GRID, :]
    return summed

def norm_rows(row_block, norm_gain, norm_shift):
    centre = lax.optimization_barrier(jnp.mean(row_block, axis=1, keepdims=True))
    offset = row_block - centre
    spread = lax.optimization_barrier(jnp.mean(offset * offset, axis=1, keepdims=True))
    return offset * lax.rsqrt(spread + NORM_EPS) * norm_gain + norm_shift

def gelu_exact(values):
    return values * 0.5 * (1.0 + lax.erf(values * ROOT_HALF))

def group_forward(row_block, image_row, class_row, matrices, small_vals):
    live_grid = crop_live(class_row)
    slot_count = class_row.shape[0]
    cell_count = GRID * GRID
    live_rows = live_grid.reshape(slot_count * cell_count, 1)
    live_cube = live_grid.reshape(slot_count, cell_count, 1)
    image_onehot = image_table(image_row[None, :])
    cube_shape = (slot_count, cell_count, D)
    split_shape = (slot_count, cell_count, HEADS, HEAD_DIM)
    pos_source = (row_block * live_rows).reshape(slot_count, GRID, GRID, D)
    first_sum = row_block + conv_grid(pos_source, small_vals[13:22], 3).reshape(-1, D) + small_vals[8]
    normed_one = low(norm_rows(first_sum, small_vals[0], small_vals[1]))
    query_pre = low_back(jnp.dot(normed_one, matrices[0], precision=FULL_PRECISION))
    key_pre = low_back(jnp.dot(normed_one, matrices[1], precision=FULL_PRECISION))
    value_pre = low_back(jnp.dot(normed_one, matrices[2], precision=FULL_PRECISION))
    queries = low(query_pre + small_vals[2]).reshape(cube_shape)
    keys_all = low(key_pre).reshape(cube_shape)
    values_all = low(value_pre + small_vals[3]).reshape(cube_shape)
    masked_keys = jnp.where(live_cube > 0, keys_all, NEG_LARGE)
    slot_top = lax.optimization_barrier(jnp.max(masked_keys, axis=1))
    image_top = lax.optimization_barrier(jnp.max(jnp.where(image_onehot[:, :, None] > 0, slot_top[None, :, :], NEG_LARGE), axis=1))
    slot_shift = jnp.dot(image_onehot.T, image_top, precision=FULL_PRECISION)
    raised = jnp.where(live_cube > 0, jnp.exp(masked_keys - slot_shift[:, None, :]), 0.0)
    image_total = jnp.dot(image_onehot, lax.optimization_barrier(jnp.sum(raised, axis=1)), precision=FULL_PRECISION)
    spread_total = jnp.dot(image_onehot.T, image_total, precision=FULL_PRECISION)
    soft_keys = low(raised / spread_total[:, None, :])
    slot_context = jnp.einsum('snhd,snhe->shde', soft_keys.reshape(split_shape), values_all.reshape(split_shape), precision=FULL_PRECISION)
    image_context = low(jnp.einsum('is,shde->ihde', image_onehot, slot_context, precision=FULL_PRECISION))
    spread_context = jnp.einsum('is,ihde->shde', image_onehot, image_context, precision=FULL_PRECISION)
    factor = jnp.einsum('snhd,shde->snhe', queries.reshape(split_shape), spread_context, precision=FULL_PRECISION).reshape(cube_shape)
    rel_source = (values_all * live_cube).reshape(slot_count, GRID, GRID, D)
    relative = conv_grid(rel_source, small_vals[22:] * window_mask(0, D), WINDOW).reshape(cube_shape)
    mixed_out = low((factor * (1.0 / math.sqrt(HEAD_DIM)) + queries * relative) * live_cube).reshape(-1, D)
    second_sum = first_sum + low_back(jnp.dot(mixed_out, matrices[3].T, precision=FULL_PRECISION)) + small_vals[4]
    normed_two = low(norm_rows(second_sum, small_vals[5], small_vals[6]))
    hidden = low_back(jnp.einsum('rd,kdc->rkc', normed_two, matrices[4:8], precision=FULL_PRECISION)) + small_vals[9:13][None, :, :]
    active = low(gelu_exact(hidden))
    down_out = low_back(jnp.einsum('rkc,kdc->rd', active, matrices[8:12], precision=FULL_PRECISION))
    return second_sum + down_out + small_vals[7]

def reference(tokens, cotangent, crop_image, crop_class, weights, row_state, col_state, weights_ema, small_params, small_state, small_ema):
    matrices = lax.optimization_barrier(weights.astype(jnp.bfloat16)).astype(jnp.float32)
    group_count = crop_image.shape[0]
    group_rows = GROUP_SEQ * GRID * GRID
    inputs = tokens.astype(jnp.float32).reshape(group_count, group_rows, D)

    def whole(inputs_all, matrix_vals, small_vals):

        def one_group(packed):
            return group_forward(packed[0], packed[1], packed[2], matrix_vals, small_vals)
        return lax.map(jax.checkpoint(one_group), (inputs_all, crop_image, crop_class))
    outputs, pullback = jax.vjp(whole, inputs, matrices, small_params)
    live_all = jax.vmap(crop_live)(crop_class).reshape(group_count, group_rows, 1)
    upstream = cotangent.astype(jnp.float32).reshape(group_count, group_rows, D) * live_all
    grad_inputs, weight_grads, small_grads = pullback(upstream)
    squares = weight_grads * weight_grads + SQUARE_FLOOR
    new_rows = SECOND_DECAY * row_state + (1.0 - SECOND_DECAY) * lax.optimization_barrier(jnp.mean(squares, axis=2))
    new_cols = SECOND_DECAY * col_state + (1.0 - SECOND_DECAY) * lax.optimization_barrier(jnp.mean(squares, axis=1))
    estimate = new_rows[:, :, None] * new_cols[:, None, :] / lax.optimization_barrier(jnp.mean(new_rows, axis=1))[:, None, None]
    update = weight_grads * lax.rsqrt(estimate)
    update_rms = jnp.sqrt(lax.optimization_barrier(jnp.mean(update * update, axis=(1, 2))))
    new_weights = weights - STEP_RATE * update / jnp.maximum(1.0, update_rms)[:, None, None]
    new_ema = AVERAGE_KEEP * weights_ema + (1.0 - AVERAGE_KEEP) * new_weights
    new_small_state = SECOND_DECAY * small_state + (1.0 - SECOND_DECAY) * (small_grads * small_grads + SQUARE_FLOOR)
    small_update = small_grads * lax.rsqrt(new_small_state)
    small_rms = jnp.sqrt(lax.optimization_barrier(jnp.mean(small_update * small_update, axis=1)))
    new_small = small_params - SMALL_RATE * small_update / jnp.maximum(1.0, small_rms)[:, None]
    new_small_ema = AVERAGE_KEEP * small_ema + (1.0 - AVERAGE_KEEP) * new_small
    return (outputs.reshape(-1, D).astype(jnp.bfloat16), grad_inputs.reshape(-1, D).astype(jnp.bfloat16), weight_grads, new_rows, new_cols, new_weights, new_weights.astype(jnp.bfloat16), new_ema, small_grads, new_small_state, new_small, new_small_ema, jnp.concatenate([update_rms, small_rms]))
```

```python
import math

import jax
import jax.numpy as jnp
from jax import lax
from jax.experimental import pallas as pl
from jax.experimental.pallas import tpu as pltpu
from jax.sharding import PartitionSpec as P

D = 512
HEAD_DIM = 64
GRID = 7
SMALL_GRID = 3
WINDOW = 7
IMG_GROUP = 3
CELLS = GRID * GRID
SLOTS = 8
CELL_PAD = CELLS + 1
ROWS = CELL_PAD * SLOTS
LANES = 128
WIDE = 256
REACHES = (1, 2, 3, 3)
HALO = WINDOW // 2

NORM_EPS = 1e-06
SQUARE_FLOOR = 1e-30
SECOND_DECAY = 0.999
STEP_RATE = 0.02
SMALL_RATE = 0.05
AVERAGE_KEEP = 0.9
NEG_LARGE = -1e30
ROOT_HALF = 0.7071067811865476
INV_ROOT_TAU = 0.3989422804014327
INV_SCALE = 1.0 / math.sqrt(HEAD_DIM)

F32 = jnp.float32
BF16 = jnp.bfloat16
NN = (((1,), (0,)), ((), ()))
NT = (((1,), (1,)), ((), ()))
TN = (((0,), (0,)), ((), ()))


def dot(a, b, dims=NN):
    return lax.dot_general(a, b, dims, preferred_element_type=F32)


def lane_block(b):
    return slice(b * WIDE, (b + 1) * WIDE)


def wide(col):
    return jnp.concatenate([col] * (D // LANES), axis=1)


def rows_loop(count, size, body, init=None, unroll=1):
    def step(j, carry):
        return body(pl.multiple_of(j * size, size), carry)

    return lax.fori_loop(0, count // size, step, init, unroll=unroll)


def conv(src, halo, tap, reach, lanes, put):
    def line(y, _):
        sums = [jnp.zeros((SLOTS, LANES), F32) for _ in range(GRID)]
        for a in range(-reach, reach + 1):
            base = (y + (a + halo)) * GRID
            cells = [src[base + x, :, lanes] for x in range(GRID)]
            for b in range(-reach, reach + 1):
                t = tap(a, b)
                for x in range(GRID):
                    if 0 <= x + b < GRID:
                        sums[x] = sums[x] + t * cells[x + b]
        for x in range(GRID):
            put(y * GRID + x, sums[x])
        return 0

    lax.fori_loop(0, GRID, line, 0)


def tap_sums(up, src, halo, reach, lanes, put):
    for a in range(-reach, reach + 1):

        def line(y, sums):
            sums = list(sums)
            ups = [up(y * GRID + x) for x in range(GRID)]
            base = (y + (a + halo)) * GRID
            cells = [src[base + x, :, lanes] for x in range(GRID)]
            for i, b in enumerate(range(-reach, reach + 1)):
                for x in range(GRID):
                    if 0 <= x + b < GRID:
                        sums[i] = sums[i] + ups[x] * cells[x + b]
            return tuple(sums)

        start = tuple(jnp.zeros((SLOTS, LANES), F32) for _ in range(2 * reach + 1))
        sums = lax.fori_loop(0, GRID, line, start)
        for i, b in enumerate(range(-reach, reach + 1)):
            put(a, b, jnp.sum(sums[i], axis=0, keepdims=True))


def fold(x):
    return jnp.sum(x.reshape(x.shape[0] // SLOTS, SLOTS, x.shape[1]), axis=0)


def erf_parts(h):
    e = lax.erf(h * ROOT_HALF)
    half = 0.5 * (1.0 + e)
    return h * half, half + h * jnp.exp(-0.5 * h * h) * INV_ROOT_TAU


def norm_rows(v, gain, shift):
    centre = jnp.sum(v, axis=1, keepdims=True) * (1.0 / D)
    offset = v - centre
    spread = jnp.sum(offset * offset, axis=1, keepdims=True) * (1.0 / D)
    inverse = lax.rsqrt(spread + NORM_EPS)
    unit = offset * inverse
    return unit * gain + shift, unit, inverse


def norm_back(up, unit, inverse, gain):
    z = up * gain
    mean_z = jnp.sum(z, axis=1, keepdims=True) * (1.0 / D)
    mean_zu = jnp.sum(z * unit, axis=1, keepdims=True) * (1.0 / D)
    return inverse * (z - mean_z - unit * mean_zu)


class Block:
    def __init__(self, refs):
        self.__dict__.update(refs)

    def matrix(self, k, lo, hi):
        parts = []
        for h in range(lo, hi):
            part = self.w[h, :, k]
            if part.shape[1] % 16:
                part = part.astype(F32).reshape(D, LANES).astype(BF16)
            else:
                part = part.reshape(D, LANES)
            parts.append(part)
        return jnp.concatenate(parts, axis=1)

    def times(self, lhs, k, b):
        return dot(lhs, self.matrix(k, 2 * b, 2 * b + 2))

    def times_t(self, lhs, k, b):
        return dot(lhs, self.matrix(k, 0, 4)[lane_block(b), :], NT)

    def put_grad(self, k, lhs_t, rhs):
        for b in range(2):
            g = dot(lhs_t, rhs[:, lane_block(b)])
            for i in range(2):
                piece = g[:, i * LANES : (i + 1) * LANES]
                rows = self.g.shape[3]
                piece = piece.reshape(D // rows, rows, LANES)
                self.g[2 * b + i, :, k] = piece.astype(BF16)

    def row(self, j):
        return self.small[j : j + 1, :]

    def setup(self):
        head = lax.axis_index("head")
        slots = self.cls.shape[1]
        self.sums[...] = jnp.zeros(self.sums.shape, F32)
        sub = lax.broadcasted_iota(jnp.int32, (SLOTS, LANES), 0)
        valid = jnp.where(sub < slots, 1.0, 0.0)
        full = jnp.zeros((SLOTS, LANES), F32)
        images = [jnp.zeros((SLOTS, LANES), F32) for _ in range(IMG_GROUP)]
        for s in range(slots):
            full = jnp.where(sub == s, jnp.where(self.cls[head, s] == 0, 1.0, 0.0), full)
            for i in range(IMG_GROUP):
                images[i] = jnp.where(
                    sub == s, jnp.where(self.img[head, s] == i, 1.0, 0.0), images[i]
                )
        for cell in range(CELLS):
            small = cell // GRID < SMALL_GRID and cell % GRID < SMALL_GRID
            self.live[cell * SLOTS : (cell + 1) * SLOTS, :] = valid if small else full
        self.live[CELLS * SLOTS :, :] = jnp.zeros((SLOTS, LANES), F32)
        for i in range(IMG_GROUP):
            self.im8[i] = images[i]
            self.im16[i] = jnp.concatenate([images[i], images[i]], axis=0).astype(BF16)
        self.pos_src[0:GRID] = jnp.zeros((GRID, SLOTS, D), F32)
        self.pos_src[GRID + CELLS :] = jnp.zeros((GRID, SLOTS, D), F32)
        for pad in (self.rel_src, self.dq_src):
            pad[0 : HALO * GRID] = jnp.zeros((HALO * GRID, SLOTS, D), F32)
            pad[HALO * GRID + CELLS :] = jnp.zeros((HALO * GRID, SLOTS, D), F32)
        tap = lax.broadcasted_iota(jnp.int32, (WINDOW * WINDOW, 1), 0)
        row_off = jnp.abs(tap // WINDOW - HALO)
        col_off = jnp.abs(tap % WINDOW - HALO)
        off = jnp.maximum(row_off, col_off)
        heads = lax.broadcasted_iota(jnp.int32, (1, D), 1) // HEAD_DIM
        reach = jnp.where(heads < 2, 1, jnp.where(heads < 5, 2, 3))
        mask = jnp.where(off <= reach, 1.0, 0.0)
        self.window[...] = mask
        self.rel_taps[...] = self.small[22 : 22 + WINDOW * WINDOW, :] * mask

    def place(self, rows_ref, first, r0, size):
        count = rows_ref.shape[0]
        r = r0 + lax.broadcasted_iota(jnp.int32, (size, 1), 0)
        cell, slot = r >> 3, r & 7
        want = first + slot * CELLS + cell
        want = jnp.where((slot < self.cls.shape[1]) & (cell < CELLS), want, -1)
        col = lax.broadcasted_iota(jnp.int32, (size, count), 1)
        pick = jnp.where(col == want, 1.0, 0.0).astype(BF16)
        return dot(pick, rows_ref[...])

    def unplace(self, src_ref, out_ref):
        count = out_ref.shape[0]
        r = lax.broadcasted_iota(jnp.int32, (1, ROWS), 1)
        cell, slot = r >> 3, r & 7
        target = jnp.where((slot < self.cls.shape[1]) & (cell < CELLS), slot * CELLS + cell, -1)
        t = lax.broadcasted_iota(jnp.int32, (count, ROWS), 0)
        pick = jnp.where(t == target, 1.0, 0.0).astype(BF16)
        out_ref[...] = dot(pick, src_ref[...]).astype(BF16)

    def read(self):
        first = lax.axis_index("head") * (self.cls.shape[1] * CELLS)
        size = 80

        def body(r0, _):
            live = wide(self.live[pl.ds(r0, size), :])
            x = self.place(self.tokens, first, r0, size)
            self.first[pl.ds(r0, size), :] = x
            c0 = r0 // SLOTS
            self.pos_src[pl.ds(GRID + c0, size // SLOTS)] = (x * live).reshape(-1, SLOTS, D)
            c = self.place(self.cot, first, r0, size)
            self.go[pl.ds(r0, size), :] = (c * live).astype(BF16)
            return 0

        rows_loop(ROWS, size, body, 0)

    def norm_one(self):
        for c in range(D // LANES):
            lanes = slice(c * LANES, (c + 1) * LANES)

            def put(cell, value):
                rows = pl.ds(pl.multiple_of(cell * SLOTS, SLOTS), SLOTS)
                self.first[rows, lanes] = self.first[rows, lanes] + value + self.small[8:9, lanes]

            def tap(a, b):
                t = 13 + (a + 1) * 3 + b + 1
                return self.small[t : t + 1, lanes]

            conv(self.pos_src, 1, tap, 1, lanes, put)

        def body(r0, _):
            rows = pl.ds(r0, 16)
            n, u, inv = norm_rows(self.first[rows, :], self.row(0), self.row(1))
            self.n1[rows, :] = n.astype(BF16)
            self.u1[rows, :] = u
            self.inv1[rows, :] = jnp.broadcast_to(inv, (16, LANES))
            return 0

        rows_loop(ROWS, 16, body, 0, unroll=5)

    def project(self):
        for b in range(2):
            cols = lane_block(b)
            self.q[:, cols] = (self.times(self.n1[...], 0, b) + self.small[2:3, cols]).astype(BF16)
            self.k[:, cols] = self.times(self.n1[...], 1, b).astype(BF16)
            self.v[:, cols] = (self.times(self.n1[...], 2, b) + self.small[3:4, cols]).astype(BF16)

    def image_sum(self, x):
        total = jnp.zeros((SLOTS, D), F32)
        for i in range(IMG_GROUP):
            im = wide(self.im8[i])
            total = total + im * jnp.sum(im * x, axis=0, keepdims=True)
        return total

    def softmax(self):
        def top(r0, best):
            live = wide(self.live[pl.ds(r0, 16), :])
            keys = jnp.where(live > 0, self.k[pl.ds(r0, 16), :].astype(F32), NEG_LARGE)
            return jnp.maximum(best, jnp.max(keys.reshape(2, SLOTS, D), axis=0))

        best = rows_loop(ROWS, 16, top, jnp.full((SLOTS, D), NEG_LARGE, F32), unroll=5)
        shift = jnp.zeros((SLOTS, D), F32)
        for i in range(IMG_GROUP):
            im = wide(self.im8[i])
            most = jnp.max(jnp.where(im > 0, best, NEG_LARGE), axis=0, keepdims=True)
            shift = jnp.where(im > 0, most, shift)
        shift2 = jnp.concatenate([shift, shift], axis=0)

        def raise_(r0, total):
            rows = pl.ds(r0, 16)
            live = wide(self.live[rows, :])
            keys = self.k[rows, :].astype(F32)
            e = jnp.where(live > 0, jnp.exp(jnp.where(live > 0, keys - shift2, 0.0)), 0.0)
            self.soft[rows, :] = e
            return total + fold(e)

        total = self.image_sum(
            rows_loop(ROWS, 16, raise_, jnp.zeros((SLOTS, D), F32), unroll=5)
        )
        scale = 1.0 / jnp.where(total > 0, total, 1.0)
        scale2 = jnp.concatenate([scale, scale], axis=0)

        def divide(r0, _):
            rows = pl.ds(r0, 16)
            soft = self.soft[rows, :] * scale2
            self.soft[rows, :] = soft
            self.soft_low[rows, :] = soft.astype(BF16)
            return 0

        rows_loop(ROWS, 16, divide, 0, unroll=5)

    def by_image(self, x):
        tiles = x.reshape(ROWS // 16, 16, WIDE)
        parts = []
        for i in range(IMG_GROUP):
            im = jnp.concatenate([self.im16[i]] * (WIDE // LANES), axis=1)
            parts.append((tiles * im[None]).reshape(ROWS, WIDE))
        return jnp.concatenate(parts, axis=1)

    def head_blocks(self, x):
        r = lax.broadcasted_iota(jnp.int32, x.shape, 0) // HEAD_DIM
        c = (lax.broadcasted_iota(jnp.int32, x.shape, 1) % WIDE) // HEAD_DIM
        return jnp.where(r == c, x, 0.0).astype(BF16)

    def stacked(self, x):
        return jnp.concatenate([x[:, lane_block(i)] for i in range(IMG_GROUP)], axis=0)

    def attend(self):
        for b in range(2):
            cols = lane_block(b)
            ctx = dot(self.soft_low[:, cols], self.by_image(self.v[:, cols]), TN)
            ctx = self.head_blocks(ctx)
            self.ctx[b] = ctx
            self.factor[:, cols] = dot(self.by_image(self.q[:, cols]), self.stacked(ctx))

        def fill(r0, _):
            rows = pl.ds(r0, 16)
            v = self.v[rows, :].astype(F32) * wide(self.live[rows, :])
            c0 = r0 // SLOTS
            self.rel_src[pl.ds(HALO * GRID + c0, 2)] = v.reshape(2, SLOTS, D)
            return 0

        rows_loop(ROWS, 16, fill, 0, unroll=5)
        for c in range(D // LANES):
            lanes = slice(c * LANES, (c + 1) * LANES)

            def put(cell, value):
                rows = pl.ds(pl.multiple_of(cell * SLOTS, SLOTS), SLOTS)
                self.rel[rows, lanes] = value

            def tap(a, b):
                t = (a + HALO) * WINDOW + b + HALO
                return self.rel_taps[t : t + 1, lanes]

            conv(self.rel_src, HALO, tap, REACHES[c], lanes, put)
        self.rel[CELLS * SLOTS :, :] = jnp.zeros((SLOTS, D), F32)

        def mix(r0, _):
            rows = pl.ds(r0, 16)
            m = self.factor[rows, :] * INV_SCALE + self.q[rows, :].astype(F32) * self.rel[rows, :]
            self.mixed[rows, :] = (m * wide(self.live[rows, :])).astype(BF16)
            return 0

        rows_loop(ROWS, 16, mix, 0, unroll=5)

    def norm_two(self):
        for b in range(2):
            cols = lane_block(b)
            p = self.times_t(self.mixed[...], 3, b)
            self.second[:, cols] = self.first[:, cols] + p + self.small[4:5, cols]

        def body(r0, _):
            rows = pl.ds(r0, 16)
            n, u, inv = norm_rows(self.second[rows, :], self.row(5), self.row(6))
            self.n2[rows, :] = n.astype(BF16)
            self.u2[rows, :] = u
            self.inv2[rows, :] = jnp.broadcast_to(inv, (16, LANES))
            return 0

        rows_loop(ROWS, 16, body, 0, unroll=5)

    def up(self, r):
        for b in range(2):
            cols = lane_block(b)
            h = self.times(self.n2[...], 4 + r, b) + self.small[pl.ds(9 + r, 1), cols]
            self.slope[r, :, cols] = h

        def body(r0, _):
            rows = pl.ds(r0, 16)
            act, slope = erf_parts(self.slope[r, rows, :])
            self.active[r, rows, :] = act.astype(BF16)
            self.slope[r, rows, :] = slope
            return 0

        rows_loop(ROWS, 16, body, 0, unroll=5)

    def down(self, r):
        for b in range(2):
            cols = lane_block(b)
            self.second[:, cols] += self.times_t(self.active[r], 8 + r, b)

    def finish_out(self):
        def body(r0, _):
            rows = pl.ds(r0, 16)
            self.low[rows, :] = (self.second[rows, :] + self.row(7)).astype(BF16)
            return 0

        rows_loop(ROWS, 16, body, 0, unroll=5)
        self.unplace(self.low, self.out)

    def grad_hidden(self, r):
        go = self.go[...]
        for b in range(2):
            cols = lane_block(b)
            self.factor[:, cols] = self.times(go, 8 + r, b)

        def body(r0, total):
            rows = pl.ds(r0, 16)
            g = self.factor[rows, :] * self.slope[r, rows, :]
            self.low[rows, :] = g.astype(BF16)
            return total + fold(g)

        total = rows_loop(ROWS, 16, body, jnp.zeros((SLOTS, D), F32), unroll=5)
        self.sums[pl.ds(9 + r, 1), :] = jnp.sum(total, axis=0, keepdims=True)

    def back_mlp(self, r):
        self.grad_hidden(r)
        self.put_grad(8 + r, self.go_t[...], self.active[r])
        self.put_grad(4 + r, self.n2_t[...], self.low[...])
        for b in range(2):
            cols = lane_block(b)
            self.back[:, cols] += self.times_t(self.low[...], 4 + r, b)

    def back_two(self):
        zero = jnp.zeros((SLOTS, D), F32)

        def body(r0, sums):
            rows = pl.ds(r0, 16)
            back, u = self.back[rows, :], self.u2[rows, :]
            go = self.go[rows, :].astype(F32)
            gs = go + norm_back(back, u, wide(self.inv2[rows, :]), self.row(5))
            self.second[rows, :] = gs
            self.low[rows, :] = gs.astype(BF16)
            new = (gs, back * u, back, go)
            return tuple(s + fold(n) for s, n in zip(sums, new, strict=True))

        sums = rows_loop(ROWS, 16, body, (zero,) * 4, unroll=5)
        for j, s in zip((4, 5, 6, 7), sums, strict=True):
            self.sums[j : j + 1, :] = jnp.sum(s, axis=0, keepdims=True)

    def back_attend(self):
        self.put_grad(3, self.low[...].T, self.mixed[...])
        for b in range(2):
            cols = lane_block(b)
            self.factor[:, cols] = self.times(self.low[...], 3, b)

        def fill(r0, _):
            rows = pl.ds(r0, 16)
            d = self.factor[rows, :] * wide(self.live[rows, :])
            self.factor[rows, :] = d
            self.f[rows, :] = (d * INV_SCALE).astype(BF16)
            c0 = r0 // SLOTS
            dq = d * self.q[rows, :].astype(F32)
            self.dq_src[pl.ds(HALO * GRID + c0, 2)] = dq.reshape(2, SLOTS, D)
            return 0

        rows_loop(ROWS, 16, fill, 0, unroll=5)
        for b in range(2):
            cols = lane_block(b)
            f3 = self.by_image(self.f[:, cols])
            g = self.head_blocks(dot(self.q[:, cols], f3, TN))
            self.gq[:, cols] = dot(f3, self.ctx[b], NT)
            self.gk[:, cols] = dot(self.by_image(self.v[:, cols]), g, NT)
            self.gv[:, cols] = dot(self.by_image(self.soft_low[:, cols]), self.stacked(g))

        for c in range(D // LANES):
            lanes = slice(c * LANES, (c + 1) * LANES)

            def put(cell, value):
                rows = pl.ds(pl.multiple_of(cell * SLOTS, SLOTS), SLOTS)
                self.gv[rows, lanes] = self.gv[rows, lanes] + value * self.live[rows, :]

            def tap(a, b):
                t = (HALO - a) * WINDOW + HALO - b
                return self.rel_taps[t : t + 1, lanes]

            conv(self.dq_src, HALO, tap, REACHES[c], lanes, put)

            def up(cell):
                return self.dq_src[HALO * GRID + cell, :, lanes]

            def put_tap(a, b, value):
                t = (a + HALO) * WINDOW + b + HALO
                keep = self.window[t : t + 1, lanes]
                self.sums[22 + t : 23 + t, lanes] = value * keep

            tap_sums(up, self.rel_src, HALO, REACHES[c], lanes, put_tap)

        zero = jnp.zeros((SLOTS, D), F32)

        def inner(r0, total):
            rows = pl.ds(r0, 16)
            return total + fold(self.soft[rows, :] * self.gk[rows, :])

        shared = self.image_sum(rows_loop(ROWS, 16, inner, zero, unroll=5))
        shared2 = jnp.concatenate([shared, shared], axis=0)

        def low(r0, sums):
            rows = pl.ds(r0, 16)
            gq = self.gq[rows, :] + self.factor[rows, :] * self.rel[rows, :]
            gk = self.soft[rows, :] * (self.gk[rows, :] - shared2)
            gv = self.gv[rows, :]
            self.gl[0, rows, :] = gq.astype(BF16)
            self.gl[1, rows, :] = gk.astype(BF16)
            self.gl[2, rows, :] = gv.astype(BF16)
            return sums[0] + fold(gq), sums[1] + fold(gv)

        sums = rows_loop(ROWS, 16, low, (zero, zero), unroll=5)
        for j, s in zip((2, 3), sums, strict=True):
            self.sums[j : j + 1, :] = jnp.sum(s, axis=0, keepdims=True)

    def back_project(self):
        n1_t = self.n1[...].T
        for k in range(3):
            self.put_grad(k, n1_t, self.gl[k])
        for b in range(2):
            cols = lane_block(b)
            back = self.times_t(self.gl[0], 0, b)
            back = back + self.times_t(self.gl[1], 1, b)
            self.back[:, cols] = back + self.times_t(self.gl[2], 2, b)

    def back_one(self):
        zero = jnp.zeros((SLOTS, D), F32)
        self.pos_up[0:GRID] = jnp.zeros((GRID, SLOTS, D), F32)
        self.pos_up[GRID + CELLS :] = jnp.zeros((GRID, SLOTS, D), F32)

        def body(r0, sums):
            rows = pl.ds(r0, 16)
            back, u = self.back[rows, :], self.u1[rows, :]
            gf = self.second[rows, :] + norm_back(back, u, wide(self.inv1[rows, :]), self.row(0))
            c0 = r0 // SLOTS
            self.pos_up[pl.ds(GRID + c0, 2)] = gf.reshape(2, SLOTS, D)
            new = (back * u, back, gf)
            return tuple(s + fold(n) for s, n in zip(sums, new, strict=True))

        sums = rows_loop(ROWS, 16, body, (zero,) * 3, unroll=5)
        for j, s in zip((0, 1, 8), sums, strict=True):
            self.sums[j : j + 1, :] = jnp.sum(s, axis=0, keepdims=True)
        for c in range(D // LANES):
            lanes = slice(c * LANES, (c + 1) * LANES)

            def put(cell, value):
                rows = pl.ds(pl.multiple_of(cell * SLOTS, SLOTS), SLOTS)
                gf = self.pos_up[GRID + cell, :, lanes]
                self.first[rows, lanes] = gf + value * self.live[rows, :]

            def tap(a, b):
                t = 13 + (1 - a) * 3 + 1 - b
                return self.small[t : t + 1, lanes]

            conv(self.pos_up, 1, tap, 1, lanes, put)

            def up(cell):
                return self.pos_up[GRID + cell, :, lanes]

            def put_tap(a, b, value):
                t = 13 + (a + 1) * 3 + b + 1
                self.sums[t : t + 1, lanes] = value

            tap_sums(up, self.pos_src, 1, 1, lanes, put_tap)

        def down(r0, _):
            rows = pl.ds(r0, 16)
            self.low[rows, :] = self.first[rows, :].astype(BF16)
            return 0

        rows_loop(ROWS, 16, down, 0, unroll=5)
        self.unplace(self.low, self.grad_in)


def scratch_of():
    f, h = (ROWS, D), (ROWS, LANES)
    halo3 = ((GRID + 2 * HALO) * GRID, SLOTS, D)
    halo1 = ((GRID + 2) * GRID, SLOTS, D)
    return {
        "live": (h, F32),
        "im8": ((IMG_GROUP, SLOTS, LANES), F32),
        "im16": ((IMG_GROUP, 16, LANES), BF16),
        "window": ((WINDOW * WINDOW, D), F32),
        "rel_taps": ((WINDOW * WINDOW, D), F32),
        "pos_src": (halo1, F32),
        "pos_up": (halo1, F32),
        "rel_src": (halo3, F32),
        "dq_src": (halo3, F32),
        "first": (f, F32),
        "u1": (f, F32),
        "inv1": (h, F32),
        "second": (f, F32),
        "u2": (f, F32),
        "inv2": (h, F32),
        "n1": (f, BF16),
        "n2": (f, BF16),
        "n2_t": ((D, ROWS), BF16),
        "go": (f, BF16),
        "go_t": ((D, ROWS), BF16),
        "q": (f, BF16),
        "k": (f, BF16),
        "v": (f, BF16),
        "soft": (f, F32),
        "soft_low": (f, BF16),
        "ctx": ((2, WIDE, IMG_GROUP * WIDE), BF16),
        "factor": (f, F32),
        "rel": (f, F32),
        "mixed": (f, BF16),
        "slope": ((4, ROWS, D), F32),
        "active": ((4, ROWS, D), BF16),
        "low": (f, BF16),
        "back": (f, F32),
        "f": (f, BF16),
        "gq": (f, F32),
        "gk": (f, F32),
        "gv": (f, F32),
        "gl": ((3, ROWS, D), BF16),
    }


def run_block(blk):
    blk.setup()
    blk.read()
    blk.norm_one()
    blk.project()
    blk.softmax()
    blk.attend()
    blk.norm_two()

    def forward(r, _):
        blk.up(r)
        blk.down(r)
        return 0

    lax.fori_loop(0, 4, forward, 0)
    blk.finish_out()
    blk.n2_t[...] = blk.n2[...].T
    blk.go_t[...] = blk.go[...].T
    blk.back[...] = jnp.zeros((ROWS, D), F32)

    def backward(r, _):
        blk.back_mlp(r)
        return 0

    lax.fori_loop(0, 4, backward, 0)
    blk.back_two()
    blk.back_attend()
    blk.back_project()
    blk.back_one()


def block_kernel(cls, img, tokens, cot, w, small, out, grad_in, g, sums, *scratch):
    refs = {"cls": cls, "img": img, "tokens": tokens, "cot": cot, "w": w, "small": small}
    refs.update({"out": out, "grad_in": grad_in, "g": g, "sums": sums})
    refs.update(zip(scratch_of(), scratch, strict=True))
    run_block(Block(refs))


def block_call(cls, img, tokens, cot, w, small):
    own = cls.shape[1] * CELLS
    smem = pl.BlockSpec(memory_space=pltpu.SMEM)
    vmem = pl.BlockSpec(memory_space=pltpu.VMEM)
    return pl.pallas_call(
        block_kernel,
        out_shape=(
            jax.ShapeDtypeStruct((own, D), BF16),
            jax.ShapeDtypeStruct((own, D), BF16),
            jax.ShapeDtypeStruct(w.shape, BF16),
            jax.ShapeDtypeStruct(small.shape, F32),
        ),
        in_specs=[smem, smem, vmem, vmem, vmem, vmem],
        out_specs=(vmem,) * 4,
        scratch_shapes=[pltpu.VMEM(*v) for v in scratch_of().values()],
        compiler_params=pltpu.CompilerParams(vmem_limit_bytes=63 << 20),
        name="block",
    )(cls, img, tokens, cot, w, small)


def local(
    tokens,
    cotangent,
    crop_image,
    crop_class,
    weights,
    row_state,
    col_state,
    weights_ema,
    small_params,
    small_state,
    small_ema,
):
    heads, parts = lax.axis_size("head"), lax.axis_size("dp")
    both = ("head", "dp")
    w = lax.all_gather(weights.astype(BF16), both, axis=0, tiled=False)
    w = w.reshape(heads, parts, *weights.shape)
    out, grad_in, g, sums = block_call(crop_class, crop_image, tokens, cotangent, w, small_params)
    out = lax.all_gather(out, "head", axis=0, tiled=True)
    grad_in = lax.all_gather(grad_in, "head", axis=0, tiled=True)
    g = g.reshape(heads * parts, *weights.shape)
    weight_grad = lax.all_to_all(g, both, split_axis=0, concat_axis=0, tiled=True)
    weight_grad = weight_grad.astype(F32).sum(axis=0)
    small_total = lax.psum(sums, ("dp", "head"))
    squares = weight_grad * weight_grad + SQUARE_FLOOR
    row_total = lax.psum(jnp.sum(squares, axis=2), "head")
    new_rows = SECOND_DECAY * row_state + (1.0 - SECOND_DECAY) * (row_total / D)
    col_total, row_mass = lax.psum((jnp.sum(squares, axis=1), jnp.sum(new_rows, axis=1)), "dp")
    new_cols = SECOND_DECAY * col_state + (1.0 - SECOND_DECAY) * (col_total / D)
    estimate = new_rows[:, :, None] * new_cols[:, None, :] / (row_mass / D)[:, None, None]
    update = weight_grad * lax.rsqrt(estimate)
    update_sq = lax.psum(jnp.sum(update * update, axis=(1, 2)), ("dp", "head"))
    update_rms = jnp.sqrt(update_sq / (D * D))
    new_weights = weights - STEP_RATE * update / jnp.maximum(1.0, update_rms)[:, None, None]
    new_ema = AVERAGE_KEEP * weights_ema + (1.0 - AVERAGE_KEEP) * new_weights
    new_small_state = SECOND_DECAY * small_state + (1.0 - SECOND_DECAY) * (
        small_total * small_total + SQUARE_FLOOR
    )
    small_update = small_total * lax.rsqrt(new_small_state)
    small_rms = jnp.sqrt(jnp.mean(small_update * small_update, axis=1))
    new_small = small_params - SMALL_RATE * small_update / jnp.maximum(1.0, small_rms)[:, None]
    new_small_ema = AVERAGE_KEEP * small_ema + (1.0 - AVERAGE_KEEP) * new_small
    return (
        out,
        grad_in,
        weight_grad,
        new_rows,
        new_cols,
        new_weights,
        new_weights.astype(BF16),
        new_ema,
        small_total,
        new_small_state,
        new_small,
        new_small_ema,
        jnp.concatenate([update_rms, small_rms]),
    )


def solution(mesh):
    in_specs = (
        P("dp", None),
        P("dp", None),
        P("dp", None),
        P("dp", None),
        P(None, "dp", "head"),
        P(None, "dp"),
        P(None, "head"),
        P(None, "dp", "head"),
        P(),
        P(),
        P(),
    )
    out_specs = (
        P("dp", None),
        P("dp", None),
        P(None, "dp", "head"),
        P(None, "dp"),
        P(None, "head"),
        P(None, "dp", "head"),
        P(None, "dp", "head"),
        P(None, "dp", "head"),
        P(),
        P(),
        P(),
        P(),
        P(),
    )
    return jax.shard_map(local, mesh=mesh, in_specs=in_specs, out_specs=out_specs, check_vma=False)
```

```python
import math

import jax
import jax.numpy as jnp
from jax import lax
from jax.experimental import pallas as pl
from jax.experimental.pallas import tpu as pltpu
from jax.sharding import PartitionSpec as P

D = 512
HEAD_DIM = 64
GRID = 7
SMALL_GRID = 3
WINDOW = 7
IMG_GROUP = 3
CELLS = GRID * GRID
SLOTS = 8
CELL_PAD = CELLS + 1
ROWS = CELL_PAD * SLOTS
LANES = 128
WIDE = 256
REACHES = (1, 2, 3, 3)
HALO = WINDOW // 2

NORM_EPS = 1e-06
SQUARE_FLOOR = 1e-30
SECOND_DECAY = 0.999
STEP_RATE = 0.02
SMALL_RATE = 0.05
AVERAGE_KEEP = 0.9
NEG_LARGE = -1e30
ROOT_HALF = 0.7071067811865476
INV_ROOT_TAU = 0.3989422804014327
INV_SCALE = 1.0 / math.sqrt(HEAD_DIM)

F32 = jnp.float32
BF16 = jnp.bfloat16
NN = (((1,), (0,)), ((), ()))
NT = (((1,), (1,)), ((), ()))
TN = (((0,), (0,)), ((), ()))


def dot(a, b, dims=NN):
    return lax.dot_general(a, b, dims, preferred_element_type=F32)


def lane_block(b):
    return slice(b * WIDE, (b + 1) * WIDE)


def wide(col):
    return jnp.concatenate([col] * (D // LANES), axis=1)


def rows_loop(count, size, body, init=None, unroll=1):
    def step(j, carry):
        return body(pl.multiple_of(j * size, size), carry)

    return lax.fori_loop(0, count // size, step, init, unroll=unroll)


def conv(src, halo, tap, reach, lanes, put):
    def line(y, _):
        sums = [jnp.zeros((SLOTS, LANES), F32) for _ in range(GRID)]
        for a in range(-reach, reach + 1):
            base = (y + (a + halo)) * GRID
            cells = [src[base + x, :, lanes] for x in range(GRID)]
            for b in range(-reach, reach + 1):
                t = tap(a, b)
                for x in range(GRID):
                    if 0 <= x + b < GRID:
                        sums[x] = sums[x] + t * cells[x + b]
        for x in range(GRID):
            put(y * GRID + x, sums[x])
        return 0

    lax.fori_loop(0, GRID, line, 0)


def tap_sums(up, src, halo, reach, lanes, put):
    for a in range(-reach, reach + 1):

        def line(y, sums):
            sums = list(sums)
            ups = [up(y * GRID + x) for x in range(GRID)]
            base = (y + (a + halo)) * GRID
            cells = [src[base + x, :, lanes] for x in range(GRID)]
            for i, b in enumerate(range(-reach, reach + 1)):
                for x in range(GRID):
                    if 0 <= x + b < GRID:
                        sums[i] = sums[i] + ups[x] * cells[x + b]
            return tuple(sums)

        start = tuple(jnp.zeros((SLOTS, LANES), F32) for _ in range(2 * reach + 1))
        sums = lax.fori_loop(0, GRID, line, start)
        for i, b in enumerate(range(-reach, reach + 1)):
            put(a, b, jnp.sum(sums[i], axis=0, keepdims=True))


def fold(x):
    return jnp.sum(x.reshape(x.shape[0] // SLOTS, SLOTS, x.shape[1]), axis=0)


def erf_parts(h):
    e = lax.erf(h * ROOT_HALF)
    half = 0.5 * (1.0 + e)
    return h * half, half + h * jnp.exp(-0.5 * h * h) * INV_ROOT_TAU


def norm_rows(v, gain, shift):
    centre = jnp.sum(v, axis=1, keepdims=True) * (1.0 / D)
    offset = v - centre
    spread = jnp.sum(offset * offset, axis=1, keepdims=True) * (1.0 / D)
    inverse = lax.rsqrt(spread + NORM_EPS)
    unit = offset * inverse
    return unit * gain + shift, unit, inverse


def norm_back(up, unit, inverse, gain):
    z = up * gain
    mean_z = jnp.sum(z, axis=1, keepdims=True) * (1.0 / D)
    mean_zu = jnp.sum(z * unit, axis=1, keepdims=True) * (1.0 / D)
    return inverse * (z - mean_z - unit * mean_zu)


class Block:
    def __init__(self, refs):
        self.__dict__.update(refs)

    def matrix(self, k, lo, hi):
        parts = []
        for h in range(lo, hi):
            part = self.w[h // 2, h % 2, :, :, k]
            if part.shape[-2] % 16:
                part = part.astype(F32).reshape(D, LANES).astype(BF16)
            else:
                part = part.reshape(D, LANES)
            parts.append(part)
        return jnp.concatenate(parts, axis=1)

    def times(self, lhs, k, b):
        return dot(lhs, self.matrix(k, 2 * b, 2 * b + 2))

    def times_t(self, lhs, k, b):
        return dot(lhs, self.matrix(k, 0, 4)[lane_block(b), :], NT)

    def put_grad(self, k, lhs_t, rhs):
        for b in range(2):
            g = dot(lhs_t, rhs[:, lane_block(b)])
            for i in range(2):
                piece = g[:, i * LANES : (i + 1) * LANES]
                parts, two, _, rows, _ = self.g.shape[2:]
                piece = piece.reshape(parts, two, rows, LANES)
                self.g[b, i, :, :, k] = piece.astype(BF16)

    def row(self, j):
        return self.small[j : j + 1, :]

    def setup(self):
        head = lax.axis_index("head")
        slots = self.cls.shape[1]
        self.sums[...] = jnp.zeros(self.sums.shape, F32)
        sub = lax.broadcasted_iota(jnp.int32, (SLOTS, LANES), 0)
        valid = jnp.where(sub < slots, 1.0, 0.0)
        full = jnp.zeros((SLOTS, LANES), F32)
        images = [jnp.zeros((SLOTS, LANES), F32) for _ in range(IMG_GROUP)]
        for s in range(slots):
            full = jnp.where(sub == s, jnp.where(self.cls[head, s] == 0, 1.0, 0.0), full)
            for i in range(IMG_GROUP):
                images[i] = jnp.where(
                    sub == s, jnp.where(self.img[head, s] == i, 1.0, 0.0), images[i]
                )
        for cell in range(CELLS):
            small = cell // GRID < SMALL_GRID and cell % GRID < SMALL_GRID
            self.live[cell * SLOTS : (cell + 1) * SLOTS, :] = valid if small else full
        self.live[CELLS * SLOTS :, :] = jnp.zeros((SLOTS, LANES), F32)
        for i in range(IMG_GROUP):
            self.im8[i] = images[i]
            self.im16[i] = jnp.concatenate([images[i], images[i]], axis=0).astype(BF16)
        self.pos_src[0:GRID] = jnp.zeros((GRID, SLOTS, D), F32)
        self.pos_src[GRID + CELLS :] = jnp.zeros((GRID, SLOTS, D), F32)
        for pad in (self.rel_src, self.dq_src):
            pad[0 : HALO * GRID] = jnp.zeros((HALO * GRID, SLOTS, D), F32)
            pad[HALO * GRID + CELLS :] = jnp.zeros((HALO * GRID, SLOTS, D), F32)
        tap = lax.broadcasted_iota(jnp.int32, (WINDOW * WINDOW, 1), 0)
        row_off = jnp.abs(tap // WINDOW - HALO)
        col_off = jnp.abs(tap % WINDOW - HALO)
        off = jnp.maximum(row_off, col_off)
        heads = lax.broadcasted_iota(jnp.int32, (1, D), 1) // HEAD_DIM
        reach = jnp.where(heads < 2, 1, jnp.where(heads < 5, 2, 3))
        mask = jnp.where(off <= reach, 1.0, 0.0)
        self.window[...] = mask
        self.rel_taps[...] = self.small[22 : 22 + WINDOW * WINDOW, :] * mask

    def place(self, rows_ref, first, r0, size):
        count = rows_ref.shape[0]
        r = r0 + lax.broadcasted_iota(jnp.int32, (size, 1), 0)
        cell, slot = r >> 3, r & 7
        want = first + slot * CELLS + cell
        want = jnp.where((slot < self.cls.shape[1]) & (cell < CELLS), want, -1)
        col = lax.broadcasted_iota(jnp.int32, (size, count), 1)
        pick = jnp.where(col == want, 1.0, 0.0).astype(BF16)
        return dot(pick, rows_ref[...])

    def unplace(self, src_ref, out_ref):
        count = out_ref.shape[0]
        r = lax.broadcasted_iota(jnp.int32, (1, ROWS), 1)
        cell, slot = r >> 3, r & 7
        target = jnp.where((slot < self.cls.shape[1]) & (cell < CELLS), slot * CELLS + cell, -1)
        t = lax.broadcasted_iota(jnp.int32, (count, ROWS), 0)
        pick = jnp.where(t == target, 1.0, 0.0).astype(BF16)
        out_ref[...] = dot(pick, src_ref[...]).astype(BF16)

    def read(self):
        first = lax.axis_index("head") * (self.cls.shape[1] * CELLS)
        size = 80

        def body(r0, _):
            live = wide(self.live[pl.ds(r0, size), :])
            x = self.place(self.tokens, first, r0, size)
            self.first[pl.ds(r0, size), :] = x
            c0 = r0 // SLOTS
            self.pos_src[pl.ds(GRID + c0, size // SLOTS)] = (x * live).reshape(-1, SLOTS, D)
            c = self.place(self.cot, first, r0, size)
            self.go[pl.ds(r0, size), :] = (c * live).astype(BF16)
            return 0

        rows_loop(ROWS, size, body, 0)

    def norm_one(self):
        for c in range(D // LANES):
            lanes = slice(c * LANES, (c + 1) * LANES)

            def put(cell, value):
                rows = pl.ds(pl.multiple_of(cell * SLOTS, SLOTS), SLOTS)
                self.first[rows, lanes] = self.first[rows, lanes] + value + self.small[8:9, lanes]

            def tap(a, b):
                t = 13 + (a + 1) * 3 + b + 1
                return self.small[t : t + 1, lanes]

            conv(self.pos_src, 1, tap, 1, lanes, put)

        def body(r0, _):
            rows = pl.ds(r0, 16)
            n, u, inv = norm_rows(self.first[rows, :], self.row(0), self.row(1))
            self.n1[rows, :] = n.astype(BF16)
            self.u1[rows, :] = u
            self.inv1[rows, :] = jnp.broadcast_to(inv, (16, LANES))
            return 0

        rows_loop(ROWS, 16, body, 0, unroll=5)

    def project(self, k):
        low = (self.q, self.k, self.v)[k]
        for b in range(2):
            cols = lane_block(b)
            p = self.times(self.n1[...], k, b)
            if k != 1:
                p = p + self.small[2 + k // 2 : 3 + k // 2, cols]
            low[:, cols] = p.astype(BF16)

    def image_sum(self, x):
        total = jnp.zeros((SLOTS, D), F32)
        for i in range(IMG_GROUP):
            im = wide(self.im8[i])
            total = total + im * jnp.sum(im * x, axis=0, keepdims=True)
        return total

    def softmax(self):
        def top(r0, best):
            live = wide(self.live[pl.ds(r0, 16), :])
            keys = jnp.where(live > 0, self.k[pl.ds(r0, 16), :].astype(F32), NEG_LARGE)
            return jnp.maximum(best, jnp.max(keys.reshape(2, SLOTS, D), axis=0))

        best = rows_loop(ROWS, 16, top, jnp.full((SLOTS, D), NEG_LARGE, F32), unroll=5)
        shift = jnp.zeros((SLOTS, D), F32)
        for i in range(IMG_GROUP):
            im = wide(self.im8[i])
            most = jnp.max(jnp.where(im > 0, best, NEG_LARGE), axis=0, keepdims=True)
            shift = jnp.where(im > 0, most, shift)
        shift2 = jnp.concatenate([shift, shift], axis=0)

        def raise_(r0, total):
            rows = pl.ds(r0, 16)
            live = wide(self.live[rows, :])
            keys = self.k[rows, :].astype(F32)
            e = jnp.where(live > 0, jnp.exp(jnp.where(live > 0, keys - shift2, 0.0)), 0.0)
            self.soft[rows, :] = e
            return total + fold(e)

        total = self.image_sum(
            rows_loop(ROWS, 16, raise_, jnp.zeros((SLOTS, D), F32), unroll=5)
        )
        scale = 1.0 / jnp.where(total > 0, total, 1.0)
        scale2 = jnp.concatenate([scale, scale], axis=0)

        def divide(r0, _):
            rows = pl.ds(r0, 16)
            soft = self.soft[rows, :] * scale2
            self.soft[rows, :] = soft
            self.soft_low[rows, :] = soft.astype(BF16)
            return 0

        rows_loop(ROWS, 16, divide, 0, unroll=5)

    def by_image(self, x):
        tiles = x.reshape(ROWS // 16, 16, WIDE)
        parts = []
        for i in range(IMG_GROUP):
            im = jnp.concatenate([self.im16[i]] * (WIDE // LANES), axis=1)
            parts.append((tiles * im[None]).reshape(ROWS, WIDE))
        return jnp.concatenate(parts, axis=1)

    def head_blocks(self, x):
        r = lax.broadcasted_iota(jnp.int32, x.shape, 0) // HEAD_DIM
        c = (lax.broadcasted_iota(jnp.int32, x.shape, 1) % WIDE) // HEAD_DIM
        return jnp.where(r == c, x, 0.0).astype(BF16)

    def stacked(self, x):
        return jnp.concatenate([x[:, lane_block(i)] for i in range(IMG_GROUP)], axis=0)

    def attend(self):
        for b in range(2):
            cols = lane_block(b)
            ctx = dot(self.soft_low[:, cols], self.by_image(self.v[:, cols]), TN)
            ctx = self.head_blocks(ctx)
            self.ctx[b] = ctx
            self.factor[:, cols] = dot(self.by_image(self.q[:, cols]), self.stacked(ctx))

        def fill(r0, _):
            rows = pl.ds(r0, 16)
            v = self.v[rows, :].astype(F32) * wide(self.live[rows, :])
            c0 = r0 // SLOTS
            self.rel_src[pl.ds(HALO * GRID + c0, 2)] = v.reshape(2, SLOTS, D)
            return 0

        rows_loop(ROWS, 16, fill, 0, unroll=5)
        for c in range(D // LANES):
            lanes = slice(c * LANES, (c + 1) * LANES)

            def put(cell, value):
                rows = pl.ds(pl.multiple_of(cell * SLOTS, SLOTS), SLOTS)
                self.rel[rows, lanes] = value

            def tap(a, b):
                t = (a + HALO) * WINDOW + b + HALO
                return self.rel_taps[t : t + 1, lanes]

            conv(self.rel_src, HALO, tap, REACHES[c], lanes, put)
        self.rel[CELLS * SLOTS :, :] = jnp.zeros((SLOTS, D), F32)

        def mix(r0, _):
            rows = pl.ds(r0, 16)
            m = self.factor[rows, :] * INV_SCALE + self.q[rows, :].astype(F32) * self.rel[rows, :]
            self.mixed[rows, :] = (m * wide(self.live[rows, :])).astype(BF16)
            return 0

        rows_loop(ROWS, 16, mix, 0, unroll=5)

    def norm_two(self):
        for b in range(2):
            cols = lane_block(b)
            p = self.times_t(self.mixed[...], 3, b)
            self.second[:, cols] = self.first[:, cols] + p + self.small[4:5, cols]

        def body(r0, _):
            rows = pl.ds(r0, 16)
            n, u, inv = norm_rows(self.second[rows, :], self.row(5), self.row(6))
            self.n2[rows, :] = n.astype(BF16)
            self.u2[rows, :] = u
            self.inv2[rows, :] = jnp.broadcast_to(inv, (16, LANES))
            return 0

        rows_loop(ROWS, 16, body, 0, unroll=5)

    def mlp(self, r):
        up, down = 4 + 2 * r, 5 + 2 * r
        for b in range(2):
            cols = lane_block(b)
            h = self.times(self.n2[...], up, b) + self.small[pl.ds(9 + r, 1), cols]
            self.hidden[:, cols] = h
            self.factor[:, cols] = self.times(self.go[...], down, b)

        def body(r0, total):
            rows = pl.ds(r0, 16)
            act, slope = erf_parts(self.hidden[rows, :])
            g = self.factor[rows, :] * slope
            self.active[rows, :] = act.astype(BF16)
            self.low[rows, :] = g.astype(BF16)
            return total + fold(g)

        total = rows_loop(ROWS, 16, body, jnp.zeros((SLOTS, D), F32), unroll=5)
        self.sums[pl.ds(9 + r, 1), :] = jnp.sum(total, axis=0, keepdims=True)
        self.put_grad(down, self.go_t[...], self.active)
        self.put_grad(up, self.n2_t[...], self.low)
        for b in range(2):
            cols = lane_block(b)
            self.second[:, cols] += self.times_t(self.active[...], down, b)
            self.back[:, cols] += self.times_t(self.low[...], up, b)

    def finish_out(self):
        def body(r0, _):
            rows = pl.ds(r0, 16)
            self.low[rows, :] = (self.second[rows, :] + self.row(7)).astype(BF16)
            return 0

        rows_loop(ROWS, 16, body, 0, unroll=5)
        self.unplace(self.low, self.out)

    def back_two(self):
        zero = jnp.zeros((SLOTS, D), F32)

        def body(r0, sums):
            rows = pl.ds(r0, 16)
            back, u = self.back[rows, :], self.u2[rows, :]
            go = self.go[rows, :].astype(F32)
            gs = go + norm_back(back, u, wide(self.inv2[rows, :]), self.row(5))
            self.second[rows, :] = gs
            self.low[rows, :] = gs.astype(BF16)
            new = (gs, back * u, back, go)
            return tuple(s + fold(n) for s, n in zip(sums, new, strict=True))

        sums = rows_loop(ROWS, 16, body, (zero,) * 4, unroll=5)
        for j, s in zip((4, 5, 6, 7), sums, strict=True):
            self.sums[j : j + 1, :] = jnp.sum(s, axis=0, keepdims=True)

    def back_attend(self):
        self.put_grad(3, self.low[...].T, self.mixed)
        for b in range(2):
            cols = lane_block(b)
            self.factor[:, cols] = self.times(self.low[...], 3, b)

        def fill(r0, _):
            rows = pl.ds(r0, 16)
            d = self.factor[rows, :] * wide(self.live[rows, :])
            self.factor[rows, :] = d
            self.f[rows, :] = (d * INV_SCALE).astype(BF16)
            c0 = r0 // SLOTS
            dq = d * self.q[rows, :].astype(F32)
            self.dq_src[pl.ds(HALO * GRID + c0, 2)] = dq.reshape(2, SLOTS, D)
            return 0

        rows_loop(ROWS, 16, fill, 0, unroll=5)
        for b in range(2):
            cols = lane_block(b)
            f3 = self.by_image(self.f[:, cols])
            g = self.head_blocks(dot(self.q[:, cols], f3, TN))
            self.gq[:, cols] = dot(f3, self.ctx[b], NT)
            self.gk[:, cols] = dot(self.by_image(self.v[:, cols]), g, NT)
            self.gv[:, cols] = dot(self.by_image(self.soft_low[:, cols]), self.stacked(g))

        for c in range(D // LANES):
            lanes = slice(c * LANES, (c + 1) * LANES)

            def put(cell, value):
                rows = pl.ds(pl.multiple_of(cell * SLOTS, SLOTS), SLOTS)
                self.gv[rows, lanes] = self.gv[rows, lanes] + value * self.live[rows, :]

            def tap(a, b):
                t = (HALO - a) * WINDOW + HALO - b
                return self.rel_taps[t : t + 1, lanes]

            conv(self.dq_src, HALO, tap, REACHES[c], lanes, put)

            def up(cell):
                return self.dq_src[HALO * GRID + cell, :, lanes]

            def put_tap(a, b, value):
                t = (a + HALO) * WINDOW + b + HALO
                keep = self.window[t : t + 1, lanes]
                self.sums[22 + t : 23 + t, lanes] = value * keep

            tap_sums(up, self.rel_src, HALO, REACHES[c], lanes, put_tap)

        zero = jnp.zeros((SLOTS, D), F32)

        def inner(r0, total):
            rows = pl.ds(r0, 16)
            return total + fold(self.soft[rows, :] * self.gk[rows, :])

        shared = self.image_sum(rows_loop(ROWS, 16, inner, zero, unroll=5))
        shared2 = jnp.concatenate([shared, shared], axis=0)

        def low(r0, sums):
            rows = pl.ds(r0, 16)
            gq = self.gq[rows, :] + self.factor[rows, :] * self.rel[rows, :]
            gk = self.soft[rows, :] * (self.gk[rows, :] - shared2)
            gv = self.gv[rows, :]
            self.gl[0, rows, :] = gq.astype(BF16)
            self.gl[1, rows, :] = gk.astype(BF16)
            self.gl[2, rows, :] = gv.astype(BF16)
            return sums[0] + fold(gq), sums[1] + fold(gv)

        sums = rows_loop(ROWS, 16, low, (zero, zero), unroll=5)
        for j, s in zip((2, 3), sums, strict=True):
            self.sums[j : j + 1, :] = jnp.sum(s, axis=0, keepdims=True)

    def back_project(self):
        n1_t = self.n1[...].T
        for k in range(3):
            self.put_grad(k, n1_t, self.gl.at[k])
        for b in range(2):
            cols = lane_block(b)
            back = self.times_t(self.gl[0], 0, b)
            back = back + self.times_t(self.gl[1], 1, b)
            self.back[:, cols] = back + self.times_t(self.gl[2], 2, b)

    def back_one(self):
        zero = jnp.zeros((SLOTS, D), F32)
        self.pos_up[0:GRID] = jnp.zeros((GRID, SLOTS, D), F32)
        self.pos_up[GRID + CELLS :] = jnp.zeros((GRID, SLOTS, D), F32)

        def body(r0, sums):
            rows = pl.ds(r0, 16)
            back, u = self.back[rows, :], self.u1[rows, :]
            gf = self.second[rows, :] + norm_back(back, u, wide(self.inv1[rows, :]), self.row(0))
            c0 = r0 // SLOTS
            self.pos_up[pl.ds(GRID + c0, 2)] = gf.reshape(2, SLOTS, D)
            new = (back * u, back, gf)
            return tuple(s + fold(n) for s, n in zip(sums, new, strict=True))

        sums = rows_loop(ROWS, 16, body, (zero,) * 3, unroll=5)
        for j, s in zip((0, 1, 8), sums, strict=True):
            self.sums[j : j + 1, :] = jnp.sum(s, axis=0, keepdims=True)
        for c in range(D // LANES):
            lanes = slice(c * LANES, (c + 1) * LANES)

            def put(cell, value):
                rows = pl.ds(pl.multiple_of(cell * SLOTS, SLOTS), SLOTS)
                gf = self.pos_up[GRID + cell, :, lanes]
                self.first[rows, lanes] = gf + value * self.live[rows, :]

            def tap(a, b):
                t = 13 + (1 - a) * 3 + 1 - b
                return self.small[t : t + 1, lanes]

            conv(self.pos_up, 1, tap, 1, lanes, put)

            def up(cell):
                return self.pos_up[GRID + cell, :, lanes]

            def put_tap(a, b, value):
                t = 13 + (a + 1) * 3 + b + 1
                self.sums[t : t + 1, lanes] = value

            tap_sums(up, self.pos_src, 1, 1, lanes, put_tap)

        def down(r0, _):
            rows = pl.ds(r0, 16)
            self.low[rows, :] = self.first[rows, :].astype(BF16)
            return 0

        rows_loop(ROWS, 16, down, 0, unroll=5)
        self.unplace(self.low, self.grad_in)


SLOT_OF = (0, 1, 2, 3, 4, 6, 8, 10, 5, 7, 9, 11)
EARLY = 4


def route(slot):
    if slot < EARLY:
        return ("xzy", "yzx")[slot % 2] + "c"
    return ("zxy", "zyx")[slot % 2] + "c"


def scratch_of():
    f, h = (ROWS, D), (ROWS, LANES)
    halo3 = ((GRID + 2 * HALO) * GRID, SLOTS, D)
    halo1 = ((GRID + 2) * GRID, SLOTS, D)
    return {
        "live": (h, F32),
        "im8": ((IMG_GROUP, SLOTS, LANES), F32),
        "im16": ((IMG_GROUP, 16, LANES), BF16),
        "window": ((WINDOW * WINDOW, D), F32),
        "rel_taps": ((WINDOW * WINDOW, D), F32),
        "pos_src": (halo1, F32),
        "pos_up": (halo1, F32),
        "rel_src": (halo3, F32),
        "dq_src": (halo3, F32),
        "first": (f, F32),
        "u1": (f, F32),
        "inv1": (h, F32),
        "second": (f, F32),
        "u2": (f, F32),
        "inv2": (h, F32),
        "n1": (f, BF16),
        "n2": (f, BF16),
        "n2_t": ((D, ROWS), BF16),
        "go": (f, BF16),
        "go_t": ((D, ROWS), BF16),
        "q": (f, BF16),
        "k": (f, BF16),
        "v": (f, BF16),
        "soft": (f, F32),
        "soft_low": (f, BF16),
        "ctx": ((2, WIDE, IMG_GROUP * WIDE), BF16),
        "factor": (f, F32),
        "rel": (f, F32),
        "mixed": (f, BF16),
        "hidden": (f, F32),
        "active": (f, BF16),
        "low": (f, BF16),
        "back": (f, F32),
        "f": (f, BF16),
        "gq": (f, F32),
        "gk": (f, F32),
        "gv": (f, F32),
        "gl": ((3, ROWS, D), BF16),
    }


class Links:
    def __init__(self):
        dp, head = lax.axis_index("dp"), lax.axis_index("head")
        self.depth = lax.axis_size("dp") // 2
        self.at = {"x": head // 2, "c": head % 2, "z": dp // 2, "y": dp % 2}

    def count(self, axis):
        return self.depth if axis == "z" else 2

    def peer(self, axis, step):
        return lax.rem(self.at[axis] + step, self.count(axis))

    def device(self, axis, step):
        at = dict(self.at)
        at[axis] = self.peer(axis, step)
        return (at["z"] * 2 + at["y"], at["x"] * 2 + at["c"])

    def steps(self, axis, do):
        last = self.count(axis)
        if last <= 4:
            for step in range(1, last):
                do(step)
        else:

            def body(step, _):
                do(step)
                return 0

            lax.fori_loop(1, last, body, 0)

    def greet(self):
        barrier = pltpu.get_barrier_semaphore()
        for axis in "zyxc":

            def signal(step, axis=axis):
                pl.semaphore_signal(
                    barrier,
                    inc=1,
                    device_id=self.device(axis, step),
                    device_id_type=pl.DeviceIdType.MESH,
                )

            self.steps(axis, signal)
        pl.semaphore_wait(barrier, self.depth + 2)

    def copy(self, src, dst, send, recv, device):
        return pltpu.make_async_remote_copy(
            src_ref=src,
            dst_ref=dst,
            send_sem=send,
            recv_sem=recv,
            device_id=device,
            device_id_type=pl.DeviceIdType.MESH,
        )


class Gather:
    def __init__(self, links, w, send, recv):
        self.links, self.w, self.send, self.recv = links, w, send, recv

    def region(self, slot, whole, **at):
        at = {**self.links.at, **at}
        place = [slice(None) if axis in whole else at[axis] for axis in "xczy"]
        return self.w.at[(*place, slot)]

    def some(self, slot, axis, whole):
        at = {}
        if axis == "z":
            at["z"] = pl.ds(0, self.links.depth - 1)
        return self.region(slot, whole, **at)

    def start(self, slot, phase):
        path = route(slot)
        axis = path[phase]
        part = self.region(slot, path[:phase])

        def go(step):
            self.links.copy(
                part,
                part,
                self.send.at[slot, phase],
                self.recv.at[slot, phase],
                self.links.device(axis, step),
            ).start()

        self.links.steps(axis, go)

    def descriptor(self, slot, phase):
        path = route(slot)
        part = self.some(slot, path[phase], path[:phase])
        sems = (self.send.at[slot, phase], self.recv.at[slot, phase])
        return self.links.copy(part, part, *sems, self.links.device(path[phase], 1))

    def arrive(self, slot, phase):
        self.descriptor(slot, phase).wait_recv()

    def sent(self, slot, phase):
        self.descriptor(slot, phase).wait_send()

    def wave(self, w):
        for pair in range(6):
            phase = w - pair
            for slot in (2 * pair, 2 * pair + 1):
                if 1 <= phase <= 4:
                    self.arrive(slot, phase - 1)
                if 1 <= phase <= 3:
                    self.start(slot, phase)


def block_kernel(
    cls, img, tokens, cot, weights, small, out, grad_in, g, sums, w, ag_send, ag_recv, *scratch
):
    refs = {"cls": cls, "img": img, "tokens": tokens, "cot": cot, "w": w, "small": small}
    refs.update({"out": out, "grad_in": grad_in, "g": g, "sums": sums})
    refs.update(zip(scratch_of(), scratch, strict=True))
    blk = Block(refs)
    links = Links()
    at = links.at
    for k in range(12):
        w[at["x"], at["c"], at["z"], at["y"], SLOT_OF[k]] = weights[k].astype(BF16)
    links.greet()
    gather = Gather(links, w, ag_send, ag_recv)
    for slot in range(12):
        gather.start(slot, 0)
    blk.setup()
    blk.read()
    blk.norm_one()
    blk.go_t[...] = blk.go[...].T
    blk.back[...] = jnp.zeros((ROWS, D), F32)
    for i in range(1, 5):
        gather.wave(i)
    blk.project(0)
    blk.project(1)
    blk.softmax()
    gather.wave(5)
    blk.project(2)
    blk.attend()
    blk.norm_two()
    blk.n2_t[...] = blk.n2[...].T
    for r in range(4):
        gather.wave(6 + r)
        blk.mlp(r)
    blk.finish_out()
    blk.back_two()
    blk.back_attend()
    blk.back_project()
    blk.back_one()
    for slot in range(12):
        for phase in range(4):
            gather.sent(slot, phase)


def block_call(cls, img, tokens, cot, weights, small):
    own = cls.shape[1] * CELLS
    smem = pl.BlockSpec(memory_space=pltpu.SMEM)
    vmem = pl.BlockSpec(memory_space=pltpu.VMEM)
    spread = (2, 2, lax.axis_size("dp") // 2, 2, *weights.shape)
    return pl.pallas_call(
        block_kernel,
        out_shape=(
            jax.ShapeDtypeStruct((own, D), BF16),
            jax.ShapeDtypeStruct((own, D), BF16),
            jax.ShapeDtypeStruct(spread, BF16),
            jax.ShapeDtypeStruct(small.shape, F32),
        ),
        in_specs=[smem, smem, vmem, vmem, vmem, vmem],
        out_specs=(vmem,) * 4,
        scratch_shapes=[
            pltpu.VMEM(spread, BF16),
            pltpu.SemaphoreType.DMA((12, 4)),
            pltpu.SemaphoreType.DMA((12, 4)),
            *[pltpu.VMEM(*v) for v in scratch_of().values()],
        ],
        compiler_params=pltpu.CompilerParams(
            collective_id=0, has_side_effects=True, vmem_limit_bytes=63 << 20
        ),
        name="block",
    )(cls, img, tokens, cot, weights, small)


def local(
    tokens,
    cotangent,
    crop_image,
    crop_class,
    weights,
    row_state,
    col_state,
    weights_ema,
    small_params,
    small_state,
    small_ema,
):
    heads, parts = lax.axis_size("head"), lax.axis_size("dp")
    both = ("head", "dp")
    out, grad_in, g, sums = block_call(
        crop_class, crop_image, tokens, cotangent, weights, small_params
    )
    out = lax.all_gather(out, "head", axis=0, tiled=True)
    grad_in = lax.all_gather(grad_in, "head", axis=0, tiled=True)
    g = g.reshape(heads * parts, *weights.shape)
    weight_grad = lax.all_to_all(g, both, split_axis=0, concat_axis=0, tiled=True)
    weight_grad = weight_grad.astype(F32).sum(axis=0)[jnp.array(SLOT_OF)]
    small_total = lax.psum(sums, ("dp", "head"))
    squares = weight_grad * weight_grad + SQUARE_FLOOR
    row_total = lax.psum(jnp.sum(squares, axis=2), "head")
    new_rows = SECOND_DECAY * row_state + (1.0 - SECOND_DECAY) * (row_total / D)
    col_total, row_mass = lax.psum((jnp.sum(squares, axis=1), jnp.sum(new_rows, axis=1)), "dp")
    new_cols = SECOND_DECAY * col_state + (1.0 - SECOND_DECAY) * (col_total / D)
    estimate = new_rows[:, :, None] * new_cols[:, None, :] / (row_mass / D)[:, None, None]
    update = weight_grad * lax.rsqrt(estimate)
    update_sq = lax.psum(jnp.sum(update * update, axis=(1, 2)), ("dp", "head"))
    update_rms = jnp.sqrt(update_sq / (D * D))
    new_weights = weights - STEP_RATE * update / jnp.maximum(1.0, update_rms)[:, None, None]
    new_ema = AVERAGE_KEEP * weights_ema + (1.0 - AVERAGE_KEEP) * new_weights
    new_small_state = SECOND_DECAY * small_state + (1.0 - SECOND_DECAY) * (
        small_total * small_total + SQUARE_FLOOR
    )
    small_update = small_total * lax.rsqrt(new_small_state)
    small_rms = jnp.sqrt(jnp.mean(small_update * small_update, axis=1))
    new_small = small_params - SMALL_RATE * small_update / jnp.maximum(1.0, small_rms)[:, None]
    new_small_ema = AVERAGE_KEEP * small_ema + (1.0 - AVERAGE_KEEP) * new_small
    return (
        out,
        grad_in,
        weight_grad,
        new_rows,
        new_cols,
        new_weights,
        new_weights.astype(BF16),
        new_ema,
        small_total,
        new_small_state,
        new_small,
        new_small_ema,
        jnp.concatenate([update_rms, small_rms]),
    )


def solution(mesh):
    in_specs = (
        P("dp", None),
        P("dp", None),
        P("dp", None),
        P("dp", None),
        P(None, "dp", "head"),
        P(None, "dp"),
        P(None, "head"),
        P(None, "dp", "head"),
        P(),
        P(),
        P(),
    )
    out_specs = (
        P("dp", None),
        P("dp", None),
        P(None, "dp", "head"),
        P(None, "dp"),
        P(None, "head"),
        P(None, "dp", "head"),
        P(None, "dp", "head"),
        P(None, "dp", "head"),
        P(),
        P(),
        P(),
        P(),
        P(),
    )
    return jax.shard_map(local, mesh=mesh, in_specs=in_specs, out_specs=out_specs, check_vma=False)
```

```python
import functools
import math
import types
from typing import Any, NamedTuple

import jax
import jax.numpy as jnp
from jax import lax
from jax.experimental import pallas as pl
from jax.experimental.pallas import tpu as pltpu
from jax.sharding import PartitionSpec as P

DP, HEAD = "dp", "head"
D = 512
HEAD_DIM = 64
GRID = 7
SMALL_GRID = 3
WINDOW = 7
IMG_GROUP = 3
CELLS = GRID * GRID
SLOTS = 8
CELL_PAD = CELLS + 1
ROWS = CELL_PAD * SLOTS
LANES = 128
WIDE = 256
REACHES = (1, 2, 3, 3)
HALO = WINDOW // 2

NORM_EPS = 1e-06
SQUARE_FLOOR = 1e-30
SECOND_DECAY = 0.999
STEP_RATE = 0.02
SMALL_RATE = 0.05
AVERAGE_KEEP = 0.9
NEG_LARGE = -1e30
ROOT_HALF = 0.7071067811865476
INV_ROOT_TAU = 0.3989422804014327
INV_SCALE = 1.0 / math.sqrt(HEAD_DIM)

F32 = jnp.float32
BF16 = jnp.bfloat16
NN = (((1,), (0,)), ((), ()))
NT = (((1,), (1,)), ((), ()))
TN = (((0,), (0,)), ((), ()))


def dot(a, b, dims=NN):
    return lax.dot_general(a, b, dims, preferred_element_type=F32)


def lane_block(b):
    return slice(b * WIDE, (b + 1) * WIDE)


def wide(col):
    return jnp.concatenate([col] * (D // LANES), axis=1)


def rows_loop(count, size, body, init=None, unroll=1):
    def step(j, carry):
        return body(pl.multiple_of(j * size, size), carry)

    return lax.fori_loop(0, count // size, step, init, unroll=unroll)


def conv(src, halo, tap, reach, lanes, put):
    def line(y, _):
        sums = [jnp.zeros((SLOTS, LANES), F32) for _ in range(GRID)]
        for a in range(-reach, reach + 1):
            base = (y + (a + halo)) * GRID
            cells = [src[base + x, :, lanes] for x in range(GRID)]
            for b in range(-reach, reach + 1):
                t = tap(a, b)
                for x in range(GRID):
                    if 0 <= x + b < GRID:
                        sums[x] = sums[x] + t * cells[x + b]
        for x in range(GRID):
            put(y * GRID + x, sums[x])
        return 0

    lax.fori_loop(0, GRID, line, 0)


def tap_sums(up, src, halo, reach, lanes, put):
    for a in range(-reach, reach + 1):

        def line(y, sums):
            sums = list(sums)
            ups = [up(y * GRID + x) for x in range(GRID)]
            base = (y + (a + halo)) * GRID
            cells = [src[base + x, :, lanes] for x in range(GRID)]
            for i, b in enumerate(range(-reach, reach + 1)):
                for x in range(GRID):
                    if 0 <= x + b < GRID:
                        sums[i] = sums[i] + ups[x] * cells[x + b]
            return tuple(sums)

        start = tuple(jnp.zeros((SLOTS, LANES), F32) for _ in range(2 * reach + 1))
        sums = lax.fori_loop(0, GRID, line, start)
        for i, b in enumerate(range(-reach, reach + 1)):
            put(a, b, jnp.sum(sums[i], axis=0, keepdims=True))


def fold(x):
    return jnp.sum(x.reshape(x.shape[0] // SLOTS, SLOTS, x.shape[1]), axis=0)


def erf_parts(h):
    e = lax.erf(h * ROOT_HALF)
    half = 0.5 * (1.0 + e)
    return h * half, half + h * jnp.exp(-0.5 * h * h) * INV_ROOT_TAU


def norm_rows(v, gain, shift):
    centre = jnp.sum(v, axis=1, keepdims=True) * (1.0 / D)
    offset = v - centre
    spread = jnp.sum(offset * offset, axis=1, keepdims=True) * (1.0 / D)
    inverse = lax.rsqrt(spread + NORM_EPS)
    unit = offset * inverse
    return unit * gain + shift, unit, inverse


def norm_back(up, unit, inverse, gain):
    z = up * gain
    mean_z = jnp.sum(z, axis=1, keepdims=True) * (1.0 / D)
    mean_zu = jnp.sum(z * unit, axis=1, keepdims=True) * (1.0 / D)
    return inverse * (z - mean_z - unit * mean_zu)


class Block:
    def __init__(self, refs):
        self.__dict__.update(refs)

    def matrix(self, k, lo, hi):
        parts = []
        for h in range(lo, hi):
            part = self.w[h // 2, h % 2, :, :, k]
            if part.shape[-2] % 16:
                part = part.astype(F32).reshape(D, LANES).astype(BF16)
            else:
                part = part.reshape(D, LANES)
            parts.append(part)
        return jnp.concatenate(parts, axis=1)

    def times(self, lhs, k, b):
        return dot(lhs, self.matrix(k, 2 * b, 2 * b + 2))

    def times_t(self, lhs, k, b):
        return dot(lhs, self.matrix(k, 0, 4)[lane_block(b), :], NT)

    def put_grad(self, k, lhs_t, rhs):
        for b in range(2):
            g = dot(lhs_t, rhs[:, lane_block(b)])
            for i in range(2):
                piece = g[:, i * LANES : (i + 1) * LANES]
                parts, two, _, rows, _ = self.g.shape[2:]
                piece = piece.reshape(parts, two, rows, LANES)
                self.g[b, i, :, :, k] = piece.astype(BF16)

    def row(self, j):
        return self.small[j : j + 1, :]

    def setup(self):
        head = lax.axis_index(HEAD)
        slots = self.cls.shape[1]
        self.sums[...] = jnp.zeros(self.sums.shape, F32)
        sub = lax.broadcasted_iota(jnp.int32, (SLOTS, LANES), 0)
        valid = jnp.where(sub < slots, 1.0, 0.0)
        full = jnp.zeros((SLOTS, LANES), F32)
        images = [jnp.zeros((SLOTS, LANES), F32) for _ in range(IMG_GROUP)]
        for s in range(slots):
            full = jnp.where(sub == s, jnp.where(self.cls[head, s] == 0, 1.0, 0.0), full)
            for i in range(IMG_GROUP):
                images[i] = jnp.where(
                    sub == s, jnp.where(self.img[head, s] == i, 1.0, 0.0), images[i]
                )
        for cell in range(CELLS):
            small = cell // GRID < SMALL_GRID and cell % GRID < SMALL_GRID
            self.live[cell * SLOTS : (cell + 1) * SLOTS, :] = valid if small else full
        self.live[CELLS * SLOTS :, :] = jnp.zeros((SLOTS, LANES), F32)
        for i in range(IMG_GROUP):
            self.im8[i] = images[i]
            self.im16[i] = jnp.concatenate([images[i], images[i]], axis=0).astype(BF16)
        self.pos_src[0:GRID] = jnp.zeros((GRID, SLOTS, D), F32)
        self.pos_src[GRID + CELLS :] = jnp.zeros((GRID, SLOTS, D), F32)
        for pad in (self.rel_src, self.dq_src):
            pad[0 : HALO * GRID] = jnp.zeros((HALO * GRID, SLOTS, D), F32)
            pad[HALO * GRID + CELLS :] = jnp.zeros((HALO * GRID, SLOTS, D), F32)
        tap = lax.broadcasted_iota(jnp.int32, (WINDOW * WINDOW, 1), 0)
        row_off = jnp.abs(tap // WINDOW - HALO)
        col_off = jnp.abs(tap % WINDOW - HALO)
        off = jnp.maximum(row_off, col_off)
        heads = lax.broadcasted_iota(jnp.int32, (1, D), 1) // HEAD_DIM
        reach = jnp.where(heads < 2, 1, jnp.where(heads < 5, 2, 3))
        mask = jnp.where(off <= reach, 1.0, 0.0)
        self.window[...] = mask
        self.rel_taps[...] = self.small[22 : 22 + WINDOW * WINDOW, :] * mask

    def place(self, rows_ref, first, r0, size):
        count = rows_ref.shape[0]
        r = r0 + lax.broadcasted_iota(jnp.int32, (size, 1), 0)
        cell, slot = r >> 3, r & 7
        want = first + slot * CELLS + cell
        want = jnp.where((slot < self.cls.shape[1]) & (cell < CELLS), want, -1)
        col = lax.broadcasted_iota(jnp.int32, (size, count), 1)
        pick = jnp.where(col == want, 1.0, 0.0).astype(BF16)
        return dot(pick, rows_ref[...])

    def unplace(self, src_ref, out_ref):
        count = out_ref.shape[0]
        own = self.cls.shape[1] * CELLS
        lead = lax.rem(lax.axis_index(HEAD) * own, 16)
        r = lax.broadcasted_iota(jnp.int32, (1, ROWS), 1)
        cell, slot = r >> 3, r & 7
        target = lead + slot * CELLS + cell
        target = jnp.where((slot < self.cls.shape[1]) & (cell < CELLS), target, -1)
        t = lax.broadcasted_iota(jnp.int32, (count, ROWS), 0)
        pick = jnp.where(t == target, 1.0, 0.0).astype(BF16)
        out_ref[...] = dot(pick, src_ref[...]).astype(BF16)

    def read(self):
        first = lax.axis_index(HEAD) * (self.cls.shape[1] * CELLS)
        size = 80

        def body(r0, _):
            live = wide(self.live[pl.ds(r0, size), :])
            x = self.place(self.tokens, first, r0, size)
            self.first[pl.ds(r0, size), :] = x
            c0 = r0 // SLOTS
            self.pos_src[pl.ds(GRID + c0, size // SLOTS)] = (x * live).reshape(-1, SLOTS, D)
            c = self.place(self.cot, first, r0, size)
            self.go[pl.ds(r0, size), :] = (c * live).astype(BF16)
            return 0

        rows_loop(ROWS, size, body, 0)

    def norm_one(self):
        for c in range(D // LANES):
            lanes = slice(c * LANES, (c + 1) * LANES)

            def put(cell, value):
                rows = pl.ds(pl.multiple_of(cell * SLOTS, SLOTS), SLOTS)
                self.first[rows, lanes] = self.first[rows, lanes] + value + self.small[8:9, lanes]

            def tap(a, b):
                t = 13 + (a + 1) * 3 + b + 1
                return self.small[t : t + 1, lanes]

            conv(self.pos_src, 1, tap, 1, lanes, put)

        def body(r0, _):
            rows = pl.ds(r0, 16)
            n, u, inv = norm_rows(self.first[rows, :], self.row(0), self.row(1))
            self.n1[rows, :] = n.astype(BF16)
            self.u1[rows, :] = u
            self.inv1[rows, :] = jnp.broadcast_to(inv, (16, LANES))
            return 0

        rows_loop(ROWS, 16, body, 0, unroll=5)

    def project(self, k):
        low = (self.q, self.k, self.v)[k]
        for b in range(2):
            cols = lane_block(b)
            p = self.times(self.n1[...], k, b)
            if k != 1:
                p = p + self.small[2 + k // 2 : 3 + k // 2, cols]
            low[:, cols] = p.astype(BF16)

    def image_sum(self, x):
        total = jnp.zeros((SLOTS, D), F32)
        for i in range(IMG_GROUP):
            im = wide(self.im8[i])
            total = total + im * jnp.sum(im * x, axis=0, keepdims=True)
        return total

    def softmax(self):
        def top(r0, best):
            live = wide(self.live[pl.ds(r0, 16), :])
            keys = jnp.where(live > 0, self.k[pl.ds(r0, 16), :].astype(F32), NEG_LARGE)
            return jnp.maximum(best, jnp.max(keys.reshape(2, SLOTS, D), axis=0))

        best = rows_loop(ROWS, 16, top, jnp.full((SLOTS, D), NEG_LARGE, F32), unroll=5)
        shift = jnp.zeros((SLOTS, D), F32)
        for i in range(IMG_GROUP):
            im = wide(self.im8[i])
            most = jnp.max(jnp.where(im > 0, best, NEG_LARGE), axis=0, keepdims=True)
            shift = jnp.where(im > 0, most, shift)
        shift2 = jnp.concatenate([shift, shift], axis=0)

        def raise_(r0, total):
            rows = pl.ds(r0, 16)
            live = wide(self.live[rows, :])
            keys = self.k[rows, :].astype(F32)
            e = jnp.where(live > 0, jnp.exp(jnp.where(live > 0, keys - shift2, 0.0)), 0.0)
            self.soft[rows, :] = e
            return total + fold(e)

        total = self.image_sum(
            rows_loop(ROWS, 16, raise_, jnp.zeros((SLOTS, D), F32), unroll=5)
        )
        scale = 1.0 / jnp.where(total > 0, total, 1.0)
        scale2 = jnp.concatenate([scale, scale], axis=0)

        def divide(r0, _):
            rows = pl.ds(r0, 16)
            soft = self.soft[rows, :] * scale2
            self.soft[rows, :] = soft
            self.soft_low[rows, :] = soft.astype(BF16)
            return 0

        rows_loop(ROWS, 16, divide, 0, unroll=5)

    def by_image(self, x):
        tiles = x.reshape(ROWS // 16, 16, WIDE)
        parts = []
        for i in range(IMG_GROUP):
            im = jnp.concatenate([self.im16[i]] * (WIDE // LANES), axis=1)
            parts.append((tiles * im[None]).reshape(ROWS, WIDE))
        return jnp.concatenate(parts, axis=1)

    def head_blocks(self, x):
        r = lax.broadcasted_iota(jnp.int32, x.shape, 0) // HEAD_DIM
        c = (lax.broadcasted_iota(jnp.int32, x.shape, 1) % WIDE) // HEAD_DIM
        return jnp.where(r == c, x, 0.0).astype(BF16)

    def stacked(self, x):
        return jnp.concatenate([x[:, lane_block(i)] for i in range(IMG_GROUP)], axis=0)

    def attend(self):
        for b in range(2):
            cols = lane_block(b)
            ctx = dot(self.soft_low[:, cols], self.by_image(self.v[:, cols]), TN)
            ctx = self.head_blocks(ctx)
            self.ctx[b] = ctx
            self.factor[:, cols] = dot(self.by_image(self.q[:, cols]), self.stacked(ctx))

        def fill(r0, _):
            rows = pl.ds(r0, 16)
            v = self.v[rows, :].astype(F32) * wide(self.live[rows, :])
            c0 = r0 // SLOTS
            self.rel_src[pl.ds(HALO * GRID + c0, 2)] = v.reshape(2, SLOTS, D)
            return 0

        rows_loop(ROWS, 16, fill, 0, unroll=5)
        for c in range(D // LANES):
            lanes = slice(c * LANES, (c + 1) * LANES)

            def put(cell, value):
                rows = pl.ds(pl.multiple_of(cell * SLOTS, SLOTS), SLOTS)
                self.rel[rows, lanes] = value

            def tap(a, b):
                t = (a + HALO) * WINDOW + b + HALO
                return self.rel_taps[t : t + 1, lanes]

            conv(self.rel_src, HALO, tap, REACHES[c], lanes, put)
        self.rel[CELLS * SLOTS :, :] = jnp.zeros((SLOTS, D), F32)

        def mix(r0, _):
            rows = pl.ds(r0, 16)
            m = self.factor[rows, :] * INV_SCALE + self.q[rows, :].astype(F32) * self.rel[rows, :]
            self.mixed[rows, :] = (m * wide(self.live[rows, :])).astype(BF16)
            return 0

        rows_loop(ROWS, 16, mix, 0, unroll=5)

    def norm_two(self):
        for b in range(2):
            cols = lane_block(b)
            p = self.times_t(self.mixed[...], 3, b)
            self.second[:, cols] = self.first[:, cols] + p + self.small[4:5, cols]

        def body(r0, _):
            rows = pl.ds(r0, 16)
            n, u, inv = norm_rows(self.second[rows, :], self.row(5), self.row(6))
            self.n2[rows, :] = n.astype(BF16)
            self.u2[rows, :] = u
            self.inv2[rows, :] = jnp.broadcast_to(inv, (16, LANES))
            return 0

        rows_loop(ROWS, 16, body, 0, unroll=5)

    def mlp(self, r):
        up, down = 4 + 2 * r, 5 + 2 * r
        for b in range(2):
            cols = lane_block(b)
            h = self.times(self.n2[...], up, b) + self.small[pl.ds(9 + r, 1), cols]
            self.hidden[:, cols] = h
            self.factor[:, cols] = self.times(self.go[...], down, b)

        def body(r0, total):
            rows = pl.ds(r0, 16)
            act, slope = erf_parts(self.hidden[rows, :])
            g = self.factor[rows, :] * slope
            self.active[rows, :] = act.astype(BF16)
            self.low[rows, :] = g.astype(BF16)
            return total + fold(g)

        total = rows_loop(ROWS, 16, body, jnp.zeros((SLOTS, D), F32), unroll=5)
        self.sums[pl.ds(9 + r, 1), :] = jnp.sum(total, axis=0, keepdims=True)
        self.put_grad(down, self.go_t[...], self.active)
        self.put_grad(up, self.n2_t[...], self.low)
        for b in range(2):
            cols = lane_block(b)
            self.second[:, cols] += self.times_t(self.active[...], down, b)
            self.back[:, cols] += self.times_t(self.low[...], up, b)

    def finish_out(self):
        def body(r0, _):
            rows = pl.ds(r0, 16)
            self.low[rows, :] = (self.second[rows, :] + self.row(7)).astype(BF16)
            return 0

        rows_loop(ROWS, 16, body, 0, unroll=5)
        self.unplace(self.low, self.out_own)

    def back_two(self):
        zero = jnp.zeros((SLOTS, D), F32)

        def body(r0, sums):
            rows = pl.ds(r0, 16)
            back, u = self.back[rows, :], self.u2[rows, :]
            go = self.go[rows, :].astype(F32)
            gs = go + norm_back(back, u, wide(self.inv2[rows, :]), self.row(5))
            self.second[rows, :] = gs
            self.low[rows, :] = gs.astype(BF16)
            new = (gs, back * u, back, go)
            return tuple(s + fold(n) for s, n in zip(sums, new, strict=True))

        sums = rows_loop(ROWS, 16, body, (zero,) * 4, unroll=5)
        for j, s in zip((4, 5, 6, 7), sums, strict=True):
            self.sums[j : j + 1, :] = jnp.sum(s, axis=0, keepdims=True)

    def grad_proj(self):
        self.put_grad(3, self.low[...].T, self.mixed)

    def back_heads(self):
        for b in range(2):
            cols = lane_block(b)
            self.factor[:, cols] = self.times(self.low[...], 3, b)

        def fill(r0, _):
            rows = pl.ds(r0, 16)
            d = self.factor[rows, :] * wide(self.live[rows, :])
            self.factor[rows, :] = d
            self.f[rows, :] = (d * INV_SCALE).astype(BF16)
            c0 = r0 // SLOTS
            dq = d * self.q[rows, :].astype(F32)
            self.dq_src[pl.ds(HALO * GRID + c0, 2)] = dq.reshape(2, SLOTS, D)
            return 0

        rows_loop(ROWS, 16, fill, 0, unroll=5)
        for b in range(2):
            cols = lane_block(b)
            f3 = self.by_image(self.f[:, cols])
            g = self.head_blocks(dot(self.q[:, cols], f3, TN))
            self.gq[:, cols] = dot(f3, self.ctx[b], NT)
            self.gk[:, cols] = dot(self.by_image(self.v[:, cols]), g, NT)
            self.gv[:, cols] = dot(self.by_image(self.soft_low[:, cols]), self.stacked(g))

    def back_window(self, tiles):
        for c in tiles:
            lanes = slice(c * LANES, (c + 1) * LANES)

            def put(cell, value):
                rows = pl.ds(pl.multiple_of(cell * SLOTS, SLOTS), SLOTS)
                self.gv[rows, lanes] = self.gv[rows, lanes] + value * self.live[rows, :]

            def tap(a, b):
                t = (HALO - a) * WINDOW + HALO - b
                return self.rel_taps[t : t + 1, lanes]

            conv(self.dq_src, HALO, tap, REACHES[c], lanes, put)

            def up(cell):
                return self.dq_src[HALO * GRID + cell, :, lanes]

            def put_tap(a, b, value):
                t = (a + HALO) * WINDOW + b + HALO
                keep = self.window[t : t + 1, lanes]
                self.sums[22 + t : 23 + t, lanes] = value * keep

            tap_sums(up, self.rel_src, HALO, REACHES[c], lanes, put_tap)

    def back_qkv(self):
        zero = jnp.zeros((SLOTS, D), F32)

        def inner(r0, total):
            rows = pl.ds(r0, 16)
            return total + fold(self.soft[rows, :] * self.gk[rows, :])

        shared = self.image_sum(rows_loop(ROWS, 16, inner, zero, unroll=5))
        shared2 = jnp.concatenate([shared, shared], axis=0)

        def low(r0, sums):
            rows = pl.ds(r0, 16)
            gq = self.gq[rows, :] + self.factor[rows, :] * self.rel[rows, :]
            gk = self.soft[rows, :] * (self.gk[rows, :] - shared2)
            gv = self.gv[rows, :]
            self.gl[0, rows, :] = gq.astype(BF16)
            self.gl[1, rows, :] = gk.astype(BF16)
            self.gl[2, rows, :] = gv.astype(BF16)
            return sums[0] + fold(gq), sums[1] + fold(gv)

        sums = rows_loop(ROWS, 16, low, (zero, zero), unroll=5)
        for j, s in zip((2, 3), sums, strict=True):
            self.sums[j : j + 1, :] = jnp.sum(s, axis=0, keepdims=True)

    def grad_qkv(self):
        n1_t = self.n1[...].T
        for k in range(3):
            self.put_grad(k, n1_t, self.gl.at[k])

    def back_project(self):
        for b in range(2):
            cols = lane_block(b)
            back = self.times_t(self.gl[0], 0, b)
            back = back + self.times_t(self.gl[1], 1, b)
            self.back[:, cols] = back + self.times_t(self.gl[2], 2, b)

    def back_one(self):
        zero = jnp.zeros((SLOTS, D), F32)
        self.pos_up[0:GRID] = jnp.zeros((GRID, SLOTS, D), F32)
        self.pos_up[GRID + CELLS :] = jnp.zeros((GRID, SLOTS, D), F32)

        def body(r0, sums):
            rows = pl.ds(r0, 16)
            back, u = self.back[rows, :], self.u1[rows, :]
            gf = self.second[rows, :] + norm_back(back, u, wide(self.inv1[rows, :]), self.row(0))
            c0 = r0 // SLOTS
            self.pos_up[pl.ds(GRID + c0, 2)] = gf.reshape(2, SLOTS, D)
            new = (back * u, back, gf)
            return tuple(s + fold(n) for s, n in zip(sums, new, strict=True))

        sums = rows_loop(ROWS, 16, body, (zero,) * 3, unroll=5)
        for j, s in zip((0, 1, 8), sums, strict=True):
            self.sums[j : j + 1, :] = jnp.sum(s, axis=0, keepdims=True)

    def back_first(self):
        for c in range(D // LANES):
            lanes = slice(c * LANES, (c + 1) * LANES)

            def put(cell, value):
                rows = pl.ds(pl.multiple_of(cell * SLOTS, SLOTS), SLOTS)
                gf = self.pos_up[GRID + cell, :, lanes]
                self.first[rows, lanes] = gf + value * self.live[rows, :]

            def tap(a, b):
                t = 13 + (1 - a) * 3 + 1 - b
                return self.small[t : t + 1, lanes]

            conv(self.pos_up, 1, tap, 1, lanes, put)

            def up(cell):
                return self.pos_up[GRID + cell, :, lanes]

            def put_tap(a, b, value):
                t = 13 + (a + 1) * 3 + b + 1
                self.sums[t : t + 1, lanes] = value

            tap_sums(up, self.pos_src, 1, 1, lanes, put_tap)

        def down(r0, _):
            rows = pl.ds(r0, 16)
            self.low[rows, :] = self.first[rows, :].astype(BF16)
            return 0

        rows_loop(ROWS, 16, down, 0, unroll=5)
        self.unplace(self.low, self.in_own)


SLOT_OF = (0, 1, 2, 3, 4, 6, 8, 10, 5, 7, 9, 11)
EARLY = 4


def route(slot):
    if slot < EARLY:
        return ("xzy", "yzx")[slot % 2] + "c"
    return ("zxy", "zyx")[slot % 2] + "c"


def scratch_of():
    f, h = (ROWS, D), (ROWS, LANES)
    halo3 = ((GRID + 2 * HALO) * GRID, SLOTS, D)
    halo1 = ((GRID + 2) * GRID, SLOTS, D)
    return dict(
        live=(h, F32),
        im8=((IMG_GROUP, SLOTS, LANES), F32),
        im16=((IMG_GROUP, 16, LANES), BF16),
        window=((WINDOW * WINDOW, D), F32),
        rel_taps=((WINDOW * WINDOW, D), F32),
        pos_src=(halo1, F32),
        pos_up=(halo1, F32),
        rel_src=(halo3, F32),
        dq_src=(halo3, F32),
        first=(f, F32),
        u1=(f, F32),
        inv1=(h, F32),
        second=(f, F32),
        u2=(f, F32),
        inv2=(h, F32),
        n1=(f, BF16),
        n2=(f, BF16),
        n2_t=((D, ROWS), BF16),
        go=(f, BF16),
        go_t=((D, ROWS), BF16),
        q=(f, BF16),
        k=(f, BF16),
        v=(f, BF16),
        soft=(f, F32),
        soft_low=(f, BF16),
        ctx=((2, WIDE, IMG_GROUP * WIDE), BF16),
        factor=(f, F32),
        rel=(f, F32),
        mixed=(f, BF16),
        hidden=(f, F32),
        active=(f, BF16),
        low=(f, BF16),
        back=(f, F32),
        f=(f, BF16),
        gq=(f, F32),
        gk=(f, F32),
        gv=(f, F32),
        gl=((3, ROWS, D), BF16),
    )


class Links:
    def __init__(self):
        dp, head = lax.axis_index(DP), lax.axis_index(HEAD)
        self.depth = lax.axis_size(DP) // 2
        self.at = {"x": head // 2, "c": head % 2, "z": dp // 2, "y": dp % 2}

    def count(self, axis):
        return self.depth if axis == "z" else 2

    def peer(self, axis, step):
        return lax.rem(self.at[axis] + step, self.count(axis))

    def device(self, axis, step):
        at = dict(self.at)
        at[axis] = self.peer(axis, step)
        return (at["z"] * 2 + at["y"], at["x"] * 2 + at["c"])

    def steps(self, axis, do):
        last = self.count(axis)
        if last <= 4:
            for step in range(1, last):
                do(step)
        else:

            def body(step, _):
                do(step)
                return 0

            lax.fori_loop(1, last, body, 0)

    def others(self, name, do):
        size = lax.axis_size(name)
        index = {DP: lax.axis_index(DP), HEAD: lax.axis_index(HEAD)}
        own = index[name]

        def one(step):
            peer = lax.rem(own + step, size)
            at = {**index, name: peer}
            do(step, (at[DP], at[HEAD]))

        if size <= 8:
            for step in range(1, size):
                one(step)
        else:

            def body(step, _):
                one(step)
                return 0

            lax.fori_loop(1, size, body, 0)

    def greet(self):
        barrier = pltpu.get_barrier_semaphore()

        def signal(step, device):
            pl.semaphore_signal(
                barrier, inc=1, device_id=device, device_id_type=pl.DeviceIdType.MESH
            )

        self.others(HEAD, signal)
        self.others(DP, signal)
        pl.semaphore_wait(barrier, lax.axis_size(HEAD) + lax.axis_size(DP) - 2)

    def copy(self, src, dst, send, recv, device):
        return pltpu.make_async_remote_copy(
            src_ref=src,
            dst_ref=dst,
            send_sem=send,
            recv_sem=recv,
            device_id=device,
            device_id_type=pl.DeviceIdType.MESH,
        )


class Gather:
    def __init__(self, links, w, send, recv):
        self.links, self.w, self.send, self.recv = links, w, send, recv

    def region(self, slot, whole, **at):
        at = {**self.links.at, **at}
        place = [slice(None) if axis in whole else at[axis] for axis in "xczy"]
        return self.w.at[(*place, slot)]

    def some(self, slot, axis, whole):
        at = {}
        if axis == "z":
            at["z"] = pl.ds(0, self.links.depth - 1)
        return self.region(slot, whole, **at)

    def start(self, slot, phase):
        path = route(slot)
        axis = path[phase]
        part = self.region(slot, path[:phase])

        def go(step):
            self.links.copy(
                part,
                part,
                self.send.at[slot, phase],
                self.recv.at[slot, phase],
                self.links.device(axis, step),
            ).start()

        self.links.steps(axis, go)

    def descriptor(self, slot, phase):
        path = route(slot)
        part = self.some(slot, path[phase], path[:phase])
        sems = (self.send.at[slot, phase], self.recv.at[slot, phase])
        return self.links.copy(part, part, *sems, self.links.device(path[phase], 1))

    def arrive(self, slot, phase):
        self.descriptor(slot, phase).wait_recv()

    def sent(self, slot, phase):
        self.descriptor(slot, phase).wait_send()

    def wave(self, w):
        for pair in range(6):
            phase = w - pair
            for slot in (2 * pair, 2 * pair + 1):
                if 1 <= phase <= 4:
                    self.arrive(slot, phase - 1)
                if 1 <= phase <= 3:
                    self.start(slot, phase)


class Scatter:
    def __init__(self, links, refs, send, recv):
        self.links, self.g, self.refs, self.total = links, refs.g, refs, refs.wg
        self.send, self.recv = send, recv

    def path(self, slot):
        return route(slot)[::-1]

    def region(self, slot, whole, **at):
        at = {**self.links.at, **at}
        place = [slice(None) if axis in whole else at[axis] for axis in "xczy"]
        return self.g.at[(*place, slot)]

    def box(self, slot, phase):
        r = self.refs
        if phase == 0:
            return r.box_c.at[slot]
        if phase == 1:
            return (r.box_y, r.box_x)[slot % 2].at[slot // 2]
        if slot < EARLY:
            return (r.box_early2, r.box_early3)[phase - 2].at[slot]
        return (r.box_late2, r.box_late3)[phase - 2].at[slot - EARLY]

    def start(self, slot, phase):
        path = self.path(slot)
        axis, rest = path[phase], path[phase + 1 :]

        def go(step):
            box = self.box(slot, phase)
            if axis == "z":
                box = box.at[step - 1]
            self.links.copy(
                self.region(slot, rest, **{axis: self.links.peer(axis, step)}),
                box,
                self.send.at[slot, phase],
                self.recv.at[slot, phase],
                self.links.device(axis, step),
            ).start()

        self.links.steps(axis, go)

    def descriptor(self, slot, phase):
        box = self.box(slot, phase)
        sems = (self.send.at[slot, phase], self.recv.at[slot, phase])
        return self.links.copy(box, box, *sems, self.links.device(self.path(slot)[phase], 1))

    def sent(self, slot, phase):
        self.descriptor(slot, phase).wait_send()

    def tick(self, slot, phase):
        path = self.path(slot)
        self.descriptor(slot, phase - 1).wait_recv()
        axis, rest = path[phase - 1], path[phase:]
        own = self.region(slot, rest)
        box = self.box(slot, phase - 1)
        if phase == 4:
            value = own[...].astype(F32)
            parts = [box.at[j] for j in range(box.shape[0])] if axis == "z" else [box]
            for part in parts:
                value = value + part[...].astype(F32)
            self.total[SLOT_OF.index(slot)] = value
            return
        if axis == "z":
            value = own[...].astype(F32)
            for j in range(box.shape[0]):
                value = value + box[j].astype(F32)
            own[...] = value.astype(BF16)
        else:
            own[...] = own[...] + box[...]
        self.start(slot, phase)


class Small:
    def __init__(self, links, parts, in_c, in_x, in_y, in_z, full, send, recv):
        self.links, self.parts, self.full = links, parts, full
        self.in_c, self.in_x, self.in_y, self.in_z = in_c, in_x, in_y, in_z
        self.send, self.recv = send, recv

    def go(self, stage, src, dst, axis):
        sems = (self.send.at[stage], self.recv.at[stage])
        self.links.steps(
            axis, lambda step: self.links.copy(src, dst, *sems, self.links.device(axis, step)).start()
        )

    def wait(self, stage, ref, axis):
        sems = (self.send.at[stage], self.recv.at[stage])
        return self.links.copy(ref, ref, *sems, self.links.device(axis, 1))

    def tick(self, stage):
        at = self.links.at
        x, c, z = at["x"], at["c"], at["z"]
        mine = self.parts.at[c, x]
        if stage == 0:
            self.go(0, self.parts.at[1 - c], self.in_c, "c")
        if stage == 1:
            self.wait(0, self.in_c, "c").wait_recv()
            self.parts[c] = self.parts[c] + self.in_c[...]
            self.go(1, self.parts.at[c, 1 - x], self.in_x, "x")
        if stage == 2:
            self.wait(1, self.in_x, "x").wait_recv()
            mine[...] = mine[...] + self.in_x[...]
            self.go(2, mine, self.in_y, "y")
        if stage == 3:
            self.wait(2, self.in_y, "y").wait_recv()
            self.in_z[z] = mine[...] + self.in_y[...]
            self.go(3, self.in_z.at[z], self.in_z.at[z], "z")
        if stage == 4:
            self.wait(3, self.in_z.at[pl.ds(0, self.links.depth - 1)], "z").wait_recv()
            self.full[c, x] = jnp.sum(self.in_z[...], axis=0)
            self.go(4, self.full.at[c, x], self.full.at[c, x], "x")
        if stage == 5:
            self.wait(4, self.full.at[c, x], "x").wait_recv()
            self.go(5, self.full.at[c], self.full.at[c], "c")
        if stage == 6:
            self.wait(5, self.full.at[c], "c").wait_recv()

    def sent(self):
        at = self.links.at
        refs = (self.in_c, self.in_x, self.in_y, None, self.full.at[at["c"], at["x"]])
        for stage, axis in enumerate("cxyzxc"):
            if axis == "z":
                ref = self.in_z.at[pl.ds(0, self.links.depth - 1)]
            else:
                ref = self.full.at[at["c"]] if stage == 5 else refs[stage]
            self.wait(stage, ref, axis).wait_send()


class Rows:
    def __init__(self, links, blocks, send, recv):
        self.links, self.blocks, self.send, self.recv = links, blocks, send, recv

    def block(self, x, c):
        return self.blocks.at[2 * x + c]

    def hop(self, i):
        x, c = self.links.at["x"], self.links.at["c"]
        ref, axis = (((x, c), "x"), ((x, c), "c"), ((1 - x, c), "c"))[i]
        block = self.block(*ref)
        return self.links.copy(
            block, block, self.send.at[i], self.recv.at[i], self.links.device(axis, 1)
        )

    def spread(self):
        self.hop(0).start()
        self.hop(1).start()

    def forward(self):
        self.hop(0).wait_recv()
        self.hop(2).start()

    def arrive(self):
        self.hop(1).wait_recv()
        self.hop(2).wait_recv()

    def sent(self):
        for i in range(3):
            self.hop(i).wait_send()

    def join(self, own, out):
        heads, end = self.blocks.shape[0], out.shape[0]
        for h in range(heads):
            lo, hi = h * own, (h + 1) * own
            base = lo // 16 * 16
            first = base + 16 if lo % 16 else base
            last = hi // 16 * 16 if h + 1 < heads else end
            out[first:last, :] = self.blocks[h, first - base : last - base, :]
            if lo % 16:
                before = (lo - own) // 16 * 16
                tail = self.blocks[h - 1, base - before : base - before + 16, :]
                out[base : base + 16, :] = tail + self.blocks[h, 0:16, :]


class Exchange:
    def __init__(self, links, name, buffer, send, recv):
        self.links, self.name, self.buffer, self.send, self.recv = links, name, buffer, send, recv

    def start(self, value):
        own = lax.axis_index(self.name)
        self.buffer[own] = value
        mine = self.buffer.at[own]
        self.links.others(
            self.name,
            lambda step, device: self.links.copy(mine, mine, self.send, self.recv, device).start(),
        )

    def descriptor(self):
        ref = self.buffer.at[pl.ds(0, self.buffer.shape[0] - 1)]
        index = {DP: lax.axis_index(DP), HEAD: lax.axis_index(HEAD)}
        return self.links.copy(ref, ref, self.send, self.recv, (index[DP], index[HEAD]))

    def total(self):
        self.descriptor().wait_recv()
        return jnp.sum(self.buffer[...], axis=0)

    def sent(self):
        self.descriptor().wait_send()


def exact(a, b, dims):
    return lax.dot_general(
        a, b, dims, precision=lax.Precision.HIGHEST, preferred_element_type=F32
    )


class Adafactor:
    def __init__(self, refs):
        self.__dict__.update(refs)

    def eye(self, count):
        r = lax.broadcasted_iota(jnp.int32, (count, LANES), 0)
        c = lax.broadcasted_iota(jnp.int32, (count, LANES), 1)
        return jnp.where(r == c, 1.0, 0.0)

    def lane(self, shape, k, value, rest):
        lanes = lax.broadcasted_iota(jnp.int32, shape, 1)
        return jnp.where(lanes == k, value, rest)

    def squares(self):
        count, rows, _ = self.wg.shape
        by_row = jnp.zeros((rows, LANES), F32)
        by_col = []
        for k in range(count):
            g = self.wg[k]
            s = g * g + SQUARE_FLOOR
            by_row = self.lane(by_row.shape, k, jnp.sum(s, axis=1, keepdims=True), by_row)
            by_col.append(jnp.sum(s, axis=0, keepdims=True))
        self.col_part[0:count, :] = jnp.concatenate(by_col, axis=0)
        self.row_share.start(by_row)

    def rows(self):
        count = self.wg.shape[0]
        state = exact(self.row_state[...], self.eye(count), TN)
        total = self.row_share.total()
        new = SECOND_DECAY * state + (1.0 - SECOND_DECAY) * (total * (1.0 / D))
        self.row_new[...] = new
        self.new_rows[...] = exact(self.eye(count), new, NT)
        self.col_part[count : count + 1, :] = jnp.sum(new, axis=0, keepdims=True)
        self.col_share.start(self.col_part[...])

    def update(self):
        count = self.wg.shape[0]
        total = self.col_share.total()
        cols = SECOND_DECAY * self.col_state[...] + (1.0 - SECOND_DECAY) * (
            total[0:count] * (1.0 / D)
        )
        self.new_cols[...] = cols
        mean = total[count : count + 1] * (1.0 / D)
        rows = self.row_new[...]
        sums = jnp.zeros((1, LANES), F32)
        for k in range(count):
            r, m = rows[:, k : k + 1], mean[:, k : k + 1]
            u = self.wg[k] * lax.rsqrt(r * cols[k : k + 1, :] / m)
            self.upd[k] = u
            s = jnp.sum(jnp.sum(u * u, axis=0, keepdims=True), axis=1, keepdims=True)
            sums = self.lane(sums.shape, k, s, sums)
        self.sq_dp.start(jnp.broadcast_to(sums, (SLOTS, LANES)))

    def pass_on(self):
        self.sq_head.start(self.sq_dp.total())

    def apply(self):
        count = self.wg.shape[0]
        total = self.sq_head.total()[0:1]
        rms = jnp.sqrt(total * (1.0 / (D * D)))
        rate = STEP_RATE / jnp.maximum(1.0, rms)
        for k in range(count):
            new = self.weights[k] - rate[:, k : k + 1] * self.upd[k]
            self.new_weights[k] = new
            self.copy[k] = new.astype(BF16)
            self.new_ema[k] = AVERAGE_KEEP * self.ema[k] + (1.0 - AVERAGE_KEEP) * new
        lanes = lax.broadcasted_iota(jnp.int32, (1, LANES), 1)
        clip = jnp.where(lanes < count, rms, self.small_clip[...])
        self.clip[...] = clip[:, 0 : self.clip.shape[1]]

    def small_step(self, full):
        count = self.small.shape[0]
        g = jnp.concatenate([full[b // 2, b % 2, 0:count, :] for b in range(D // LANES)], axis=1)
        self.small_grads[...] = g
        state = SECOND_DECAY * self.small_state[...] + (1.0 - SECOND_DECAY) * (
            g * g + SQUARE_FLOOR
        )
        self.new_small_state[...] = state
        u = g * lax.rsqrt(state)
        rms = jnp.sqrt(jnp.sum(u * u, axis=1, keepdims=True) * (1.0 / D))
        new = self.small[...] - SMALL_RATE * u / jnp.maximum(1.0, rms)
        self.new_small[...] = new
        self.new_small_ema[...] = AVERAGE_KEEP * self.small_ema[...] + (1.0 - AVERAGE_KEEP) * new
        r = lax.broadcasted_iota(jnp.int32, (count, LANES), 0)
        c = lax.broadcasted_iota(jnp.int32, (count, LANES), 1)
        first = self.wg.shape[0]
        picked = jnp.where(c == r + first, rms, 0.0)
        self.small_clip[...] = jnp.sum(picked, axis=0, keepdims=True)


class Inputs(NamedTuple):
    cls: Any
    img: Any
    tokens: Any
    cot: Any
    weights: Any
    row_state: Any
    col_state: Any
    ema: Any
    small: Any
    small_state: Any
    small_ema: Any


class Outputs(NamedTuple):
    out: Any
    grad_in: Any
    wg: Any
    new_rows: Any
    new_cols: Any
    new_weights: Any
    copy: Any
    new_ema: Any
    small_grads: Any
    new_small_state: Any
    new_small: Any
    new_small_ema: Any
    clip: Any


HEAD_ROWS = 320


def shared_of(weights, parts, heads):
    depth, (_, rows, _) = parts // 2, weights.shape
    block = (rows, LANES)
    dma = pltpu.SemaphoreType.DMA

    def b(*lead):
        return pltpu.VMEM((*lead, *block), BF16)

    def f(*shape):
        return pltpu.VMEM(shape, F32)

    return dict(
        w=b(2, 2, depth, 2, 12),
        g=b(2, 2, depth, 2, 12),
        box_c=b(12, 2, depth, 2),
        box_y=b(6, 2, depth),
        box_x=b(6, depth, 2),
        box_early2=b(EARLY, depth - 1, 2),
        box_early3=b(EARLY),
        box_late2=b(12 - EARLY, depth),
        box_late3=b(12 - EARLY, depth - 1),
        out_rows=pltpu.VMEM((heads, HEAD_ROWS, D), BF16),
        in_rows=pltpu.VMEM((heads, HEAD_ROWS, D), BF16),
        sums=f(72, D),
        parts=f(2, 2, 72, LANES),
        in_c=f(2, 72, LANES),
        in_x=f(72, LANES),
        in_y=f(72, LANES),
        in_z=f(depth, 72, LANES),
        full=f(2, 2, 72, LANES),
        row_box=f(heads, *block),
        col_box=f(parts, 16, LANES),
        sq_dp_box=f(parts, SLOTS, LANES),
        sq_head_box=f(heads, SLOTS, LANES),
        row_new=f(*block),
        col_part=f(16, LANES),
        upd=f(12, *block),
        small_clip=f(1, LANES),
        ag_send=dma((12, 4)),
        ag_recv=dma((12, 4)),
        rs_send=dma((12, 4)),
        rs_recv=dma((12, 4)),
        small_send=dma((6,)),
        small_recv=dma((6,)),
        out_send=dma((3,)),
        out_recv=dma((3,)),
        in_send=dma((3,)),
        in_recv=dma((3,)),
        opt_send=dma((4,)),
        opt_recv=dma((4,)),
    )


def block_kernel(names, *refs):
    r = types.SimpleNamespace(**dict(zip(names, refs, strict=True)))
    at_head = lax.axis_index(HEAD)
    r.out_own = r.out_rows.at[at_head]
    r.in_own = r.in_rows.at[at_head]
    own = r.cls.shape[1] * CELLS
    blk = Block(vars(r))
    links = Links()
    at = links.at
    gather = Gather(links, r.w, r.ag_send, r.ag_recv)
    scatter = Scatter(links, r, r.rs_send, r.rs_recv)
    small = Small(
        links,
        *(r.parts, r.in_c, r.in_x, r.in_y, r.in_z, r.full),
        r.small_send,
        r.small_recv,
    )
    out_rows = Rows(links, r.out_rows, r.out_send, r.out_recv)
    in_rows = Rows(links, r.in_rows, r.in_send, r.in_recv)
    boxes = dict(row_share=r.row_box, col_share=r.col_box, sq_dp=r.sq_dp_box, sq_head=r.sq_head_box)
    shares = {}
    for i, (name, box) in enumerate(boxes.items()):
        axis = HEAD if i in (0, 3) else DP
        shares[name] = Exchange(links, axis, box, r.opt_send.at[i], r.opt_recv.at[i])
    opt = types.SimpleNamespace(**vars(r), **shares)
    opt = Adafactor(vars(opt))

    for k in range(12):
        r.w[at["x"], at["c"], at["z"], at["y"], SLOT_OF[k]] = r.weights[k].astype(BF16)
    links.greet()
    for slot in range(12):
        gather.start(slot, 0)
    blk.setup()
    r.col_part[...] = jnp.zeros((16, LANES), F32)
    blk.read()
    blk.norm_one()
    blk.go_t[...] = blk.go[...].T
    blk.back[...] = jnp.zeros((ROWS, D), F32)
    for i in range(1, 5):
        gather.wave(i)
    blk.project(0)
    blk.project(1)
    blk.softmax()
    gather.wave(5)
    blk.project(2)
    blk.attend()
    blk.norm_two()
    blk.n2_t[...] = blk.n2[...].T
    for i in range(4):
        gather.wave(6 + i)
        blk.mlp(i)
        scatter.start(4 + 2 * i, 0)
        scatter.start(5 + 2 * i, 0)
    for i in range(3):
        scatter.tick(4 + 2 * i, 1)
        scatter.tick(5 + 2 * i, 1)
    blk.finish_out()
    scatter.tick(10, 1)
    scatter.tick(11, 1)
    blk.back_two()
    blk.grad_proj()
    scatter.start(3, 0)
    for i in (4, 5, 6, 7):
        scatter.tick(i, 2)
    blk.back_heads()
    for i in (8, 9, 10, 11):
        scatter.tick(i, 2)
    scatter.tick(3, 1)
    out_rows.spread()
    blk.back_window((0, 1, 2))
    for i in (4, 5, 6, 7):
        scatter.tick(i, 3)
    blk.back_window((3,))
    for i in (8, 9, 10, 11):
        scatter.tick(i, 3)
    scatter.tick(3, 2)
    blk.back_qkv()
    blk.grad_qkv()
    for i in (0, 1, 2):
        scatter.start(i, 0)
    blk.back_project()
    for i in (0, 1, 2):
        scatter.tick(i, 1)
    blk.back_one()
    for i in (0, 1, 2):
        scatter.tick(i, 2)
    blk.back_first()
    in_rows.spread()
    for b in range(D // LANES):
        r.parts[b // 2, b % 2] = r.sums[:, b * LANES : (b + 1) * LANES]
    small.tick(0)
    for i in (0, 1, 2):
        scatter.tick(i, 3)
    scatter.tick(3, 3)
    out_rows.forward()
    for i in range(4, 12):
        scatter.tick(i, 4)
    small.tick(1)
    scatter.tick(3, 4)
    for i in (0, 1, 2):
        scatter.tick(i, 4)
    opt.squares()
    small.tick(2)
    out_rows.arrive()
    out_rows.join(own, r.out)
    opt.rows()
    small.tick(3)
    in_rows.forward()
    opt.update()
    small.tick(4)
    opt.pass_on()
    small.tick(5)
    in_rows.arrive()
    in_rows.join(own, r.grad_in)
    small.tick(6)
    opt.small_step(r.full)
    opt.apply()
    for slot in range(12):
        for phase in range(4):
            gather.sent(slot, phase)
            scatter.sent(slot, phase)
    small.sent()
    out_rows.sent()
    in_rows.sent()
    for share in shares.values():
        share.sent()


def local(
    tokens,
    cotangent,
    crop_image,
    crop_class,
    weights,
    row_state,
    col_state,
    weights_ema,
    small_params,
    small_state,
    small_ema,
):
    parts, heads = lax.axis_size(DP), lax.axis_size(HEAD)
    smem = pl.BlockSpec(memory_space=pltpu.SMEM)
    vmem = pl.BlockSpec(memory_space=pltpu.VMEM)
    shared = shared_of(weights, parts, heads)
    own = scratch_of()

    def like(x, dtype=None):
        return jax.ShapeDtypeStruct(x.shape, dtype or x.dtype)

    clips = weights.shape[0] + small_params.shape[0]
    outs = (
        like(tokens),
        like(tokens),
        like(weights),
        like(row_state),
        like(col_state),
        like(weights),
        like(weights, BF16),
        like(weights),
        like(small_params),
        like(small_params),
        like(small_params),
        like(small_params),
        jax.ShapeDtypeStruct((1, clips), F32),
    )
    names = (*Inputs._fields, *Outputs._fields, *shared, *own)
    res = pl.pallas_call(
        functools.partial(block_kernel, names),
        out_shape=outs,
        in_specs=[smem, smem] + [vmem] * 9,
        out_specs=(vmem,) * len(outs),
        scratch_shapes=[*shared.values(), *[pltpu.VMEM(*v) for v in own.values()]],
        compiler_params=pltpu.CompilerParams(
            collective_id=0, has_side_effects=True, vmem_limit_bytes=63 << 20
        ),
        name="block",
    )(
        crop_class,
        crop_image,
        tokens,
        cotangent,
        weights,
        row_state,
        col_state,
        weights_ema,
        small_params,
        small_state,
        small_ema,
    )
    return (*res[:-1], res[-1].reshape(clips))


def solution(mesh):
    in_specs = (
        P(DP, None),
        P(DP, None),
        P(DP, None),
        P(DP, None),
        P(None, DP, HEAD),
        P(None, DP),
        P(None, HEAD),
        P(None, DP, HEAD),
        P(),
        P(),
        P(),
    )
    out_specs = (
        P(DP, None),
        P(DP, None),
        P(None, DP, HEAD),
        P(None, DP),
        P(None, HEAD),
        P(None, DP, HEAD),
        P(None, DP, HEAD),
        P(None, DP, HEAD),
        P(),
        P(),
        P(),
        P(),
        P(),
    )
    return jax.shard_map(local, mesh=mesh, in_specs=in_specs, out_specs=out_specs, check_vma=False)
```

```python
import functools
import math
import types
from typing import Any, NamedTuple

import jax
import jax.numpy as jnp
from jax import lax
from jax.experimental import pallas as pl
from jax.experimental.pallas import tpu as pltpu
from jax.sharding import PartitionSpec as P

DP, HEAD = "dp", "head"
D = 512
HEAD_DIM = 64
GRID = 7
SMALL_GRID = 3
WINDOW = 7
IMG_GROUP = 3
CELLS = GRID * GRID
SLOTS = 8
CELL_PAD = CELLS + 1
ROWS = CELL_PAD * SLOTS
LANES = 128
WIDE = 256
REACHES = (1, 2, 3, 3)
HALO = WINDOW // 2

NORM_EPS = 1e-06
SQUARE_FLOOR = 1e-30
SECOND_DECAY = 0.999
STEP_RATE = 0.02
SMALL_RATE = 0.05
AVERAGE_KEEP = 0.9
NEG_LARGE = -1e30
ROOT_HALF = 0.7071067811865476
INV_ROOT_TAU = 0.3989422804014327
INV_SCALE = 1.0 / math.sqrt(HEAD_DIM)

F32 = jnp.float32
BF16 = jnp.bfloat16
NN = (((1,), (0,)), ((), ()))
NT = (((1,), (1,)), ((), ()))
TN = (((0,), (0,)), ((), ()))


def dot(a, b, dims=NN):
    return lax.dot_general(a, b, dims, preferred_element_type=F32)


def lane_block(b):
    return slice(b * WIDE, (b + 1) * WIDE)


def wide(col):
    return jnp.concatenate([col] * (D // LANES), axis=1)


def rows_loop(count, size, body, init=None, unroll=1):
    def step(j, carry):
        return body(pl.multiple_of(j * size, size), carry)

    return lax.fori_loop(0, count // size, step, init, unroll=unroll)


def conv(src, halo, tap, reach, lanes, put):
    def line(y, _):
        sums = [jnp.zeros((SLOTS, LANES), F32) for _ in range(GRID)]
        for a in range(-reach, reach + 1):
            base = (y + (a + halo)) * GRID
            cells = [src[base + x, :, lanes] for x in range(GRID)]
            for b in range(-reach, reach + 1):
                t = tap(a, b)
                for x in range(GRID):
                    if 0 <= x + b < GRID:
                        sums[x] = sums[x] + t * cells[x + b]
        for x in range(GRID):
            put(y * GRID + x, sums[x])
        return 0

    lax.fori_loop(0, GRID, line, 0)


def tap_sums(up, src, halo, reach, lanes, put):
    for a in range(-reach, reach + 1):

        def line(y, sums):
            sums = list(sums)
            ups = [up(y * GRID + x) for x in range(GRID)]
            base = (y + (a + halo)) * GRID
            cells = [src[base + x, :, lanes] for x in range(GRID)]
            for i, b in enumerate(range(-reach, reach + 1)):
                for x in range(GRID):
                    if 0 <= x + b < GRID:
                        sums[i] = sums[i] + ups[x] * cells[x + b]
            return tuple(sums)

        start = tuple(jnp.zeros((SLOTS, LANES), F32) for _ in range(2 * reach + 1))
        sums = lax.fori_loop(0, GRID, line, start)
        for i, b in enumerate(range(-reach, reach + 1)):
            put(a, b, jnp.sum(sums[i], axis=0, keepdims=True))


def fold(x):
    return jnp.sum(x.reshape(x.shape[0] // SLOTS, SLOTS, x.shape[1]), axis=0)


def erf_parts(h):
    e = lax.erf(h * ROOT_HALF)
    half = 0.5 * (1.0 + e)
    return h * half, half + h * jnp.exp(-0.5 * h * h) * INV_ROOT_TAU


def norm_rows(v, gain, shift):
    centre = jnp.sum(v, axis=1, keepdims=True) * (1.0 / D)
    offset = v - centre
    spread = jnp.sum(offset * offset, axis=1, keepdims=True) * (1.0 / D)
    inverse = lax.rsqrt(spread + NORM_EPS)
    unit = offset * inverse
    return unit * gain + shift, unit, inverse


def norm_back(up, unit, inverse, gain):
    z = up * gain
    mean_z = jnp.sum(z, axis=1, keepdims=True) * (1.0 / D)
    mean_zu = jnp.sum(z * unit, axis=1, keepdims=True) * (1.0 / D)
    return inverse * (z - mean_z - unit * mean_zu)


class Block:
    def __init__(self, refs):
        self.__dict__.update(refs)

    def matrix(self, k, lo, hi):
        parts = []
        for h in range(lo, hi):
            part = self.w[h // 2, h % 2, :, :, :, k]
            if part.shape[-2] % 16:
                part = part.astype(F32).reshape(D, LANES).astype(BF16)
            else:
                part = part.reshape(D, LANES)
            parts.append(part)
        return jnp.concatenate(parts, axis=1)

    def times(self, lhs, k, b):
        return dot(lhs, self.matrix(k, 2 * b, 2 * b + 2))

    def times_t(self, lhs, k, b):
        return dot(lhs, self.matrix(k, 0, 4)[lane_block(b), :], NT)

    def put_grad(self, k, lhs_t, rhs):
        for b in range(2):
            g = dot(lhs_t, rhs[:, lane_block(b)])
            for i in range(2):
                piece = g[:, i * LANES : (i + 1) * LANES]
                place = self.g.shape[2:5]
                piece = piece.reshape(*place, self.g.shape[-2], LANES)
                self.g[b, i, :, :, :, k] = piece.astype(BF16)

    def row(self, j):
        return self.small[j : j + 1, :]

    def setup(self):
        head = lax.axis_index(HEAD)
        slots = self.cls.shape[1]
        self.sums[...] = jnp.zeros(self.sums.shape, F32)
        sub = lax.broadcasted_iota(jnp.int32, (SLOTS, LANES), 0)
        valid = jnp.where(sub < slots, 1.0, 0.0)
        full = jnp.zeros((SLOTS, LANES), F32)
        images = [jnp.zeros((SLOTS, LANES), F32) for _ in range(IMG_GROUP)]
        for s in range(slots):
            full = jnp.where(sub == s, jnp.where(self.cls[head, s] == 0, 1.0, 0.0), full)
            for i in range(IMG_GROUP):
                images[i] = jnp.where(
                    sub == s, jnp.where(self.img[head, s] == i, 1.0, 0.0), images[i]
                )
        for cell in range(CELLS):
            small = cell // GRID < SMALL_GRID and cell % GRID < SMALL_GRID
            self.live[cell * SLOTS : (cell + 1) * SLOTS, :] = valid if small else full
        self.live[CELLS * SLOTS :, :] = jnp.zeros((SLOTS, LANES), F32)
        for i in range(IMG_GROUP):
            self.im8[i] = images[i]
            self.im16[i] = jnp.concatenate([images[i], images[i]], axis=0).astype(BF16)
        self.pos_src[0:GRID] = jnp.zeros((GRID, SLOTS, D), F32)
        self.pos_src[GRID + CELLS :] = jnp.zeros((GRID, SLOTS, D), F32)
        for pad in (self.rel_src, self.dq_src):
            pad[0 : HALO * GRID] = jnp.zeros((HALO * GRID, SLOTS, D), F32)
            pad[HALO * GRID + CELLS :] = jnp.zeros((HALO * GRID, SLOTS, D), F32)
        tap = lax.broadcasted_iota(jnp.int32, (WINDOW * WINDOW, 1), 0)
        row_off = jnp.abs(tap // WINDOW - HALO)
        col_off = jnp.abs(tap % WINDOW - HALO)
        off = jnp.maximum(row_off, col_off)
        heads = lax.broadcasted_iota(jnp.int32, (1, D), 1) // HEAD_DIM
        reach = jnp.where(heads < 2, 1, jnp.where(heads < 5, 2, 3))
        mask = jnp.where(off <= reach, 1.0, 0.0)
        self.window[...] = mask
        self.rel_taps[...] = self.small[22 : 22 + WINDOW * WINDOW, :] * mask

    def place(self, rows_ref, first, r0, size):
        count = rows_ref.shape[0]
        r = r0 + lax.broadcasted_iota(jnp.int32, (size, 1), 0)
        cell, slot = r >> 3, r & 7
        want = first + slot * CELLS + cell
        want = jnp.where((slot < self.cls.shape[1]) & (cell < CELLS), want, -1)
        col = lax.broadcasted_iota(jnp.int32, (size, count), 1)
        pick = jnp.where(col == want, 1.0, 0.0).astype(BF16)
        return dot(pick, rows_ref[...])

    def unplace(self, src_ref, out_ref):
        count = out_ref.shape[0]
        own = self.cls.shape[1] * CELLS
        lead = lax.rem(lax.axis_index(HEAD) * own, 16)
        r = lax.broadcasted_iota(jnp.int32, (1, ROWS), 1)
        cell, slot = r >> 3, r & 7
        target = lead + slot * CELLS + cell
        target = jnp.where((slot < self.cls.shape[1]) & (cell < CELLS), target, -1)
        t = lax.broadcasted_iota(jnp.int32, (count, ROWS), 0)
        pick = jnp.where(t == target, 1.0, 0.0).astype(BF16)
        out_ref[...] = dot(pick, src_ref[...]).astype(BF16)

    def read_tokens(self):
        first = lax.axis_index(HEAD) * (self.cls.shape[1] * CELLS)
        size = 80

        def body(r0, _):
            live = wide(self.live[pl.ds(r0, size), :])
            x = self.place(self.tokens, first, r0, size)
            self.first[pl.ds(r0, size), :] = x
            c0 = r0 // SLOTS
            self.pos_src[pl.ds(GRID + c0, size // SLOTS)] = (x * live).reshape(-1, SLOTS, D)
            return 0

        rows_loop(ROWS, size, body, 0)

    def read_cotangent(self):
        first = lax.axis_index(HEAD) * (self.cls.shape[1] * CELLS)
        size = 80

        def body(r0, _):
            live = wide(self.live[pl.ds(r0, size), :])
            c = self.place(self.cot, first, r0, size)
            self.go[pl.ds(r0, size), :] = (c * live).astype(BF16)
            return 0

        rows_loop(ROWS, size, body, 0)
        self.go_t[...] = self.go[...].T
        self.back[...] = jnp.zeros((ROWS, D), F32)

    def norm_one(self):
        for c in range(D // LANES):
            lanes = slice(c * LANES, (c + 1) * LANES)

            def put(cell, value):
                rows = pl.ds(pl.multiple_of(cell * SLOTS, SLOTS), SLOTS)
                self.first[rows, lanes] = self.first[rows, lanes] + value + self.small[8:9, lanes]

            def tap(a, b):
                t = 13 + (a + 1) * 3 + b + 1
                return self.small[t : t + 1, lanes]

            conv(self.pos_src, 1, tap, 1, lanes, put)

        def body(r0, _):
            rows = pl.ds(r0, 16)
            n, u, inv = norm_rows(self.first[rows, :], self.row(0), self.row(1))
            self.n1[rows, :] = n.astype(BF16)
            self.u1[rows, :] = u
            self.inv1[rows, :] = jnp.broadcast_to(inv, (16, LANES))
            return 0

        rows_loop(ROWS, 16, body, 0, unroll=5)
        self.n1_t[...] = self.n1[...].T

    def project(self, k):
        low = (self.q, self.k, self.v)[k]
        for b in range(2):
            cols = lane_block(b)
            p = self.times(self.n1[...], k, b)
            if k != 1:
                p = p + self.small[2 + k // 2 : 3 + k // 2, cols]
            low[:, cols] = p.astype(BF16)

    def image_sum(self, x):
        total = jnp.zeros((SLOTS, D), F32)
        for i in range(IMG_GROUP):
            im = wide(self.im8[i])
            total = total + im * jnp.sum(im * x, axis=0, keepdims=True)
        return total

    def softmax(self):
        def top(r0, best):
            live = wide(self.live[pl.ds(r0, 16), :])
            keys = jnp.where(live > 0, self.k[pl.ds(r0, 16), :].astype(F32), NEG_LARGE)
            return jnp.maximum(best, jnp.max(keys.reshape(2, SLOTS, D), axis=0))

        best = rows_loop(ROWS, 16, top, jnp.full((SLOTS, D), NEG_LARGE, F32), unroll=5)
        shift = jnp.zeros((SLOTS, D), F32)
        for i in range(IMG_GROUP):
            im = wide(self.im8[i])
            most = jnp.max(jnp.where(im > 0, best, NEG_LARGE), axis=0, keepdims=True)
            shift = jnp.where(im > 0, most, shift)
        shift2 = jnp.concatenate([shift, shift], axis=0)

        def raise_(r0, total):
            rows = pl.ds(r0, 16)
            live = wide(self.live[rows, :])
            keys = self.k[rows, :].astype(F32)
            e = jnp.where(live > 0, jnp.exp(jnp.where(live > 0, keys - shift2, 0.0)), 0.0)
            self.soft[rows, :] = e
            return total + fold(e)

        total = self.image_sum(
            rows_loop(ROWS, 16, raise_, jnp.zeros((SLOTS, D), F32), unroll=5)
        )
        scale = 1.0 / jnp.where(total > 0, total, 1.0)
        scale2 = jnp.concatenate([scale, scale], axis=0)

        def divide(r0, _):
            rows = pl.ds(r0, 16)
            soft = self.soft[rows, :] * scale2
            self.soft[rows, :] = soft
            self.soft_low[rows, :] = soft.astype(BF16)
            return 0

        rows_loop(ROWS, 16, divide, 0, unroll=5)

    def by_image(self, x):
        tiles = x.reshape(ROWS // 16, 16, WIDE)
        parts = []
        for i in range(IMG_GROUP):
            im = jnp.concatenate([self.im16[i]] * (WIDE // LANES), axis=1)
            parts.append((tiles * im[None]).reshape(ROWS, WIDE))
        return jnp.concatenate(parts, axis=1)

    def head_blocks(self, x):
        r = lax.broadcasted_iota(jnp.int32, x.shape, 0) // HEAD_DIM
        c = (lax.broadcasted_iota(jnp.int32, x.shape, 1) % WIDE) // HEAD_DIM
        return jnp.where(r == c, x, 0.0).astype(BF16)

    def stacked(self, x):
        return jnp.concatenate([x[:, lane_block(i)] for i in range(IMG_GROUP)], axis=0)

    def contexts(self):
        for b in range(2):
            cols = lane_block(b)
            ctx = dot(self.soft_low[:, cols], self.by_image(self.v[:, cols]), TN)
            ctx = self.head_blocks(ctx)
            self.ctx[b] = ctx
            self.factor[:, cols] = dot(self.by_image(self.q[:, cols]), self.stacked(ctx))

    def fill_window(self):
        def fill(r0, _):
            rows = pl.ds(r0, 16)
            v = self.v[rows, :].astype(F32) * wide(self.live[rows, :])
            c0 = r0 // SLOTS
            self.rel_src[pl.ds(HALO * GRID + c0, 2)] = v.reshape(2, SLOTS, D)
            return 0

        rows_loop(ROWS, 16, fill, 0, unroll=5)
        self.rel[CELLS * SLOTS :, :] = jnp.zeros((SLOTS, D), F32)

    def window_sum(self, c):
        lanes = slice(c * LANES, (c + 1) * LANES)

        def put(cell, value):
            rows = pl.ds(pl.multiple_of(cell * SLOTS, SLOTS), SLOTS)
            self.rel[rows, lanes] = value

        def tap(a, b):
            t = (a + HALO) * WINDOW + b + HALO
            return self.rel_taps[t : t + 1, lanes]

        conv(self.rel_src, HALO, tap, REACHES[c], lanes, put)

    def mix(self):
        def mix(r0, _):
            rows = pl.ds(r0, 16)
            m = self.factor[rows, :] * INV_SCALE + self.q[rows, :].astype(F32) * self.rel[rows, :]
            self.mixed[rows, :] = (m * wide(self.live[rows, :])).astype(BF16)
            return 0

        rows_loop(ROWS, 16, mix, 0, unroll=5)

    def norm_two(self):
        for b in range(2):
            cols = lane_block(b)
            p = self.times_t(self.mixed[...], 3, b)
            self.second[:, cols] = self.first[:, cols] + p + self.small[4:5, cols]

        def body(r0, _):
            rows = pl.ds(r0, 16)
            n, u, inv = norm_rows(self.second[rows, :], self.row(5), self.row(6))
            self.n2[rows, :] = n.astype(BF16)
            self.u2[rows, :] = u
            self.inv2[rows, :] = jnp.broadcast_to(inv, (16, LANES))
            return 0

        rows_loop(ROWS, 16, body, 0, unroll=5)
        self.n2_t[...] = self.n2[...].T

    def hidden_block(self, r):
        up, down = 4 + 2 * r, 5 + 2 * r
        for b in range(2):
            cols = lane_block(b)
            h = self.times(self.n2[...], up, b) + self.small[pl.ds(9 + r, 1), cols]
            self.hidden[:, cols] = h
            self.factor[:, cols] = self.times(self.go[...], down, b)

        def body(r0, total):
            rows = pl.ds(r0, 16)
            act, slope = erf_parts(self.hidden[rows, :])
            g = self.factor[rows, :] * slope
            self.active[rows, :] = act.astype(BF16)
            self.low[rows, :] = g.astype(BF16)
            return total + fold(g)

        total = rows_loop(ROWS, 16, body, jnp.zeros((SLOTS, D), F32), unroll=5)
        self.sums[pl.ds(9 + r, 1), :] = jnp.sum(total, axis=0, keepdims=True)

    def hidden_grads(self, r):
        up, down = 4 + 2 * r, 5 + 2 * r
        self.put_grad(down, self.go_t[...], self.active)
        self.put_grad(up, self.n2_t[...], self.low)
        for b in range(2):
            cols = lane_block(b)
            self.second[:, cols] += self.times_t(self.active[...], down, b)
            self.back[:, cols] += self.times_t(self.low[...], up, b)

    def finish_out(self):
        def body(r0, _):
            rows = pl.ds(r0, 16)
            self.out_low[rows, :] = (self.second[rows, :] + self.row(7)).astype(BF16)
            return 0

        rows_loop(ROWS, 16, body, 0, unroll=5)
        self.unplace(self.out_low, self.out_own)

    def back_two(self):
        zero = jnp.zeros((SLOTS, D), F32)

        def body(r0, sums):
            rows = pl.ds(r0, 16)
            back, u = self.back[rows, :], self.u2[rows, :]
            go = self.go[rows, :].astype(F32)
            gs = go + norm_back(back, u, wide(self.inv2[rows, :]), self.row(5))
            self.gs[rows, :] = gs
            self.gs_low[rows, :] = gs.astype(BF16)
            new = (gs, back * u, back, go)
            return tuple(s + fold(n) for s, n in zip(sums, new, strict=True))

        sums = rows_loop(ROWS, 16, body, (zero,) * 4, unroll=5)
        for j, s in zip((4, 5, 6, 7), sums, strict=True):
            self.sums[j : j + 1, :] = jnp.sum(s, axis=0, keepdims=True)

    def grad_proj(self):
        self.put_grad(3, self.gs_low[...].T, self.mixed)

    def back_heads(self):
        for b in range(2):
            cols = lane_block(b)
            self.d[:, cols] = self.times(self.gs_low[...], 3, b)

        def fill(r0, _):
            rows = pl.ds(r0, 16)
            d = self.d[rows, :] * wide(self.live[rows, :])
            self.d[rows, :] = d
            self.f[rows, :] = (d * INV_SCALE).astype(BF16)
            c0 = r0 // SLOTS
            dq = d * self.q[rows, :].astype(F32)
            self.dq_src[pl.ds(HALO * GRID + c0, 2)] = dq.reshape(2, SLOTS, D)
            return 0

        rows_loop(ROWS, 16, fill, 0, unroll=5)
        for b in range(2):
            cols = lane_block(b)
            f3 = self.by_image(self.f[:, cols])
            g = self.head_blocks(dot(self.q[:, cols], f3, TN))
            self.gq[:, cols] = dot(f3, self.ctx[b], NT)
            self.gk[:, cols] = dot(self.by_image(self.v[:, cols]), g, NT)
            self.gv[:, cols] = dot(self.by_image(self.soft_low[:, cols]), self.stacked(g))

    def back_window(self, c):
        lanes = slice(c * LANES, (c + 1) * LANES)

        def put(cell, value):
            rows = pl.ds(pl.multiple_of(cell * SLOTS, SLOTS), SLOTS)
            self.gv[rows, lanes] = self.gv[rows, lanes] + value * self.live[rows, :]

        def tap(a, b):
            t = (HALO - a) * WINDOW + HALO - b
            return self.rel_taps[t : t + 1, lanes]

        conv(self.dq_src, HALO, tap, REACHES[c], lanes, put)

    def window_taps(self, c):
        lanes = slice(c * LANES, (c + 1) * LANES)

        def up(cell):
            return self.dq_src[HALO * GRID + cell, :, lanes]

        def put_tap(a, b, value):
            t = (a + HALO) * WINDOW + b + HALO
            keep = self.window[t : t + 1, lanes]
            self.sums[22 + t : 23 + t, lanes] = value * keep

        tap_sums(up, self.rel_src, HALO, REACHES[c], lanes, put_tap)

    def back_query_key(self):
        zero = jnp.zeros((SLOTS, D), F32)

        def inner(r0, total):
            rows = pl.ds(r0, 16)
            return total + fold(self.soft[rows, :] * self.gk[rows, :])

        shared = self.image_sum(rows_loop(ROWS, 16, inner, zero, unroll=5))
        shared2 = jnp.concatenate([shared, shared], axis=0)

        def low(r0, total):
            rows = pl.ds(r0, 16)
            gq = self.gq[rows, :] + self.d[rows, :] * self.rel[rows, :]
            gk = self.soft[rows, :] * (self.gk[rows, :] - shared2)
            self.gl[0, rows, :] = gq.astype(BF16)
            self.gl[1, rows, :] = gk.astype(BF16)
            return total + fold(gq)

        total = rows_loop(ROWS, 16, low, zero, unroll=5)
        self.sums[2:3, :] = jnp.sum(total, axis=0, keepdims=True)

    def back_value(self):
        def low(r0, total):
            rows = pl.ds(r0, 16)
            gv = self.gv[rows, :]
            self.gl[2, rows, :] = gv.astype(BF16)
            return total + fold(gv)

        total = rows_loop(ROWS, 16, low, jnp.zeros((SLOTS, D), F32), unroll=5)
        self.sums[3:4, :] = jnp.sum(total, axis=0, keepdims=True)
        self.grad_of(2)

    def grad_of(self, k):
        self.put_grad(k, self.n1_t[...], self.gl.at[k])

    def back_project(self):
        for b in range(2):
            cols = lane_block(b)
            back = self.times_t(self.gl[0], 0, b)
            back = back + self.times_t(self.gl[1], 1, b)
            self.back[:, cols] = back + self.times_t(self.gl[2], 2, b)

    def back_one(self):
        zero = jnp.zeros((SLOTS, D), F32)
        self.pos_up[0:GRID] = jnp.zeros((GRID, SLOTS, D), F32)
        self.pos_up[GRID + CELLS :] = jnp.zeros((GRID, SLOTS, D), F32)

        def body(r0, sums):
            rows = pl.ds(r0, 16)
            back, u = self.back[rows, :], self.u1[rows, :]
            gf = self.gs[rows, :] + norm_back(back, u, wide(self.inv1[rows, :]), self.row(0))
            c0 = r0 // SLOTS
            self.pos_up[pl.ds(GRID + c0, 2)] = gf.reshape(2, SLOTS, D)
            new = (back * u, back, gf)
            return tuple(s + fold(n) for s, n in zip(sums, new, strict=True))

        sums = rows_loop(ROWS, 16, body, (zero,) * 3, unroll=5)
        for j, s in zip((0, 1, 8), sums, strict=True):
            self.sums[j : j + 1, :] = jnp.sum(s, axis=0, keepdims=True)

    def back_position(self):
        for c in range(D // LANES):
            lanes = slice(c * LANES, (c + 1) * LANES)

            def put(cell, value):
                rows = pl.ds(pl.multiple_of(cell * SLOTS, SLOTS), SLOTS)
                gf = self.pos_up[GRID + cell, :, lanes]
                self.first[rows, lanes] = gf + value * self.live[rows, :]

            def tap(a, b):
                t = 13 + (1 - a) * 3 + 1 - b
                return self.small[t : t + 1, lanes]

            conv(self.pos_up, 1, tap, 1, lanes, put)

    def position_taps(self):
        for c in range(D // LANES):
            lanes = slice(c * LANES, (c + 1) * LANES)

            def up(cell):
                return self.pos_up[GRID + cell, :, lanes]

            def put_tap(a, b, value):
                t = 13 + (a + 1) * 3 + b + 1
                self.sums[t : t + 1, lanes] = value

            tap_sums(up, self.pos_src, 1, 1, lanes, put_tap)

    def finish_in(self):
        def down(r0, _):
            rows = pl.ds(r0, 16)
            self.in_low[rows, :] = self.first[rows, :].astype(BF16)
            return 0

        rows_loop(ROWS, 16, down, 0, unroll=5)
        self.unplace(self.in_low, self.in_own)


SLOT_OF = (0, 1, 2, 3, 4, 6, 8, 10, 5, 7, 9, 11)
MATS = len(SLOT_OF)
AXES = "xchly"
HEAD_ROWS = 320
SMALL_ROWS = 72
AG_ROUTES = ("hlxyc", "lyhxc", "hlxyc", "hlyxc", "xyhlc", "xhlyc", "yhlxc", "lyhxc", "hlxyc", "xhylc", "hlxyc", "lxyhc")
RS_ROUTES = ("cylhx", "clyxh", "cyxlh", "clxyh", "cyxhl", "cxylh", "clhxy", "cxylh", "cylxh", "cxylh", "cyxlh", "cxylh")
ORDER = (
    30, 6, 12, 0, 18, 24, 36, 42, 48, 54, 60, 66, 144, 145, 31, 7, 146, 13, 1, 19,
    8, 25, 49, 37, 43, 55, 61, 67, 147, 32, 14, 26, 2, 44, 68, 20, 9, 50, 15, 38,
    69, 3, 62, 56, 21, 33, 10, 27, 16, 51, 11, 149, 151, 4, 45, 39, 17, 150, 153, 157,
    22, 156, 5, 148, 152, 34, 155, 28, 57, 23, 63, 46, 70, 154, 158, 159, 29, 52, 40, 47,
    35, 160, 161, 58, 53, 64, 71, 102, 96, 41, 162, 163, 59, 164, 65, 108, 103, 97, 114, 165,
    166, 120, 167, 132, 126, 138, 109, 115, 168, 121, 133, 98, 127, 104, 139, 189, 169, 171, 177, 178,
    176, 172, 175, 170, 179, 184, 84, 173, 174, 90, 72, 78, 122, 185, 85, 187, 91, 73, 183, 79,
    181, 180, 128, 123, 110, 134, 140, 99, 186, 86, 105, 188, 92, 192, 116, 182, 74, 195, 135, 124,
    80, 129, 87, 190, 196, 141, 111, 93, 106, 117, 100, 191, 75, 81, 136, 94, 125, 130, 88, 142,
    107, 118, 101, 193, 197, 76, 112, 137, 82, 95, 194, 131, 77, 89, 198, 113, 143, 119, 83, 204,
    199, 205, 200, 201, 206, 202, 203, 207,
)


def scratch_of():
    f, h, low = (ROWS, D), (ROWS, LANES), pltpu.VMEM((ROWS, D), BF16)
    halo3 = pltpu.VMEM(((GRID + 2 * HALO) * GRID, SLOTS, D), F32)
    halo1 = pltpu.VMEM(((GRID + 2) * GRID, SLOTS, D), F32)
    high, column, turned = pltpu.VMEM(f, F32), pltpu.VMEM(h, F32), pltpu.VMEM((D, ROWS), BF16)
    taps = pltpu.VMEM((WINDOW * WINDOW, D), F32)
    return dict(
        live=column,
        im8=pltpu.VMEM((IMG_GROUP, SLOTS, LANES), F32),
        im16=pltpu.VMEM((IMG_GROUP, 16, LANES), BF16),
        window=taps,
        rel_taps=taps,
        pos_src=halo1,
        pos_up=halo1,
        rel_src=halo3,
        dq_src=halo3,
        first=high,
        u1=high,
        inv1=column,
        second=high,
        u2=high,
        inv2=column,
        n1=low,
        n1_t=turned,
        n2=low,
        n2_t=turned,
        go=low,
        go_t=turned,
        q=low,
        k=low,
        v=low,
        soft=high,
        soft_low=low,
        ctx=pltpu.VMEM((2, WIDE, IMG_GROUP * WIDE), BF16),
        factor=high,
        rel=high,
        mixed=low,
        hidden=high,
        active=low,
        low=low,
        out_low=low,
        back=high,
        gs=high,
        gs_low=low,
        d=high,
        f=low,
        gq=high,
        gk=high,
        gv=high,
        gl=pltpu.VMEM((3, ROWS, D), BF16),
        in_low=low,
    )


class Links:
    def __init__(self):
        dp, head = lax.axis_index(DP), lax.axis_index(HEAD)
        self.far = lax.axis_size(DP) // 4
        self.at = dict(x=head // 2, c=head % 2, h=dp // 4, l=dp // 2 % 2, y=dp % 2)

    def count(self, axis):
        return self.far if axis == "h" else 2

    def peer(self, axis, step):
        return lax.rem(self.at[axis] + step, self.count(axis))

    def device(self, axis, step):
        at = {**self.at, axis: self.peer(axis, step)}
        return (at["h"] * 4 + at["l"] * 2 + at["y"], at["x"] * 2 + at["c"])

    def steps(self, axis, do):
        self.repeat(self.count(axis), do)

    def repeat(self, size, do):
        if size <= 8:
            for step in range(1, size):
                do(step)
        else:

            def body(step, _):
                do(step)
                return 0

            lax.fori_loop(1, size, body, 0)

    def others(self, name, do):
        index = {DP: lax.axis_index(DP), HEAD: lax.axis_index(HEAD)}

        def one(step):
            at = {**index, name: lax.rem(index[name] + step, lax.axis_size(name))}
            do(step, (at[DP], at[HEAD]))

        self.repeat(lax.axis_size(name), one)

    def greet(self):
        barrier = pltpu.get_barrier_semaphore()

        def signal(step, device):
            pl.semaphore_signal(
                barrier, inc=1, device_id=device, device_id_type=pl.DeviceIdType.MESH
            )

        self.others(HEAD, signal)
        self.others(DP, signal)
        pl.semaphore_wait(barrier, lax.axis_size(HEAD) + lax.axis_size(DP) - 2)

    def copy(self, src, dst, send, recv, device):
        return pltpu.make_async_remote_copy(
            src_ref=src,
            dst_ref=dst,
            send_sem=send,
            recv_sem=recv,
            device_id=device,
            device_id_type=pl.DeviceIdType.MESH,
        )

    def region(self, blocks, slot, whole, **at):
        at = {**self.at, **at}
        place = [slice(None) if axis in whole else at[axis] for axis in AXES]
        return blocks.at[(*place, slot)]


class Gather:
    def __init__(self, links, w, send, recv):
        self.links, self.w, self.send, self.recv = links, w, send, recv

    def start(self, slot, phase):
        path = AG_ROUTES[slot]
        part = self.links.region(self.w, slot, path[:phase])
        sems = self.send.at[slot, phase], self.recv.at[slot, phase]

        def go(step):
            self.links.copy(part, part, *sems, self.links.device(path[phase], step)).start()

        self.links.steps(path[phase], go)

    def descriptor(self, slot, phase):
        path = AG_ROUTES[slot]
        at = {"h": pl.ds(0, self.links.far - 1)} if path[phase] == "h" else {}
        part = self.links.region(self.w, slot, path[:phase], **at)
        sems = self.send.at[slot, phase], self.recv.at[slot, phase]
        return self.links.copy(part, part, *sems, self.links.device(path[phase], 1))

    def tick(self, slot, phase):
        if phase:
            self.descriptor(slot, phase - 1).wait_recv()
        if phase < len(AXES):
            self.start(slot, phase)

    def sent(self):
        for slot in range(MATS):
            for phase in range(len(AXES)):
                self.descriptor(slot, phase).wait_send()


class Scatter:
    def __init__(self, links, g, boxes, total, send, recv):
        self.links, self.g, self.boxes, self.total = links, g, boxes, total
        self.send, self.recv = send, recv

    def descriptor(self, slot, phase):
        box = self.boxes[slot * len(AXES) + phase]
        sems = self.send.at[slot, phase], self.recv.at[slot, phase]
        return self.links.copy(box, box, *sems, self.links.device(RS_ROUTES[slot][phase], 1))

    def take(self, slot, phase):
        path = RS_ROUTES[slot]
        self.descriptor(slot, phase).wait_recv()
        own = self.links.region(self.g, slot, path[phase + 1 :])
        box = self.boxes[slot * len(AXES) + phase]
        if path[phase] == "h" and box.shape[0] == 1:
            box = box.at[0]
        elif path[phase] == "h":
            value = own[...].astype(F32)
            return own, value + jnp.sum(box[...].astype(F32), axis=0)
        return own, own[...] + box[...] if phase + 1 < len(AXES) else (
            own[...].astype(F32) + box[...].astype(F32)
        )

    def start(self, slot, phase):
        path = RS_ROUTES[slot]
        axis, rest = path[phase], path[phase + 1 :]
        box = self.boxes[slot * len(AXES) + phase]
        sems = self.send.at[slot, phase], self.recv.at[slot, phase]

        def go(step):
            at = {axis: self.links.peer(axis, step)}
            part = self.links.region(self.g, slot, rest, **at)
            into = box.at[step - 1] if axis == "h" else box
            self.links.copy(part, into, *sems, self.links.device(axis, step)).start()

        self.links.steps(axis, go)

    def tick(self, slot, phase):
        if phase:
            own, value = self.take(slot, phase - 1)
            if phase == len(AXES):
                self.total[SLOT_OF.index(slot)] = value
                return
            own[...] = value.astype(BF16)
        self.start(slot, phase)

    def sent(self):
        for slot in range(MATS):
            for phase in range(len(AXES)):
                self.descriptor(slot, phase).wait_send()


class Small:
    def __init__(self, links, sums, parts, in_c, in_x, in_y, in_h, in_l, full, send, recv):
        self.links, self.sums, self.parts, self.full = links, sums, parts, full
        self.in_c, self.in_x, self.in_y, self.in_h, self.in_l = in_c, in_x, in_y, in_h, in_l
        self.send, self.recv = send, recv

    def go(self, stage, src, dst, axis):
        sems = (self.send.at[stage], self.recv.at[stage])
        self.links.steps(
            axis, lambda step: self.links.copy(src, dst, *sems, self.links.device(axis, step)).start()
        )

    def wait(self, stage):
        x, c = self.links.at["x"], self.links.at["c"]
        ref = (
            self.in_c,
            self.in_x,
            self.in_y,
            self.in_h.at[pl.ds(0, self.links.far - 1)],
            self.in_l,
            self.full.at[c, x],
            self.full.at[c],
        )[stage]
        sems = (self.send.at[stage], self.recv.at[stage])
        return self.links.copy(ref, ref, *sems, self.links.device("cxyhlxc"[stage], 1))

    def tick(self, stage):
        at = self.links.at
        x, c, h = at["x"], at["c"], at["h"]
        mine = self.parts.at[c, x]
        if stage:
            self.wait(stage - 1).wait_recv()
        if stage == 0:
            for b in range(D // LANES):
                self.parts[b // 2, b % 2] = self.sums[:, b * LANES : (b + 1) * LANES]
            self.go(0, self.parts.at[1 - c], self.in_c, "c")
        if stage == 1:
            self.parts[c] = self.parts[c] + self.in_c[...]
            self.go(1, self.parts.at[c, 1 - x], self.in_x, "x")
        if stage == 2:
            mine[...] = mine[...] + self.in_x[...]
            self.go(2, mine, self.in_y, "y")
        if stage == 3:
            self.in_h[h] = mine[...] + self.in_y[...]
            self.go(3, self.in_h.at[h], self.in_h.at[h], "h")
        if stage == 4:
            total = self.in_h[0]
            for i in range(1, self.links.far):
                total = total + self.in_h[i]
            self.sums[:, 0:LANES] = total
            self.go(4, self.sums.at[:, pl.ds(0, LANES)], self.in_l, "l")
        if stage == 5:
            self.full[c, x] = self.sums[:, 0:LANES] + self.in_l[...]
            self.go(5, self.full.at[c, x], self.full.at[c, x], "x")
        if stage == 6:
            self.go(6, self.full.at[c], self.full.at[c], "c")

    def sent(self):
        for stage in range(7):
            self.wait(stage).wait_send()


class Rows:
    def __init__(self, links, blocks, out, own, send, recv):
        self.links, self.blocks, self.out, self.own = links, blocks, out, own
        self.send, self.recv = send, recv

    def hop(self, i):
        x, c = self.links.at["x"], self.links.at["c"]
        x, axis = ((x, "x"), (x, "c"), (1 - x, "c"))[i]
        block = self.blocks.at[2 * x + c]
        return self.links.copy(
            block, block, self.send.at[i], self.recv.at[i], self.links.device(axis, 1)
        )

    def tick(self, stage):
        if stage == 0:
            self.hop(0).start()
            self.hop(1).start()
        if stage == 1:
            self.hop(0).wait_recv()
            self.hop(2).start()
        if stage == 2:
            self.hop(1).wait_recv()
            self.hop(2).wait_recv()
            self.join()

    def sent(self):
        for i in range(3):
            self.hop(i).wait_send()

    def join(self):
        heads, end, own = self.blocks.shape[0], self.out.shape[0], self.own
        for h in range(heads):
            lo, hi = h * own, (h + 1) * own
            base = lo // 16 * 16
            first = base + 16 if lo % 16 else base
            last = hi // 16 * 16 if h + 1 < heads else end
            self.out[first:last, :] = self.blocks[h, first - base : last - base, :]
            if lo % 16:
                before = (lo - own) // 16 * 16
                tail = self.blocks[h - 1, base - before : base - before + 16, :]
                self.out[base : base + 16, :] = tail + self.blocks[h, 0:16, :]


class Exchange:
    def __init__(self, links, name, buffer, send, recv):
        self.links, self.name, self.buffer, self.send, self.recv = links, name, buffer, send, recv

    def start(self, value):
        own = lax.axis_index(self.name)
        self.buffer[own] = value
        mine = self.buffer.at[own]
        self.links.others(
            self.name,
            lambda step, device: self.links.copy(mine, mine, self.send, self.recv, device).start(),
        )

    def descriptor(self):
        ref = self.buffer.at[pl.ds(0, self.buffer.shape[0] - 1)]
        return self.links.copy(ref, ref, self.send, self.recv, self.links.device("c", 1))

    def total(self):
        self.descriptor().wait_recv()
        return jnp.sum(self.buffer[...], axis=0)

    def sent(self):
        self.descriptor().wait_send()


def exact(a, b, dims):
    return lax.dot_general(
        a, b, dims, precision=lax.Precision.HIGHEST, preferred_element_type=F32
    )


class Adafactor:
    def __init__(self, refs, row_share, col_share, sq_dp, sq_head):
        self.__dict__.update(refs)
        self.row_share, self.col_share = row_share, col_share
        self.sq_dp, self.sq_head = sq_dp, sq_head

    def eye(self, count):
        r = lax.broadcasted_iota(jnp.int32, (count, LANES), 0)
        c = lax.broadcasted_iota(jnp.int32, (count, LANES), 1)
        return jnp.where(r == c, 1.0, 0.0)

    def lane(self, k, value, rest):
        lanes = lax.broadcasted_iota(jnp.int32, rest.shape, 1)
        return jnp.where(lanes == k, value, rest)

    def squares(self):
        rows = self.wg.shape[1]
        by_row = jnp.zeros((rows, LANES), F32)
        by_col = []
        for k in range(MATS):
            g = self.wg[k]
            s = g * g + SQUARE_FLOOR
            by_row = self.lane(k, jnp.sum(s, axis=1, keepdims=True), by_row)
            by_col.append(jnp.sum(s, axis=0, keepdims=True))
        self.col_share.start(jnp.concatenate([*by_col, jnp.zeros((4, LANES), F32)], axis=0))
        turned = exact(self.eye(16), by_row, NT)
        if rows < LANES:
            turned = jnp.concatenate([turned, jnp.zeros((16, LANES - rows), F32)], axis=1)
        self.row_share.start(turned)

    def scale(self):
        rows = self.wg.shape[1]
        total = self.row_share.total()[0:MATS, 0:rows]
        new_rows = SECOND_DECAY * self.row_state[...] + (1.0 - SECOND_DECAY) * (total * (1.0 / D))
        self.new_rows[...] = new_rows
        row = exact(new_rows, self.eye(MATS), TN)
        total = self.col_share.total()[0:MATS]
        cols = SECOND_DECAY * self.col_state[...] + (1.0 - SECOND_DECAY) * (total * (1.0 / D))
        self.new_cols[...] = cols
        sums = jnp.zeros((1, LANES), F32)
        for k in range(MATS):
            u = self.wg[k] * lax.rsqrt(row[:, k : k + 1] * cols[k : k + 1, :])
            self.upd[k] = u
            s = jnp.sum(jnp.sum(u * u, axis=0, keepdims=True), axis=1, keepdims=True)
            sums = self.lane(k, s, sums)
        mass = jnp.sum(row, axis=0, keepdims=True)
        self.sq_dp.start(jnp.concatenate([sums, mass, jnp.zeros((6, LANES), F32)], axis=0))

    def pass_on(self):
        self.sq_head.start(self.sq_dp.total())

    def apply(self):
        heads = self.sq_head.buffer.shape[0]
        total = self.sq_head.total()
        mean = total[1:2] * (1.0 / (D * heads))
        rms = jnp.sqrt(total[0:1] * mean * (1.0 / (D * D)))
        rate = STEP_RATE * jnp.sqrt(mean) / jnp.maximum(1.0, rms)
        for k in range(MATS):
            new = self.weights[k] - rate[:, k : k + 1] * self.upd[k]
            self.new_weights[k] = new
            self.copy[k] = new.astype(BF16)
            self.new_ema[k] = AVERAGE_KEEP * self.ema[k] + (1.0 - AVERAGE_KEEP) * new
        lanes = lax.broadcasted_iota(jnp.int32, (1, LANES), 1)
        clip = jnp.where(lanes < MATS, rms, self.small_clip[...])
        self.clip[...] = clip[:, 0 : self.clip.shape[1]]

    def small_step(self):
        count, full = self.small.shape[0], self.full
        g = jnp.concatenate([full[b // 2, b % 2, 0:count, :] for b in range(D // LANES)], axis=1)
        self.small_grads[...] = g
        state = SECOND_DECAY * self.small_state[...] + (1.0 - SECOND_DECAY) * (
            g * g + SQUARE_FLOOR
        )
        self.new_small_state[...] = state
        u = g * lax.rsqrt(state)
        rms = jnp.sqrt(jnp.sum(u * u, axis=1, keepdims=True) * (1.0 / D))
        new = self.small[...] - SMALL_RATE * u / jnp.maximum(1.0, rms)
        self.new_small[...] = new
        self.new_small_ema[...] = AVERAGE_KEEP * self.small_ema[...] + (1.0 - AVERAGE_KEEP) * new
        r = lax.broadcasted_iota(jnp.int32, (count, LANES), 0)
        c = lax.broadcasted_iota(jnp.int32, (count, LANES), 1)
        picked = jnp.where(c == r + MATS, rms, 0.0)
        self.small_clip[...] = jnp.sum(picked, axis=0, keepdims=True)


class Inputs(NamedTuple):
    cls: Any
    img: Any
    tokens: Any
    cot: Any
    weights: Any
    row_state: Any
    col_state: Any
    ema: Any
    small: Any
    small_state: Any
    small_ema: Any


class Outputs(NamedTuple):
    out: Any
    grad_in: Any
    wg: Any
    new_rows: Any
    new_cols: Any
    new_weights: Any
    copy: Any
    new_ema: Any
    small_grads: Any
    new_small_state: Any
    new_small: Any
    new_small_ema: Any
    clip: Any


def box_shapes(links, block):
    for slot in range(MATS):
        path = RS_ROUTES[slot]
        for phase, axis in enumerate(path):
            lead = [links.count(a) for a in AXES if a in path[phase + 1 :]]
            if axis == "h":
                lead = [links.far - 1, *lead]
            yield pltpu.VMEM((*lead, *block), BF16)


def shared_of(weights, parts, heads):
    links, (_, rows, _) = Links(), weights.shape
    block = (rows, LANES)
    every = pltpu.VMEM((2, 2, links.far, 2, 2, MATS, *block), BF16)
    out_rows = pltpu.VMEM((heads, HEAD_ROWS, D), BF16)
    dma = pltpu.SemaphoreType.DMA

    def f(*shape):
        return pltpu.VMEM(shape, F32)

    part = f(SMALL_ROWS, LANES)
    return dict(
        w=every,
        g=every,
        out_rows=out_rows,
        in_rows=out_rows,
        sums=f(SMALL_ROWS, D),
        parts=f(2, 2, SMALL_ROWS, LANES),
        in_c=f(2, SMALL_ROWS, LANES),
        in_x=part,
        in_y=part,
        in_h=f(links.far, SMALL_ROWS, LANES),
        in_l=part,
        full=f(2, 2, SMALL_ROWS, LANES),
        row_box=f(heads, 16, LANES),
        col_box=f(parts, 16, LANES),
        sq_dp_box=f(parts, SLOTS, LANES),
        sq_head_box=f(heads, SLOTS, LANES),
        upd=f(MATS, *block),
        small_clip=f(1, LANES),
        ag_send=dma((MATS, len(AXES))),
        ag_recv=dma((MATS, len(AXES))),
        rs_send=dma((MATS, len(AXES))),
        rs_recv=dma((MATS, len(AXES))),
        small_send=dma((7,)),
        small_recv=dma((7,)),
        out_send=dma((3,)),
        out_recv=dma((3,)),
        in_send=dma((3,)),
        in_recv=dma((3,)),
        opt_send=dma((4,)),
        opt_recv=dma((4,)),
    )


def block_kernel(names, *refs):
    r = types.SimpleNamespace(**dict(zip(names, refs)))
    boxes = refs[len(names) :]
    r.out_own = r.out_rows.at[lax.axis_index(HEAD)]
    r.in_own = r.in_rows.at[lax.axis_index(HEAD)]
    own = r.cls.shape[1] * CELLS
    blk = Block(vars(r))
    links = Links()
    gather = Gather(links, r.w, r.ag_send, r.ag_recv)
    scatter = Scatter(links, r.g, boxes, r.wg, r.rs_send, r.rs_recv)
    small = Small(
        links,
        *(r.sums, r.parts, r.in_c, r.in_x, r.in_y, r.in_h, r.in_l, r.full),
        r.small_send,
        r.small_recv,
    )
    out_rows = Rows(links, r.out_rows, r.out, own, r.out_send, r.out_recv)
    in_rows = Rows(links, r.in_rows, r.grad_in, own, r.in_send, r.in_recv)
    shares = [
        Exchange(links, axis, box, r.opt_send.at[i], r.opt_recv.at[i])
        for i, (axis, box) in enumerate(
            ((HEAD, r.row_box), (DP, r.col_box), (DP, r.sq_dp_box), (HEAD, r.sq_head_box))
        )
    ]
    opt = Adafactor(vars(r), *shares)

    for k in range(MATS):
        mine = links.region(r.w, SLOT_OF[k], "")
        mine[...] = r.weights[k].astype(BF16)
    links.greet()

    ops = []
    for tick in (gather.tick, scatter.tick):
        ops += [
            functools.partial(tick, slot, phase)
            for slot in range(MATS)
            for phase in range(len(AXES) + 1)
        ]
    ops += [blk.setup, blk.read_tokens, blk.norm_one, blk.read_cotangent]
    ops += [functools.partial(blk.project, k) for k in range(3)]
    ops += [blk.softmax, blk.contexts, blk.fill_window]
    ops += [functools.partial(blk.window_sum, c) for c in range(D // LANES)]
    ops += [blk.mix, blk.norm_two]
    for i in range(4):
        ops += [functools.partial(blk.hidden_block, i), functools.partial(blk.hidden_grads, i)]
    ops += [blk.finish_out, blk.back_two, blk.grad_proj, blk.back_heads, blk.back_query_key]
    ops += [functools.partial(blk.grad_of, k) for k in range(2)]
    ops += [functools.partial(blk.back_window, c) for c in range(D // LANES)]
    ops += [blk.back_value]
    ops += [functools.partial(blk.window_taps, c) for c in range(D // LANES)]
    ops += [blk.back_project, blk.back_one, blk.back_position, blk.position_taps, blk.finish_in]
    for rows in (out_rows, in_rows):
        ops += [functools.partial(rows.tick, stage) for stage in range(3)]
    ops += [functools.partial(small.tick, stage) for stage in range(8)]
    ops += [opt.small_step, opt.squares, opt.scale, opt.pass_on, opt.apply]
    for i in ORDER:
        ops[i]()
    for transfer in (gather, scatter, small, out_rows, in_rows, *shares):
        transfer.sent()


def local(
    tokens,
    cotangent,
    crop_image,
    crop_class,
    weights,
    row_state,
    col_state,
    weights_ema,
    small_params,
    small_state,
    small_ema,
):
    parts, heads = lax.axis_size(DP), lax.axis_size(HEAD)
    smem = pl.BlockSpec(memory_space=pltpu.SMEM)
    vmem = pl.BlockSpec(memory_space=pltpu.VMEM)
    shared = shared_of(weights, parts, heads)
    own = scratch_of()

    def like(x, dtype=None):
        return jax.ShapeDtypeStruct(x.shape, dtype or x.dtype)

    clips = weights.shape[0] + small_params.shape[0]
    outs = (
        like(tokens),
        like(tokens),
        like(weights),
        like(row_state),
        like(col_state),
        like(weights),
        like(weights, BF16),
        like(weights),
        like(small_params),
        like(small_params),
        like(small_params),
        like(small_params),
        jax.ShapeDtypeStruct((1, clips), F32),
    )
    names = (*Inputs._fields, *Outputs._fields, *shared, *own)
    res = pl.pallas_call(
        functools.partial(block_kernel, names),
        out_shape=outs,
        in_specs=[smem, smem] + [vmem] * 9,
        out_specs=(vmem,) * len(outs),
        scratch_shapes=[
            *shared.values(),
            *own.values(),
            *box_shapes(Links(), weights.shape[1:]),
        ],
        compiler_params=pltpu.CompilerParams(
            collective_id=0, has_side_effects=True, vmem_limit_bytes=63 << 20
        ),
        name="block",
    )(
        crop_class,
        crop_image,
        tokens,
        cotangent,
        weights,
        row_state,
        col_state,
        weights_ema,
        small_params,
        small_state,
        small_ema,
    )
    return (*res[:-1], res[-1].reshape(clips))


def solution(mesh):
    in_specs = (
        P(DP, None),
        P(DP, None),
        P(DP, None),
        P(DP, None),
        P(None, DP, HEAD),
        P(None, DP),
        P(None, HEAD),
        P(None, DP, HEAD),
        P(),
        P(),
        P(),
    )
    out_specs = (
        P(DP, None),
        P(DP, None),
        P(None, DP, HEAD),
        P(None, DP),
        P(None, HEAD),
        P(None, DP, HEAD),
        P(None, DP, HEAD),
        P(None, DP, HEAD),
        P(),
        P(),
        P(),
        P(),
        P(),
    )
    return jax.shard_map(local, mesh=mesh, in_specs=in_specs, out_specs=out_specs, check_vma=False)
```

```python
import functools
import math
import types
from typing import Any, NamedTuple

import jax
import jax.numpy as jnp
from jax import lax
from jax.experimental import pallas as pl
from jax.experimental.pallas import tpu as pltpu
from jax.sharding import PartitionSpec as P

DP, HEAD = "dp", "head"
ALL = (DP, HEAD)
D = 512
HEAD_DIM = 64
GRID = 7
SMALL_GRID = 3
WINDOW = 7
IMG_GROUP = 3
CELLS = GRID * GRID
SLOTS = 8
CELL_PAD = CELLS + 1
ROWS = CELL_PAD * SLOTS
LANES = 128
WIDE = 256
REACHES = (1, 2, 3, 3)
HALO = WINDOW // 2

NORM_EPS = 1e-06
SQUARE_FLOOR = 1e-30
SECOND_DECAY = 0.999
STEP_RATE = 0.02
SMALL_RATE = 0.05
AVERAGE_KEEP = 0.9
NEG_LARGE = -1e30
ROOT_HALF = 0.7071067811865476
INV_ROOT_TAU = 0.3989422804014327
INV_SCALE = 1.0 / math.sqrt(HEAD_DIM)

F32 = jnp.float32
BF16 = jnp.bfloat16
NN = (((1,), (0,)), ((), ()))
NT = (((1,), (1,)), ((), ()))
TN = (((0,), (0,)), ((), ()))


def dot(a, b, dims=NN):
    return lax.dot_general(a, b, dims, preferred_element_type=F32)


def lane_block(b):
    return slice(b * WIDE, (b + 1) * WIDE)


def wide(col):
    return jnp.concatenate([col] * (D // LANES), axis=1)


def rows_loop(count, size, body, init=None, unroll=1):
    def step(j, carry):
        return body(pl.multiple_of(j * size, size), carry)

    return lax.fori_loop(0, count // size, step, init, unroll=unroll)


def conv(src, halo, tap, reach, lanes, put):
    def line(y, _):
        sums = [jnp.zeros((SLOTS, LANES), F32) for _ in range(GRID)]
        for a in range(-reach, reach + 1):
            base = (y + (a + halo)) * GRID
            cells = [src[base + x, :, lanes] for x in range(GRID)]
            for b in range(-reach, reach + 1):
                t = tap(a, b)
                for x in range(GRID):
                    if 0 <= x + b < GRID:
                        sums[x] = sums[x] + t * cells[x + b]
        for x in range(GRID):
            put(y * GRID + x, sums[x])
        return 0

    lax.fori_loop(0, GRID, line, 0)


def tap_sums(up, src, halo, reach, lanes, put):
    for a in range(-reach, reach + 1):

        def line(y, sums):
            sums = list(sums)
            ups = [up(y * GRID + x) for x in range(GRID)]
            base = (y + (a + halo)) * GRID
            cells = [src[base + x, :, lanes] for x in range(GRID)]
            for i, b in enumerate(range(-reach, reach + 1)):
                for x in range(GRID):
                    if 0 <= x + b < GRID:
                        sums[i] = sums[i] + ups[x] * cells[x + b]
            return tuple(sums)

        start = tuple(jnp.zeros((SLOTS, LANES), F32) for _ in range(2 * reach + 1))
        sums = lax.fori_loop(0, GRID, line, start)
        for i, b in enumerate(range(-reach, reach + 1)):
            put(a, b, jnp.sum(sums[i], axis=0, keepdims=True))


def fold(x):
    return jnp.sum(x.reshape(x.shape[0] // SLOTS, SLOTS, x.shape[1]), axis=0)


def erf_parts(h):
    e = lax.erf(h * ROOT_HALF)
    half = 0.5 * (1.0 + e)
    return h * half, half + h * jnp.exp(-0.5 * h * h) * INV_ROOT_TAU


def norm_rows(v, gain, shift):
    centre = jnp.sum(v, axis=1, keepdims=True) * (1.0 / D)
    offset = v - centre
    spread = jnp.sum(offset * offset, axis=1, keepdims=True) * (1.0 / D)
    inverse = lax.rsqrt(spread + NORM_EPS)
    unit = offset * inverse
    return unit * gain + shift, unit, inverse


def norm_back(up, unit, inverse, gain):
    z = up * gain
    mean_z = jnp.sum(z, axis=1, keepdims=True) * (1.0 / D)
    mean_zu = jnp.sum(z * unit, axis=1, keepdims=True) * (1.0 / D)
    return inverse * (z - mean_z - unit * mean_zu)


class Block:
    def __init__(self, refs):
        self.__dict__.update(refs)

    def matrix(self, k, lo, hi):
        parts = []
        for h in range(lo, hi):
            part = self.w[h // 2, h % 2, :, :, :, k]
            if part.shape[-2] % 16:
                part = part.astype(F32).reshape(D, LANES).astype(BF16)
            else:
                part = part.reshape(D, LANES)
            parts.append(part)
        return jnp.concatenate(parts, axis=1)

    def times(self, lhs, k, b):
        return dot(lhs, self.matrix(k, 2 * b, 2 * b + 2))

    def times_t(self, lhs, k, b):
        return dot(lhs, self.matrix(k, 0, 4)[lane_block(b), :], NT)

    def put_grad(self, k, lhs_t, rhs):
        for b in range(2):
            g = dot(lhs_t, rhs[:, lane_block(b)])
            for i in range(2):
                piece = g[:, i * LANES : (i + 1) * LANES]
                place = self.g.shape[2:5]
                piece = piece.reshape(*place, self.g.shape[-2], LANES)
                self.g[b, i, :, :, :, k] = piece.astype(BF16)

    def row(self, j):
        return self.small[j : j + 1, :]

    def setup(self):
        head = lax.axis_index(HEAD)
        slots = self.cls.shape[1]
        self.sums[...] = jnp.zeros(self.sums.shape, F32)
        sub = lax.broadcasted_iota(jnp.int32, (SLOTS, LANES), 0)
        valid = jnp.where(sub < slots, 1.0, 0.0)
        full = jnp.zeros((SLOTS, LANES), F32)
        images = [jnp.zeros((SLOTS, LANES), F32) for _ in range(IMG_GROUP)]
        for s in range(slots):
            full = jnp.where(sub == s, jnp.where(self.cls[head, s] == 0, 1.0, 0.0), full)
            for i in range(IMG_GROUP):
                images[i] = jnp.where(
                    sub == s, jnp.where(self.img[head, s] == i, 1.0, 0.0), images[i]
                )
        for cell in range(CELLS):
            small = cell // GRID < SMALL_GRID and cell % GRID < SMALL_GRID
            self.live[cell * SLOTS : (cell + 1) * SLOTS, :] = valid if small else full
        self.live[CELLS * SLOTS :, :] = jnp.zeros((SLOTS, LANES), F32)
        for i in range(IMG_GROUP):
            self.im8[i] = images[i]
            self.im16[i] = jnp.concatenate([images[i], images[i]], axis=0).astype(BF16)
        self.pos_src[0:GRID] = jnp.zeros((GRID, SLOTS, D), F32)
        self.pos_src[GRID + CELLS :] = jnp.zeros((GRID, SLOTS, D), F32)
        for pad in (self.rel_src, self.dq_src):
            pad[0 : HALO * GRID] = jnp.zeros((HALO * GRID, SLOTS, D), F32)
            pad[HALO * GRID + CELLS :] = jnp.zeros((HALO * GRID, SLOTS, D), F32)
        tap = lax.broadcasted_iota(jnp.int32, (WINDOW * WINDOW, 1), 0)
        row_off = jnp.abs(tap // WINDOW - HALO)
        col_off = jnp.abs(tap % WINDOW - HALO)
        off = jnp.maximum(row_off, col_off)
        heads = lax.broadcasted_iota(jnp.int32, (1, D), 1) // HEAD_DIM
        reach = jnp.where(heads < 2, 1, jnp.where(heads < 5, 2, 3))
        mask = jnp.where(off <= reach, 1.0, 0.0)
        self.window[...] = mask
        self.rel_taps[...] = self.small[22 : 22 + WINDOW * WINDOW, :] * mask

    def place(self, rows_ref, first, r0, size):
        count = rows_ref.shape[0]
        r = r0 + lax.broadcasted_iota(jnp.int32, (size, 1), 0)
        cell, slot = r >> 3, r & 7
        want = first + slot * CELLS + cell
        want = jnp.where((slot < self.cls.shape[1]) & (cell < CELLS), want, -1)
        col = lax.broadcasted_iota(jnp.int32, (size, count), 1)
        pick = jnp.where(col == want, 1.0, 0.0).astype(BF16)
        return dot(pick, rows_ref[...])

    def unplace(self, src_ref, out_ref):
        count = out_ref.shape[0]
        own = self.cls.shape[1] * CELLS
        lead = lax.rem(lax.axis_index(HEAD) * own, 16)
        r = lax.broadcasted_iota(jnp.int32, (1, ROWS), 1)
        cell, slot = r >> 3, r & 7
        target = lead + slot * CELLS + cell
        target = jnp.where((slot < self.cls.shape[1]) & (cell < CELLS), target, -1)
        t = lax.broadcasted_iota(jnp.int32, (count, ROWS), 0)
        pick = jnp.where(t == target, 1.0, 0.0).astype(BF16)
        out_ref[...] = dot(pick, src_ref[...]).astype(BF16)

    def read_tokens(self):
        first = lax.axis_index(HEAD) * (self.cls.shape[1] * CELLS)
        size = 80

        def body(r0, _):
            live = wide(self.live[pl.ds(r0, size), :])
            x = self.place(self.tokens, first, r0, size)
            self.first[pl.ds(r0, size), :] = x
            c0 = r0 // SLOTS
            self.pos_src[pl.ds(GRID + c0, size // SLOTS)] = (x * live).reshape(-1, SLOTS, D)
            return 0

        rows_loop(ROWS, size, body, 0)

    def read_cotangent(self):
        first = lax.axis_index(HEAD) * (self.cls.shape[1] * CELLS)
        size = 80

        def body(r0, _):
            live = wide(self.live[pl.ds(r0, size), :])
            c = self.place(self.cot, first, r0, size)
            self.go[pl.ds(r0, size), :] = (c * live).astype(BF16)
            return 0

        rows_loop(ROWS, size, body, 0)
        self.go_t[...] = self.go[...].T
        self.back[...] = jnp.zeros((ROWS, D), F32)

    def norm_one(self):
        for c in range(D // LANES):
            lanes = slice(c * LANES, (c + 1) * LANES)

            def put(cell, value):
                rows = pl.ds(pl.multiple_of(cell * SLOTS, SLOTS), SLOTS)
                self.first[rows, lanes] = self.first[rows, lanes] + value + self.small[8:9, lanes]

            def tap(a, b):
                t = 13 + (a + 1) * 3 + b + 1
                return self.small[t : t + 1, lanes]

            conv(self.pos_src, 1, tap, 1, lanes, put)

        def body(r0, _):
            rows = pl.ds(r0, 16)
            n, u, inv = norm_rows(self.first[rows, :], self.row(0), self.row(1))
            self.n1[rows, :] = n.astype(BF16)
            self.u1[rows, :] = u
            self.inv1[rows, :] = jnp.broadcast_to(inv, (16, LANES))
            return 0

        rows_loop(ROWS, 16, body, 0, unroll=5)
        self.n1_t[...] = self.n1[...].T

    def project(self, k):
        low = (self.q, self.k, self.v)[k]
        for b in range(2):
            cols = lane_block(b)
            p = self.times(self.n1[...], k, b)
            if k != 1:
                p = p + self.small[2 + k // 2 : 3 + k // 2, cols]
            low[:, cols] = p.astype(BF16)

    def image_sum(self, x):
        total = jnp.zeros((SLOTS, D), F32)
        for i in range(IMG_GROUP):
            im = wide(self.im8[i])
            total = total + im * jnp.sum(im * x, axis=0, keepdims=True)
        return total

    def softmax(self):
        def top(r0, best):
            live = wide(self.live[pl.ds(r0, 16), :])
            keys = jnp.where(live > 0, self.k[pl.ds(r0, 16), :].astype(F32), NEG_LARGE)
            return jnp.maximum(best, jnp.max(keys.reshape(2, SLOTS, D), axis=0))

        best = rows_loop(ROWS, 16, top, jnp.full((SLOTS, D), NEG_LARGE, F32), unroll=5)
        shift = jnp.zeros((SLOTS, D), F32)
        for i in range(IMG_GROUP):
            im = wide(self.im8[i])
            most = jnp.max(jnp.where(im > 0, best, NEG_LARGE), axis=0, keepdims=True)
            shift = jnp.where(im > 0, most, shift)
        shift2 = jnp.concatenate([shift, shift], axis=0)

        def raise_(r0, total):
            rows = pl.ds(r0, 16)
            live = wide(self.live[rows, :])
            keys = self.k[rows, :].astype(F32)
            e = jnp.where(live > 0, jnp.exp(jnp.where(live > 0, keys - shift2, 0.0)), 0.0)
            self.soft[rows, :] = e
            return total + fold(e)

        total = self.image_sum(
            rows_loop(ROWS, 16, raise_, jnp.zeros((SLOTS, D), F32), unroll=5)
        )
        scale = 1.0 / jnp.where(total > 0, total, 1.0)
        scale2 = jnp.concatenate([scale, scale], axis=0)

        def divide(r0, _):
            rows = pl.ds(r0, 16)
            soft = self.soft[rows, :] * scale2
            self.soft[rows, :] = soft
            self.soft_low[rows, :] = soft.astype(BF16)
            return 0

        rows_loop(ROWS, 16, divide, 0, unroll=5)

    def by_image(self, x):
        tiles = x.reshape(ROWS // 16, 16, WIDE)
        parts = []
        for i in range(IMG_GROUP):
            im = jnp.concatenate([self.im16[i]] * (WIDE // LANES), axis=1)
            parts.append((tiles * im[None]).reshape(ROWS, WIDE))
        return jnp.concatenate(parts, axis=1)

    def head_blocks(self, x):
        r = lax.broadcasted_iota(jnp.int32, x.shape, 0) // HEAD_DIM
        c = (lax.broadcasted_iota(jnp.int32, x.shape, 1) % WIDE) // HEAD_DIM
        return jnp.where(r == c, x, 0.0).astype(BF16)

    def stacked(self, x):
        return jnp.concatenate([x[:, lane_block(i)] for i in range(IMG_GROUP)], axis=0)

    def contexts(self):
        for b in range(2):
            cols = lane_block(b)
            ctx = dot(self.soft_low[:, cols], self.by_image(self.v[:, cols]), TN)
            ctx = self.head_blocks(ctx)
            self.ctx[b] = ctx
            self.factor[:, cols] = dot(self.by_image(self.q[:, cols]), self.stacked(ctx))

    def fill_window(self):
        def fill(r0, _):
            rows = pl.ds(r0, 16)
            v = self.v[rows, :].astype(F32) * wide(self.live[rows, :])
            c0 = r0 // SLOTS
            self.rel_src[pl.ds(HALO * GRID + c0, 2)] = v.reshape(2, SLOTS, D)
            return 0

        rows_loop(ROWS, 16, fill, 0, unroll=5)
        self.rel[CELLS * SLOTS :, :] = jnp.zeros((SLOTS, D), F32)

    def window_sum(self, c):
        lanes = slice(c * LANES, (c + 1) * LANES)

        def put(cell, value):
            rows = pl.ds(pl.multiple_of(cell * SLOTS, SLOTS), SLOTS)
            self.rel[rows, lanes] = value

        def tap(a, b):
            t = (a + HALO) * WINDOW + b + HALO
            return self.rel_taps[t : t + 1, lanes]

        conv(self.rel_src, HALO, tap, REACHES[c], lanes, put)

    def mix(self):
        def mix(r0, _):
            rows = pl.ds(r0, 16)
            m = self.factor[rows, :] * INV_SCALE + self.q[rows, :].astype(F32) * self.rel[rows, :]
            self.mixed[rows, :] = (m * wide(self.live[rows, :])).astype(BF16)
            return 0

        rows_loop(ROWS, 16, mix, 0, unroll=5)

    def norm_two(self):
        for b in range(2):
            cols = lane_block(b)
            p = self.times_t(self.mixed[...], 3, b)
            self.second[:, cols] = self.first[:, cols] + p + self.small[4:5, cols]

        def body(r0, _):
            rows = pl.ds(r0, 16)
            n, u, inv = norm_rows(self.second[rows, :], self.row(5), self.row(6))
            self.n2[rows, :] = n.astype(BF16)
            self.u2[rows, :] = u
            self.inv2[rows, :] = jnp.broadcast_to(inv, (16, LANES))
            return 0

        rows_loop(ROWS, 16, body, 0, unroll=5)
        self.n2_t[...] = self.n2[...].T

    def hidden_block(self, r):
        up, down = 4 + 2 * r, 5 + 2 * r
        for b in range(2):
            cols = lane_block(b)
            h = self.times(self.n2[...], up, b) + self.small[pl.ds(9 + r, 1), cols]
            self.hidden[:, cols] = h
            self.factor[:, cols] = self.times(self.go[...], down, b)

        def body(r0, total):
            rows = pl.ds(r0, 16)
            act, slope = erf_parts(self.hidden[rows, :])
            g = self.factor[rows, :] * slope
            self.active[rows, :] = act.astype(BF16)
            self.low[rows, :] = g.astype(BF16)
            return total + fold(g)

        total = rows_loop(ROWS, 16, body, jnp.zeros((SLOTS, D), F32), unroll=5)
        self.sums[pl.ds(9 + r, 1), :] = jnp.sum(total, axis=0, keepdims=True)

    def hidden_grads(self, r):
        up, down = 4 + 2 * r, 5 + 2 * r
        self.put_grad(down, self.go_t[...], self.active)
        self.put_grad(up, self.n2_t[...], self.low)
        for b in range(2):
            cols = lane_block(b)
            self.second[:, cols] += self.times_t(self.active[...], down, b)
            self.back[:, cols] += self.times_t(self.low[...], up, b)

    def finish_out(self):
        def body(r0, _):
            rows = pl.ds(r0, 16)
            self.out_low[rows, :] = (self.second[rows, :] + self.row(7)).astype(BF16)
            return 0

        rows_loop(ROWS, 16, body, 0, unroll=5)
        self.unplace(self.out_low, self.out_own)

    def back_two(self):
        zero = jnp.zeros((SLOTS, D), F32)

        def body(r0, sums):
            rows = pl.ds(r0, 16)
            back, u = self.back[rows, :], self.u2[rows, :]
            go = self.go[rows, :].astype(F32)
            gs = go + norm_back(back, u, wide(self.inv2[rows, :]), self.row(5))
            self.gs[rows, :] = gs
            self.gs_low[rows, :] = gs.astype(BF16)
            new = (gs, back * u, back, go)
            return tuple(s + fold(n) for s, n in zip(sums, new, strict=True))

        sums = rows_loop(ROWS, 16, body, (zero,) * 4, unroll=5)
        for j, s in zip((4, 5, 6, 7), sums, strict=True):
            self.sums[j : j + 1, :] = jnp.sum(s, axis=0, keepdims=True)

    def grad_proj(self):
        self.put_grad(3, self.gs_low[...].T, self.mixed)

    def back_heads(self):
        for b in range(2):
            cols = lane_block(b)
            self.d[:, cols] = self.times(self.gs_low[...], 3, b)

        def fill(r0, _):
            rows = pl.ds(r0, 16)
            d = self.d[rows, :] * wide(self.live[rows, :])
            self.d[rows, :] = d
            self.f[rows, :] = (d * INV_SCALE).astype(BF16)
            c0 = r0 // SLOTS
            dq = d * self.q[rows, :].astype(F32)
            self.dq_src[pl.ds(HALO * GRID + c0, 2)] = dq.reshape(2, SLOTS, D)
            return 0

        rows_loop(ROWS, 16, fill, 0, unroll=5)
        for b in range(2):
            cols = lane_block(b)
            f3 = self.by_image(self.f[:, cols])
            g = self.head_blocks(dot(self.q[:, cols], f3, TN))
            self.gq[:, cols] = dot(f3, self.ctx[b], NT)
            self.gk[:, cols] = dot(self.by_image(self.v[:, cols]), g, NT)
            self.gv[:, cols] = dot(self.by_image(self.soft_low[:, cols]), self.stacked(g))

    def back_window(self, c):
        lanes = slice(c * LANES, (c + 1) * LANES)

        def put(cell, value):
            rows = pl.ds(pl.multiple_of(cell * SLOTS, SLOTS), SLOTS)
            self.gv[rows, lanes] = self.gv[rows, lanes] + value * self.live[rows, :]

        def tap(a, b):
            t = (HALO - a) * WINDOW + HALO - b
            return self.rel_taps[t : t + 1, lanes]

        conv(self.dq_src, HALO, tap, REACHES[c], lanes, put)

    def window_taps(self, c):
        lanes = slice(c * LANES, (c + 1) * LANES)

        def up(cell):
            return self.dq_src[HALO * GRID + cell, :, lanes]

        def put_tap(a, b, value):
            t = (a + HALO) * WINDOW + b + HALO
            keep = self.window[t : t + 1, lanes]
            self.sums[22 + t : 23 + t, lanes] = value * keep

        tap_sums(up, self.rel_src, HALO, REACHES[c], lanes, put_tap)

    def back_query_key(self):
        zero = jnp.zeros((SLOTS, D), F32)

        def inner(r0, total):
            rows = pl.ds(r0, 16)
            return total + fold(self.soft[rows, :] * self.gk[rows, :])

        shared = self.image_sum(rows_loop(ROWS, 16, inner, zero, unroll=5))
        shared2 = jnp.concatenate([shared, shared], axis=0)

        def low(r0, total):
            rows = pl.ds(r0, 16)
            gq = self.gq[rows, :] + self.d[rows, :] * self.rel[rows, :]
            gk = self.soft[rows, :] * (self.gk[rows, :] - shared2)
            self.gl[0, rows, :] = gq.astype(BF16)
            self.gl[1, rows, :] = gk.astype(BF16)
            return total + fold(gq)

        total = rows_loop(ROWS, 16, low, zero, unroll=5)
        self.sums[2:3, :] = jnp.sum(total, axis=0, keepdims=True)

    def back_value(self):
        def low(r0, total):
            rows = pl.ds(r0, 16)
            gv = self.gv[rows, :]
            self.gl[2, rows, :] = gv.astype(BF16)
            return total + fold(gv)

        total = rows_loop(ROWS, 16, low, jnp.zeros((SLOTS, D), F32), unroll=5)
        self.sums[3:4, :] = jnp.sum(total, axis=0, keepdims=True)
        self.grad_of(2)

    def grad_of(self, k):
        self.put_grad(k, self.n1_t[...], self.gl.at[k])

    def back_project(self):
        for b in range(2):
            cols = lane_block(b)
            back = self.times_t(self.gl[0], 0, b)
            back = back + self.times_t(self.gl[1], 1, b)
            self.back[:, cols] = back + self.times_t(self.gl[2], 2, b)

    def back_one(self):
        zero = jnp.zeros((SLOTS, D), F32)
        self.pos_up[0:GRID] = jnp.zeros((GRID, SLOTS, D), F32)
        self.pos_up[GRID + CELLS :] = jnp.zeros((GRID, SLOTS, D), F32)

        def body(r0, sums):
            rows = pl.ds(r0, 16)
            back, u = self.back[rows, :], self.u1[rows, :]
            gf = self.gs[rows, :] + norm_back(back, u, wide(self.inv1[rows, :]), self.row(0))
            c0 = r0 // SLOTS
            self.pos_up[pl.ds(GRID + c0, 2)] = gf.reshape(2, SLOTS, D)
            new = (back * u, back, gf)
            return tuple(s + fold(n) for s, n in zip(sums, new, strict=True))

        sums = rows_loop(ROWS, 16, body, (zero,) * 3, unroll=5)
        for j, s in zip((0, 1, 8), sums, strict=True):
            self.sums[j : j + 1, :] = jnp.sum(s, axis=0, keepdims=True)

    def back_position(self):
        for c in range(D // LANES):
            lanes = slice(c * LANES, (c + 1) * LANES)

            def put(cell, value):
                rows = pl.ds(pl.multiple_of(cell * SLOTS, SLOTS), SLOTS)
                gf = self.pos_up[GRID + cell, :, lanes]
                self.first[rows, lanes] = gf + value * self.live[rows, :]

            def tap(a, b):
                t = 13 + (1 - a) * 3 + 1 - b
                return self.small[t : t + 1, lanes]

            conv(self.pos_up, 1, tap, 1, lanes, put)

    def position_taps(self):
        for c in range(D // LANES):
            lanes = slice(c * LANES, (c + 1) * LANES)

            def up(cell):
                return self.pos_up[GRID + cell, :, lanes]

            def put_tap(a, b, value):
                t = 13 + (a + 1) * 3 + b + 1
                self.sums[t : t + 1, lanes] = value

            tap_sums(up, self.pos_src, 1, 1, lanes, put_tap)

    def finish_in(self):
        def down(r0, _):
            rows = pl.ds(r0, 16)
            self.in_low[rows, :] = self.first[rows, :].astype(BF16)
            return 0

        rows_loop(ROWS, 16, down, 0, unroll=5)
        self.unplace(self.in_low, self.in_own)


SLOT_OF = (0, 1, 2, 3, 4, 6, 8, 10, 5, 7, 9, 11)
MATS = len(SLOT_OF)
AXES = "xchly"
HEAD_ROWS = 320
SMALL_ROWS = 72
AG_ROUTES = ("lhyxc", "hlxyc", "lhyxc", "hxlyc", "hlxyc", "xylhc", "hylxc", "hylxc", "lxhyc", "xyhlc", "lhxyc", "xylhc")
RS_ROUTES = ("cxylh", "clyhx", "cxylh", "cyhlx", "cxyhl", "clhyx", "cylxh", "cxylh", "cyxhl", "chlyx", "clyxh", "cylhx")
ORDER = (
    6, 12, 0, 66, 18, 30, 42, 48, 36, 60, 54, 24, 144, 147, 145, 13, 31, 7, 55, 1,
    146, 19, 25, 49, 37, 43, 61, 67, 32, 8, 56, 14, 2, 20, 26, 38, 50, 44, 62, 68,
    9, 33, 15, 27, 57, 3, 21, 63, 39, 10, 16, 51, 45, 11, 149, 151, 69, 17, 4, 150,
    153, 154, 156, 155, 22, 28, 157, 5, 34, 148, 152, 40, 158, 23, 159, 46, 29, 64, 58, 35,
    160, 161, 52, 96, 102, 41, 47, 162, 70, 163, 108, 59, 65, 114, 53, 164, 97, 165, 126, 120,
    103, 71, 166, 109, 115, 167, 127, 132, 138, 168, 189, 121, 169, 133, 98, 170, 90, 171, 139, 172,
    173, 72, 110, 181, 174, 78, 91, 177, 180, 183, 128, 134, 104, 73, 175, 79, 99, 176, 111, 116,
    122, 178, 179, 84, 140, 184, 185, 129, 186, 85, 92, 190, 187, 105, 182, 135, 195, 112, 74, 188,
    80, 191, 130, 117, 196, 123, 192, 100, 106, 141, 86, 75, 136, 93, 131, 118, 113, 81, 197, 101,
    124, 87, 76, 142, 94, 137, 198, 119, 125, 88, 82, 77, 193, 107, 199, 143, 95, 83, 89, 204,
    194, 200, 205, 201, 202, 203, 206, 207,
)


def scratch_of():
    f, h, low = (ROWS, D), (ROWS, LANES), pltpu.VMEM((ROWS, D), BF16)
    halo3 = pltpu.VMEM(((GRID + 2 * HALO) * GRID, SLOTS, D), F32)
    halo1 = pltpu.VMEM(((GRID + 2) * GRID, SLOTS, D), F32)
    high, column, turned = pltpu.VMEM(f, F32), pltpu.VMEM(h, F32), pltpu.VMEM((D, ROWS), BF16)
    taps = pltpu.VMEM((WINDOW * WINDOW, D), F32)
    return dict(
        live=column,
        im8=pltpu.VMEM((IMG_GROUP, SLOTS, LANES), F32),
        im16=pltpu.VMEM((IMG_GROUP, 16, LANES), BF16),
        window=taps,
        rel_taps=taps,
        pos_src=halo1,
        pos_up=halo1,
        rel_src=halo3,
        dq_src=halo3,
        first=high,
        u1=high,
        inv1=column,
        second=high,
        u2=high,
        inv2=column,
        n1=low,
        n1_t=turned,
        n2=low,
        n2_t=turned,
        go=low,
        go_t=turned,
        q=low,
        k=low,
        v=low,
        soft=high,
        soft_low=low,
        ctx=pltpu.VMEM((2, WIDE, IMG_GROUP * WIDE), BF16),
        factor=high,
        rel=high,
        mixed=low,
        hidden=high,
        active=low,
        low=low,
        out_low=low,
        back=high,
        gs=high,
        gs_low=low,
        d=high,
        f=low,
        gq=high,
        gk=high,
        gv=high,
        gl=pltpu.VMEM((3, ROWS, D), BF16),
        in_low=low,
    )


class Links:
    def __init__(self):
        dp, head = lax.axis_index(DP), lax.axis_index(HEAD)
        self.far = lax.axis_size(DP) // 4
        self.at = dict(x=head // 2, c=head % 2, h=dp // 4, l=dp // 2 % 2, y=dp % 2)

    def count(self, axis):
        return self.far if axis == "h" else 2

    def peer(self, axis, step):
        return lax.rem(self.at[axis] + step, self.count(axis))

    def device(self, axis, step):
        at = {**self.at, axis: self.peer(axis, step)}
        return (at["h"] * 4 + at["l"] * 2 + at["y"], at["x"] * 2 + at["c"])

    def steps(self, axis, do):
        self.repeat(self.count(axis), do)

    def repeat(self, size, do):
        if size <= 32:
            for step in range(1, size):
                do(step)
        else:

            def body(step, _):
                do(step)
                return 0

            lax.fori_loop(1, size, body, 0)

    def others(self, name, do):
        dp, head, heads = lax.axis_index(DP), lax.axis_index(HEAD), lax.axis_size(HEAD)

        def one(step):
            if name == ALL:
                i = lax.rem(dp * heads + head + step, lax.axis_size(ALL))
                do((i // heads, lax.rem(i, heads)))
            elif name == DP:
                do((lax.rem(dp + step, lax.axis_size(DP)), head))
            else:
                do((dp, lax.rem(head + step, heads)))

        self.repeat(lax.axis_size(name), one)

    def signal(self):
        def one(device):
            pl.semaphore_signal(
                pltpu.get_barrier_semaphore(),
                inc=1,
                device_id=device,
                device_id_type=pl.DeviceIdType.MESH,
            )

        self.others(ALL, one)

    def meet(self):
        pl.semaphore_wait(pltpu.get_barrier_semaphore(), lax.axis_size(ALL) - 1)

    def copy(self, src, dst, send, recv, device):
        return pltpu.make_async_remote_copy(
            src_ref=src,
            dst_ref=dst,
            send_sem=send,
            recv_sem=recv,
            device_id=device,
            device_id_type=pl.DeviceIdType.MESH,
        )

    def region(self, blocks, slot, whole, **at):
        at = {**self.at, **at}
        place = [slice(None) if axis in whole else at[axis] for axis in AXES]
        return blocks.at[(*place, slot)]


class Gather:
    def __init__(self, links, w, send, recv):
        self.links, self.w, self.send, self.recv = links, w, send, recv

    def start(self, slot, phase):
        path = AG_ROUTES[slot]
        part = self.links.region(self.w, slot, path[:phase])
        sems = self.send.at[slot, phase], self.recv.at[slot, phase]

        def go(step):
            self.links.copy(part, part, *sems, self.links.device(path[phase], step)).start()

        self.links.steps(path[phase], go)

    def descriptor(self, slot, phase):
        path = AG_ROUTES[slot]
        at = {"h": pl.ds(0, self.links.far - 1)} if path[phase] == "h" else {}
        part = self.links.region(self.w, slot, path[:phase], **at)
        sems = self.send.at[slot, phase], self.recv.at[slot, phase]
        return self.links.copy(part, part, *sems, self.links.device(path[phase], 1))

    def tick(self, slot, phase):
        if phase:
            self.descriptor(slot, phase - 1).wait_recv()
        if phase < len(AXES):
            self.start(slot, phase)

    def sent(self):
        for slot in range(MATS):
            for phase in range(len(AXES)):
                self.descriptor(slot, phase).wait_send()


class Scatter:
    def __init__(self, links, g, boxes, total, send, recv):
        self.links, self.g, self.boxes, self.total = links, g, boxes, total
        self.send, self.recv = send, recv

    def descriptor(self, slot, phase):
        box = self.boxes[slot * len(AXES) + phase]
        sems = self.send.at[slot, phase], self.recv.at[slot, phase]
        return self.links.copy(box, box, *sems, self.links.device(RS_ROUTES[slot][phase], 1))

    def take(self, slot, phase):
        path = RS_ROUTES[slot]
        self.descriptor(slot, phase).wait_recv()
        own = self.links.region(self.g, slot, path[phase + 1 :])
        box = self.boxes[slot * len(AXES) + phase]
        if path[phase] == "h" and box.shape[0] == 1:
            box = box.at[0]
        elif path[phase] == "h":
            value = own[...].astype(F32)
            return own, value + jnp.sum(box[...].astype(F32), axis=0)
        return own, own[...] + box[...] if phase + 1 < len(AXES) else (
            own[...].astype(F32) + box[...].astype(F32)
        )

    def start(self, slot, phase):
        path = RS_ROUTES[slot]
        axis, rest = path[phase], path[phase + 1 :]
        box = self.boxes[slot * len(AXES) + phase]
        sems = self.send.at[slot, phase], self.recv.at[slot, phase]

        def go(step):
            at = {axis: self.links.peer(axis, step)}
            part = self.links.region(self.g, slot, rest, **at)
            into = box.at[step - 1] if axis == "h" else box
            self.links.copy(part, into, *sems, self.links.device(axis, step)).start()

        self.links.steps(axis, go)

    def tick(self, slot, phase):
        if phase:
            own, value = self.take(slot, phase - 1)
            if phase == len(AXES):
                self.total[SLOT_OF.index(slot)] = value
                return
            own[...] = value.astype(BF16)
        self.start(slot, phase)

    def sent(self):
        for slot in range(MATS):
            for phase in range(len(AXES)):
                self.descriptor(slot, phase).wait_send()


class Small:
    def __init__(self, links, sums, parts, in_c, in_x, in_y, in_h, in_l, full, send, recv):
        self.links, self.sums, self.parts, self.full = links, sums, parts, full
        self.in_c, self.in_x, self.in_y, self.in_h, self.in_l = in_c, in_x, in_y, in_h, in_l
        self.send, self.recv = send, recv

    def go(self, stage, src, dst, axis):
        sems = (self.send.at[stage], self.recv.at[stage])
        self.links.steps(
            axis, lambda step: self.links.copy(src, dst, *sems, self.links.device(axis, step)).start()
        )

    def wait(self, stage):
        x, c = self.links.at["x"], self.links.at["c"]
        ref = (
            self.in_c,
            self.in_x,
            self.in_y,
            self.in_h.at[pl.ds(0, self.links.far - 1)],
            self.in_l,
            self.full.at[c, x],
            self.full.at[c],
        )[stage]
        sems = (self.send.at[stage], self.recv.at[stage])
        return self.links.copy(ref, ref, *sems, self.links.device("cxyhlxc"[stage], 1))

    def tick(self, stage):
        at = self.links.at
        x, c, h = at["x"], at["c"], at["h"]
        mine = self.parts.at[c, x]
        if stage:
            self.wait(stage - 1).wait_recv()
        if stage == 0:
            for b in range(D // LANES):
                self.parts[b // 2, b % 2] = self.sums[:, b * LANES : (b + 1) * LANES]
            self.go(0, self.parts.at[1 - c], self.in_c, "c")
        if stage == 1:
            self.parts[c] = self.parts[c] + self.in_c[...]
            self.go(1, self.parts.at[c, 1 - x], self.in_x, "x")
        if stage == 2:
            mine[...] = mine[...] + self.in_x[...]
            self.go(2, mine, self.in_y, "y")
        if stage == 3:
            self.in_h[h] = mine[...] + self.in_y[...]
            self.go(3, self.in_h.at[h], self.in_h.at[h], "h")
        if stage == 4:
            total = self.in_h[0]
            for i in range(1, self.links.far):
                total = total + self.in_h[i]
            self.sums[:, 0:LANES] = total
            self.go(4, self.sums.at[:, pl.ds(0, LANES)], self.in_l, "l")
        if stage == 5:
            self.full[c, x] = self.sums[:, 0:LANES] + self.in_l[...]
            self.go(5, self.full.at[c, x], self.full.at[c, x], "x")
        if stage == 6:
            self.go(6, self.full.at[c], self.full.at[c], "c")

    def sent(self):
        for stage in range(7):
            self.wait(stage).wait_send()


class Rows:
    def __init__(self, links, blocks, out, own, send, recv):
        self.links, self.blocks, self.out, self.own = links, blocks, out, own
        self.send, self.recv = send, recv

    def hop(self, i):
        x, c = self.links.at["x"], self.links.at["c"]
        x, axis = ((x, "x"), (x, "c"), (1 - x, "c"))[i]
        block = self.blocks.at[2 * x + c]
        return self.links.copy(
            block, block, self.send.at[i], self.recv.at[i], self.links.device(axis, 1)
        )

    def tick(self, stage):
        if stage == 0:
            self.hop(0).start()
            self.hop(1).start()
        if stage == 1:
            self.hop(0).wait_recv()
            self.hop(2).start()
        if stage == 2:
            self.hop(1).wait_recv()
            self.hop(2).wait_recv()
            self.join()

    def sent(self):
        for i in range(3):
            self.hop(i).wait_send()

    def join(self):
        heads, end, own = self.blocks.shape[0], self.out.shape[0], self.own
        for h in range(heads):
            lo, hi = h * own, (h + 1) * own
            base = lo // 16 * 16
            first = base + 16 if lo % 16 else base
            last = hi // 16 * 16 if h + 1 < heads else end
            self.out[first:last, :] = self.blocks[h, first - base : last - base, :]
            if lo % 16:
                before = (lo - own) // 16 * 16
                tail = self.blocks[h - 1, base - before : base - before + 16, :]
                self.out[base : base + 16, :] = tail + self.blocks[h, 0:16, :]


class Exchange:
    def __init__(self, links, name, buffer, send, recv):
        self.links, self.name, self.buffer, self.send, self.recv = links, name, buffer, send, recv

    def start(self, value):
        own = lax.axis_index(self.name)
        self.buffer[own] = value
        mine = self.buffer.at[own]
        self.links.others(
            self.name,
            lambda device: self.links.copy(mine, mine, self.send, self.recv, device).start(),
        )

    def descriptor(self):
        ref = self.buffer.at[pl.ds(0, self.buffer.shape[0] - 1)]
        return self.links.copy(ref, ref, self.send, self.recv, self.links.device("c", 1))

    def total(self):
        self.descriptor().wait_recv()
        return jnp.sum(self.buffer[...], axis=0)

    def sent(self):
        self.descriptor().wait_send()


def exact(a, b, dims):
    return lax.dot_general(
        a, b, dims, precision=lax.Precision.HIGHEST, preferred_element_type=F32
    )


class Adafactor:
    def __init__(self, refs, row_share, col_share, sq_share):
        self.__dict__.update(refs)
        self.row_share, self.col_share, self.sq_share = row_share, col_share, sq_share

    def eye(self, count):
        r = lax.broadcasted_iota(jnp.int32, (count, LANES), 0)
        c = lax.broadcasted_iota(jnp.int32, (count, LANES), 1)
        return jnp.where(r == c, 1.0, 0.0)

    def lane(self, k, value, rest):
        lanes = lax.broadcasted_iota(jnp.int32, rest.shape, 1)
        return jnp.where(lanes == k, value, rest)

    def squares(self):
        rows = self.wg.shape[1]
        by_row = jnp.zeros((rows, LANES), F32)
        by_col = []
        for k in range(MATS):
            g = self.wg[k]
            s = g * g + SQUARE_FLOOR
            by_row = self.lane(k, jnp.sum(s, axis=1, keepdims=True), by_row)
            by_col.append(jnp.sum(s, axis=0, keepdims=True))
        self.col_share.start(jnp.concatenate([*by_col, jnp.zeros((4, LANES), F32)], axis=0))
        turned = exact(self.eye(16), by_row, NT)
        if rows < LANES:
            turned = jnp.concatenate([turned, jnp.zeros((16, LANES - rows), F32)], axis=1)
        self.row_share.start(turned)

    def scale(self):
        rows = self.wg.shape[1]
        total = self.row_share.total()[0:MATS, 0:rows]
        new_rows = SECOND_DECAY * self.row_state[...] + (1.0 - SECOND_DECAY) * (total * (1.0 / D))
        self.new_rows[...] = new_rows
        row = exact(new_rows, self.eye(MATS), TN)
        total = self.col_share.total()[0:MATS]
        cols = SECOND_DECAY * self.col_state[...] + (1.0 - SECOND_DECAY) * (total * (1.0 / D))
        self.new_cols[...] = cols
        sums = jnp.zeros((1, LANES), F32)
        for k in range(MATS):
            u = self.wg[k] * lax.rsqrt(row[:, k : k + 1] * cols[k : k + 1, :])
            self.upd[k] = u
            s = jnp.sum(jnp.sum(u * u, axis=0, keepdims=True), axis=1, keepdims=True)
            sums = self.lane(k, s, sums)
        mass = jnp.sum(row, axis=0, keepdims=True)
        self.sq_share.start(jnp.concatenate([sums, mass], axis=0))

    def apply(self):
        total = self.sq_share.total()
        mean = total[1:2] * (1.0 / (D * lax.axis_size(HEAD)))
        rms = jnp.sqrt(total[0:1] * mean * (1.0 / (D * D)))
        rate = STEP_RATE * jnp.sqrt(mean) / jnp.maximum(1.0, rms)
        for k in range(MATS):
            new = self.weights[k] - rate[:, k : k + 1] * self.upd[k]
            self.new_weights[k] = new
            self.copy[k] = new.astype(BF16)
            self.new_ema[k] = AVERAGE_KEEP * self.ema[k] + (1.0 - AVERAGE_KEEP) * new
        self.rms[...] = rms

    def clips(self):
        lanes = lax.broadcasted_iota(jnp.int32, (1, LANES), 1)
        clip = jnp.where(lanes < MATS, self.rms[...], self.small_clip[...])
        self.clip[...] = clip[:, 0 : self.clip.shape[1]]

    def small_step(self):
        count, full = self.small.shape[0], self.full
        g = jnp.concatenate([full[b // 2, b % 2, 0:count, :] for b in range(D // LANES)], axis=1)
        self.small_grads[...] = g
        state = SECOND_DECAY * self.small_state[...] + (1.0 - SECOND_DECAY) * (
            g * g + SQUARE_FLOOR
        )
        self.new_small_state[...] = state
        u = g * lax.rsqrt(state)
        rms = jnp.sqrt(jnp.sum(u * u, axis=1, keepdims=True) * (1.0 / D))
        new = self.small[...] - SMALL_RATE * u / jnp.maximum(1.0, rms)
        self.new_small[...] = new
        self.new_small_ema[...] = AVERAGE_KEEP * self.small_ema[...] + (1.0 - AVERAGE_KEEP) * new
        r = lax.broadcasted_iota(jnp.int32, (count, LANES), 0)
        c = lax.broadcasted_iota(jnp.int32, (count, LANES), 1)
        picked = jnp.where(c == r + MATS, rms, 0.0)
        self.small_clip[...] = jnp.sum(picked, axis=0, keepdims=True)


class Inputs(NamedTuple):
    cls: Any
    img: Any
    tokens: Any
    cot: Any
    weights: Any
    row_state: Any
    col_state: Any
    ema: Any
    small: Any
    small_state: Any
    small_ema: Any


class Outputs(NamedTuple):
    out: Any
    grad_in: Any
    wg: Any
    new_rows: Any
    new_cols: Any
    new_weights: Any
    copy: Any
    new_ema: Any
    small_grads: Any
    new_small_state: Any
    new_small: Any
    new_small_ema: Any
    clip: Any


def box_shapes(links, block):
    for slot in range(MATS):
        path = RS_ROUTES[slot]
        for phase, axis in enumerate(path):
            lead = [links.count(a) for a in AXES if a in path[phase + 1 :]]
            if axis == "h":
                lead = [links.far - 1, *lead]
            yield pltpu.VMEM((*lead, *block), BF16)


def shared_of(weights, parts, heads):
    links, (_, rows, _) = Links(), weights.shape
    block = (rows, LANES)
    every = pltpu.VMEM((2, 2, links.far, 2, 2, MATS, *block), BF16)
    out_rows = pltpu.VMEM((heads, HEAD_ROWS, D), BF16)
    dma = pltpu.SemaphoreType.DMA

    def f(*shape):
        return pltpu.VMEM(shape, F32)

    part = f(SMALL_ROWS, LANES)
    return dict(
        w=every,
        g=every,
        out_rows=out_rows,
        in_rows=out_rows,
        sums=f(SMALL_ROWS, D),
        parts=f(2, 2, SMALL_ROWS, LANES),
        in_c=f(2, SMALL_ROWS, LANES),
        in_x=part,
        in_y=part,
        in_h=f(links.far, SMALL_ROWS, LANES),
        in_l=part,
        full=f(2, 2, SMALL_ROWS, LANES),
        row_box=f(heads, 16, LANES),
        col_box=f(parts, 16, LANES),
        sq_box=f(parts * heads, 2, LANES),
        upd=f(MATS, *block),
        small_clip=f(1, LANES),
        rms=f(1, LANES),
        ag_send=dma((MATS, len(AXES))),
        ag_recv=dma((MATS, len(AXES))),
        rs_send=dma((MATS, len(AXES))),
        rs_recv=dma((MATS, len(AXES))),
        small_send=dma((7,)),
        small_recv=dma((7,)),
        out_send=dma((3,)),
        out_recv=dma((3,)),
        in_send=dma((3,)),
        in_recv=dma((3,)),
        opt_send=dma((3,)),
        opt_recv=dma((3,)),
        fetched=dma((len(Inputs._fields),)),
        stored=dma((len(Outputs._fields),)),
    )


class Ready:
    def __init__(self, src, dst, sem):
        self.copy = pltpu.make_async_copy(src, dst, sem)
        self.start, self.wait = self.copy.start, self.copy.wait


def then(*steps):
    def run():
        for step in steps:
            step()

    return run


def block_kernel(names, *refs):
    n_in, n_out = len(Inputs._fields), len(Outputs._fields)
    ins, outs, refs = Inputs(*refs[:n_in]), Outputs(*refs[n_in : n_in + n_out]), refs[n_in + n_out :]
    r = types.SimpleNamespace(**dict(zip(names, refs)))
    r.cls, r.img = ins.cls, ins.img
    fetch = Inputs(
        *[
            None if i < 2 else Ready(ref, getattr(r, name), r.fetched.at[i])
            for i, (name, ref) in enumerate(zip(Inputs._fields, ins))
        ]
    )
    store = Outputs(
        *[
            Ready(getattr(r, name), ref, r.stored.at[i])
            for i, (name, ref) in enumerate(zip(Outputs._fields, outs))
        ]
    )
    boxes = refs[len(names) :]
    links = Links()
    links.signal()
    for one in (fetch.weights, fetch.small, fetch.tokens, fetch.cot, *fetch[5:8], *fetch[9:]):
        one.start()
    r.out_own = r.out_rows.at[lax.axis_index(HEAD)]
    r.in_own = r.in_rows.at[lax.axis_index(HEAD)]
    own = r.cls.shape[1] * CELLS
    blk = Block(vars(r))
    gather = Gather(links, r.w, r.ag_send, r.ag_recv)
    scatter = Scatter(links, r.g, boxes, r.wg, r.rs_send, r.rs_recv)
    small = Small(
        links,
        *(r.sums, r.parts, r.in_c, r.in_x, r.in_y, r.in_h, r.in_l, r.full),
        r.small_send,
        r.small_recv,
    )
    out_rows = Rows(links, r.out_rows, r.out, own, r.out_send, r.out_recv)
    in_rows = Rows(links, r.in_rows, r.grad_in, own, r.in_send, r.in_recv)
    shares = [
        Exchange(links, axis, box, r.opt_send.at[i], r.opt_recv.at[i])
        for i, (axis, box) in enumerate(((HEAD, r.row_box), (DP, r.col_box), (ALL, r.sq_box)))
    ]
    opt = Adafactor(vars(r), *shares)

    fetch.weights.wait()
    for k in range(MATS):
        mine = links.region(r.w, SLOT_OF[k], "")
        mine[...] = r.weights[k].astype(BF16)
    links.meet()

    ops = []
    for tick in (gather.tick, scatter.tick):
        ops += [
            functools.partial(tick, slot, phase)
            for slot in range(MATS)
            for phase in range(len(AXES) + 1)
        ]
    ops += [
        then(fetch.small.wait, blk.setup),
        then(fetch.tokens.wait, blk.read_tokens),
        blk.norm_one,
        then(fetch.cot.wait, blk.read_cotangent),
    ]
    ops += [functools.partial(blk.project, k) for k in range(3)]
    ops += [blk.softmax, blk.contexts, blk.fill_window]
    ops += [functools.partial(blk.window_sum, c) for c in range(D // LANES)]
    ops += [blk.mix, blk.norm_two]
    for i in range(4):
        ops += [functools.partial(blk.hidden_block, i), functools.partial(blk.hidden_grads, i)]
    ops += [blk.finish_out, blk.back_two, blk.grad_proj, blk.back_heads, blk.back_query_key]
    ops += [functools.partial(blk.grad_of, k) for k in range(2)]
    ops += [functools.partial(blk.back_window, c) for c in range(D // LANES)]
    ops += [blk.back_value]
    ops += [functools.partial(blk.window_taps, c) for c in range(D // LANES)]
    ops += [blk.back_project, blk.back_one, blk.back_position, blk.position_taps, blk.finish_in]
    for rows, done in ((out_rows, store.out), (in_rows, store.grad_in)):
        ops += [functools.partial(rows.tick, stage) for stage in range(2)]
        ops += [then(functools.partial(rows.tick, 2), done.start)]
    ops += [functools.partial(small.tick, stage) for stage in range(8)]
    ops += [
        then(
            fetch.small_state.wait,
            fetch.small_ema.wait,
            opt.small_step,
            store.small_grads.start,
            store.new_small_state.start,
            store.new_small.start,
            store.new_small_ema.start,
        ),
        then(store.wg.start, opt.squares),
        then(
            fetch.row_state.wait,
            fetch.col_state.wait,
            opt.scale,
            store.new_rows.start,
            store.new_cols.start,
        ),
        then(
            fetch.ema.wait,
            opt.apply,
            store.new_weights.start,
            store.copy.start,
            store.new_ema.start,
        ),
        then(opt.clips, store.clip.start),
    ]
    for i in ORDER:
        ops[i]()
    for transfer in (gather, scatter, small, out_rows, in_rows, *shares):
        transfer.sent()
    for one in store:
        one.wait()


def finish_kernel(count, *refs):
    copies = [
        pltpu.make_async_copy(refs[i], refs[count + i], refs[-1].at[i]) for i in range(count)
    ]
    for one in copies:
        one.start()
    for one in copies:
        one.wait()


def local(
    tokens,
    cotangent,
    crop_image,
    crop_class,
    weights,
    row_state,
    col_state,
    weights_ema,
    small_params,
    small_state,
    small_ema,
):
    parts, heads = lax.axis_size(DP), lax.axis_size(HEAD)
    smem = pl.BlockSpec(memory_space=pltpu.SMEM)
    shared = shared_of(weights, parts, heads)
    own = scratch_of()

    def like(x, dtype=None):
        return jax.ShapeDtypeStruct(x.shape, dtype or x.dtype)

    clips = weights.shape[0] + small_params.shape[0]
    outs = (
        like(tokens),
        like(tokens),
        like(weights),
        like(row_state),
        like(col_state),
        like(weights),
        like(weights, BF16),
        like(weights),
        like(small_params),
        like(small_params),
        like(small_params),
        like(small_params),
        jax.ShapeDtypeStruct((1, clips), F32),
    )
    args = Inputs(
        crop_class,
        crop_image,
        tokens,
        cotangent,
        weights,
        row_state,
        col_state,
        weights_ema,
        small_params,
        small_state,
        small_ema,
    )
    staged = [pltpu.VMEM(x.shape, x.dtype) for x in (*args[2:], *outs)]
    names = (*shared, *own, *Inputs._fields[2:], *Outputs._fields)
    far = pl.BlockSpec(memory_space=pl.ANY)
    res = pl.pallas_call(
        functools.partial(block_kernel, names),
        out_shape=outs,
        in_specs=[smem, smem] + [far] * 9,
        out_specs=(far,) * len(outs),
        scratch_shapes=[
            *shared.values(),
            *own.values(),
            *staged,
            *box_shapes(Links(), weights.shape[1:]),
        ],
        compiler_params=pltpu.CompilerParams(
            collective_id=0, has_side_effects=True, vmem_limit_bytes=63 << 20
        ),
        name="block",
    )(*args)
    res = pl.pallas_call(
        functools.partial(finish_kernel, len(outs)),
        out_shape=outs,
        in_specs=[far] * len(outs),
        out_specs=(far,) * len(outs),
        scratch_shapes=[pltpu.SemaphoreType.DMA((len(outs),))],
        name="finish",
    )(*res)
    return (*res[:-1], res[-1].reshape(clips))


def solution(mesh):
    in_specs = (
        P(DP, None),
        P(DP, None),
        P(DP, None),
        P(DP, None),
        P(None, DP, HEAD),
        P(None, DP),
        P(None, HEAD),
        P(None, DP, HEAD),
        P(),
        P(),
        P(),
    )
    out_specs = (
        P(DP, None),
        P(DP, None),
        P(None, DP, HEAD),
        P(None, DP),
        P(None, HEAD),
        P(None, DP, HEAD),
        P(None, DP, HEAD),
        P(None, DP, HEAD),
        P(),
        P(),
        P(),
        P(),
        P(),
    )
    return jax.shard_map(local, mesh=mesh, in_specs=in_specs, out_specs=out_specs, check_vma=False)
```

```python
import functools
import math
import types
from typing import Any, NamedTuple

import jax
import jax.numpy as jnp
from jax import lax
from jax.experimental import pallas as pl
from jax.experimental.pallas import tpu as pltpu
from jax.sharding import PartitionSpec as P

DP, HEAD = "dp", "head"
ALL = (DP, HEAD)
D = 512
HEAD_DIM = 64
GRID = 7
SMALL_GRID = 3
WINDOW = 7
IMG_GROUP = 3
CELLS = GRID * GRID
SLOTS = 8
CELL_PAD = CELLS + 1
ROWS = CELL_PAD * SLOTS
LANES = 128
WIDE = 256
REACHES = (1, 2, 3, 3)
HALO = WINDOW // 2

NORM_EPS = 1e-06
SQUARE_FLOOR = 1e-30
SECOND_DECAY = 0.999
STEP_RATE = 0.02
SMALL_RATE = 0.05
AVERAGE_KEEP = 0.9
NEG_LARGE = -1e30
ROOT_HALF = 0.7071067811865476
INV_ROOT_TAU = 0.3989422804014327
INV_SCALE = 1.0 / math.sqrt(HEAD_DIM)

F32 = jnp.float32
BF16 = jnp.bfloat16
NN = (((1,), (0,)), ((), ()))
NT = (((1,), (1,)), ((), ()))
TN = (((0,), (0,)), ((), ()))


def dot(a, b, dims=NN):
    return lax.dot_general(a, b, dims, preferred_element_type=F32)


def lane_block(b):
    return slice(b * WIDE, (b + 1) * WIDE)


def wide(col):
    return jnp.concatenate([col] * (D // LANES), axis=1)


def rows_loop(count, size, body, init=None, unroll=1):
    def step(j, carry):
        return body(pl.multiple_of(j * size, size), carry)

    return lax.fori_loop(0, count // size, step, init, unroll=unroll)


def conv(src, halo, tap, reach, lanes, put):
    def line(y, _):
        sums = [jnp.zeros((SLOTS, LANES), F32) for _ in range(GRID)]
        for a in range(-reach, reach + 1):
            base = (y + (a + halo)) * GRID
            cells = [src[base + x, :, lanes] for x in range(GRID)]
            for b in range(-reach, reach + 1):
                t = tap(a, b)
                for x in range(GRID):
                    if 0 <= x + b < GRID:
                        sums[x] = sums[x] + t * cells[x + b]
        for x in range(GRID):
            put(y * GRID + x, sums[x])
        return 0

    lax.fori_loop(0, GRID, line, 0)


def tap_sums(up, src, halo, reach, lanes, put):
    for a in range(-reach, reach + 1):

        def line(y, sums):
            sums = list(sums)
            ups = [up(y * GRID + x) for x in range(GRID)]
            base = (y + (a + halo)) * GRID
            cells = [src[base + x, :, lanes] for x in range(GRID)]
            for i, b in enumerate(range(-reach, reach + 1)):
                for x in range(GRID):
                    if 0 <= x + b < GRID:
                        sums[i] = sums[i] + ups[x] * cells[x + b]
            return tuple(sums)

        start = tuple(jnp.zeros((SLOTS, LANES), F32) for _ in range(2 * reach + 1))
        sums = lax.fori_loop(0, GRID, line, start)
        for i, b in enumerate(range(-reach, reach + 1)):
            put(a, b, jnp.sum(sums[i], axis=0, keepdims=True))


def fold(x):
    return jnp.sum(x.reshape(x.shape[0] // SLOTS, SLOTS, x.shape[1]), axis=0)


def erf_parts(h):
    e = lax.erf(h * ROOT_HALF)
    half = 0.5 * (1.0 + e)
    return h * half, half + h * jnp.exp(-0.5 * h * h) * INV_ROOT_TAU


def norm_rows(v, gain, shift):
    centre = jnp.sum(v, axis=1, keepdims=True) * (1.0 / D)
    offset = v - centre
    spread = jnp.sum(offset * offset, axis=1, keepdims=True) * (1.0 / D)
    inverse = lax.rsqrt(spread + NORM_EPS)
    unit = offset * inverse
    return unit * gain + shift, unit, inverse


def norm_back(up, unit, inverse, gain):
    z = up * gain
    mean_z = jnp.sum(z, axis=1, keepdims=True) * (1.0 / D)
    mean_zu = jnp.sum(z * unit, axis=1, keepdims=True) * (1.0 / D)
    return inverse * (z - mean_z - unit * mean_zu)


class Block:
    def __init__(self, refs):
        self.__dict__.update(refs)

    def matrix(self, k, lo, hi):
        parts = []
        for h in range(lo, hi):
            part = self.w[h // 2, h % 2, :, :, :, k]
            if part.shape[-2] % 16:
                part = part.astype(F32).reshape(D, LANES).astype(BF16)
            else:
                part = part.reshape(D, LANES)
            parts.append(part)
        return jnp.concatenate(parts, axis=1)

    def times(self, lhs, k, b):
        return dot(lhs, self.matrix(k, 2 * b, 2 * b + 2))

    def times_t(self, lhs, k, b):
        return dot(lhs, self.matrix(k, 0, 4)[lane_block(b), :], NT)

    def put_grad(self, k, lhs_t, rhs):
        for b in range(2):
            g = dot(lhs_t, rhs[:, lane_block(b)])
            for i in range(2):
                piece = g[:, i * LANES : (i + 1) * LANES]
                place = self.g.shape[2:5]
                piece = piece.reshape(*place, self.g.shape[-2], LANES)
                self.g[b, i, :, :, :, k] = piece.astype(BF16)

    def row(self, j):
        return self.small[j : j + 1, :]

    def setup(self):
        head = lax.axis_index(HEAD)
        slots = self.cls.shape[1]
        self.sums[...] = jnp.zeros(self.sums.shape, F32)
        sub = lax.broadcasted_iota(jnp.int32, (SLOTS, LANES), 0)
        valid = jnp.where(sub < slots, 1.0, 0.0)
        full = jnp.zeros((SLOTS, LANES), F32)
        images = [jnp.zeros((SLOTS, LANES), F32) for _ in range(IMG_GROUP)]
        for s in range(slots):
            full = jnp.where(sub == s, jnp.where(self.cls[head, s] == 0, 1.0, 0.0), full)
            for i in range(IMG_GROUP):
                images[i] = jnp.where(
                    sub == s, jnp.where(self.img[head, s] == i, 1.0, 0.0), images[i]
                )
        for cell in range(CELLS):
            small = cell // GRID < SMALL_GRID and cell % GRID < SMALL_GRID
            self.live[cell * SLOTS : (cell + 1) * SLOTS, :] = valid if small else full
        self.live[CELLS * SLOTS :, :] = jnp.zeros((SLOTS, LANES), F32)
        for i in range(IMG_GROUP):
            self.im8[i] = images[i]
            self.im16[i] = jnp.concatenate([images[i], images[i]], axis=0).astype(BF16)
        self.pos_src[0:GRID] = jnp.zeros((GRID, SLOTS, D), F32)
        self.pos_src[GRID + CELLS :] = jnp.zeros((GRID, SLOTS, D), F32)
        for pad in (self.rel_src, self.dq_src):
            pad[0 : HALO * GRID] = jnp.zeros((HALO * GRID, SLOTS, D), F32)
            pad[HALO * GRID + CELLS :] = jnp.zeros((HALO * GRID, SLOTS, D), F32)
        tap = lax.broadcasted_iota(jnp.int32, (WINDOW * WINDOW, 1), 0)
        row_off = jnp.abs(tap // WINDOW - HALO)
        col_off = jnp.abs(tap % WINDOW - HALO)
        off = jnp.maximum(row_off, col_off)
        heads = lax.broadcasted_iota(jnp.int32, (1, D), 1) // HEAD_DIM
        reach = jnp.where(heads < 2, 1, jnp.where(heads < 5, 2, 3))
        mask = jnp.where(off <= reach, 1.0, 0.0)
        self.window[...] = mask
        self.rel_taps[...] = self.small[22 : 22 + WINDOW * WINDOW, :] * mask

    def place(self, rows_ref, first, r0, size):
        count = rows_ref.shape[0]
        r = r0 + lax.broadcasted_iota(jnp.int32, (size, 1), 0)
        cell, slot = r >> 3, r & 7
        want = first + slot * CELLS + cell
        want = jnp.where((slot < self.cls.shape[1]) & (cell < CELLS), want, -1)
        col = lax.broadcasted_iota(jnp.int32, (size, count), 1)
        pick = jnp.where(col == want, 1.0, 0.0).astype(BF16)
        return dot(pick, rows_ref[...])

    def unplace(self, src_ref, out_ref):
        count = out_ref.shape[0]
        own = self.cls.shape[1] * CELLS
        lead = lax.rem(lax.axis_index(HEAD) * own, 16)
        r = lax.broadcasted_iota(jnp.int32, (1, ROWS), 1)
        cell, slot = r >> 3, r & 7
        target = lead + slot * CELLS + cell
        target = jnp.where((slot < self.cls.shape[1]) & (cell < CELLS), target, -1)
        t = lax.broadcasted_iota(jnp.int32, (count, ROWS), 0)
        pick = jnp.where(t == target, 1.0, 0.0).astype(BF16)
        out_ref[...] = dot(pick, src_ref[...]).astype(BF16)

    def read_tokens(self):
        first = lax.axis_index(HEAD) * (self.cls.shape[1] * CELLS)
        size = 80

        def body(r0, _):
            live = wide(self.live[pl.ds(r0, size), :])
            x = self.place(self.tokens, first, r0, size)
            self.first[pl.ds(r0, size), :] = x
            c0 = r0 // SLOTS
            self.pos_src[pl.ds(GRID + c0, size // SLOTS)] = (x * live).reshape(-1, SLOTS, D)
            return 0

        rows_loop(ROWS, size, body, 0)

    def read_cotangent(self):
        first = lax.axis_index(HEAD) * (self.cls.shape[1] * CELLS)
        size = 80

        def body(r0, _):
            live = wide(self.live[pl.ds(r0, size), :])
            c = self.place(self.cot, first, r0, size)
            self.go[pl.ds(r0, size), :] = (c * live).astype(BF16)
            return 0

        rows_loop(ROWS, size, body, 0)
        self.go_t[...] = self.go[...].T
        self.back[...] = jnp.zeros((ROWS, D), F32)

    def norm_one(self):
        for c in range(D // LANES):
            lanes = slice(c * LANES, (c + 1) * LANES)

            def put(cell, value):
                rows = pl.ds(pl.multiple_of(cell * SLOTS, SLOTS), SLOTS)
                self.first[rows, lanes] = self.first[rows, lanes] + value + self.small[8:9, lanes]

            def tap(a, b):
                t = 13 + (a + 1) * 3 + b + 1
                return self.small[t : t + 1, lanes]

            conv(self.pos_src, 1, tap, 1, lanes, put)

        def body(r0, _):
            rows = pl.ds(r0, 16)
            n, u, inv = norm_rows(self.first[rows, :], self.row(0), self.row(1))
            self.n1[rows, :] = n.astype(BF16)
            self.u1[rows, :] = u
            self.inv1[rows, :] = jnp.broadcast_to(inv, (16, LANES))
            return 0

        rows_loop(ROWS, 16, body, 0, unroll=5)
        self.n1_t[...] = self.n1[...].T

    def project(self, k):
        low = (self.q, self.k, self.v)[k]
        for b in range(2):
            cols = lane_block(b)
            p = self.times(self.n1[...], k, b)
            if k != 1:
                p = p + self.small[2 + k // 2 : 3 + k // 2, cols]
            low[:, cols] = p.astype(BF16)

    def image_sum(self, x):
        total = jnp.zeros((SLOTS, D), F32)
        for i in range(IMG_GROUP):
            im = wide(self.im8[i])
            total = total + im * jnp.sum(im * x, axis=0, keepdims=True)
        return total

    def softmax(self):
        def top(r0, best):
            live = wide(self.live[pl.ds(r0, 16), :])
            keys = jnp.where(live > 0, self.k[pl.ds(r0, 16), :].astype(F32), NEG_LARGE)
            return jnp.maximum(best, jnp.max(keys.reshape(2, SLOTS, D), axis=0))

        best = rows_loop(ROWS, 16, top, jnp.full((SLOTS, D), NEG_LARGE, F32), unroll=5)
        shift = jnp.zeros((SLOTS, D), F32)
        for i in range(IMG_GROUP):
            im = wide(self.im8[i])
            most = jnp.max(jnp.where(im > 0, best, NEG_LARGE), axis=0, keepdims=True)
            shift = jnp.where(im > 0, most, shift)
        shift2 = jnp.concatenate([shift, shift], axis=0)

        def raise_(r0, total):
            rows = pl.ds(r0, 16)
            live = wide(self.live[rows, :])
            keys = self.k[rows, :].astype(F32)
            e = jnp.where(live > 0, jnp.exp(jnp.where(live > 0, keys - shift2, 0.0)), 0.0)
            self.soft[rows, :] = e
            return total + fold(e)

        total = self.image_sum(
            rows_loop(ROWS, 16, raise_, jnp.zeros((SLOTS, D), F32), unroll=5)
        )
        scale = 1.0 / jnp.where(total > 0, total, 1.0)
        scale2 = jnp.concatenate([scale, scale], axis=0)

        def divide(r0, _):
            rows = pl.ds(r0, 16)
            soft = self.soft[rows, :] * scale2
            self.soft[rows, :] = soft
            self.soft_low[rows, :] = soft.astype(BF16)
            return 0

        rows_loop(ROWS, 16, divide, 0, unroll=5)

    def by_image(self, x):
        tiles = x.reshape(ROWS // 16, 16, WIDE)
        parts = []
        for i in range(IMG_GROUP):
            im = jnp.concatenate([self.im16[i]] * (WIDE // LANES), axis=1)
            parts.append((tiles * im[None]).reshape(ROWS, WIDE))
        return jnp.concatenate(parts, axis=1)

    def head_blocks(self, x):
        r = lax.broadcasted_iota(jnp.int32, x.shape, 0) // HEAD_DIM
        c = (lax.broadcasted_iota(jnp.int32, x.shape, 1) % WIDE) // HEAD_DIM
        return jnp.where(r == c, x, 0.0).astype(BF16)

    def stacked(self, x):
        return jnp.concatenate([x[:, lane_block(i)] for i in range(IMG_GROUP)], axis=0)

    def contexts(self):
        for b in range(2):
            cols = lane_block(b)
            ctx = dot(self.soft_low[:, cols], self.by_image(self.v[:, cols]), TN)
            ctx = self.head_blocks(ctx)
            self.ctx[b] = ctx
            self.factor[:, cols] = dot(self.by_image(self.q[:, cols]), self.stacked(ctx))

    def fill_window(self):
        def fill(r0, _):
            rows = pl.ds(r0, 16)
            v = self.v[rows, :].astype(F32) * wide(self.live[rows, :])
            c0 = r0 // SLOTS
            self.rel_src[pl.ds(HALO * GRID + c0, 2)] = v.reshape(2, SLOTS, D)
            return 0

        rows_loop(ROWS, 16, fill, 0, unroll=5)
        self.rel[CELLS * SLOTS :, :] = jnp.zeros((SLOTS, D), F32)

    def window_sum(self, c):
        lanes = slice(c * LANES, (c + 1) * LANES)

        def put(cell, value):
            rows = pl.ds(pl.multiple_of(cell * SLOTS, SLOTS), SLOTS)
            self.rel[rows, lanes] = value

        def tap(a, b):
            t = (a + HALO) * WINDOW + b + HALO
            return self.rel_taps[t : t + 1, lanes]

        conv(self.rel_src, HALO, tap, REACHES[c], lanes, put)

    def mix(self):
        def mix(r0, _):
            rows = pl.ds(r0, 16)
            m = self.factor[rows, :] * INV_SCALE + self.q[rows, :].astype(F32) * self.rel[rows, :]
            self.mixed[rows, :] = (m * wide(self.live[rows, :])).astype(BF16)
            return 0

        rows_loop(ROWS, 16, mix, 0, unroll=5)

    def norm_two(self):
        for b in range(2):
            cols = lane_block(b)
            p = self.times_t(self.mixed[...], 3, b)
            self.second[:, cols] = self.first[:, cols] + p + self.small[4:5, cols]

        def body(r0, _):
            rows = pl.ds(r0, 16)
            n, u, inv = norm_rows(self.second[rows, :], self.row(5), self.row(6))
            self.n2[rows, :] = n.astype(BF16)
            self.u2[rows, :] = u
            self.inv2[rows, :] = jnp.broadcast_to(inv, (16, LANES))
            return 0

        rows_loop(ROWS, 16, body, 0, unroll=5)
        self.n2_t[...] = self.n2[...].T

    def hidden_block(self, r):
        up, down = 4 + 2 * r, 5 + 2 * r
        for b in range(2):
            cols = lane_block(b)
            h = self.times(self.n2[...], up, b) + self.small[pl.ds(9 + r, 1), cols]
            self.hidden[:, cols] = h
            self.factor[:, cols] = self.times(self.go[...], down, b)

        def body(r0, total):
            rows = pl.ds(r0, 16)
            act, slope = erf_parts(self.hidden[rows, :])
            g = self.factor[rows, :] * slope
            self.active[rows, :] = act.astype(BF16)
            self.low[rows, :] = g.astype(BF16)
            return total + fold(g)

        total = rows_loop(ROWS, 16, body, jnp.zeros((SLOTS, D), F32), unroll=5)
        self.sums[pl.ds(9 + r, 1), :] = jnp.sum(total, axis=0, keepdims=True)

    def hidden_grads(self, r):
        up, down = 4 + 2 * r, 5 + 2 * r
        self.put_grad(down, self.go_t[...], self.active)
        self.put_grad(up, self.n2_t[...], self.low)
        for b in range(2):
            cols = lane_block(b)
            self.second[:, cols] += self.times_t(self.active[...], down, b)
            self.back[:, cols] += self.times_t(self.low[...], up, b)

    def finish_out(self):
        def body(r0, _):
            rows = pl.ds(r0, 16)
            self.out_low[rows, :] = (self.second[rows, :] + self.row(7)).astype(BF16)
            return 0

        rows_loop(ROWS, 16, body, 0, unroll=5)
        self.unplace(self.out_low, self.out_own)

    def back_two(self):
        zero = jnp.zeros((SLOTS, D), F32)

        def body(r0, sums):
            rows = pl.ds(r0, 16)
            back, u = self.back[rows, :], self.u2[rows, :]
            go = self.go[rows, :].astype(F32)
            gs = go + norm_back(back, u, wide(self.inv2[rows, :]), self.row(5))
            self.gs[rows, :] = gs
            self.gs_low[rows, :] = gs.astype(BF16)
            new = (gs, back * u, back, go)
            return tuple(s + fold(n) for s, n in zip(sums, new, strict=True))

        sums = rows_loop(ROWS, 16, body, (zero,) * 4, unroll=5)
        for j, s in zip((4, 5, 6, 7), sums, strict=True):
            self.sums[j : j + 1, :] = jnp.sum(s, axis=0, keepdims=True)

    def grad_proj(self):
        self.put_grad(3, self.gs_low[...].T, self.mixed)

    def back_heads(self):
        for b in range(2):
            cols = lane_block(b)
            self.d[:, cols] = self.times(self.gs_low[...], 3, b)

        def fill(r0, _):
            rows = pl.ds(r0, 16)
            d = self.d[rows, :] * wide(self.live[rows, :])
            self.d[rows, :] = d
            self.f[rows, :] = (d * INV_SCALE).astype(BF16)
            c0 = r0 // SLOTS
            dq = d * self.q[rows, :].astype(F32)
            self.dq_src[pl.ds(HALO * GRID + c0, 2)] = dq.reshape(2, SLOTS, D)
            return 0

        rows_loop(ROWS, 16, fill, 0, unroll=5)
        for b in range(2):
            cols = lane_block(b)
            f3 = self.by_image(self.f[:, cols])
            g = self.head_blocks(dot(self.q[:, cols], f3, TN))
            self.gq[:, cols] = dot(f3, self.ctx[b], NT)
            self.gk[:, cols] = dot(self.by_image(self.v[:, cols]), g, NT)
            self.gv[:, cols] = dot(self.by_image(self.soft_low[:, cols]), self.stacked(g))

    def back_window(self, c):
        lanes = slice(c * LANES, (c + 1) * LANES)

        def put(cell, value):
            rows = pl.ds(pl.multiple_of(cell * SLOTS, SLOTS), SLOTS)
            self.gv[rows, lanes] = self.gv[rows, lanes] + value * self.live[rows, :]

        def tap(a, b):
            t = (HALO - a) * WINDOW + HALO - b
            return self.rel_taps[t : t + 1, lanes]

        conv(self.dq_src, HALO, tap, REACHES[c], lanes, put)

    def window_taps(self, c):
        lanes = slice(c * LANES, (c + 1) * LANES)

        def up(cell):
            return self.dq_src[HALO * GRID + cell, :, lanes]

        def put_tap(a, b, value):
            t = (a + HALO) * WINDOW + b + HALO
            keep = self.window[t : t + 1, lanes]
            self.sums[22 + t : 23 + t, lanes] = value * keep

        tap_sums(up, self.rel_src, HALO, REACHES[c], lanes, put_tap)

    def back_query_key(self):
        zero = jnp.zeros((SLOTS, D), F32)

        def inner(r0, total):
            rows = pl.ds(r0, 16)
            return total + fold(self.soft[rows, :] * self.gk[rows, :])

        shared = self.image_sum(rows_loop(ROWS, 16, inner, zero, unroll=5))
        shared2 = jnp.concatenate([shared, shared], axis=0)

        def low(r0, total):
            rows = pl.ds(r0, 16)
            gq = self.gq[rows, :] + self.d[rows, :] * self.rel[rows, :]
            gk = self.soft[rows, :] * (self.gk[rows, :] - shared2)
            self.gl[0, rows, :] = gq.astype(BF16)
            self.gl[1, rows, :] = gk.astype(BF16)
            return total + fold(gq)

        total = rows_loop(ROWS, 16, low, zero, unroll=5)
        self.sums[2:3, :] = jnp.sum(total, axis=0, keepdims=True)

    def back_value(self):
        def low(r0, total):
            rows = pl.ds(r0, 16)
            gv = self.gv[rows, :]
            self.gl[2, rows, :] = gv.astype(BF16)
            return total + fold(gv)

        total = rows_loop(ROWS, 16, low, jnp.zeros((SLOTS, D), F32), unroll=5)
        self.sums[3:4, :] = jnp.sum(total, axis=0, keepdims=True)
        self.grad_of(2)

    def grad_of(self, k):
        self.put_grad(k, self.n1_t[...], self.gl.at[k])

    def back_project(self):
        for b in range(2):
            cols = lane_block(b)
            back = self.times_t(self.gl[0], 0, b)
            back = back + self.times_t(self.gl[1], 1, b)
            self.back[:, cols] = back + self.times_t(self.gl[2], 2, b)

    def back_one(self):
        zero = jnp.zeros((SLOTS, D), F32)
        self.pos_up[0:GRID] = jnp.zeros((GRID, SLOTS, D), F32)
        self.pos_up[GRID + CELLS :] = jnp.zeros((GRID, SLOTS, D), F32)

        def body(r0, sums):
            rows = pl.ds(r0, 16)
            back, u = self.back[rows, :], self.u1[rows, :]
            gf = self.gs[rows, :] + norm_back(back, u, wide(self.inv1[rows, :]), self.row(0))
            c0 = r0 // SLOTS
            self.pos_up[pl.ds(GRID + c0, 2)] = gf.reshape(2, SLOTS, D)
            new = (back * u, back, gf)
            return tuple(s + fold(n) for s, n in zip(sums, new, strict=True))

        sums = rows_loop(ROWS, 16, body, (zero,) * 3, unroll=5)
        for j, s in zip((0, 1, 8), sums, strict=True):
            self.sums[j : j + 1, :] = jnp.sum(s, axis=0, keepdims=True)

    def back_position(self):
        for c in range(D // LANES):
            lanes = slice(c * LANES, (c + 1) * LANES)

            def put(cell, value):
                rows = pl.ds(pl.multiple_of(cell * SLOTS, SLOTS), SLOTS)
                gf = self.pos_up[GRID + cell, :, lanes]
                self.first[rows, lanes] = gf + value * self.live[rows, :]

            def tap(a, b):
                t = 13 + (1 - a) * 3 + 1 - b
                return self.small[t : t + 1, lanes]

            conv(self.pos_up, 1, tap, 1, lanes, put)

    def position_taps(self):
        for c in range(D // LANES):
            lanes = slice(c * LANES, (c + 1) * LANES)

            def up(cell):
                return self.pos_up[GRID + cell, :, lanes]

            def put_tap(a, b, value):
                t = 13 + (a + 1) * 3 + b + 1
                self.sums[t : t + 1, lanes] = value

            tap_sums(up, self.pos_src, 1, 1, lanes, put_tap)

    def finish_in(self):
        def down(r0, _):
            rows = pl.ds(r0, 16)
            self.in_low[rows, :] = self.first[rows, :].astype(BF16)
            return 0

        rows_loop(ROWS, 16, down, 0, unroll=5)
        self.unplace(self.in_low, self.in_own)


SLOT_OF = (0, 1, 2, 3, 4, 6, 8, 10, 5, 7, 9, 11)
MATS = len(SLOT_OF)
AXES = "xchly"
HEAD_ROWS = 320
SMALL_ROWS = 72
AG_ROUTES = ("lhyxc", "hlxyc", "lhyxc", "hxlyc", "hlxyc", "xylhc", "hylxc", "hylxc", "lxhyc", "xyhlc", "lhxyc", "xylhc")
RS_ROUTES = ("cxylh", "clyhx", "cxylh", "cyhlx", "cxyhl", "clhyx", "cylxh", "cxylh", "cyxhl", "chlyx", "clyxh", "cylhx")
ORDER = (
    6, 12, 0, 66, 18, 30, 42, 48, 36, 60, 54, 24, 144, 147, 145, 13, 31, 7, 55, 1,
    146, 19, 25, 49, 37, 43, 61, 67, 32, 8, 56, 14, 2, 20, 26, 38, 50, 44, 62, 68,
    9, 33, 15, 27, 57, 3, 21, 63, 39, 10, 16, 51, 45, 11, 149, 151, 69, 17, 4, 150,
    153, 154, 156, 155, 22, 28, 157, 5, 34, 148, 152, 40, 158, 23, 159, 46, 29, 64, 58, 35,
    160, 161, 52, 96, 102, 41, 47, 162, 70, 163, 108, 59, 65, 114, 53, 164, 97, 165, 126, 120,
    103, 71, 166, 109, 115, 167, 127, 132, 138, 168, 189, 121, 169, 133, 98, 170, 90, 171, 139, 172,
    173, 72, 110, 181, 174, 78, 91, 177, 180, 183, 128, 134, 104, 73, 175, 79, 99, 176, 111, 116,
    122, 178, 179, 84, 140, 184, 185, 129, 186, 85, 92, 190, 187, 105, 182, 135, 195, 112, 74, 188,
    80, 191, 130, 117, 196, 123, 192, 100, 106, 141, 86, 75, 136, 93, 131, 118, 113, 81, 197, 101,
    124, 87, 76, 142, 94, 137, 198, 119, 125, 88, 82, 77, 193, 107, 199, 143, 95, 83, 89, 204,
    194, 200, 205, 201, 202, 203, 206, 207,
)


def scratch_of():
    f, h, low = (ROWS, D), (ROWS, LANES), pltpu.VMEM((ROWS, D), BF16)
    halo3 = pltpu.VMEM(((GRID + 2 * HALO) * GRID, SLOTS, D), F32)
    halo1 = pltpu.VMEM(((GRID + 2) * GRID, SLOTS, D), F32)
    high, column, turned = pltpu.VMEM(f, F32), pltpu.VMEM(h, F32), pltpu.VMEM((D, ROWS), BF16)
    taps = pltpu.VMEM((WINDOW * WINDOW, D), F32)
    return dict(
        live=column,
        im8=pltpu.VMEM((IMG_GROUP, SLOTS, LANES), F32),
        im16=pltpu.VMEM((IMG_GROUP, 16, LANES), BF16),
        window=taps,
        rel_taps=taps,
        pos_src=halo1,
        pos_up=halo1,
        rel_src=halo3,
        dq_src=halo3,
        first=high,
        u1=high,
        inv1=column,
        second=high,
        u2=high,
        inv2=column,
        n1=low,
        n1_t=turned,
        n2=low,
        n2_t=turned,
        go=low,
        go_t=turned,
        q=low,
        k=low,
        v=low,
        soft=high,
        soft_low=low,
        ctx=pltpu.VMEM((2, WIDE, IMG_GROUP * WIDE), BF16),
        factor=high,
        rel=high,
        mixed=low,
        hidden=high,
        active=low,
        low=low,
        out_low=low,
        back=high,
        gs=high,
        gs_low=low,
        d=high,
        f=low,
        gq=high,
        gk=high,
        gv=high,
        gl=pltpu.VMEM((3, ROWS, D), BF16),
        in_low=low,
    )


class Links:
    def __init__(self):
        dp, head = lax.axis_index(DP), lax.axis_index(HEAD)
        self.far = lax.axis_size(DP) // 4
        self.at = dict(x=head // 2, c=head % 2, h=dp // 4, l=dp // 2 % 2, y=dp % 2)

    def count(self, axis):
        return self.far if axis == "h" else 2

    def peer(self, axis, step):
        return lax.rem(self.at[axis] + step, self.count(axis))

    def device(self, axis, step):
        at = {**self.at, axis: self.peer(axis, step)}
        return (at["h"] * 4 + at["l"] * 2 + at["y"], at["x"] * 2 + at["c"])

    def steps(self, axis, do):
        self.repeat(self.count(axis), do)

    def repeat(self, size, do):
        if size <= 32:
            for step in range(1, size):
                do(step)
        else:

            def body(step, _):
                do(step)
                return 0

            lax.fori_loop(1, size, body, 0)

    def others(self, name, do):
        dp, head, heads = lax.axis_index(DP), lax.axis_index(HEAD), lax.axis_size(HEAD)

        def one(step):
            if name == ALL:
                i = lax.rem(dp * heads + head + step, lax.axis_size(ALL))
                do((i // heads, lax.rem(i, heads)))
            elif name == DP:
                do((lax.rem(dp + step, lax.axis_size(DP)), head))
            else:
                do((dp, lax.rem(head + step, heads)))

        self.repeat(lax.axis_size(name), one)

    def signal(self):
        def one(device):
            pl.semaphore_signal(
                pltpu.get_barrier_semaphore(),
                inc=1,
                device_id=device,
                device_id_type=pl.DeviceIdType.MESH,
            )

        self.others(ALL, one)

    def meet(self):
        pl.semaphore_wait(pltpu.get_barrier_semaphore(), lax.axis_size(ALL) - 1)

    def copy(self, src, dst, send, recv, device):
        return pltpu.make_async_remote_copy(
            src_ref=src,
            dst_ref=dst,
            send_sem=send,
            recv_sem=recv,
            device_id=device,
            device_id_type=pl.DeviceIdType.MESH,
        )

    def region(self, blocks, slot, whole, **at):
        at = {**self.at, **at}
        place = [slice(None) if axis in whole else at[axis] for axis in AXES]
        return blocks.at[(*place, slot)]


class Gather:
    def __init__(self, links, w, send, recv):
        self.links, self.w, self.send, self.recv = links, w, send, recv

    def start(self, slot, phase):
        path = AG_ROUTES[slot]
        part = self.links.region(self.w, slot, path[:phase])
        sems = self.send.at[slot, phase], self.recv.at[slot, phase]

        def go(step):
            self.links.copy(part, part, *sems, self.links.device(path[phase], step)).start()

        self.links.steps(path[phase], go)

    def descriptor(self, slot, phase):
        path = AG_ROUTES[slot]
        at = {"h": pl.ds(0, self.links.far - 1)} if path[phase] == "h" else {}
        part = self.links.region(self.w, slot, path[:phase], **at)
        sems = self.send.at[slot, phase], self.recv.at[slot, phase]
        return self.links.copy(part, part, *sems, self.links.device(path[phase], 1))

    def tick(self, slot, phase):
        if phase:
            self.descriptor(slot, phase - 1).wait_recv()
        if phase < len(AXES):
            self.start(slot, phase)

    def sent(self):
        for slot in range(MATS):
            for phase in range(len(AXES)):
                self.descriptor(slot, phase).wait_send()


class Scatter:
    def __init__(self, links, g, boxes, total, send, recv):
        self.links, self.g, self.boxes, self.total = links, g, boxes, total
        self.send, self.recv = send, recv

    def descriptor(self, slot, phase):
        box = self.boxes[slot * len(AXES) + phase]
        sems = self.send.at[slot, phase], self.recv.at[slot, phase]
        return self.links.copy(box, box, *sems, self.links.device(RS_ROUTES[slot][phase], 1))

    def take(self, slot, phase):
        path = RS_ROUTES[slot]
        self.descriptor(slot, phase).wait_recv()
        own = self.links.region(self.g, slot, path[phase + 1 :])
        box = self.boxes[slot * len(AXES) + phase]
        if path[phase] == "h" and box.shape[0] == 1:
            box = box.at[0]
        elif path[phase] == "h":
            value = own[...].astype(F32)
            return own, value + jnp.sum(box[...].astype(F32), axis=0)
        return own, own[...] + box[...] if phase + 1 < len(AXES) else (
            own[...].astype(F32) + box[...].astype(F32)
        )

    def start(self, slot, phase):
        path = RS_ROUTES[slot]
        axis, rest = path[phase], path[phase + 1 :]
        box = self.boxes[slot * len(AXES) + phase]
        sems = self.send.at[slot, phase], self.recv.at[slot, phase]

        def go(step):
            at = {axis: self.links.peer(axis, step)}
            part = self.links.region(self.g, slot, rest, **at)
            into = box.at[step - 1] if axis == "h" else box
            self.links.copy(part, into, *sems, self.links.device(axis, step)).start()

        self.links.steps(axis, go)

    def tick(self, slot, phase):
        if phase:
            own, value = self.take(slot, phase - 1)
            if phase == len(AXES):
                self.total[SLOT_OF.index(slot)] = value
                return
            own[...] = value.astype(BF16)
        self.start(slot, phase)

    def sent(self):
        for slot in range(MATS):
            for phase in range(len(AXES)):
                self.descriptor(slot, phase).wait_send()


class Small:
    def __init__(self, links, sums, parts, in_c, in_x, in_y, in_h, in_l, full, send, recv):
        self.links, self.sums, self.parts, self.full = links, sums, parts, full
        self.in_c, self.in_x, self.in_y, self.in_h, self.in_l = in_c, in_x, in_y, in_h, in_l
        self.send, self.recv = send, recv

    def go(self, stage, src, dst, axis):
        sems = (self.send.at[stage], self.recv.at[stage])
        self.links.steps(
            axis, lambda step: self.links.copy(src, dst, *sems, self.links.device(axis, step)).start()
        )

    def wait(self, stage):
        x, c = self.links.at["x"], self.links.at["c"]
        ref = (
            self.in_c,
            self.in_x,
            self.in_y,
            self.in_h.at[pl.ds(0, self.links.far - 1)],
            self.in_l,
            self.full.at[c, x],
            self.full.at[c],
        )[stage]
        sems = (self.send.at[stage], self.recv.at[stage])
        return self.links.copy(ref, ref, *sems, self.links.device("cxyhlxc"[stage], 1))

    def tick(self, stage):
        at = self.links.at
        x, c, h = at["x"], at["c"], at["h"]
        mine = self.parts.at[c, x]
        if stage:
            self.wait(stage - 1).wait_recv()
        if stage == 0:
            for b in range(D // LANES):
                self.parts[b // 2, b % 2] = self.sums[:, b * LANES : (b + 1) * LANES]
            self.go(0, self.parts.at[1 - c], self.in_c, "c")
        if stage == 1:
            self.parts[c] = self.parts[c] + self.in_c[...]
            self.go(1, self.parts.at[c, 1 - x], self.in_x, "x")
        if stage == 2:
            mine[...] = mine[...] + self.in_x[...]
            self.go(2, mine, self.in_y, "y")
        if stage == 3:
            self.in_h[h] = mine[...] + self.in_y[...]
            self.go(3, self.in_h.at[h], self.in_h.at[h], "h")
        if stage == 4:
            total = self.in_h[0]
            for i in range(1, self.links.far):
                total = total + self.in_h[i]
            self.sums[:, 0:LANES] = total
            self.go(4, self.sums.at[:, pl.ds(0, LANES)], self.in_l, "l")
        if stage == 5:
            self.full[c, x] = self.sums[:, 0:LANES] + self.in_l[...]
            self.go(5, self.full.at[c, x], self.full.at[c, x], "x")
        if stage == 6:
            self.go(6, self.full.at[c], self.full.at[c], "c")

    def sent(self):
        for stage in range(7):
            self.wait(stage).wait_send()


class Rows:
    def __init__(self, links, blocks, out, own, send, recv):
        self.links, self.blocks, self.out, self.own = links, blocks, out, own
        self.send, self.recv = send, recv

    def hop(self, i):
        x, c = self.links.at["x"], self.links.at["c"]
        x, axis = ((x, "x"), (x, "c"), (1 - x, "c"))[i]
        block = self.blocks.at[2 * x + c]
        return self.links.copy(
            block, block, self.send.at[i], self.recv.at[i], self.links.device(axis, 1)
        )

    def tick(self, stage):
        if stage == 0:
            self.hop(0).start()
            self.hop(1).start()
        if stage == 1:
            self.hop(0).wait_recv()
            self.hop(2).start()
        if stage == 2:
            self.hop(1).wait_recv()
            self.hop(2).wait_recv()
            self.join()

    def sent(self):
        for i in range(3):
            self.hop(i).wait_send()

    def join(self):
        heads, end, own = self.blocks.shape[0], self.out.shape[0], self.own
        for h in range(heads):
            lo, hi = h * own, (h + 1) * own
            base = lo // 16 * 16
            first = base + 16 if lo % 16 else base
            last = hi // 16 * 16 if h + 1 < heads else end
            self.out[first:last, :] = self.blocks[h, first - base : last - base, :]
            if lo % 16:
                before = (lo - own) // 16 * 16
                tail = self.blocks[h - 1, base - before : base - before + 16, :]
                self.out[base : base + 16, :] = tail + self.blocks[h, 0:16, :]


class Exchange:
    def __init__(self, links, name, buffer, send, recv):
        self.links, self.name, self.buffer, self.send, self.recv = links, name, buffer, send, recv

    def start(self, value):
        own = lax.axis_index(self.name)
        self.buffer[own] = value
        mine = self.buffer.at[own]
        self.links.others(
            self.name,
            lambda device: self.links.copy(mine, mine, self.send, self.recv, device).start(),
        )

    def descriptor(self):
        ref = self.buffer.at[pl.ds(0, self.buffer.shape[0] - 1)]
        return self.links.copy(ref, ref, self.send, self.recv, self.links.device("c", 1))

    def total(self):
        self.descriptor().wait_recv()
        return jnp.sum(self.buffer[...], axis=0)

    def sent(self):
        self.descriptor().wait_send()


def exact(a, b, dims):
    return lax.dot_general(
        a, b, dims, precision=lax.Precision.HIGHEST, preferred_element_type=F32
    )


class Adafactor:
    def __init__(self, refs, row_share, col_share, sq_share):
        self.__dict__.update(refs)
        self.row_share, self.col_share, self.sq_share = row_share, col_share, sq_share

    def eye(self, count):
        r = lax.broadcasted_iota(jnp.int32, (count, LANES), 0)
        c = lax.broadcasted_iota(jnp.int32, (count, LANES), 1)
        return jnp.where(r == c, 1.0, 0.0)

    def lane(self, k, value, rest):
        lanes = lax.broadcasted_iota(jnp.int32, rest.shape, 1)
        return jnp.where(lanes == k, value, rest)

    def squares(self):
        rows = self.wg.shape[1]
        by_row = jnp.zeros((rows, LANES), F32)
        by_col = []
        for k in range(MATS):
            g = self.wg[k]
            s = g * g + SQUARE_FLOOR
            by_row = self.lane(k, jnp.sum(s, axis=1, keepdims=True), by_row)
            by_col.append(jnp.sum(s, axis=0, keepdims=True))
        self.col_share.start(jnp.concatenate([*by_col, jnp.zeros((4, LANES), F32)], axis=0))
        turned = exact(self.eye(16), by_row, NT)
        if rows < LANES:
            turned = jnp.concatenate([turned, jnp.zeros((16, LANES - rows), F32)], axis=1)
        self.row_share.start(turned)

    def scale(self):
        rows = self.wg.shape[1]
        total = self.row_share.total()[0:MATS, 0:rows]
        new_rows = SECOND_DECAY * self.row_state[...] + (1.0 - SECOND_DECAY) * (total * (1.0 / D))
        self.new_rows[...] = new_rows
        row = exact(new_rows, self.eye(MATS), TN)
        total = self.col_share.total()[0:MATS]
        cols = SECOND_DECAY * self.col_state[...] + (1.0 - SECOND_DECAY) * (total * (1.0 / D))
        self.new_cols[...] = cols
        sums = jnp.zeros((1, LANES), F32)
        for k in range(MATS):
            u = self.wg[k] * lax.rsqrt(row[:, k : k + 1] * cols[k : k + 1, :])
            self.upd[k] = u
            s = jnp.sum(jnp.sum(u * u, axis=0, keepdims=True), axis=1, keepdims=True)
            sums = self.lane(k, s, sums)
        mass = jnp.sum(row, axis=0, keepdims=True)
        self.sq_share.start(jnp.concatenate([sums, mass], axis=0))

    def apply(self):
        total = self.sq_share.total()
        mean = total[1:2] * (1.0 / (D * lax.axis_size(HEAD)))
        rms = jnp.sqrt(total[0:1] * mean * (1.0 / (D * D)))
        rate = STEP_RATE * jnp.sqrt(mean) / jnp.maximum(1.0, rms)
        for k in range(MATS):
            new = self.weights[k] - rate[:, k : k + 1] * self.upd[k]
            self.new_weights[k] = new
            self.copy[k] = new.astype(BF16)
            self.new_ema[k] = AVERAGE_KEEP * self.ema[k] + (1.0 - AVERAGE_KEEP) * new
        self.rms[...] = rms

    def clips(self):
        lanes = lax.broadcasted_iota(jnp.int32, (1, LANES), 1)
        clip = jnp.where(lanes < MATS, self.rms[...], self.small_clip[...])
        self.clip[...] = clip[:, 0 : self.clip.shape[1]]

    def small_step(self):
        count, full = self.small.shape[0], self.full
        g = jnp.concatenate([full[b // 2, b % 2, 0:count, :] for b in range(D // LANES)], axis=1)
        self.small_grads[...] = g
        state = SECOND_DECAY * self.small_state[...] + (1.0 - SECOND_DECAY) * (
            g * g + SQUARE_FLOOR
        )
        self.new_small_state[...] = state
        u = g * lax.rsqrt(state)
        rms = jnp.sqrt(jnp.sum(u * u, axis=1, keepdims=True) * (1.0 / D))
        new = self.small[...] - SMALL_RATE * u / jnp.maximum(1.0, rms)
        self.new_small[...] = new
        self.new_small_ema[...] = AVERAGE_KEEP * self.small_ema[...] + (1.0 - AVERAGE_KEEP) * new
        r = lax.broadcasted_iota(jnp.int32, (count, LANES), 0)
        c = lax.broadcasted_iota(jnp.int32, (count, LANES), 1)
        picked = jnp.where(c == r + MATS, rms, 0.0)
        self.small_clip[...] = jnp.sum(picked, axis=0, keepdims=True)


class Inputs(NamedTuple):
    cls: Any
    img: Any
    tokens: Any
    cot: Any
    weights: Any
    row_state: Any
    col_state: Any
    ema: Any
    small: Any
    small_state: Any
    small_ema: Any


class Outputs(NamedTuple):
    out: Any
    grad_in: Any
    wg: Any
    new_rows: Any
    new_cols: Any
    new_weights: Any
    copy: Any
    new_ema: Any
    small_grads: Any
    new_small_state: Any
    new_small: Any
    new_small_ema: Any
    clip: Any


def box_shapes(links, block):
    for slot in range(MATS):
        path = RS_ROUTES[slot]
        for phase, axis in enumerate(path):
            lead = [links.count(a) for a in AXES if a in path[phase + 1 :]]
            if axis == "h":
                lead = [links.far - 1, *lead]
            yield pltpu.VMEM((*lead, *block), BF16)


def shared_of(weights, parts, heads):
    links, (_, rows, _) = Links(), weights.shape
    block = (rows, LANES)
    every = pltpu.VMEM((2, 2, links.far, 2, 2, MATS, *block), BF16)
    out_rows = pltpu.VMEM((heads, HEAD_ROWS, D), BF16)
    dma = pltpu.SemaphoreType.DMA

    def f(*shape):
        return pltpu.VMEM(shape, F32)

    part = f(SMALL_ROWS, LANES)
    return dict(
        w=every,
        g=every,
        out_rows=out_rows,
        in_rows=out_rows,
        sums=f(SMALL_ROWS, D),
        parts=f(2, 2, SMALL_ROWS, LANES),
        in_c=f(2, SMALL_ROWS, LANES),
        in_x=part,
        in_y=part,
        in_h=f(links.far, SMALL_ROWS, LANES),
        in_l=part,
        full=f(2, 2, SMALL_ROWS, LANES),
        row_box=f(heads, 16, LANES),
        col_box=f(parts, 16, LANES),
        sq_box=f(parts * heads, 2, LANES),
        upd=f(MATS, *block),
        small_clip=f(1, LANES),
        rms=f(1, LANES),
        ag_send=dma((MATS, len(AXES))),
        ag_recv=dma((MATS, len(AXES))),
        rs_send=dma((MATS, len(AXES))),
        rs_recv=dma((MATS, len(AXES))),
        small_send=dma((7,)),
        small_recv=dma((7,)),
        out_send=dma((3,)),
        out_recv=dma((3,)),
        in_send=dma((3,)),
        in_recv=dma((3,)),
        opt_send=dma((3,)),
        opt_recv=dma((3,)),
        fetched=dma((len(Inputs._fields),)),
        stored=dma((len(Outputs._fields),)),
    )


class Ready:
    def __init__(self, src, dst, sem):
        self.copy = pltpu.make_async_copy(src, dst, sem)
        self.start, self.wait = self.copy.start, self.copy.wait


def then(*steps):
    def run():
        for step in steps:
            step()

    return run


def block_kernel(names, *refs):
    n_in, n_out = len(Inputs._fields), len(Outputs._fields)
    ins, outs, refs = Inputs(*refs[:n_in]), Outputs(*refs[n_in : n_in + n_out]), refs[n_in + n_out :]
    r = types.SimpleNamespace(**dict(zip(names, refs)))
    r.cls, r.img = ins.cls, ins.img
    fetch = Inputs(
        *[
            None if i < 2 else Ready(ref, getattr(r, name), r.fetched.at[i])
            for i, (name, ref) in enumerate(zip(Inputs._fields, ins))
        ]
    )
    store = Outputs(
        *[
            Ready(getattr(r, name), ref, r.stored.at[i])
            for i, (name, ref) in enumerate(zip(Outputs._fields, outs))
        ]
    )
    boxes = refs[len(names) :]
    links = Links()
    links.signal()
    for one in (fetch.weights, fetch.small, fetch.tokens, fetch.cot, *fetch[5:8], *fetch[9:]):
        one.start()
    r.out_own = r.out_rows.at[lax.axis_index(HEAD)]
    r.in_own = r.in_rows.at[lax.axis_index(HEAD)]
    own = r.cls.shape[1] * CELLS
    blk = Block(vars(r))
    gather = Gather(links, r.w, r.ag_send, r.ag_recv)
    scatter = Scatter(links, r.g, boxes, r.wg, r.rs_send, r.rs_recv)
    small = Small(
        links,
        *(r.sums, r.parts, r.in_c, r.in_x, r.in_y, r.in_h, r.in_l, r.full),
        r.small_send,
        r.small_recv,
    )
    out_rows = Rows(links, r.out_rows, r.out, own, r.out_send, r.out_recv)
    in_rows = Rows(links, r.in_rows, r.grad_in, own, r.in_send, r.in_recv)
    shares = [
        Exchange(links, axis, box, r.opt_send.at[i], r.opt_recv.at[i])
        for i, (axis, box) in enumerate(((HEAD, r.row_box), (DP, r.col_box), (ALL, r.sq_box)))
    ]
    opt = Adafactor(vars(r), *shares)

    fetch.weights.wait()
    for k in range(MATS):
        mine = links.region(r.w, SLOT_OF[k], "")
        mine[...] = r.weights[k].astype(BF16)
    links.meet()

    ops = []
    for tick in (gather.tick, scatter.tick):
        ops += [
            functools.partial(tick, slot, phase)
            for slot in range(MATS)
            for phase in range(len(AXES) + 1)
        ]
    ops += [
        then(fetch.small.wait, blk.setup),
        then(fetch.tokens.wait, blk.read_tokens),
        blk.norm_one,
        then(fetch.cot.wait, blk.read_cotangent),
    ]
    ops += [functools.partial(blk.project, k) for k in range(3)]
    ops += [blk.softmax, blk.contexts, blk.fill_window]
    ops += [functools.partial(blk.window_sum, c) for c in range(D // LANES)]
    ops += [blk.mix, blk.norm_two]
    for i in range(4):
        ops += [functools.partial(blk.hidden_block, i), functools.partial(blk.hidden_grads, i)]
    ops += [blk.finish_out, blk.back_two, blk.grad_proj, blk.back_heads, blk.back_query_key]
    ops += [functools.partial(blk.grad_of, k) for k in range(2)]
    ops += [functools.partial(blk.back_window, c) for c in range(D // LANES)]
    ops += [blk.back_value]
    ops += [functools.partial(blk.window_taps, c) for c in range(D // LANES)]
    ops += [blk.back_project, blk.back_one, blk.back_position, blk.position_taps, blk.finish_in]
    for rows, done in ((out_rows, store.out), (in_rows, store.grad_in)):
        ops += [functools.partial(rows.tick, stage) for stage in range(2)]
        ops += [then(functools.partial(rows.tick, 2), done.start)]
    ops += [functools.partial(small.tick, stage) for stage in range(8)]
    ops += [
        then(
            fetch.small_state.wait,
            fetch.small_ema.wait,
            opt.small_step,
            store.small_grads.start,
            store.new_small_state.start,
            store.new_small.start,
            store.new_small_ema.start,
        ),
        then(store.wg.start, opt.squares),
        then(
            fetch.row_state.wait,
            fetch.col_state.wait,
            opt.scale,
            store.new_rows.start,
            store.new_cols.start,
        ),
        then(
            fetch.ema.wait,
            opt.apply,
            store.new_weights.start,
            store.copy.start,
            store.new_ema.start,
        ),
        then(opt.clips, store.clip.start),
    ]
    for i in ORDER:
        ops[i]()
    for transfer in (gather, scatter, small, out_rows, in_rows, *shares):
        transfer.sent()
    for one in store:
        one.wait()


def finish_kernel(count, *refs):
    ins, outs, held = refs[:count], refs[count : 2 * count], refs[2 * count : 3 * count]
    took, gave = refs[3 * count :]
    come = [pltpu.make_async_copy(a, b, took.at[i]) for i, (a, b) in enumerate(zip(ins, held))]
    leave = [pltpu.make_async_copy(a, b, gave.at[i]) for i, (a, b) in enumerate(zip(held, outs))]
    for one in come:
        one.start()
    for one, other in zip(come, leave):
        one.wait()
        other.start()
    for one in leave:
        one.wait()


def local(
    tokens,
    cotangent,
    crop_image,
    crop_class,
    weights,
    row_state,
    col_state,
    weights_ema,
    small_params,
    small_state,
    small_ema,
):
    parts, heads = lax.axis_size(DP), lax.axis_size(HEAD)
    smem = pl.BlockSpec(memory_space=pltpu.SMEM)
    shared = shared_of(weights, parts, heads)
    own = scratch_of()

    def like(x, dtype=None):
        return jax.ShapeDtypeStruct(x.shape, dtype or x.dtype)

    clips = weights.shape[0] + small_params.shape[0]
    outs = (
        like(tokens),
        like(tokens),
        like(weights),
        like(row_state),
        like(col_state),
        like(weights),
        like(weights, BF16),
        like(weights),
        like(small_params),
        like(small_params),
        like(small_params),
        like(small_params),
        jax.ShapeDtypeStruct((1, clips), F32),
    )
    args = Inputs(
        crop_class,
        crop_image,
        tokens,
        cotangent,
        weights,
        row_state,
        col_state,
        weights_ema,
        small_params,
        small_state,
        small_ema,
    )
    staged = [pltpu.VMEM(x.shape, x.dtype) for x in (*args[2:], *outs)]
    names = (*shared, *own, *Inputs._fields[2:], *Outputs._fields)
    far = pl.BlockSpec(memory_space=pl.ANY)
    res = pl.pallas_call(
        functools.partial(block_kernel, names),
        out_shape=outs,
        in_specs=[smem, smem] + [far] * 9,
        out_specs=(far,) * len(outs),
        scratch_shapes=[
            *shared.values(),
            *own.values(),
            *staged,
            *box_shapes(Links(), weights.shape[1:]),
        ],
        compiler_params=pltpu.CompilerParams(
            collective_id=0, has_side_effects=True, vmem_limit_bytes=63 << 20
        ),
        name="block",
    )(*args)
    res = pl.pallas_call(
        functools.partial(finish_kernel, len(outs)),
        out_shape=outs,
        in_specs=[far] * len(outs),
        out_specs=(far,) * len(outs),
        scratch_shapes=[
            *[pltpu.VMEM(x.shape, x.dtype) for x in outs],
            pltpu.SemaphoreType.DMA((len(outs),)),
            pltpu.SemaphoreType.DMA((len(outs),)),
        ],
        compiler_params=pltpu.CompilerParams(vmem_limit_bytes=32 << 20),
        name="finish",
    )(*res)
    return (*res[:-1], res[-1].reshape(clips))


def solution(mesh):
    in_specs = (
        P(DP, None),
        P(DP, None),
        P(DP, None),
        P(DP, None),
        P(None, DP, HEAD),
        P(None, DP),
        P(None, HEAD),
        P(None, DP, HEAD),
        P(),
        P(),
        P(),
    )
    out_specs = (
        P(DP, None),
        P(DP, None),
        P(None, DP, HEAD),
        P(None, DP),
        P(None, HEAD),
        P(None, DP, HEAD),
        P(None, DP, HEAD),
        P(None, DP, HEAD),
        P(),
        P(),
        P(),
        P(),
        P(),
    )
    return jax.shard_map(local, mesh=mesh, in_specs=in_specs, out_specs=out_specs, check_vma=False)
```

```python
import functools
import math
import types
from typing import Any, NamedTuple

import jax
import jax.numpy as jnp
from jax import lax
from jax.experimental import pallas as pl
from jax.experimental.pallas import tpu as pltpu
from jax.sharding import PartitionSpec as P

DP, HEAD = "dp", "head"
ALL = (DP, HEAD)
D = 512
HEAD_DIM = 64
GRID = 7
SMALL_GRID = 3
WINDOW = 7
IMG_GROUP = 3
CELLS = GRID * GRID
SLOTS = 8
CELL_PAD = CELLS + 1
ROWS = CELL_PAD * SLOTS
LANES = 128
WIDE = 256
REACHES = (1, 2, 3, 3)
HALO = WINDOW // 2

NORM_EPS = 1e-06
SQUARE_FLOOR = 1e-30
SECOND_DECAY = 0.999
STEP_RATE = 0.02
SMALL_RATE = 0.05
AVERAGE_KEEP = 0.9
NEG_LARGE = -1e30
ROOT_HALF = 0.7071067811865476
INV_ROOT_TAU = 0.3989422804014327
INV_SCALE = 1.0 / math.sqrt(HEAD_DIM)

F32 = jnp.float32
BF16 = jnp.bfloat16
NN = (((1,), (0,)), ((), ()))
NT = (((1,), (1,)), ((), ()))
TN = (((0,), (0,)), ((), ()))


def dot(a, b, dims=NN):
    return lax.dot_general(a, b, dims, preferred_element_type=F32)


def lane_block(b):
    return slice(b * WIDE, (b + 1) * WIDE)


def wide(col):
    return jnp.concatenate([col] * (D // LANES), axis=1)


def rows_loop(count, size, body, init=None, unroll=1):
    def step(j, carry):
        return body(pl.multiple_of(j * size, size), carry)

    return lax.fori_loop(0, count // size, step, init, unroll=unroll)


def conv(src, halo, tap, reach, lanes, put):
    def line(y, _):
        sums = [jnp.zeros((SLOTS, LANES), F32) for _ in range(GRID)]
        for a in range(-reach, reach + 1):
            base = (y + (a + halo)) * GRID
            cells = [src[base + x, :, lanes] for x in range(GRID)]
            for b in range(-reach, reach + 1):
                t = tap(a, b)
                for x in range(GRID):
                    if 0 <= x + b < GRID:
                        sums[x] = sums[x] + t * cells[x + b]
        for x in range(GRID):
            put(y * GRID + x, sums[x])
        return 0

    lax.fori_loop(0, GRID, line, 0)


def tap_sums(up, src, halo, reach, lanes, put):
    for a in range(-reach, reach + 1):

        def line(y, sums):
            sums = list(sums)
            ups = [up(y * GRID + x) for x in range(GRID)]
            base = (y + (a + halo)) * GRID
            cells = [src[base + x, :, lanes] for x in range(GRID)]
            for i, b in enumerate(range(-reach, reach + 1)):
                for x in range(GRID):
                    if 0 <= x + b < GRID:
                        sums[i] = sums[i] + ups[x] * cells[x + b]
            return tuple(sums)

        start = tuple(jnp.zeros((SLOTS, LANES), F32) for _ in range(2 * reach + 1))
        sums = lax.fori_loop(0, GRID, line, start)
        for i, b in enumerate(range(-reach, reach + 1)):
            put(a, b, jnp.sum(sums[i], axis=0, keepdims=True))


def fold(x):
    return jnp.sum(x.reshape(x.shape[0] // SLOTS, SLOTS, x.shape[1]), axis=0)


def erf_parts(h):
    e = lax.erf(h * ROOT_HALF)
    half = 0.5 * (1.0 + e)
    return h * half, half + h * jnp.exp(-0.5 * h * h) * INV_ROOT_TAU


def norm_rows(v, gain, shift):
    centre = jnp.sum(v, axis=1, keepdims=True) * (1.0 / D)
    offset = v - centre
    spread = jnp.sum(offset * offset, axis=1, keepdims=True) * (1.0 / D)
    inverse = lax.rsqrt(spread + NORM_EPS)
    unit = offset * inverse
    return unit * gain + shift, unit, inverse


def norm_back(up, unit, inverse, gain):
    z = up * gain
    mean_z = jnp.sum(z, axis=1, keepdims=True) * (1.0 / D)
    mean_zu = jnp.sum(z * unit, axis=1, keepdims=True) * (1.0 / D)
    return inverse * (z - mean_z - unit * mean_zu)


class Block:
    def __init__(self, refs):
        self.__dict__.update(refs)

    def matrix(self, k, lo, hi):
        parts = []
        for h in range(lo, hi):
            part = self.w[h // 2, h % 2, :, :, :, k]
            if part.shape[-2] % 16:
                part = part.astype(F32).reshape(D, LANES).astype(BF16)
            else:
                part = part.reshape(D, LANES)
            parts.append(part)
        return jnp.concatenate(parts, axis=1)

    def times(self, lhs, k, b):
        return dot(lhs, self.matrix(k, 2 * b, 2 * b + 2))

    def times_t(self, lhs, k, b):
        return dot(lhs, self.matrix(k, 0, 4)[lane_block(b), :], NT)

    def put_grad(self, k, lhs_t, rhs):
        for b in range(2):
            g = dot(lhs_t, rhs[:, lane_block(b)])
            for i in range(2):
                piece = g[:, i * LANES : (i + 1) * LANES]
                place = self.g.shape[2:5]
                piece = piece.reshape(*place, self.g.shape[-2], LANES)
                self.g[b, i, :, :, :, k] = piece.astype(BF16)

    def row(self, j):
        return self.small[j : j + 1, :]

    def setup(self):
        head = lax.axis_index(HEAD)
        slots = self.cls.shape[1]
        self.sums[...] = jnp.zeros(self.sums.shape, F32)
        sub = lax.broadcasted_iota(jnp.int32, (SLOTS, LANES), 0)
        valid = jnp.where(sub < slots, 1.0, 0.0)
        full = jnp.zeros((SLOTS, LANES), F32)
        images = [jnp.zeros((SLOTS, LANES), F32) for _ in range(IMG_GROUP)]
        for s in range(slots):
            full = jnp.where(sub == s, jnp.where(self.cls[head, s] == 0, 1.0, 0.0), full)
            for i in range(IMG_GROUP):
                images[i] = jnp.where(
                    sub == s, jnp.where(self.img[head, s] == i, 1.0, 0.0), images[i]
                )
        for cell in range(CELLS):
            small = cell // GRID < SMALL_GRID and cell % GRID < SMALL_GRID
            self.live[cell * SLOTS : (cell + 1) * SLOTS, :] = valid if small else full
        self.live[CELLS * SLOTS :, :] = jnp.zeros((SLOTS, LANES), F32)
        for i in range(IMG_GROUP):
            self.im8[i] = images[i]
            self.im16[i] = jnp.concatenate([images[i], images[i]], axis=0).astype(BF16)
        self.pos_src[0:GRID] = jnp.zeros((GRID, SLOTS, D), F32)
        self.pos_src[GRID + CELLS :] = jnp.zeros((GRID, SLOTS, D), F32)
        for pad in (self.rel_src, self.dq_src):
            pad[0 : HALO * GRID] = jnp.zeros((HALO * GRID, SLOTS, D), F32)
            pad[HALO * GRID + CELLS :] = jnp.zeros((HALO * GRID, SLOTS, D), F32)
        tap = lax.broadcasted_iota(jnp.int32, (WINDOW * WINDOW, 1), 0)
        row_off = jnp.abs(tap // WINDOW - HALO)
        col_off = jnp.abs(tap % WINDOW - HALO)
        off = jnp.maximum(row_off, col_off)
        heads = lax.broadcasted_iota(jnp.int32, (1, D), 1) // HEAD_DIM
        reach = jnp.where(heads < 2, 1, jnp.where(heads < 5, 2, 3))
        mask = jnp.where(off <= reach, 1.0, 0.0)
        self.window[...] = mask
        self.rel_taps[...] = self.small[22 : 22 + WINDOW * WINDOW, :] * mask

    def place(self, rows_ref, first, r0, size):
        count = rows_ref.shape[0]
        r = r0 + lax.broadcasted_iota(jnp.int32, (size, 1), 0)
        cell, slot = r >> 3, r & 7
        want = first + slot * CELLS + cell
        want = jnp.where((slot < self.cls.shape[1]) & (cell < CELLS), want, -1)
        col = lax.broadcasted_iota(jnp.int32, (size, count), 1)
        pick = jnp.where(col == want, 1.0, 0.0).astype(BF16)
        return dot(pick, rows_ref[...])

    def unplace(self, src_ref, out_ref):
        count = out_ref.shape[0]
        own = self.cls.shape[1] * CELLS
        lead = lax.rem(lax.axis_index(HEAD) * own, 16)
        r = lax.broadcasted_iota(jnp.int32, (1, ROWS), 1)
        cell, slot = r >> 3, r & 7
        target = lead + slot * CELLS + cell
        target = jnp.where((slot < self.cls.shape[1]) & (cell < CELLS), target, -1)
        t = lax.broadcasted_iota(jnp.int32, (count, ROWS), 0)
        pick = jnp.where(t == target, 1.0, 0.0).astype(BF16)
        out_ref[...] = dot(pick, src_ref[...]).astype(BF16)

    def read_tokens(self):
        first = lax.axis_index(HEAD) * (self.cls.shape[1] * CELLS)
        size = 80

        def body(r0, _):
            live = wide(self.live[pl.ds(r0, size), :])
            x = self.place(self.tokens, first, r0, size)
            self.first[pl.ds(r0, size), :] = x
            c0 = r0 // SLOTS
            self.pos_src[pl.ds(GRID + c0, size // SLOTS)] = (x * live).reshape(-1, SLOTS, D)
            return 0

        rows_loop(ROWS, size, body, 0)

    def read_cotangent(self):
        first = lax.axis_index(HEAD) * (self.cls.shape[1] * CELLS)
        size = 80

        def body(r0, _):
            live = wide(self.live[pl.ds(r0, size), :])
            c = self.place(self.cot, first, r0, size)
            self.go[pl.ds(r0, size), :] = (c * live).astype(BF16)
            return 0

        rows_loop(ROWS, size, body, 0)
        self.go_t[...] = self.go[...].T
        self.back[...] = jnp.zeros((ROWS, D), F32)

    def norm_one(self):
        for c in range(D // LANES):
            lanes = slice(c * LANES, (c + 1) * LANES)

            def put(cell, value):
                rows = pl.ds(pl.multiple_of(cell * SLOTS, SLOTS), SLOTS)
                self.first[rows, lanes] = self.first[rows, lanes] + value + self.small[8:9, lanes]

            def tap(a, b):
                t = 13 + (a + 1) * 3 + b + 1
                return self.small[t : t + 1, lanes]

            conv(self.pos_src, 1, tap, 1, lanes, put)

        def body(r0, _):
            rows = pl.ds(r0, 16)
            n, u, inv = norm_rows(self.first[rows, :], self.row(0), self.row(1))
            self.n1[rows, :] = n.astype(BF16)
            self.u1[rows, :] = u
            self.inv1[rows, :] = jnp.broadcast_to(inv, (16, LANES))
            return 0

        rows_loop(ROWS, 16, body, 0, unroll=5)
        self.n1_t[...] = self.n1[...].T

    def project(self, k):
        low = (self.q, self.k, self.v)[k]
        for b in range(2):
            cols = lane_block(b)
            p = self.times(self.n1[...], k, b)
            if k != 1:
                p = p + self.small[2 + k // 2 : 3 + k // 2, cols]
            low[:, cols] = p.astype(BF16)

    def image_sum(self, x):
        total = jnp.zeros((SLOTS, D), F32)
        for i in range(IMG_GROUP):
            im = wide(self.im8[i])
            total = total + im * jnp.sum(im * x, axis=0, keepdims=True)
        return total

    def softmax(self):
        def top(r0, best):
            live = wide(self.live[pl.ds(r0, 16), :])
            keys = jnp.where(live > 0, self.k[pl.ds(r0, 16), :].astype(F32), NEG_LARGE)
            return jnp.maximum(best, jnp.max(keys.reshape(2, SLOTS, D), axis=0))

        best = rows_loop(ROWS, 16, top, jnp.full((SLOTS, D), NEG_LARGE, F32), unroll=5)
        shift = jnp.zeros((SLOTS, D), F32)
        for i in range(IMG_GROUP):
            im = wide(self.im8[i])
            most = jnp.max(jnp.where(im > 0, best, NEG_LARGE), axis=0, keepdims=True)
            shift = jnp.where(im > 0, most, shift)
        shift2 = jnp.concatenate([shift, shift], axis=0)

        def raise_(r0, total):
            rows = pl.ds(r0, 16)
            live = wide(self.live[rows, :])
            keys = self.k[rows, :].astype(F32)
            e = jnp.where(live > 0, jnp.exp(jnp.where(live > 0, keys - shift2, 0.0)), 0.0)
            self.soft[rows, :] = e
            return total + fold(e)

        total = self.image_sum(
            rows_loop(ROWS, 16, raise_, jnp.zeros((SLOTS, D), F32), unroll=5)
        )
        scale = 1.0 / jnp.where(total > 0, total, 1.0)
        scale2 = jnp.concatenate([scale, scale], axis=0)

        def divide(r0, _):
            rows = pl.ds(r0, 16)
            soft = self.soft[rows, :] * scale2
            self.soft[rows, :] = soft
            self.soft_low[rows, :] = soft.astype(BF16)
            return 0

        rows_loop(ROWS, 16, divide, 0, unroll=5)

    def by_image(self, x):
        tiles = x.reshape(ROWS // 16, 16, WIDE)
        parts = []
        for i in range(IMG_GROUP):
            im = jnp.concatenate([self.im16[i]] * (WIDE // LANES), axis=1)
            parts.append((tiles * im[None]).reshape(ROWS, WIDE))
        return jnp.concatenate(parts, axis=1)

    def head_blocks(self, x):
        r = lax.broadcasted_iota(jnp.int32, x.shape, 0) // HEAD_DIM
        c = (lax.broadcasted_iota(jnp.int32, x.shape, 1) % WIDE) // HEAD_DIM
        return jnp.where(r == c, x, 0.0).astype(BF16)

    def stacked(self, x):
        return jnp.concatenate([x[:, lane_block(i)] for i in range(IMG_GROUP)], axis=0)

    def contexts(self):
        for b in range(2):
            cols = lane_block(b)
            ctx = dot(self.soft_low[:, cols], self.by_image(self.v[:, cols]), TN)
            ctx = self.head_blocks(ctx)
            self.ctx[b] = ctx
            self.factor[:, cols] = dot(self.by_image(self.q[:, cols]), self.stacked(ctx))

    def fill_window(self):
        def fill(r0, _):
            rows = pl.ds(r0, 16)
            v = self.v[rows, :].astype(F32) * wide(self.live[rows, :])
            c0 = r0 // SLOTS
            self.rel_src[pl.ds(HALO * GRID + c0, 2)] = v.reshape(2, SLOTS, D)
            return 0

        rows_loop(ROWS, 16, fill, 0, unroll=5)
        self.rel[CELLS * SLOTS :, :] = jnp.zeros((SLOTS, D), F32)

    def window_sum(self, c):
        lanes = slice(c * LANES, (c + 1) * LANES)

        def put(cell, value):
            rows = pl.ds(pl.multiple_of(cell * SLOTS, SLOTS), SLOTS)
            self.rel[rows, lanes] = value

        def tap(a, b):
            t = (a + HALO) * WINDOW + b + HALO
            return self.rel_taps[t : t + 1, lanes]

        conv(self.rel_src, HALO, tap, REACHES[c], lanes, put)

    def mix(self):
        def mix(r0, _):
            rows = pl.ds(r0, 16)
            m = self.factor[rows, :] * INV_SCALE + self.q[rows, :].astype(F32) * self.rel[rows, :]
            self.mixed[rows, :] = (m * wide(self.live[rows, :])).astype(BF16)
            return 0

        rows_loop(ROWS, 16, mix, 0, unroll=5)

    def norm_two(self):
        for b in range(2):
            cols = lane_block(b)
            p = self.times_t(self.mixed[...], 3, b)
            self.second[:, cols] = self.first[:, cols] + p + self.small[4:5, cols]

        def body(r0, _):
            rows = pl.ds(r0, 16)
            n, u, inv = norm_rows(self.second[rows, :], self.row(5), self.row(6))
            self.n2[rows, :] = n.astype(BF16)
            self.u2[rows, :] = u
            self.inv2[rows, :] = jnp.broadcast_to(inv, (16, LANES))
            return 0

        rows_loop(ROWS, 16, body, 0, unroll=5)
        self.n2_t[...] = self.n2[...].T

    def hidden_block(self, r):
        up, down = 4 + 2 * r, 5 + 2 * r
        for b in range(2):
            cols = lane_block(b)
            h = self.times(self.n2[...], up, b) + self.small[pl.ds(9 + r, 1), cols]
            self.hidden[:, cols] = h
            self.factor[:, cols] = self.times(self.go[...], down, b)

        def body(r0, total):
            rows = pl.ds(r0, 16)
            act, slope = erf_parts(self.hidden[rows, :])
            g = self.factor[rows, :] * slope
            self.active[rows, :] = act.astype(BF16)
            self.low[rows, :] = g.astype(BF16)
            return total + fold(g)

        total = rows_loop(ROWS, 16, body, jnp.zeros((SLOTS, D), F32), unroll=5)
        self.sums[pl.ds(9 + r, 1), :] = jnp.sum(total, axis=0, keepdims=True)

    def hidden_grads(self, r):
        up, down = 4 + 2 * r, 5 + 2 * r
        self.put_grad(down, self.go_t[...], self.active)
        self.put_grad(up, self.n2_t[...], self.low)
        for b in range(2):
            cols = lane_block(b)
            self.second[:, cols] += self.times_t(self.active[...], down, b)
            self.back[:, cols] += self.times_t(self.low[...], up, b)

    def finish_out(self):
        def body(r0, _):
            rows = pl.ds(r0, 16)
            self.out_low[rows, :] = (self.second[rows, :] + self.row(7)).astype(BF16)
            return 0

        rows_loop(ROWS, 16, body, 0, unroll=5)
        self.unplace(self.out_low, self.out_own)

    def back_two(self):
        zero = jnp.zeros((SLOTS, D), F32)

        def body(r0, sums):
            rows = pl.ds(r0, 16)
            back, u = self.back[rows, :], self.u2[rows, :]
            go = self.go[rows, :].astype(F32)
            gs = go + norm_back(back, u, wide(self.inv2[rows, :]), self.row(5))
            self.gs[rows, :] = gs
            self.gs_low[rows, :] = gs.astype(BF16)
            new = (gs, back * u, back, go)
            return tuple(s + fold(n) for s, n in zip(sums, new, strict=True))

        sums = rows_loop(ROWS, 16, body, (zero,) * 4, unroll=5)
        for j, s in zip((4, 5, 6, 7), sums, strict=True):
            self.sums[j : j + 1, :] = jnp.sum(s, axis=0, keepdims=True)

    def grad_proj(self):
        self.put_grad(3, self.gs_low[...].T, self.mixed)

    def back_heads(self):
        for b in range(2):
            cols = lane_block(b)
            self.d[:, cols] = self.times(self.gs_low[...], 3, b)

        def fill(r0, _):
            rows = pl.ds(r0, 16)
            d = self.d[rows, :] * wide(self.live[rows, :])
            self.d[rows, :] = d
            self.f[rows, :] = (d * INV_SCALE).astype(BF16)
            c0 = r0 // SLOTS
            dq = d * self.q[rows, :].astype(F32)
            self.dq_src[pl.ds(HALO * GRID + c0, 2)] = dq.reshape(2, SLOTS, D)
            return 0

        rows_loop(ROWS, 16, fill, 0, unroll=5)
        for b in range(2):
            cols = lane_block(b)
            f3 = self.by_image(self.f[:, cols])
            g = self.head_blocks(dot(self.q[:, cols], f3, TN))
            self.gq[:, cols] = dot(f3, self.ctx[b], NT)
            self.gk[:, cols] = dot(self.by_image(self.v[:, cols]), g, NT)
            self.gv[:, cols] = dot(self.by_image(self.soft_low[:, cols]), self.stacked(g))

    def back_window(self, c):
        lanes = slice(c * LANES, (c + 1) * LANES)

        def put(cell, value):
            rows = pl.ds(pl.multiple_of(cell * SLOTS, SLOTS), SLOTS)
            self.gv[rows, lanes] = self.gv[rows, lanes] + value * self.live[rows, :]

        def tap(a, b):
            t = (HALO - a) * WINDOW + HALO - b
            return self.rel_taps[t : t + 1, lanes]

        conv(self.dq_src, HALO, tap, REACHES[c], lanes, put)

    def window_taps(self, c):
        lanes = slice(c * LANES, (c + 1) * LANES)

        def up(cell):
            return self.dq_src[HALO * GRID + cell, :, lanes]

        def put_tap(a, b, value):
            t = (a + HALO) * WINDOW + b + HALO
            keep = self.window[t : t + 1, lanes]
            self.sums[22 + t : 23 + t, lanes] = value * keep

        tap_sums(up, self.rel_src, HALO, REACHES[c], lanes, put_tap)

    def back_query_key(self):
        zero = jnp.zeros((SLOTS, D), F32)

        def inner(r0, total):
            rows = pl.ds(r0, 16)
            return total + fold(self.soft[rows, :] * self.gk[rows, :])

        shared = self.image_sum(rows_loop(ROWS, 16, inner, zero, unroll=5))
        shared2 = jnp.concatenate([shared, shared], axis=0)

        def low(r0, total):
            rows = pl.ds(r0, 16)
            gq = self.gq[rows, :] + self.d[rows, :] * self.rel[rows, :]
            gk = self.soft[rows, :] * (self.gk[rows, :] - shared2)
            self.gl[0, rows, :] = gq.astype(BF16)
            self.gl[1, rows, :] = gk.astype(BF16)
            return total + fold(gq)

        total = rows_loop(ROWS, 16, low, zero, unroll=5)
        self.sums[2:3, :] = jnp.sum(total, axis=0, keepdims=True)

    def back_value(self):
        def low(r0, total):
            rows = pl.ds(r0, 16)
            gv = self.gv[rows, :]
            self.gl[2, rows, :] = gv.astype(BF16)
            return total + fold(gv)

        total = rows_loop(ROWS, 16, low, jnp.zeros((SLOTS, D), F32), unroll=5)
        self.sums[3:4, :] = jnp.sum(total, axis=0, keepdims=True)
        self.grad_of(2)

    def grad_of(self, k):
        self.put_grad(k, self.n1_t[...], self.gl.at[k])

    def back_project(self):
        for b in range(2):
            cols = lane_block(b)
            back = self.times_t(self.gl[0], 0, b)
            back = back + self.times_t(self.gl[1], 1, b)
            self.back[:, cols] = back + self.times_t(self.gl[2], 2, b)

    def back_one(self):
        zero = jnp.zeros((SLOTS, D), F32)
        self.pos_up[0:GRID] = jnp.zeros((GRID, SLOTS, D), F32)
        self.pos_up[GRID + CELLS :] = jnp.zeros((GRID, SLOTS, D), F32)

        def body(r0, sums):
            rows = pl.ds(r0, 16)
            back, u = self.back[rows, :], self.u1[rows, :]
            gf = self.gs[rows, :] + norm_back(back, u, wide(self.inv1[rows, :]), self.row(0))
            c0 = r0 // SLOTS
            self.pos_up[pl.ds(GRID + c0, 2)] = gf.reshape(2, SLOTS, D)
            new = (back * u, back, gf)
            return tuple(s + fold(n) for s, n in zip(sums, new, strict=True))

        sums = rows_loop(ROWS, 16, body, (zero,) * 3, unroll=5)
        for j, s in zip((0, 1, 8), sums, strict=True):
            self.sums[j : j + 1, :] = jnp.sum(s, axis=0, keepdims=True)

    def back_position(self):
        for c in range(D // LANES):
            lanes = slice(c * LANES, (c + 1) * LANES)

            def put(cell, value):
                rows = pl.ds(pl.multiple_of(cell * SLOTS, SLOTS), SLOTS)
                gf = self.pos_up[GRID + cell, :, lanes]
                self.first[rows, lanes] = gf + value * self.live[rows, :]

            def tap(a, b):
                t = 13 + (1 - a) * 3 + 1 - b
                return self.small[t : t + 1, lanes]

            conv(self.pos_up, 1, tap, 1, lanes, put)

    def position_taps(self):
        for c in range(D // LANES):
            lanes = slice(c * LANES, (c + 1) * LANES)

            def up(cell):
                return self.pos_up[GRID + cell, :, lanes]

            def put_tap(a, b, value):
                t = 13 + (a + 1) * 3 + b + 1
                self.sums[t : t + 1, lanes] = value

            tap_sums(up, self.pos_src, 1, 1, lanes, put_tap)

    def finish_in(self):
        def down(r0, _):
            rows = pl.ds(r0, 16)
            self.in_low[rows, :] = self.first[rows, :].astype(BF16)
            return 0

        rows_loop(ROWS, 16, down, 0, unroll=5)
        self.unplace(self.in_low, self.in_own)


SLOT_OF = (0, 1, 2, 3, 4, 6, 8, 10, 5, 7, 9, 11)
MATS = len(SLOT_OF)
AXES = "xchly"
HEAD_ROWS = 320
SMALL_ROWS = 72
AG_ROUTES = ("lhyxc", "hlxyc", "lhyxc", "hxlyc", "hlxyc", "xylhc", "hylxc", "hylxc", "lxhyc", "xyhlc", "lhxyc", "xylhc")
RS_ROUTES = ("cxylh", "clyhx", "cxylh", "cyhlx", "cxyhl", "clhyx", "cylxh", "cxylh", "cyxhl", "chlyx", "clyxh", "cylhx")
ORDER = (
    6, 12, 0, 66, 18, 30, 42, 48, 36, 60, 54, 24, 144, 147, 145, 13, 31, 7, 55, 1,
    146, 19, 25, 49, 37, 43, 61, 67, 32, 8, 56, 14, 2, 20, 26, 38, 50, 44, 62, 68,
    9, 33, 15, 27, 57, 3, 21, 63, 39, 10, 16, 51, 45, 11, 149, 151, 69, 17, 4, 150,
    153, 154, 156, 155, 22, 28, 157, 5, 34, 148, 152, 40, 158, 23, 159, 46, 29, 64, 58, 35,
    160, 161, 52, 96, 102, 41, 47, 162, 70, 163, 108, 59, 65, 114, 53, 164, 97, 165, 126, 120,
    103, 71, 166, 109, 115, 167, 127, 132, 138, 168, 189, 121, 169, 133, 98, 170, 90, 171, 139, 172,
    173, 72, 110, 181, 174, 78, 91, 177, 180, 183, 128, 134, 104, 73, 175, 79, 99, 176, 111, 116,
    122, 178, 179, 84, 140, 184, 185, 129, 186, 85, 92, 190, 187, 105, 182, 135, 195, 112, 74, 188,
    80, 191, 130, 117, 196, 123, 192, 100, 106, 141, 86, 75, 136, 93, 131, 118, 113, 81, 197, 101,
    124, 87, 76, 142, 94, 137, 198, 119, 125, 88, 82, 77, 193, 107, 199, 143, 95, 83, 89, 204,
    194, 200, 205, 201, 202, 203, 206, 207,
)


def scratch_of():
    f, h, low = (ROWS, D), (ROWS, LANES), pltpu.VMEM((ROWS, D), BF16)
    halo3 = pltpu.VMEM(((GRID + 2 * HALO) * GRID, SLOTS, D), F32)
    halo1 = pltpu.VMEM(((GRID + 2) * GRID, SLOTS, D), F32)
    high, column, turned = pltpu.VMEM(f, F32), pltpu.VMEM(h, F32), pltpu.VMEM((D, ROWS), BF16)
    taps = pltpu.VMEM((WINDOW * WINDOW, D), F32)
    return dict(
        live=column,
        im8=pltpu.VMEM((IMG_GROUP, SLOTS, LANES), F32),
        im16=pltpu.VMEM((IMG_GROUP, 16, LANES), BF16),
        window=taps,
        rel_taps=taps,
        pos_src=halo1,
        pos_up=halo1,
        rel_src=halo3,
        dq_src=halo3,
        first=high,
        u1=high,
        inv1=column,
        second=high,
        u2=high,
        inv2=column,
        n1=low,
        n1_t=turned,
        n2=low,
        n2_t=turned,
        go=low,
        go_t=turned,
        q=low,
        k=low,
        v=low,
        soft=high,
        soft_low=low,
        ctx=pltpu.VMEM((2, WIDE, IMG_GROUP * WIDE), BF16),
        factor=high,
        rel=high,
        mixed=low,
        hidden=high,
        active=low,
        low=low,
        out_low=low,
        back=high,
        gs=high,
        gs_low=low,
        d=high,
        f=low,
        gq=high,
        gk=high,
        gv=high,
        gl=pltpu.VMEM((3, ROWS, D), BF16),
        in_low=low,
    )


class Links:
    def __init__(self):
        dp, head = lax.axis_index(DP), lax.axis_index(HEAD)
        self.far = lax.axis_size(DP) // 4
        self.at = dict(x=head // 2, c=head % 2, h=dp // 4, l=dp // 2 % 2, y=dp % 2)

    def count(self, axis):
        return self.far if axis == "h" else 2

    def peer(self, axis, step):
        return lax.rem(self.at[axis] + step, self.count(axis))

    def device(self, axis, step):
        at = {**self.at, axis: self.peer(axis, step)}
        return (at["h"] * 4 + at["l"] * 2 + at["y"], at["x"] * 2 + at["c"])

    def steps(self, axis, do):
        self.repeat(self.count(axis), do)

    def repeat(self, size, do):
        if size <= 32:
            for step in range(1, size):
                do(step)
        else:

            def body(step, _):
                do(step)
                return 0

            lax.fori_loop(1, size, body, 0)

    def others(self, name, do):
        dp, head, heads = lax.axis_index(DP), lax.axis_index(HEAD), lax.axis_size(HEAD)

        def one(step):
            if name == ALL:
                i = lax.rem(dp * heads + head + step, lax.axis_size(ALL))
                do((i // heads, lax.rem(i, heads)))
            elif name == DP:
                do((lax.rem(dp + step, lax.axis_size(DP)), head))
            else:
                do((dp, lax.rem(head + step, heads)))

        self.repeat(lax.axis_size(name), one)

    def signal(self):
        def one(device):
            pl.semaphore_signal(
                pltpu.get_barrier_semaphore(),
                inc=1,
                device_id=device,
                device_id_type=pl.DeviceIdType.MESH,
            )

        self.others(ALL, one)

    def meet(self):
        pl.semaphore_wait(pltpu.get_barrier_semaphore(), lax.axis_size(ALL) - 1)

    def copy(self, src, dst, send, recv, device):
        return pltpu.make_async_remote_copy(
            src_ref=src,
            dst_ref=dst,
            send_sem=send,
            recv_sem=recv,
            device_id=device,
            device_id_type=pl.DeviceIdType.MESH,
        )

    def region(self, blocks, slot, whole, **at):
        at = {**self.at, **at}
        place = [slice(None) if axis in whole else at[axis] for axis in AXES]
        return blocks.at[(*place, slot)]


class Gather:
    def __init__(self, links, w, send, recv):
        self.links, self.w, self.send, self.recv = links, w, send, recv

    def start(self, slot, phase):
        path = AG_ROUTES[slot]
        part = self.links.region(self.w, slot, path[:phase])
        sems = self.send.at[slot, phase], self.recv.at[slot, phase]

        def go(step):
            self.links.copy(part, part, *sems, self.links.device(path[phase], step)).start()

        self.links.steps(path[phase], go)

    def descriptor(self, slot, phase):
        path = AG_ROUTES[slot]
        at = {"h": pl.ds(0, self.links.far - 1)} if path[phase] == "h" else {}
        part = self.links.region(self.w, slot, path[:phase], **at)
        sems = self.send.at[slot, phase], self.recv.at[slot, phase]
        return self.links.copy(part, part, *sems, self.links.device(path[phase], 1))

    def tick(self, slot, phase):
        if phase:
            self.descriptor(slot, phase - 1).wait_recv()
        if phase < len(AXES):
            self.start(slot, phase)

    def sent(self):
        for slot in range(MATS):
            for phase in range(len(AXES)):
                self.descriptor(slot, phase).wait_send()


class Scatter:
    def __init__(self, links, g, boxes, total, send, recv):
        self.links, self.g, self.boxes, self.total = links, g, boxes, total
        self.send, self.recv = send, recv

    def descriptor(self, slot, phase):
        box = self.boxes[slot * len(AXES) + phase]
        sems = self.send.at[slot, phase], self.recv.at[slot, phase]
        return self.links.copy(box, box, *sems, self.links.device(RS_ROUTES[slot][phase], 1))

    def take(self, slot, phase):
        path = RS_ROUTES[slot]
        self.descriptor(slot, phase).wait_recv()
        own = self.links.region(self.g, slot, path[phase + 1 :])
        box = self.boxes[slot * len(AXES) + phase]
        if path[phase] == "h" and box.shape[0] == 1:
            box = box.at[0]
        elif path[phase] == "h":
            value = own[...].astype(F32)
            return own, value + jnp.sum(box[...].astype(F32), axis=0)
        return own, own[...] + box[...] if phase + 1 < len(AXES) else (
            own[...].astype(F32) + box[...].astype(F32)
        )

    def start(self, slot, phase):
        path = RS_ROUTES[slot]
        axis, rest = path[phase], path[phase + 1 :]
        box = self.boxes[slot * len(AXES) + phase]
        sems = self.send.at[slot, phase], self.recv.at[slot, phase]

        def go(step):
            at = {axis: self.links.peer(axis, step)}
            part = self.links.region(self.g, slot, rest, **at)
            into = box.at[step - 1] if axis == "h" else box
            self.links.copy(part, into, *sems, self.links.device(axis, step)).start()

        self.links.steps(axis, go)

    def tick(self, slot, phase):
        if phase:
            own, value = self.take(slot, phase - 1)
            if phase == len(AXES):
                self.total[SLOT_OF.index(slot)] = value
                return
            own[...] = value.astype(BF16)
        self.start(slot, phase)

    def sent(self):
        for slot in range(MATS):
            for phase in range(len(AXES)):
                self.descriptor(slot, phase).wait_send()


class Small:
    def __init__(self, links, sums, parts, in_c, in_x, in_y, in_h, in_l, full, send, recv):
        self.links, self.sums, self.parts, self.full = links, sums, parts, full
        self.in_c, self.in_x, self.in_y, self.in_h, self.in_l = in_c, in_x, in_y, in_h, in_l
        self.send, self.recv = send, recv

    def go(self, stage, src, dst, axis):
        sems = (self.send.at[stage], self.recv.at[stage])
        self.links.steps(
            axis, lambda step: self.links.copy(src, dst, *sems, self.links.device(axis, step)).start()
        )

    def wait(self, stage):
        x, c = self.links.at["x"], self.links.at["c"]
        ref = (
            self.in_c,
            self.in_x,
            self.in_y,
            self.in_h.at[pl.ds(0, self.links.far - 1)],
            self.in_l,
            self.full.at[c, x],
            self.full.at[c],
        )[stage]
        sems = (self.send.at[stage], self.recv.at[stage])
        return self.links.copy(ref, ref, *sems, self.links.device("cxyhlxc"[stage], 1))

    def tick(self, stage):
        at = self.links.at
        x, c, h = at["x"], at["c"], at["h"]
        mine = self.parts.at[c, x]
        if stage:
            self.wait(stage - 1).wait_recv()
        if stage == 0:
            for b in range(D // LANES):
                self.parts[b // 2, b % 2] = self.sums[:, b * LANES : (b + 1) * LANES]
            self.go(0, self.parts.at[1 - c], self.in_c, "c")
        if stage == 1:
            self.parts[c] = self.parts[c] + self.in_c[...]
            self.go(1, self.parts.at[c, 1 - x], self.in_x, "x")
        if stage == 2:
            mine[...] = mine[...] + self.in_x[...]
            self.go(2, mine, self.in_y, "y")
        if stage == 3:
            self.in_h[h] = mine[...] + self.in_y[...]
            self.go(3, self.in_h.at[h], self.in_h.at[h], "h")
        if stage == 4:
            total = self.in_h[0]
            for i in range(1, self.links.far):
                total = total + self.in_h[i]
            self.sums[:, 0:LANES] = total
            self.go(4, self.sums.at[:, pl.ds(0, LANES)], self.in_l, "l")
        if stage == 5:
            self.full[c, x] = self.sums[:, 0:LANES] + self.in_l[...]
            self.go(5, self.full.at[c, x], self.full.at[c, x], "x")
        if stage == 6:
            self.go(6, self.full.at[c], self.full.at[c], "c")

    def sent(self):
        for stage in range(7):
            self.wait(stage).wait_send()


class Rows:
    def __init__(self, links, blocks, out, own, send, recv):
        self.links, self.blocks, self.out, self.own = links, blocks, out, own
        self.send, self.recv = send, recv

    def hop(self, i):
        x, c = self.links.at["x"], self.links.at["c"]
        x, axis = ((x, "x"), (x, "c"), (1 - x, "c"))[i]
        block = self.blocks.at[2 * x + c]
        return self.links.copy(
            block, block, self.send.at[i], self.recv.at[i], self.links.device(axis, 1)
        )

    def tick(self, stage):
        if stage == 0:
            self.hop(0).start()
            self.hop(1).start()
        if stage == 1:
            self.hop(0).wait_recv()
            self.hop(2).start()
        if stage == 2:
            self.hop(1).wait_recv()
            self.hop(2).wait_recv()
            self.join()

    def sent(self):
        for i in range(3):
            self.hop(i).wait_send()

    def join(self):
        heads, end, own = self.blocks.shape[0], self.out.shape[0], self.own
        for h in range(heads):
            lo, hi = h * own, (h + 1) * own
            base = lo // 16 * 16
            first = base + 16 if lo % 16 else base
            last = hi // 16 * 16 if h + 1 < heads else end
            self.out[first:last, :] = self.blocks[h, first - base : last - base, :]
            if lo % 16:
                before = (lo - own) // 16 * 16
                tail = self.blocks[h - 1, base - before : base - before + 16, :]
                self.out[base : base + 16, :] = tail + self.blocks[h, 0:16, :]


class Exchange:
    def __init__(self, links, name, buffer, send, recv):
        self.links, self.name, self.buffer, self.send, self.recv = links, name, buffer, send, recv

    def start(self, value):
        own = lax.axis_index(self.name)
        self.buffer[own] = value
        mine = self.buffer.at[own]
        self.links.others(
            self.name,
            lambda device: self.links.copy(mine, mine, self.send, self.recv, device).start(),
        )

    def descriptor(self):
        ref = self.buffer.at[pl.ds(0, self.buffer.shape[0] - 1)]
        return self.links.copy(ref, ref, self.send, self.recv, self.links.device("c", 1))

    def total(self):
        self.descriptor().wait_recv()
        return jnp.sum(self.buffer[...], axis=0)

    def sent(self):
        self.descriptor().wait_send()


def exact(a, b, dims):
    return lax.dot_general(
        a, b, dims, precision=lax.Precision.HIGHEST, preferred_element_type=F32
    )


class Adafactor:
    def __init__(self, refs, row_share, col_share, sq_share):
        self.__dict__.update(refs)
        self.row_share, self.col_share, self.sq_share = row_share, col_share, sq_share

    def eye(self, count):
        r = lax.broadcasted_iota(jnp.int32, (count, LANES), 0)
        c = lax.broadcasted_iota(jnp.int32, (count, LANES), 1)
        return jnp.where(r == c, 1.0, 0.0)

    def lane(self, k, value, rest):
        lanes = lax.broadcasted_iota(jnp.int32, rest.shape, 1)
        return jnp.where(lanes == k, value, rest)

    def squares(self):
        rows = self.wg.shape[1]
        by_row = jnp.zeros((rows, LANES), F32)
        by_col = []
        for k in range(MATS):
            g = self.wg[k]
            s = g * g + SQUARE_FLOOR
            by_row = self.lane(k, jnp.sum(s, axis=1, keepdims=True), by_row)
            by_col.append(jnp.sum(s, axis=0, keepdims=True))
        self.col_share.start(jnp.concatenate([*by_col, jnp.zeros((4, LANES), F32)], axis=0))
        turned = exact(self.eye(16), by_row, NT)
        if rows < LANES:
            turned = jnp.concatenate([turned, jnp.zeros((16, LANES - rows), F32)], axis=1)
        self.row_share.start(turned)

    def scale(self):
        rows = self.wg.shape[1]
        total = self.row_share.total()[0:MATS, 0:rows]
        new_rows = SECOND_DECAY * self.row_state[...] + (1.0 - SECOND_DECAY) * (total * (1.0 / D))
        self.new_rows[...] = new_rows
        row = exact(new_rows, self.eye(MATS), TN)
        total = self.col_share.total()[0:MATS]
        cols = SECOND_DECAY * self.col_state[...] + (1.0 - SECOND_DECAY) * (total * (1.0 / D))
        self.new_cols[...] = cols
        sums = jnp.zeros((1, LANES), F32)
        for k in range(MATS):
            u = self.wg[k] * lax.rsqrt(row[:, k : k + 1] * cols[k : k + 1, :])
            self.upd[k] = u
            s = jnp.sum(jnp.sum(u * u, axis=0, keepdims=True), axis=1, keepdims=True)
            sums = self.lane(k, s, sums)
        mass = jnp.sum(row, axis=0, keepdims=True)
        self.sq_share.start(jnp.concatenate([sums, mass], axis=0))

    def apply(self):
        total = self.sq_share.total()
        mean = total[1:2] * (1.0 / (D * lax.axis_size(HEAD)))
        rms = jnp.sqrt(total[0:1] * mean * (1.0 / (D * D)))
        rate = STEP_RATE * jnp.sqrt(mean) / jnp.maximum(1.0, rms)
        for k in range(MATS):
            new = self.weights[k] - rate[:, k : k + 1] * self.upd[k]
            self.new_weights[k] = new
            self.copy[k] = new.astype(BF16)
            self.new_ema[k] = AVERAGE_KEEP * self.ema[k] + (1.0 - AVERAGE_KEEP) * new
        self.rms[...] = rms

    def clips(self):
        lanes = lax.broadcasted_iota(jnp.int32, (1, LANES), 1)
        clip = jnp.where(lanes < MATS, self.rms[...], self.small_clip[...])
        self.clip[...] = clip[:, 0 : self.clip.shape[1]]

    def small_step(self):
        count, full = self.small.shape[0], self.full
        g = jnp.concatenate([full[b // 2, b % 2, 0:count, :] for b in range(D // LANES)], axis=1)
        self.small_grads[...] = g
        state = SECOND_DECAY * self.small_state[...] + (1.0 - SECOND_DECAY) * (
            g * g + SQUARE_FLOOR
        )
        self.new_small_state[...] = state
        u = g * lax.rsqrt(state)
        rms = jnp.sqrt(jnp.sum(u * u, axis=1, keepdims=True) * (1.0 / D))
        new = self.small[...] - SMALL_RATE * u / jnp.maximum(1.0, rms)
        self.new_small[...] = new
        self.new_small_ema[...] = AVERAGE_KEEP * self.small_ema[...] + (1.0 - AVERAGE_KEEP) * new
        r = lax.broadcasted_iota(jnp.int32, (count, LANES), 0)
        c = lax.broadcasted_iota(jnp.int32, (count, LANES), 1)
        picked = jnp.where(c == r + MATS, rms, 0.0)
        self.small_clip[...] = jnp.sum(picked, axis=0, keepdims=True)


class Inputs(NamedTuple):
    cls: Any
    img: Any
    tokens: Any
    cot: Any
    weights: Any
    row_state: Any
    col_state: Any
    ema: Any
    small: Any
    small_state: Any
    small_ema: Any


class Outputs(NamedTuple):
    out: Any
    grad_in: Any
    wg: Any
    new_rows: Any
    new_cols: Any
    new_weights: Any
    copy: Any
    new_ema: Any
    small_grads: Any
    new_small_state: Any
    new_small: Any
    new_small_ema: Any
    clip: Any


def box_shapes(links, block):
    for slot in range(MATS):
        path = RS_ROUTES[slot]
        for phase, axis in enumerate(path):
            lead = [links.count(a) for a in AXES if a in path[phase + 1 :]]
            if axis == "h":
                lead = [links.far - 1, *lead]
            yield pltpu.VMEM((*lead, *block), BF16)


def shared_of(weights, parts, heads):
    links, (_, rows, _) = Links(), weights.shape
    block = (rows, LANES)
    every = pltpu.VMEM((2, 2, links.far, 2, 2, MATS, *block), BF16)
    out_rows = pltpu.VMEM((heads, HEAD_ROWS, D), BF16)
    dma = pltpu.SemaphoreType.DMA

    def f(*shape):
        return pltpu.VMEM(shape, F32)

    part = f(SMALL_ROWS, LANES)
    return dict(
        w=every,
        g=every,
        out_rows=out_rows,
        in_rows=out_rows,
        sums=f(SMALL_ROWS, D),
        parts=f(2, 2, SMALL_ROWS, LANES),
        in_c=f(2, SMALL_ROWS, LANES),
        in_x=part,
        in_y=part,
        in_h=f(links.far, SMALL_ROWS, LANES),
        in_l=part,
        full=f(2, 2, SMALL_ROWS, LANES),
        row_box=f(heads, 16, LANES),
        col_box=f(parts, 16, LANES),
        sq_box=f(parts * heads, 2, LANES),
        upd=f(MATS, *block),
        small_clip=f(1, LANES),
        rms=f(1, LANES),
        ag_send=dma((MATS, len(AXES))),
        ag_recv=dma((MATS, len(AXES))),
        rs_send=dma((MATS, len(AXES))),
        rs_recv=dma((MATS, len(AXES))),
        small_send=dma((7,)),
        small_recv=dma((7,)),
        out_send=dma((3,)),
        out_recv=dma((3,)),
        in_send=dma((3,)),
        in_recv=dma((3,)),
        opt_send=dma((3,)),
        opt_recv=dma((3,)),
        fetched=dma((len(Inputs._fields),)),
        stored=dma((len(Outputs._fields),)),
    )


class Ready:
    def __init__(self, src, dst, sem):
        self.copy = pltpu.make_async_copy(src, dst, sem)
        self.start, self.wait = self.copy.start, self.copy.wait


def then(*steps):
    def run():
        for step in steps:
            step()

    return run


def block_kernel(names, *refs):
    n_in, n_out = len(Inputs._fields), len(Outputs._fields)
    ins, outs, refs = Inputs(*refs[:n_in]), Outputs(*refs[n_in : n_in + n_out]), refs[n_in + n_out :]
    r = types.SimpleNamespace(**dict(zip(names, refs)))
    r.cls, r.img = ins.cls, ins.img
    fetch = Inputs(
        *[
            None if i < 2 else Ready(ref, getattr(r, name), r.fetched.at[i])
            for i, (name, ref) in enumerate(zip(Inputs._fields, ins))
        ]
    )
    store = Outputs(
        *[
            Ready(getattr(r, name), ref, r.stored.at[i])
            for i, (name, ref) in enumerate(zip(Outputs._fields, outs))
        ]
    )
    boxes = refs[len(names) :]
    links = Links()
    links.signal()
    for one in (fetch.weights, fetch.small, fetch.tokens, fetch.cot, *fetch[5:8], *fetch[9:]):
        one.start()
    r.out_own = r.out_rows.at[lax.axis_index(HEAD)]
    r.in_own = r.in_rows.at[lax.axis_index(HEAD)]
    own = r.cls.shape[1] * CELLS
    blk = Block(vars(r))
    gather = Gather(links, r.w, r.ag_send, r.ag_recv)
    scatter = Scatter(links, r.g, boxes, r.wg, r.rs_send, r.rs_recv)
    small = Small(
        links,
        *(r.sums, r.parts, r.in_c, r.in_x, r.in_y, r.in_h, r.in_l, r.full),
        r.small_send,
        r.small_recv,
    )
    out_rows = Rows(links, r.out_rows, r.out, own, r.out_send, r.out_recv)
    in_rows = Rows(links, r.in_rows, r.grad_in, own, r.in_send, r.in_recv)
    shares = [
        Exchange(links, axis, box, r.opt_send.at[i], r.opt_recv.at[i])
        for i, (axis, box) in enumerate(((HEAD, r.row_box), (DP, r.col_box), (ALL, r.sq_box)))
    ]
    opt = Adafactor(vars(r), *shares)

    fetch.weights.wait()
    for k in range(MATS):
        mine = links.region(r.w, SLOT_OF[k], "")
        mine[...] = r.weights[k].astype(BF16)
    links.meet()

    ops = []
    for tick in (gather.tick, scatter.tick):
        ops += [
            functools.partial(tick, slot, phase)
            for slot in range(MATS)
            for phase in range(len(AXES) + 1)
        ]
    ops += [
        then(fetch.small.wait, blk.setup),
        then(fetch.tokens.wait, blk.read_tokens),
        blk.norm_one,
        then(fetch.cot.wait, blk.read_cotangent),
    ]
    ops += [functools.partial(blk.project, k) for k in range(3)]
    ops += [blk.softmax, blk.contexts, blk.fill_window]
    ops += [functools.partial(blk.window_sum, c) for c in range(D // LANES)]
    ops += [blk.mix, blk.norm_two]
    for i in range(4):
        ops += [functools.partial(blk.hidden_block, i), functools.partial(blk.hidden_grads, i)]
    ops += [blk.finish_out, blk.back_two, blk.grad_proj, blk.back_heads, blk.back_query_key]
    ops += [functools.partial(blk.grad_of, k) for k in range(2)]
    ops += [functools.partial(blk.back_window, c) for c in range(D // LANES)]
    ops += [blk.back_value]
    ops += [functools.partial(blk.window_taps, c) for c in range(D // LANES)]
    ops += [blk.back_project, blk.back_one, blk.back_position, blk.position_taps, blk.finish_in]
    for rows, done in ((out_rows, store.out), (in_rows, store.grad_in)):
        ops += [functools.partial(rows.tick, stage) for stage in range(2)]
        ops += [then(functools.partial(rows.tick, 2), done.start)]
    ops += [functools.partial(small.tick, stage) for stage in range(8)]
    ops += [
        then(
            fetch.small_state.wait,
            fetch.small_ema.wait,
            opt.small_step,
            store.small_grads.start,
            store.new_small_state.start,
            store.new_small.start,
            store.new_small_ema.start,
        ),
        then(store.wg.start, opt.squares),
        then(
            fetch.row_state.wait,
            fetch.col_state.wait,
            opt.scale,
            store.new_rows.start,
            store.new_cols.start,
        ),
        then(
            fetch.ema.wait,
            opt.apply,
            store.new_weights.start,
            store.copy.start,
            store.new_ema.start,
        ),
        then(opt.clips, store.clip.start),
    ]
    for i in ORDER:
        ops[i]()
    for transfer in (gather, scatter, small, out_rows, in_rows, *shares):
        transfer.sent()
    for one in store:
        one.wait()


def finish_kernel(count, *refs):
    ins, outs, held = refs[:count], refs[count : 2 * count], refs[2 * count : 3 * count]
    took, gave = refs[3 * count :]
    come = [pltpu.make_async_copy(a, b, took.at[i]) for i, (a, b) in enumerate(zip(ins, held))]
    leave = [pltpu.make_async_copy(a, b, gave.at[i]) for i, (a, b) in enumerate(zip(held, outs))]
    for one in come:
        one.start()
    for one, other in zip(come, leave):
        one.wait()
        other.start()
    for one in leave:
        one.wait()


def local(
    tokens,
    cotangent,
    crop_image,
    crop_class,
    weights,
    row_state,
    col_state,
    weights_ema,
    small_params,
    small_state,
    small_ema,
):
    parts, heads = lax.axis_size(DP), lax.axis_size(HEAD)
    smem = pl.BlockSpec(memory_space=pltpu.SMEM)
    shared = shared_of(weights, parts, heads)
    own = scratch_of()

    def like(x, dtype=None):
        return jax.ShapeDtypeStruct(x.shape, dtype or x.dtype)

    clips = weights.shape[0] + small_params.shape[0]
    outs = (
        like(tokens),
        like(tokens),
        like(weights),
        like(row_state),
        like(col_state),
        like(weights),
        like(weights, BF16),
        like(weights),
        like(small_params),
        like(small_params),
        like(small_params),
        like(small_params),
        jax.ShapeDtypeStruct((1, clips), F32),
    )
    args = Inputs(
        crop_class,
        crop_image,
        tokens,
        cotangent,
        weights,
        row_state,
        col_state,
        weights_ema,
        small_params,
        small_state,
        small_ema,
    )
    staged = [pltpu.VMEM(x.shape, x.dtype) for x in (*args[2:], *outs)]
    names = (*shared, *own, *Inputs._fields[2:], *Outputs._fields)
    far = pl.BlockSpec(memory_space=pltpu.HBM)
    res = pl.pallas_call(
        functools.partial(block_kernel, names),
        out_shape=outs,
        in_specs=[smem, smem] + [far] * 9,
        out_specs=(far,) * len(outs),
        scratch_shapes=[
            *shared.values(),
            *own.values(),
            *staged,
            *box_shapes(Links(), weights.shape[1:]),
        ],
        compiler_params=pltpu.CompilerParams(
            collective_id=0, has_side_effects=True, vmem_limit_bytes=63 << 20
        ),
        name="block",
    )(*args)
    res = pl.pallas_call(
        functools.partial(finish_kernel, len(outs)),
        out_shape=outs,
        in_specs=[far] * len(outs),
        out_specs=(far,) * len(outs),
        scratch_shapes=[
            *[pltpu.VMEM(x.shape, x.dtype) for x in outs],
            pltpu.SemaphoreType.DMA((len(outs),)),
            pltpu.SemaphoreType.DMA((len(outs),)),
        ],
        compiler_params=pltpu.CompilerParams(vmem_limit_bytes=32 << 20),
        name="finish",
    )(*res)
    return (*res[:-1], res[-1].reshape(clips))


def solution(mesh):
    in_specs = (
        P(DP, None),
        P(DP, None),
        P(DP, None),
        P(DP, None),
        P(None, DP, HEAD),
        P(None, DP),
        P(None, HEAD),
        P(None, DP, HEAD),
        P(),
        P(),
        P(),
    )
    out_specs = (
        P(DP, None),
        P(DP, None),
        P(None, DP, HEAD),
        P(None, DP),
        P(None, HEAD),
        P(None, DP, HEAD),
        P(None, DP, HEAD),
        P(None, DP, HEAD),
        P(),
        P(),
        P(),
        P(),
        P(),
    )
    return jax.shard_map(local, mesh=mesh, in_specs=in_specs, out_specs=out_specs, check_vma=False)
```

```python
import functools
import math
import types
from typing import Any, NamedTuple

import jax
import jax.numpy as jnp
from jax import lax
from jax.experimental import pallas as pl
from jax.experimental.pallas import tpu as pltpu
from jax.sharding import PartitionSpec as P

DP, HEAD = "dp", "head"
ALL = (DP, HEAD)
D = 512
HEAD_DIM = 64
GRID = 7
SMALL_GRID = 3
WINDOW = 7
IMG_GROUP = 3
CELLS = GRID * GRID
SLOTS = 8
CELL_PAD = CELLS + 1
ROWS = CELL_PAD * SLOTS
LANES = 128
WIDE = 256
REACHES = (1, 2, 3, 3)
HALO = WINDOW // 2

NORM_EPS = 1e-06
SQUARE_FLOOR = 1e-30
SECOND_DECAY = 0.999
STEP_RATE = 0.02
SMALL_RATE = 0.05
AVERAGE_KEEP = 0.9
NEG_LARGE = -1e30
ROOT_HALF = 0.7071067811865476
INV_ROOT_TAU = 0.3989422804014327
INV_SCALE = 1.0 / math.sqrt(HEAD_DIM)

F32 = jnp.float32
BF16 = jnp.bfloat16
NN = (((1,), (0,)), ((), ()))
NT = (((1,), (1,)), ((), ()))
TN = (((0,), (0,)), ((), ()))


def dot(a, b, dims=NN):
    return lax.dot_general(a, b, dims, preferred_element_type=F32)


def lane_block(b):
    return slice(b * WIDE, (b + 1) * WIDE)


def wide(col):
    return jnp.concatenate([col] * (D // LANES), axis=1)


def rows_loop(count, size, body, init=None, unroll=1):
    def step(j, carry):
        return body(pl.multiple_of(j * size, size), carry)

    return lax.fori_loop(0, count // size, step, init, unroll=unroll)


def conv(src, halo, tap, reach, lanes, put):
    def line(y, _):
        sums = [jnp.zeros((SLOTS, LANES), F32) for _ in range(GRID)]
        for a in range(-reach, reach + 1):
            base = (y + (a + halo)) * GRID
            cells = [src[base + x, :, lanes] for x in range(GRID)]
            for b in range(-reach, reach + 1):
                t = tap(a, b)
                for x in range(GRID):
                    if 0 <= x + b < GRID:
                        sums[x] = sums[x] + t * cells[x + b]
        for x in range(GRID):
            put(y * GRID + x, sums[x])
        return 0

    lax.fori_loop(0, GRID, line, 0)


def tap_sums(up, src, halo, reach, lanes, put):
    for a in range(-reach, reach + 1):

        def line(y, sums):
            sums = list(sums)
            ups = [up(y * GRID + x) for x in range(GRID)]
            base = (y + (a + halo)) * GRID
            cells = [src[base + x, :, lanes] for x in range(GRID)]
            for i, b in enumerate(range(-reach, reach + 1)):
                for x in range(GRID):
                    if 0 <= x + b < GRID:
                        sums[i] = sums[i] + ups[x] * cells[x + b]
            return tuple(sums)

        start = tuple(jnp.zeros((SLOTS, LANES), F32) for _ in range(2 * reach + 1))
        sums = lax.fori_loop(0, GRID, line, start)
        for i, b in enumerate(range(-reach, reach + 1)):
            put(a, b, jnp.sum(sums[i], axis=0, keepdims=True))


def fold(x):
    return jnp.sum(x.reshape(x.shape[0] // SLOTS, SLOTS, x.shape[1]), axis=0)


def erf_parts(h):
    e = lax.erf(h * ROOT_HALF)
    half = 0.5 * (1.0 + e)
    return h * half, half + h * jnp.exp(-0.5 * h * h) * INV_ROOT_TAU


def norm_rows(v, gain, shift):
    centre = jnp.sum(v, axis=1, keepdims=True) * (1.0 / D)
    offset = v - centre
    spread = jnp.sum(offset * offset, axis=1, keepdims=True) * (1.0 / D)
    inverse = lax.rsqrt(spread + NORM_EPS)
    unit = offset * inverse
    return unit * gain + shift, unit, inverse


def norm_back(up, unit, inverse, gain):
    z = up * gain
    mean_z = jnp.sum(z, axis=1, keepdims=True) * (1.0 / D)
    mean_zu = jnp.sum(z * unit, axis=1, keepdims=True) * (1.0 / D)
    return inverse * (z - mean_z - unit * mean_zu)


class Block:
    def __init__(self, refs):
        self.__dict__.update(refs)

    def matrix(self, k, lo, hi):
        parts = []
        for h in range(lo, hi):
            part = self.w[h // 2, h % 2, :, :, :, k]
            if part.shape[-2] % 16:
                part = part.astype(F32).reshape(D, LANES).astype(BF16)
            else:
                part = part.reshape(D, LANES)
            parts.append(part)
        return jnp.concatenate(parts, axis=1)

    def times(self, lhs, k, b):
        return dot(lhs, self.matrix(k, 2 * b, 2 * b + 2))

    def times_t(self, lhs, k, b):
        return dot(lhs, self.matrix(k, 0, 4)[lane_block(b), :], NT)

    def put_grad(self, k, lhs_t, rhs):
        for b in range(2):
            g = dot(lhs_t, rhs[:, lane_block(b)])
            for i in range(2):
                piece = g[:, i * LANES : (i + 1) * LANES]
                place = self.g.shape[2:5]
                piece = piece.reshape(*place, self.g.shape[-2], LANES)
                self.g[b, i, :, :, :, k] = piece.astype(BF16)

    def row(self, j):
        return self.small[j : j + 1, :]

    def setup(self):
        head = lax.axis_index(HEAD)
        slots = self.cls.shape[1]
        self.sums[...] = jnp.zeros(self.sums.shape, F32)
        sub = lax.broadcasted_iota(jnp.int32, (SLOTS, LANES), 0)
        valid = jnp.where(sub < slots, 1.0, 0.0)
        full = jnp.zeros((SLOTS, LANES), F32)
        images = [jnp.zeros((SLOTS, LANES), F32) for _ in range(IMG_GROUP)]
        for s in range(slots):
            full = jnp.where(sub == s, jnp.where(self.cls[head, s] == 0, 1.0, 0.0), full)
            for i in range(IMG_GROUP):
                images[i] = jnp.where(
                    sub == s, jnp.where(self.img[head, s] == i, 1.0, 0.0), images[i]
                )
        for cell in range(CELLS):
            small = cell // GRID < SMALL_GRID and cell % GRID < SMALL_GRID
            self.live[cell * SLOTS : (cell + 1) * SLOTS, :] = valid if small else full
        self.live[CELLS * SLOTS :, :] = jnp.zeros((SLOTS, LANES), F32)
        for i in range(IMG_GROUP):
            self.im8[i] = images[i]
            self.im16[i] = jnp.concatenate([images[i], images[i]], axis=0).astype(BF16)
        self.pos_src[0:GRID] = jnp.zeros((GRID, SLOTS, D), F32)
        self.pos_src[GRID + CELLS :] = jnp.zeros((GRID, SLOTS, D), F32)
        for pad in (self.rel_src, self.dq_src):
            pad[0 : HALO * GRID] = jnp.zeros((HALO * GRID, SLOTS, D), F32)
            pad[HALO * GRID + CELLS :] = jnp.zeros((HALO * GRID, SLOTS, D), F32)
        tap = lax.broadcasted_iota(jnp.int32, (WINDOW * WINDOW, 1), 0)
        row_off = jnp.abs(tap // WINDOW - HALO)
        col_off = jnp.abs(tap % WINDOW - HALO)
        off = jnp.maximum(row_off, col_off)
        heads = lax.broadcasted_iota(jnp.int32, (1, D), 1) // HEAD_DIM
        reach = jnp.where(heads < 2, 1, jnp.where(heads < 5, 2, 3))
        mask = jnp.where(off <= reach, 1.0, 0.0)
        self.window[...] = mask
        self.rel_taps[...] = self.small[22 : 22 + WINDOW * WINDOW, :] * mask

    def place(self, rows_ref, first, r0, size):
        count = rows_ref.shape[0]
        r = r0 + lax.broadcasted_iota(jnp.int32, (size, 1), 0)
        cell, slot = r >> 3, r & 7
        want = first + slot * CELLS + cell
        want = jnp.where((slot < self.cls.shape[1]) & (cell < CELLS), want, -1)
        col = lax.broadcasted_iota(jnp.int32, (size, count), 1)
        pick = jnp.where(col == want, 1.0, 0.0).astype(BF16)
        return dot(pick, rows_ref[...])

    def unplace(self, src_ref, out_ref):
        count = out_ref.shape[0]
        own = self.cls.shape[1] * CELLS
        lead = lax.rem(lax.axis_index(HEAD) * own, 16)
        r = lax.broadcasted_iota(jnp.int32, (1, ROWS), 1)
        cell, slot = r >> 3, r & 7
        target = lead + slot * CELLS + cell
        target = jnp.where((slot < self.cls.shape[1]) & (cell < CELLS), target, -1)
        t = lax.broadcasted_iota(jnp.int32, (count, ROWS), 0)
        pick = jnp.where(t == target, 1.0, 0.0).astype(BF16)
        out_ref[...] = dot(pick, src_ref[...]).astype(BF16)

    def read_tokens(self):
        first = lax.axis_index(HEAD) * (self.cls.shape[1] * CELLS)
        size = 80

        def body(r0, _):
            live = wide(self.live[pl.ds(r0, size), :])
            x = self.place(self.tokens, first, r0, size)
            self.first[pl.ds(r0, size), :] = x
            c0 = r0 // SLOTS
            self.pos_src[pl.ds(GRID + c0, size // SLOTS)] = (x * live).reshape(-1, SLOTS, D)
            return 0

        rows_loop(ROWS, size, body, 0)

    def read_cotangent(self):
        first = lax.axis_index(HEAD) * (self.cls.shape[1] * CELLS)
        size = 80

        def body(r0, _):
            live = wide(self.live[pl.ds(r0, size), :])
            c = self.place(self.cot, first, r0, size)
            self.go[pl.ds(r0, size), :] = (c * live).astype(BF16)
            return 0

        rows_loop(ROWS, size, body, 0)
        self.go_t[...] = self.go[...].T
        self.back[...] = jnp.zeros((ROWS, D), F32)

    def norm_one(self):
        for c in range(D // LANES):
            lanes = slice(c * LANES, (c + 1) * LANES)

            def put(cell, value):
                rows = pl.ds(pl.multiple_of(cell * SLOTS, SLOTS), SLOTS)
                self.first[rows, lanes] = self.first[rows, lanes] + value + self.small[8:9, lanes]

            def tap(a, b):
                t = 13 + (a + 1) * 3 + b + 1
                return self.small[t : t + 1, lanes]

            conv(self.pos_src, 1, tap, 1, lanes, put)

        def body(r0, _):
            rows = pl.ds(r0, 16)
            n, u, inv = norm_rows(self.first[rows, :], self.row(0), self.row(1))
            self.n1[rows, :] = n.astype(BF16)
            self.u1[rows, :] = u
            self.inv1[rows, :] = jnp.broadcast_to(inv, (16, LANES))
            return 0

        rows_loop(ROWS, 16, body, 0, unroll=5)
        self.n1_t[...] = self.n1[...].T

    def project(self, k):
        low = (self.q, self.k, self.v)[k]
        for b in range(2):
            cols = lane_block(b)
            p = self.times(self.n1[...], k, b)
            if k != 1:
                p = p + self.small[2 + k // 2 : 3 + k // 2, cols]
            low[:, cols] = p.astype(BF16)

    def image_sum(self, x):
        total = jnp.zeros((SLOTS, D), F32)
        for i in range(IMG_GROUP):
            im = wide(self.im8[i])
            total = total + im * jnp.sum(im * x, axis=0, keepdims=True)
        return total

    def softmax(self):
        def top(r0, best):
            live = wide(self.live[pl.ds(r0, 16), :])
            keys = jnp.where(live > 0, self.k[pl.ds(r0, 16), :].astype(F32), NEG_LARGE)
            return jnp.maximum(best, jnp.max(keys.reshape(2, SLOTS, D), axis=0))

        best = rows_loop(ROWS, 16, top, jnp.full((SLOTS, D), NEG_LARGE, F32), unroll=5)
        shift = jnp.zeros((SLOTS, D), F32)
        for i in range(IMG_GROUP):
            im = wide(self.im8[i])
            most = jnp.max(jnp.where(im > 0, best, NEG_LARGE), axis=0, keepdims=True)
            shift = jnp.where(im > 0, most, shift)
        shift2 = jnp.concatenate([shift, shift], axis=0)

        def raise_(r0, total):
            rows = pl.ds(r0, 16)
            live = wide(self.live[rows, :])
            keys = self.k[rows, :].astype(F32)
            e = jnp.where(live > 0, jnp.exp(jnp.where(live > 0, keys - shift2, 0.0)), 0.0)
            self.soft[rows, :] = e
            return total + fold(e)

        total = self.image_sum(
            rows_loop(ROWS, 16, raise_, jnp.zeros((SLOTS, D), F32), unroll=5)
        )
        scale = 1.0 / jnp.where(total > 0, total, 1.0)
        scale2 = jnp.concatenate([scale, scale], axis=0)

        def divide(r0, _):
            rows = pl.ds(r0, 16)
            soft = self.soft[rows, :] * scale2
            self.soft[rows, :] = soft
            self.soft_low[rows, :] = soft.astype(BF16)
            return 0

        rows_loop(ROWS, 16, divide, 0, unroll=5)

    def by_image(self, x):
        tiles = x.reshape(ROWS // 16, 16, WIDE)
        parts = []
        for i in range(IMG_GROUP):
            im = jnp.concatenate([self.im16[i]] * (WIDE // LANES), axis=1)
            parts.append((tiles * im[None]).reshape(ROWS, WIDE))
        return jnp.concatenate(parts, axis=1)

    def head_blocks(self, x):
        r = lax.broadcasted_iota(jnp.int32, x.shape, 0) // HEAD_DIM
        c = (lax.broadcasted_iota(jnp.int32, x.shape, 1) % WIDE) // HEAD_DIM
        return jnp.where(r == c, x, 0.0).astype(BF16)

    def stacked(self, x):
        return jnp.concatenate([x[:, lane_block(i)] for i in range(IMG_GROUP)], axis=0)

    def contexts(self):
        for b in range(2):
            cols = lane_block(b)
            ctx = dot(self.soft_low[:, cols], self.by_image(self.v[:, cols]), TN)
            ctx = self.head_blocks(ctx)
            self.ctx[b] = ctx
            self.factor[:, cols] = dot(self.by_image(self.q[:, cols]), self.stacked(ctx))

    def fill_window(self):
        def fill(r0, _):
            rows = pl.ds(r0, 16)
            v = self.v[rows, :].astype(F32) * wide(self.live[rows, :])
            c0 = r0 // SLOTS
            self.rel_src[pl.ds(HALO * GRID + c0, 2)] = v.reshape(2, SLOTS, D)
            return 0

        rows_loop(ROWS, 16, fill, 0, unroll=5)
        self.rel[CELLS * SLOTS :, :] = jnp.zeros((SLOTS, D), F32)

    def window_sum(self, c):
        lanes = slice(c * LANES, (c + 1) * LANES)

        def put(cell, value):
            rows = pl.ds(pl.multiple_of(cell * SLOTS, SLOTS), SLOTS)
            self.rel[rows, lanes] = value

        def tap(a, b):
            t = (a + HALO) * WINDOW + b + HALO
            return self.rel_taps[t : t + 1, lanes]

        conv(self.rel_src, HALO, tap, REACHES[c], lanes, put)

    def mix(self):
        def mix(r0, _):
            rows = pl.ds(r0, 16)
            m = self.factor[rows, :] * INV_SCALE + self.q[rows, :].astype(F32) * self.rel[rows, :]
            self.mixed[rows, :] = (m * wide(self.live[rows, :])).astype(BF16)
            return 0

        rows_loop(ROWS, 16, mix, 0, unroll=5)

    def norm_two(self):
        for b in range(2):
            cols = lane_block(b)
            p = self.times_t(self.mixed[...], 3, b)
            self.second[:, cols] = self.first[:, cols] + p + self.small[4:5, cols]

        def body(r0, _):
            rows = pl.ds(r0, 16)
            n, u, inv = norm_rows(self.second[rows, :], self.row(5), self.row(6))
            self.n2[rows, :] = n.astype(BF16)
            self.u2[rows, :] = u
            self.inv2[rows, :] = jnp.broadcast_to(inv, (16, LANES))
            return 0

        rows_loop(ROWS, 16, body, 0, unroll=5)
        self.n2_t[...] = self.n2[...].T

    def hidden_block(self, r):
        up, down = 4 + 2 * r, 5 + 2 * r
        for b in range(2):
            cols = lane_block(b)
            h = self.times(self.n2[...], up, b) + self.small[pl.ds(9 + r, 1), cols]
            self.hidden[:, cols] = h
            self.factor[:, cols] = self.times(self.go[...], down, b)

        def body(r0, total):
            rows = pl.ds(r0, 16)
            act, slope = erf_parts(self.hidden[rows, :])
            g = self.factor[rows, :] * slope
            self.active[rows, :] = act.astype(BF16)
            self.low[rows, :] = g.astype(BF16)
            return total + fold(g)

        total = rows_loop(ROWS, 16, body, jnp.zeros((SLOTS, D), F32), unroll=5)
        self.sums[pl.ds(9 + r, 1), :] = jnp.sum(total, axis=0, keepdims=True)

    def hidden_grads(self, r):
        up, down = 4 + 2 * r, 5 + 2 * r
        self.put_grad(down, self.go_t[...], self.active)
        self.put_grad(up, self.n2_t[...], self.low)
        for b in range(2):
            cols = lane_block(b)
            self.second[:, cols] += self.times_t(self.active[...], down, b)
            self.back[:, cols] += self.times_t(self.low[...], up, b)

    def finish_out(self):
        def body(r0, _):
            rows = pl.ds(r0, 16)
            self.out_low[rows, :] = (self.second[rows, :] + self.row(7)).astype(BF16)
            return 0

        rows_loop(ROWS, 16, body, 0, unroll=5)
        self.unplace(self.out_low, self.out_own)

    def back_two(self):
        zero = jnp.zeros((SLOTS, D), F32)

        def body(r0, sums):
            rows = pl.ds(r0, 16)
            back, u = self.back[rows, :], self.u2[rows, :]
            go = self.go[rows, :].astype(F32)
            gs = go + norm_back(back, u, wide(self.inv2[rows, :]), self.row(5))
            self.gs[rows, :] = gs
            self.gs_low[rows, :] = gs.astype(BF16)
            new = (gs, back * u, back, go)
            return tuple(s + fold(n) for s, n in zip(sums, new, strict=True))

        sums = rows_loop(ROWS, 16, body, (zero,) * 4, unroll=5)
        for j, s in zip((4, 5, 6, 7), sums, strict=True):
            self.sums[j : j + 1, :] = jnp.sum(s, axis=0, keepdims=True)

    def grad_proj(self):
        self.put_grad(3, self.gs_low[...].T, self.mixed)

    def back_heads(self):
        for b in range(2):
            cols = lane_block(b)
            self.d[:, cols] = self.times(self.gs_low[...], 3, b)

        def fill(r0, _):
            rows = pl.ds(r0, 16)
            d = self.d[rows, :] * wide(self.live[rows, :])
            self.d[rows, :] = d
            self.f[rows, :] = (d * INV_SCALE).astype(BF16)
            c0 = r0 // SLOTS
            dq = d * self.q[rows, :].astype(F32)
            self.dq_src[pl.ds(HALO * GRID + c0, 2)] = dq.reshape(2, SLOTS, D)
            return 0

        rows_loop(ROWS, 16, fill, 0, unroll=5)
        for b in range(2):
            cols = lane_block(b)
            f3 = self.by_image(self.f[:, cols])
            g = self.head_blocks(dot(self.q[:, cols], f3, TN))
            self.gq[:, cols] = dot(f3, self.ctx[b], NT)
            self.gk[:, cols] = dot(self.by_image(self.v[:, cols]), g, NT)
            self.gv[:, cols] = dot(self.by_image(self.soft_low[:, cols]), self.stacked(g))

    def back_window(self, c):
        lanes = slice(c * LANES, (c + 1) * LANES)

        def put(cell, value):
            rows = pl.ds(pl.multiple_of(cell * SLOTS, SLOTS), SLOTS)
            self.gv[rows, lanes] = self.gv[rows, lanes] + value * self.live[rows, :]

        def tap(a, b):
            t = (HALO - a) * WINDOW + HALO - b
            return self.rel_taps[t : t + 1, lanes]

        conv(self.dq_src, HALO, tap, REACHES[c], lanes, put)

    def window_taps(self, c):
        lanes = slice(c * LANES, (c + 1) * LANES)

        def up(cell):
            return self.dq_src[HALO * GRID + cell, :, lanes]

        def put_tap(a, b, value):
            t = (a + HALO) * WINDOW + b + HALO
            keep = self.window[t : t + 1, lanes]
            self.sums[22 + t : 23 + t, lanes] = value * keep

        tap_sums(up, self.rel_src, HALO, REACHES[c], lanes, put_tap)

    def back_query_key(self):
        zero = jnp.zeros((SLOTS, D), F32)

        def inner(r0, total):
            rows = pl.ds(r0, 16)
            return total + fold(self.soft[rows, :] * self.gk[rows, :])

        shared = self.image_sum(rows_loop(ROWS, 16, inner, zero, unroll=5))
        shared2 = jnp.concatenate([shared, shared], axis=0)

        def low(r0, total):
            rows = pl.ds(r0, 16)
            gq = self.gq[rows, :] + self.d[rows, :] * self.rel[rows, :]
            gk = self.soft[rows, :] * (self.gk[rows, :] - shared2)
            self.gl[0, rows, :] = gq.astype(BF16)
            self.gl[1, rows, :] = gk.astype(BF16)
            return total + fold(gq)

        total = rows_loop(ROWS, 16, low, zero, unroll=5)
        self.sums[2:3, :] = jnp.sum(total, axis=0, keepdims=True)

    def back_value(self):
        def low(r0, total):
            rows = pl.ds(r0, 16)
            gv = self.gv[rows, :]
            self.gl[2, rows, :] = gv.astype(BF16)
            return total + fold(gv)

        total = rows_loop(ROWS, 16, low, jnp.zeros((SLOTS, D), F32), unroll=5)
        self.sums[3:4, :] = jnp.sum(total, axis=0, keepdims=True)
        self.grad_of(2)

    def grad_of(self, k):
        self.put_grad(k, self.n1_t[...], self.gl.at[k])

    def back_project(self):
        for b in range(2):
            cols = lane_block(b)
            back = self.times_t(self.gl[0], 0, b)
            back = back + self.times_t(self.gl[1], 1, b)
            self.back[:, cols] = back + self.times_t(self.gl[2], 2, b)

    def back_one(self):
        zero = jnp.zeros((SLOTS, D), F32)
        self.pos_up[0:GRID] = jnp.zeros((GRID, SLOTS, D), F32)
        self.pos_up[GRID + CELLS :] = jnp.zeros((GRID, SLOTS, D), F32)

        def body(r0, sums):
            rows = pl.ds(r0, 16)
            back, u = self.back[rows, :], self.u1[rows, :]
            gf = self.gs[rows, :] + norm_back(back, u, wide(self.inv1[rows, :]), self.row(0))
            c0 = r0 // SLOTS
            self.pos_up[pl.ds(GRID + c0, 2)] = gf.reshape(2, SLOTS, D)
            new = (back * u, back, gf)
            return tuple(s + fold(n) for s, n in zip(sums, new, strict=True))

        sums = rows_loop(ROWS, 16, body, (zero,) * 3, unroll=5)
        for j, s in zip((0, 1, 8), sums, strict=True):
            self.sums[j : j + 1, :] = jnp.sum(s, axis=0, keepdims=True)

    def back_position(self):
        for c in range(D // LANES):
            lanes = slice(c * LANES, (c + 1) * LANES)

            def put(cell, value):
                rows = pl.ds(pl.multiple_of(cell * SLOTS, SLOTS), SLOTS)
                gf = self.pos_up[GRID + cell, :, lanes]
                self.first[rows, lanes] = gf + value * self.live[rows, :]

            def tap(a, b):
                t = 13 + (1 - a) * 3 + 1 - b
                return self.small[t : t + 1, lanes]

            conv(self.pos_up, 1, tap, 1, lanes, put)

    def position_taps(self):
        for c in range(D // LANES):
            lanes = slice(c * LANES, (c + 1) * LANES)

            def up(cell):
                return self.pos_up[GRID + cell, :, lanes]

            def put_tap(a, b, value):
                t = 13 + (a + 1) * 3 + b + 1
                self.sums[t : t + 1, lanes] = value

            tap_sums(up, self.pos_src, 1, 1, lanes, put_tap)

    def finish_in(self):
        def down(r0, _):
            rows = pl.ds(r0, 16)
            self.in_low[rows, :] = self.first[rows, :].astype(BF16)
            return 0

        rows_loop(ROWS, 16, down, 0, unroll=5)
        self.unplace(self.in_low, self.in_own)


SLOT_OF = (0, 1, 2, 3, 4, 6, 8, 10, 5, 7, 9, 11)
MATS = len(SLOT_OF)
AXES = "xchly"
HEAD_ROWS = 320
SMALL_ROWS = 72
AG_ROUTES = ("lhyxc", "hlxyc", "lhyxc", "hxlyc", "hlxyc", "xylhc", "hylxc", "hylxc", "lxhyc", "xyhlc", "lhxyc", "xylhc")
RS_ROUTES = ("cxylh", "clyhx", "cxylh", "cyhlx", "cxyhl", "clhyx", "cylxh", "cxylh", "cyxhl", "chlyx", "clyxh", "cylhx")
ORDER = (
    6, 12, 0, 66, 18, 30, 42, 48, 36, 60, 54, 24, 144, 147, 145, 13, 31, 7, 55, 1,
    146, 19, 25, 49, 37, 43, 61, 67, 32, 8, 56, 14, 2, 20, 26, 38, 50, 44, 62, 68,
    9, 33, 15, 27, 57, 3, 21, 63, 39, 10, 16, 51, 45, 11, 149, 151, 69, 17, 4, 150,
    153, 154, 156, 155, 22, 28, 157, 5, 34, 148, 152, 40, 158, 23, 159, 46, 29, 64, 58, 35,
    160, 161, 52, 96, 102, 41, 47, 162, 70, 163, 108, 59, 65, 114, 53, 164, 97, 165, 126, 120,
    103, 71, 166, 109, 115, 167, 127, 132, 138, 168, 189, 121, 169, 133, 98, 170, 90, 171, 139, 172,
    173, 72, 110, 181, 174, 78, 91, 177, 180, 183, 128, 134, 104, 73, 175, 79, 99, 176, 111, 116,
    122, 178, 179, 84, 140, 184, 185, 129, 186, 85, 92, 190, 187, 105, 182, 135, 195, 112, 74, 188,
    80, 191, 130, 117, 196, 123, 192, 100, 106, 141, 86, 75, 136, 93, 131, 118, 113, 81, 197, 101,
    124, 87, 76, 142, 94, 137, 198, 119, 125, 88, 82, 77, 193, 107, 199, 143, 95, 83, 89, 204,
    194, 200, 205, 201, 202, 203, 206, 207,
)


def scratch_of():
    f, h, low = (ROWS, D), (ROWS, LANES), pltpu.VMEM((ROWS, D), BF16)
    halo3 = pltpu.VMEM(((GRID + 2 * HALO) * GRID, SLOTS, D), F32)
    halo1 = pltpu.VMEM(((GRID + 2) * GRID, SLOTS, D), F32)
    high, column, turned = pltpu.VMEM(f, F32), pltpu.VMEM(h, F32), pltpu.VMEM((D, ROWS), BF16)
    taps = pltpu.VMEM((WINDOW * WINDOW, D), F32)
    return dict(
        live=column,
        im8=pltpu.VMEM((IMG_GROUP, SLOTS, LANES), F32),
        im16=pltpu.VMEM((IMG_GROUP, 16, LANES), BF16),
        window=taps,
        rel_taps=taps,
        pos_src=halo1,
        pos_up=halo1,
        rel_src=halo3,
        dq_src=halo3,
        first=high,
        u1=high,
        inv1=column,
        second=high,
        u2=high,
        inv2=column,
        n1=low,
        n1_t=turned,
        n2=low,
        n2_t=turned,
        go=low,
        go_t=turned,
        q=low,
        k=low,
        v=low,
        soft=high,
        soft_low=low,
        ctx=pltpu.VMEM((2, WIDE, IMG_GROUP * WIDE), BF16),
        factor=high,
        rel=high,
        mixed=low,
        hidden=high,
        active=low,
        low=low,
        out_low=low,
        back=high,
        gs=high,
        gs_low=low,
        d=high,
        f=low,
        gq=high,
        gk=high,
        gv=high,
        gl=pltpu.VMEM((3, ROWS, D), BF16),
        in_low=low,
    )


class Links:
    def __init__(self):
        dp, head = lax.axis_index(DP), lax.axis_index(HEAD)
        self.far = lax.axis_size(DP) // 4
        self.at = dict(x=head // 2, c=head % 2, h=dp // 4, l=dp // 2 % 2, y=dp % 2)

    def count(self, axis):
        return self.far if axis == "h" else 2

    def peer(self, axis, step):
        return lax.rem(self.at[axis] + step, self.count(axis))

    def device(self, axis, step):
        at = {**self.at, axis: self.peer(axis, step)}
        return (at["h"] * 4 + at["l"] * 2 + at["y"], at["x"] * 2 + at["c"])

    def steps(self, axis, do):
        self.repeat(self.count(axis), do)

    def repeat(self, size, do):
        if size <= 32:
            for step in range(1, size):
                do(step)
        else:

            def body(step, _):
                do(step)
                return 0

            lax.fori_loop(1, size, body, 0)

    def others(self, name, do):
        dp, head, heads = lax.axis_index(DP), lax.axis_index(HEAD), lax.axis_size(HEAD)

        def one(step):
            if name == ALL:
                i = lax.rem(dp * heads + head + step, lax.axis_size(ALL))
                do((i // heads, lax.rem(i, heads)))
            elif name == DP:
                do((lax.rem(dp + step, lax.axis_size(DP)), head))
            else:
                do((dp, lax.rem(head + step, heads)))

        self.repeat(lax.axis_size(name), one)

    def signal(self):
        def one(device):
            pl.semaphore_signal(
                pltpu.get_barrier_semaphore(),
                inc=1,
                device_id=device,
                device_id_type=pl.DeviceIdType.MESH,
            )

        self.others(ALL, one)

    def meet(self):
        pl.semaphore_wait(pltpu.get_barrier_semaphore(), lax.axis_size(ALL) - 1)

    def copy(self, src, dst, send, recv, device):
        return pltpu.make_async_remote_copy(
            src_ref=src,
            dst_ref=dst,
            send_sem=send,
            recv_sem=recv,
            device_id=device,
            device_id_type=pl.DeviceIdType.MESH,
        )

    def region(self, blocks, slot, whole, **at):
        at = {**self.at, **at}
        place = [slice(None) if axis in whole else at[axis] for axis in AXES]
        return blocks.at[(*place, slot)]


class Gather:
    def __init__(self, links, w, send, recv):
        self.links, self.w, self.send, self.recv = links, w, send, recv

    def start(self, slot, phase):
        path = AG_ROUTES[slot]
        part = self.links.region(self.w, slot, path[:phase])
        sems = self.send.at[slot, phase], self.recv.at[slot, phase]

        def go(step):
            self.links.copy(part, part, *sems, self.links.device(path[phase], step)).start()

        self.links.steps(path[phase], go)

    def descriptor(self, slot, phase):
        path = AG_ROUTES[slot]
        at = {"h": pl.ds(0, self.links.far - 1)} if path[phase] == "h" else {}
        part = self.links.region(self.w, slot, path[:phase], **at)
        sems = self.send.at[slot, phase], self.recv.at[slot, phase]
        return self.links.copy(part, part, *sems, self.links.device(path[phase], 1))

    def tick(self, slot, phase):
        if phase:
            self.descriptor(slot, phase - 1).wait_recv()
        if phase < len(AXES):
            self.start(slot, phase)

    def sent(self):
        for slot in range(MATS):
            for phase in range(len(AXES)):
                self.descriptor(slot, phase).wait_send()


class Scatter:
    def __init__(self, links, g, boxes, total, send, recv):
        self.links, self.g, self.boxes, self.total = links, g, boxes, total
        self.send, self.recv = send, recv

    def descriptor(self, slot, phase):
        box = self.boxes[slot * len(AXES) + phase]
        sems = self.send.at[slot, phase], self.recv.at[slot, phase]
        return self.links.copy(box, box, *sems, self.links.device(RS_ROUTES[slot][phase], 1))

    def take(self, slot, phase):
        path = RS_ROUTES[slot]
        self.descriptor(slot, phase).wait_recv()
        own = self.links.region(self.g, slot, path[phase + 1 :])
        box = self.boxes[slot * len(AXES) + phase]
        if path[phase] == "h" and box.shape[0] == 1:
            box = box.at[0]
        elif path[phase] == "h":
            value = own[...].astype(F32)
            return own, value + jnp.sum(box[...].astype(F32), axis=0)
        return own, own[...] + box[...] if phase + 1 < len(AXES) else (
            own[...].astype(F32) + box[...].astype(F32)
        )

    def start(self, slot, phase):
        path = RS_ROUTES[slot]
        axis, rest = path[phase], path[phase + 1 :]
        box = self.boxes[slot * len(AXES) + phase]
        sems = self.send.at[slot, phase], self.recv.at[slot, phase]

        def go(step):
            at = {axis: self.links.peer(axis, step)}
            part = self.links.region(self.g, slot, rest, **at)
            into = box.at[step - 1] if axis == "h" else box
            self.links.copy(part, into, *sems, self.links.device(axis, step)).start()

        self.links.steps(axis, go)

    def tick(self, slot, phase):
        if phase:
            own, value = self.take(slot, phase - 1)
            if phase == len(AXES):
                self.total[SLOT_OF.index(slot)] = value
                return
            own[...] = value.astype(BF16)
        self.start(slot, phase)

    def sent(self):
        for slot in range(MATS):
            for phase in range(len(AXES)):
                self.descriptor(slot, phase).wait_send()


class Small:
    def __init__(self, links, sums, parts, in_c, in_x, in_y, in_h, in_l, full, send, recv):
        self.links, self.sums, self.parts, self.full = links, sums, parts, full
        self.in_c, self.in_x, self.in_y, self.in_h, self.in_l = in_c, in_x, in_y, in_h, in_l
        self.send, self.recv = send, recv

    def go(self, stage, src, dst, axis):
        sems = (self.send.at[stage], self.recv.at[stage])
        self.links.steps(
            axis, lambda step: self.links.copy(src, dst, *sems, self.links.device(axis, step)).start()
        )

    def wait(self, stage):
        x, c = self.links.at["x"], self.links.at["c"]
        ref = (
            self.in_c,
            self.in_x,
            self.in_y,
            self.in_h.at[pl.ds(0, self.links.far - 1)],
            self.in_l,
            self.full.at[c, x],
            self.full.at[c],
        )[stage]
        sems = (self.send.at[stage], self.recv.at[stage])
        return self.links.copy(ref, ref, *sems, self.links.device("cxyhlxc"[stage], 1))

    def tick(self, stage):
        at = self.links.at
        x, c, h = at["x"], at["c"], at["h"]
        mine = self.parts.at[c, x]
        if stage:
            self.wait(stage - 1).wait_recv()
        if stage == 0:
            for b in range(D // LANES):
                self.parts[b // 2, b % 2] = self.sums[:, b * LANES : (b + 1) * LANES]
            self.go(0, self.parts.at[1 - c], self.in_c, "c")
        if stage == 1:
            self.parts[c] = self.parts[c] + self.in_c[...]
            self.go(1, self.parts.at[c, 1 - x], self.in_x, "x")
        if stage == 2:
            mine[...] = mine[...] + self.in_x[...]
            self.go(2, mine, self.in_y, "y")
        if stage == 3:
            self.in_h[h] = mine[...] + self.in_y[...]
            self.go(3, self.in_h.at[h], self.in_h.at[h], "h")
        if stage == 4:
            total = self.in_h[0]
            for i in range(1, self.links.far):
                total = total + self.in_h[i]
            self.sums[:, 0:LANES] = total
            self.go(4, self.sums.at[:, pl.ds(0, LANES)], self.in_l, "l")
        if stage == 5:
            self.full[c, x] = self.sums[:, 0:LANES] + self.in_l[...]
            self.go(5, self.full.at[c, x], self.full.at[c, x], "x")
        if stage == 6:
            self.go(6, self.full.at[c], self.full.at[c], "c")

    def sent(self):
        for stage in range(7):
            self.wait(stage).wait_send()


class Rows:
    def __init__(self, links, blocks, out, own, send, recv):
        self.links, self.blocks, self.out, self.own = links, blocks, out, own
        self.send, self.recv = send, recv

    def hop(self, i):
        x, c = self.links.at["x"], self.links.at["c"]
        x, axis = ((x, "x"), (x, "c"), (1 - x, "c"))[i]
        block = self.blocks.at[2 * x + c]
        return self.links.copy(
            block, block, self.send.at[i], self.recv.at[i], self.links.device(axis, 1)
        )

    def tick(self, stage):
        if stage == 0:
            self.hop(0).start()
            self.hop(1).start()
        if stage == 1:
            self.hop(0).wait_recv()
            self.hop(2).start()
        if stage == 2:
            self.hop(1).wait_recv()
            self.hop(2).wait_recv()
            self.join()

    def sent(self):
        for i in range(3):
            self.hop(i).wait_send()

    def join(self):
        heads, end, own = self.blocks.shape[0], self.out.shape[0], self.own
        for h in range(heads):
            lo, hi = h * own, (h + 1) * own
            base = lo // 16 * 16
            first = base + 16 if lo % 16 else base
            last = hi // 16 * 16 if h + 1 < heads else end
            self.out[first:last, :] = self.blocks[h, first - base : last - base, :]
            if lo % 16:
                before = (lo - own) // 16 * 16
                tail = self.blocks[h - 1, base - before : base - before + 16, :]
                self.out[base : base + 16, :] = tail + self.blocks[h, 0:16, :]


class Exchange:
    def __init__(self, links, name, buffer, send, recv):
        self.links, self.name, self.buffer, self.send, self.recv = links, name, buffer, send, recv

    def start(self, value):
        own = lax.axis_index(self.name)
        self.buffer[own] = value
        mine = self.buffer.at[own]
        self.links.others(
            self.name,
            lambda device: self.links.copy(mine, mine, self.send, self.recv, device).start(),
        )

    def descriptor(self):
        ref = self.buffer.at[pl.ds(0, self.buffer.shape[0] - 1)]
        return self.links.copy(ref, ref, self.send, self.recv, self.links.device("c", 1))

    def total(self):
        self.descriptor().wait_recv()
        return jnp.sum(self.buffer[...], axis=0)

    def sent(self):
        self.descriptor().wait_send()


def exact(a, b, dims):
    return lax.dot_general(
        a, b, dims, precision=lax.Precision.HIGHEST, preferred_element_type=F32
    )


class Adafactor:
    def __init__(self, refs, row_share, col_share, sq_share):
        self.__dict__.update(refs)
        self.row_share, self.col_share, self.sq_share = row_share, col_share, sq_share

    def eye(self, count):
        r = lax.broadcasted_iota(jnp.int32, (count, LANES), 0)
        c = lax.broadcasted_iota(jnp.int32, (count, LANES), 1)
        return jnp.where(r == c, 1.0, 0.0)

    def lane(self, k, value, rest):
        lanes = lax.broadcasted_iota(jnp.int32, rest.shape, 1)
        return jnp.where(lanes == k, value, rest)

    def squares(self):
        rows = self.wg.shape[1]
        by_row = jnp.zeros((rows, LANES), F32)
        by_col = []
        for k in range(MATS):
            g = self.wg[k]
            s = g * g + SQUARE_FLOOR
            by_row = self.lane(k, jnp.sum(s, axis=1, keepdims=True), by_row)
            by_col.append(jnp.sum(s, axis=0, keepdims=True))
        self.col_share.start(jnp.concatenate([*by_col, jnp.zeros((4, LANES), F32)], axis=0))
        turned = exact(self.eye(16), by_row, NT)
        if rows < LANES:
            turned = jnp.concatenate([turned, jnp.zeros((16, LANES - rows), F32)], axis=1)
        self.row_share.start(turned)

    def scale(self):
        rows = self.wg.shape[1]
        total = self.row_share.total()[0:MATS, 0:rows]
        new_rows = SECOND_DECAY * self.row_state[...] + (1.0 - SECOND_DECAY) * (total * (1.0 / D))
        self.new_rows[...] = new_rows
        row = exact(new_rows, self.eye(MATS), TN)
        total = self.col_share.total()[0:MATS]
        cols = SECOND_DECAY * self.col_state[...] + (1.0 - SECOND_DECAY) * (total * (1.0 / D))
        self.new_cols[...] = cols
        sums = jnp.zeros((1, LANES), F32)
        for k in range(MATS):
            u = self.wg[k] * lax.rsqrt(row[:, k : k + 1] * cols[k : k + 1, :])
            self.upd[k] = u
            s = jnp.sum(jnp.sum(u * u, axis=0, keepdims=True), axis=1, keepdims=True)
            sums = self.lane(k, s, sums)
        mass = jnp.sum(row, axis=0, keepdims=True)
        self.sq_share.start(jnp.concatenate([sums, mass], axis=0))

    def apply(self):
        total = self.sq_share.total()
        mean = total[1:2] * (1.0 / (D * lax.axis_size(HEAD)))
        rms = jnp.sqrt(total[0:1] * mean * (1.0 / (D * D)))
        rate = STEP_RATE * jnp.sqrt(mean) / jnp.maximum(1.0, rms)
        for k in range(MATS):
            new = self.weights[k] - rate[:, k : k + 1] * self.upd[k]
            self.new_weights[k] = new
            self.copy[k] = new.astype(BF16)
            self.new_ema[k] = AVERAGE_KEEP * self.ema[k] + (1.0 - AVERAGE_KEEP) * new
        self.rms[...] = rms

    def clips(self):
        lanes = lax.broadcasted_iota(jnp.int32, (1, LANES), 1)
        clip = jnp.where(lanes < MATS, self.rms[...], self.small_clip[...])
        self.clip[...] = clip[:, 0 : self.clip.shape[1]]

    def small_step(self):
        count, full = self.small.shape[0], self.full
        g = jnp.concatenate([full[b // 2, b % 2, 0:count, :] for b in range(D // LANES)], axis=1)
        self.small_grads[...] = g
        state = SECOND_DECAY * self.small_state[...] + (1.0 - SECOND_DECAY) * (
            g * g + SQUARE_FLOOR
        )
        self.new_small_state[...] = state
        u = g * lax.rsqrt(state)
        rms = jnp.sqrt(jnp.sum(u * u, axis=1, keepdims=True) * (1.0 / D))
        new = self.small[...] - SMALL_RATE * u / jnp.maximum(1.0, rms)
        self.new_small[...] = new
        self.new_small_ema[...] = AVERAGE_KEEP * self.small_ema[...] + (1.0 - AVERAGE_KEEP) * new
        r = lax.broadcasted_iota(jnp.int32, (count, LANES), 0)
        c = lax.broadcasted_iota(jnp.int32, (count, LANES), 1)
        picked = jnp.where(c == r + MATS, rms, 0.0)
        self.small_clip[...] = jnp.sum(picked, axis=0, keepdims=True)


class Inputs(NamedTuple):
    cls: Any
    img: Any
    tokens: Any
    cot: Any
    weights: Any
    row_state: Any
    col_state: Any
    ema: Any
    small: Any
    small_state: Any
    small_ema: Any


class Outputs(NamedTuple):
    out: Any
    grad_in: Any
    wg: Any
    new_rows: Any
    new_cols: Any
    new_weights: Any
    copy: Any
    new_ema: Any
    small_grads: Any
    new_small_state: Any
    new_small: Any
    new_small_ema: Any
    clip: Any


def box_shapes(links, block):
    for slot in range(MATS):
        path = RS_ROUTES[slot]
        for phase, axis in enumerate(path):
            lead = [links.count(a) for a in AXES if a in path[phase + 1 :]]
            if axis == "h":
                lead = [links.far - 1, *lead]
            yield pltpu.VMEM((*lead, *block), BF16)


def shared_of(weights, parts, heads):
    links, (_, rows, _) = Links(), weights.shape
    block = (rows, LANES)
    every = pltpu.VMEM((2, 2, links.far, 2, 2, MATS, *block), BF16)
    out_rows = pltpu.VMEM((heads, HEAD_ROWS, D), BF16)
    dma = pltpu.SemaphoreType.DMA

    def f(*shape):
        return pltpu.VMEM(shape, F32)

    part = f(SMALL_ROWS, LANES)
    return dict(
        w=every,
        g=every,
        out_rows=out_rows,
        in_rows=out_rows,
        sums=f(SMALL_ROWS, D),
        parts=f(2, 2, SMALL_ROWS, LANES),
        in_c=f(2, SMALL_ROWS, LANES),
        in_x=part,
        in_y=part,
        in_h=f(links.far, SMALL_ROWS, LANES),
        in_l=part,
        full=f(2, 2, SMALL_ROWS, LANES),
        row_box=f(heads, 16, LANES),
        col_box=f(parts, 16, LANES),
        sq_box=f(parts * heads, 2, LANES),
        upd=f(MATS, *block),
        small_clip=f(1, LANES),
        rms=f(1, LANES),
        ag_send=dma((MATS, len(AXES))),
        ag_recv=dma((MATS, len(AXES))),
        rs_send=dma((MATS, len(AXES))),
        rs_recv=dma((MATS, len(AXES))),
        small_send=dma((7,)),
        small_recv=dma((7,)),
        out_send=dma((3,)),
        out_recv=dma((3,)),
        in_send=dma((3,)),
        in_recv=dma((3,)),
        opt_send=dma((3,)),
        opt_recv=dma((3,)),
        fetched=dma((len(Inputs._fields),)),
        stored=dma((len(Outputs._fields),)),
    )


class Ready:
    def __init__(self, src, dst, sem):
        self.copy = pltpu.make_async_copy(src, dst, sem)
        self.start, self.wait = self.copy.start, self.copy.wait


def then(*steps):
    def run():
        for step in steps:
            step()

    return run


def block_kernel(names, *refs):
    n_in, n_out = len(Inputs._fields), len(Outputs._fields)
    ins, outs, refs = Inputs(*refs[:n_in]), Outputs(*refs[n_in : n_in + n_out]), refs[n_in + n_out :]
    r = types.SimpleNamespace(**dict(zip(names, refs)))
    r.cls, r.img = ins.cls, ins.img
    fetch = Inputs(
        *[
            None if i < 2 else Ready(ref, getattr(r, name), r.fetched.at[i])
            for i, (name, ref) in enumerate(zip(Inputs._fields, ins))
        ]
    )
    store = Outputs(
        *[
            Ready(getattr(r, name), ref, r.stored.at[i])
            for i, (name, ref) in enumerate(zip(Outputs._fields, outs))
        ]
    )
    boxes = refs[len(names) :]
    links = Links()
    links.signal()
    for one in (fetch.weights, fetch.small, fetch.tokens, fetch.cot, *fetch[5:8], *fetch[9:]):
        one.start()
    r.out_own = r.out_rows.at[lax.axis_index(HEAD)]
    r.in_own = r.in_rows.at[lax.axis_index(HEAD)]
    own = r.cls.shape[1] * CELLS
    blk = Block(vars(r))
    gather = Gather(links, r.w, r.ag_send, r.ag_recv)
    scatter = Scatter(links, r.g, boxes, r.wg, r.rs_send, r.rs_recv)
    small = Small(
        links,
        *(r.sums, r.parts, r.in_c, r.in_x, r.in_y, r.in_h, r.in_l, r.full),
        r.small_send,
        r.small_recv,
    )
    out_rows = Rows(links, r.out_rows, r.out, own, r.out_send, r.out_recv)
    in_rows = Rows(links, r.in_rows, r.grad_in, own, r.in_send, r.in_recv)
    shares = [
        Exchange(links, axis, box, r.opt_send.at[i], r.opt_recv.at[i])
        for i, (axis, box) in enumerate(((HEAD, r.row_box), (DP, r.col_box), (ALL, r.sq_box)))
    ]
    opt = Adafactor(vars(r), *shares)

    fetch.weights.wait()
    for k in range(MATS):
        mine = links.region(r.w, SLOT_OF[k], "")
        mine[...] = r.weights[k].astype(BF16)
    links.meet()

    ops = []
    for tick in (gather.tick, scatter.tick):
        ops += [
            functools.partial(tick, slot, phase)
            for slot in range(MATS)
            for phase in range(len(AXES) + 1)
        ]
    ops += [
        then(fetch.small.wait, blk.setup),
        then(fetch.tokens.wait, blk.read_tokens),
        blk.norm_one,
        then(fetch.cot.wait, blk.read_cotangent),
    ]
    ops += [functools.partial(blk.project, k) for k in range(3)]
    ops += [blk.softmax, blk.contexts, blk.fill_window]
    ops += [functools.partial(blk.window_sum, c) for c in range(D // LANES)]
    ops += [blk.mix, blk.norm_two]
    for i in range(4):
        ops += [functools.partial(blk.hidden_block, i), functools.partial(blk.hidden_grads, i)]
    ops += [blk.finish_out, blk.back_two, blk.grad_proj, blk.back_heads, blk.back_query_key]
    ops += [functools.partial(blk.grad_of, k) for k in range(2)]
    ops += [functools.partial(blk.back_window, c) for c in range(D // LANES)]
    ops += [blk.back_value]
    ops += [functools.partial(blk.window_taps, c) for c in range(D // LANES)]
    ops += [blk.back_project, blk.back_one, blk.back_position, blk.position_taps, blk.finish_in]
    for rows, done in ((out_rows, store.out), (in_rows, store.grad_in)):
        ops += [functools.partial(rows.tick, stage) for stage in range(2)]
        ops += [then(functools.partial(rows.tick, 2), done.start)]
    ops += [functools.partial(small.tick, stage) for stage in range(8)]
    ops += [
        then(
            fetch.small_state.wait,
            fetch.small_ema.wait,
            opt.small_step,
            store.small_grads.start,
            store.new_small_state.start,
            store.new_small.start,
            store.new_small_ema.start,
        ),
        then(store.wg.start, opt.squares),
        then(
            fetch.row_state.wait,
            fetch.col_state.wait,
            opt.scale,
            store.new_rows.start,
            store.new_cols.start,
        ),
        then(
            fetch.ema.wait,
            opt.apply,
            store.new_weights.start,
            store.copy.start,
            store.new_ema.start,
        ),
        then(opt.clips, store.clip.start),
    ]
    for i in ORDER:
        ops[i]()
    for transfer in (gather, scatter, small, out_rows, in_rows, *shares):
        transfer.sent()
    for one in store:
        one.wait()


def finish_kernel(count, *refs):
    ins, outs, held = refs[:count], refs[count : 2 * count], refs[2 * count : 3 * count]
    took, gave = refs[3 * count :]
    come = [pltpu.make_async_copy(a, b, took.at[i]) for i, (a, b) in enumerate(zip(ins, held))]
    leave = [pltpu.make_async_copy(a, b, gave.at[i]) for i, (a, b) in enumerate(zip(held, outs))]
    for one in come:
        one.start()
    for one, other in zip(come, leave):
        one.wait()
        other.start()
    for one in leave:
        one.wait()


def local(
    tokens,
    cotangent,
    crop_image,
    crop_class,
    weights,
    row_state,
    col_state,
    weights_ema,
    small_params,
    small_state,
    small_ema,
):
    parts, heads = lax.axis_size(DP), lax.axis_size(HEAD)
    smem = pl.BlockSpec(memory_space=pltpu.SMEM)
    shared = shared_of(weights, parts, heads)
    own = scratch_of()

    def like(x, dtype=None):
        return jax.ShapeDtypeStruct(x.shape, dtype or x.dtype)

    clips = weights.shape[0] + small_params.shape[0]
    outs = (
        like(tokens),
        like(tokens),
        like(weights),
        like(row_state),
        like(col_state),
        like(weights),
        like(weights, BF16),
        like(weights),
        like(small_params),
        like(small_params),
        like(small_params),
        like(small_params),
        jax.ShapeDtypeStruct((1, clips), F32),
    )
    args = Inputs(
        crop_class,
        crop_image,
        tokens,
        cotangent,
        weights,
        row_state,
        col_state,
        weights_ema,
        small_params,
        small_state,
        small_ema,
    )
    staged = [pltpu.VMEM(x.shape, x.dtype) for x in (*args[2:], *outs)]
    names = (*shared, *own, *Inputs._fields[2:], *Outputs._fields)
    far = pl.BlockSpec(memory_space=pltpu.HBM)
    res = pl.pallas_call(
        functools.partial(block_kernel, names),
        out_shape=outs,
        in_specs=[smem, smem] + [far] * 9,
        out_specs=(far,) * len(outs),
        scratch_shapes=[
            *shared.values(),
            *own.values(),
            *staged,
            *box_shapes(Links(), weights.shape[1:]),
        ],
        compiler_params=pltpu.CompilerParams(
            collective_id=0, has_side_effects=True, vmem_limit_bytes=63 << 20
        ),
        name="block",
    )(*args)
    res = pl.pallas_call(
        functools.partial(finish_kernel, len(outs)),
        out_shape=outs,
        in_specs=[far] * len(outs),
        out_specs=(far,) * len(outs),
        scratch_shapes=[
            *[pltpu.VMEM(x.shape, x.dtype) for x in outs],
            pltpu.SemaphoreType.DMA((len(outs),)),
            pltpu.SemaphoreType.DMA((len(outs),)),
        ],
        compiler_params=pltpu.CompilerParams(vmem_limit_bytes=63 << 20),
        name="finish",
    )(*res)
    return (*res[:-1], res[-1].reshape(clips))


def solution(mesh):
    in_specs = (
        P(DP, None),
        P(DP, None),
        P(DP, None),
        P(DP, None),
        P(None, DP, HEAD),
        P(None, DP),
        P(None, HEAD),
        P(None, DP, HEAD),
        P(),
        P(),
        P(),
    )
    out_specs = (
        P(DP, None),
        P(DP, None),
        P(None, DP, HEAD),
        P(None, DP),
        P(None, HEAD),
        P(None, DP, HEAD),
        P(None, DP, HEAD),
        P(None, DP, HEAD),
        P(),
        P(),
        P(),
        P(),
        P(),
    )
    return jax.shard_map(local, mesh=mesh, in_specs=in_specs, out_specs=out_specs, check_vma=False)
```

```python
import functools
import math
import types
from typing import Any, NamedTuple

import jax
import jax.numpy as jnp
from jax import lax
from jax.experimental import pallas as pl
from jax.experimental.pallas import tpu as pltpu
from jax.sharding import PartitionSpec as P

DP, HEAD = "dp", "head"
ALL = (DP, HEAD)
D = 512
HEAD_DIM = 64
GRID = 7
SMALL_GRID = 3
WINDOW = 7
IMG_GROUP = 3
CELLS = GRID * GRID
SLOTS = 8
CELL_PAD = CELLS + 1
ROWS = CELL_PAD * SLOTS
LANES = 128
WIDE = 256
REACHES = (1, 2, 3, 3)
HALO = WINDOW // 2

NORM_EPS = 1e-06
SQUARE_FLOOR = 1e-30
SECOND_DECAY = 0.999
STEP_RATE = 0.02
SMALL_RATE = 0.05
AVERAGE_KEEP = 0.9
NEG_LARGE = -1e30
ROOT_HALF = 0.7071067811865476
INV_ROOT_TAU = 0.3989422804014327
INV_SCALE = 1.0 / math.sqrt(HEAD_DIM)

F32 = jnp.float32
BF16 = jnp.bfloat16
NN = (((1,), (0,)), ((), ()))
NT = (((1,), (1,)), ((), ()))
TN = (((0,), (0,)), ((), ()))


def dot(a, b, dims=NN):
    return lax.dot_general(a, b, dims, preferred_element_type=F32)


def lane_block(b):
    return slice(b * WIDE, (b + 1) * WIDE)


def wide(col):
    return jnp.concatenate([col] * (D // LANES), axis=1)


def rows_loop(count, size, body, init=None, unroll=1):
    def step(j, carry):
        return body(pl.multiple_of(j * size, size), carry)

    return lax.fori_loop(0, count // size, step, init, unroll=unroll)


def conv(src, halo, tap, reach, lanes, put):
    def line(y, _):
        sums = [jnp.zeros((SLOTS, LANES), F32) for _ in range(GRID)]
        for a in range(-reach, reach + 1):
            base = (y + (a + halo)) * GRID
            cells = [src[base + x, :, lanes] for x in range(GRID)]
            for b in range(-reach, reach + 1):
                t = tap(a, b)
                for x in range(GRID):
                    if 0 <= x + b < GRID:
                        sums[x] = sums[x] + t * cells[x + b]
        for x in range(GRID):
            put(y * GRID + x, sums[x])
        return 0

    lax.fori_loop(0, GRID, line, 0)


def tap_sums(up, src, halo, reach, lanes, put):
    for a in range(-reach, reach + 1):

        def line(y, sums):
            sums = list(sums)
            ups = [up(y * GRID + x) for x in range(GRID)]
            base = (y + (a + halo)) * GRID
            cells = [src[base + x, :, lanes] for x in range(GRID)]
            for i, b in enumerate(range(-reach, reach + 1)):
                for x in range(GRID):
                    if 0 <= x + b < GRID:
                        sums[i] = sums[i] + ups[x] * cells[x + b]
            return tuple(sums)

        start = tuple(jnp.zeros((SLOTS, LANES), F32) for _ in range(2 * reach + 1))
        sums = lax.fori_loop(0, GRID, line, start)
        for i, b in enumerate(range(-reach, reach + 1)):
            put(a, b, jnp.sum(sums[i], axis=0, keepdims=True))


def fold(x):
    return jnp.sum(x.reshape(x.shape[0] // SLOTS, SLOTS, x.shape[1]), axis=0)


def erf_parts(h):
    e = lax.erf(h * ROOT_HALF)
    half = 0.5 * (1.0 + e)
    return h * half, half + h * jnp.exp(-0.5 * h * h) * INV_ROOT_TAU


def norm_rows(v, gain, shift):
    centre = jnp.sum(v, axis=1, keepdims=True) * (1.0 / D)
    offset = v - centre
    spread = jnp.sum(offset * offset, axis=1, keepdims=True) * (1.0 / D)
    inverse = lax.rsqrt(spread + NORM_EPS)
    unit = offset * inverse
    return unit * gain + shift, unit, inverse


def norm_back(up, unit, inverse, gain):
    z = up * gain
    mean_z = jnp.sum(z, axis=1, keepdims=True) * (1.0 / D)
    mean_zu = jnp.sum(z * unit, axis=1, keepdims=True) * (1.0 / D)
    return inverse * (z - mean_z - unit * mean_zu)


class Block:
    def __init__(self, refs):
        self.__dict__.update(refs)

    def matrix(self, k, lo, hi):
        parts = []
        for h in range(lo, hi):
            part = self.w[h // 2, h % 2, :, :, :, k]
            if part.shape[-2] % 16:
                part = part.astype(F32).reshape(D, LANES).astype(BF16)
            else:
                part = part.reshape(D, LANES)
            parts.append(part)
        return jnp.concatenate(parts, axis=1)

    def times(self, lhs, k, b):
        return dot(lhs, self.matrix(k, 2 * b, 2 * b + 2))

    def times_t(self, lhs, k, b):
        return dot(lhs, self.matrix(k, 0, 4)[lane_block(b), :], NT)

    def put_grad(self, k, lhs_t, rhs):
        for b in range(2):
            g = dot(lhs_t, rhs[:, lane_block(b)])
            for i in range(2):
                piece = g[:, i * LANES : (i + 1) * LANES]
                place = self.g.shape[2:5]
                piece = piece.reshape(*place, self.g.shape[-2], LANES)
                self.g[b, i, :, :, :, k] = piece.astype(BF16)

    def row(self, j):
        return self.small[j : j + 1, :]

    def setup(self):
        head = lax.axis_index(HEAD)
        slots = self.cls.shape[1]
        self.sums[...] = jnp.zeros(self.sums.shape, F32)
        sub = lax.broadcasted_iota(jnp.int32, (SLOTS, LANES), 0)
        valid = jnp.where(sub < slots, 1.0, 0.0)
        full = jnp.zeros((SLOTS, LANES), F32)
        images = [jnp.zeros((SLOTS, LANES), F32) for _ in range(IMG_GROUP)]
        for s in range(slots):
            full = jnp.where(sub == s, jnp.where(self.cls[head, s] == 0, 1.0, 0.0), full)
            for i in range(IMG_GROUP):
                images[i] = jnp.where(
                    sub == s, jnp.where(self.img[head, s] == i, 1.0, 0.0), images[i]
                )
        for cell in range(CELLS):
            small = cell // GRID < SMALL_GRID and cell % GRID < SMALL_GRID
            self.live[cell * SLOTS : (cell + 1) * SLOTS, :] = valid if small else full
        self.live[CELLS * SLOTS :, :] = jnp.zeros((SLOTS, LANES), F32)
        for i in range(IMG_GROUP):
            self.im8[i] = images[i]
            self.im16[i] = jnp.concatenate([images[i], images[i]], axis=0).astype(BF16)
        self.pos_src[0:GRID] = jnp.zeros((GRID, SLOTS, D), F32)
        self.pos_src[GRID + CELLS :] = jnp.zeros((GRID, SLOTS, D), F32)
        for pad in (self.rel_src, self.dq_src):
            pad[0 : HALO * GRID] = jnp.zeros((HALO * GRID, SLOTS, D), F32)
            pad[HALO * GRID + CELLS :] = jnp.zeros((HALO * GRID, SLOTS, D), F32)
        tap = lax.broadcasted_iota(jnp.int32, (WINDOW * WINDOW, 1), 0)
        row_off = jnp.abs(tap // WINDOW - HALO)
        col_off = jnp.abs(tap % WINDOW - HALO)
        off = jnp.maximum(row_off, col_off)
        heads = lax.broadcasted_iota(jnp.int32, (1, D), 1) // HEAD_DIM
        reach = jnp.where(heads < 2, 1, jnp.where(heads < 5, 2, 3))
        mask = jnp.where(off <= reach, 1.0, 0.0)
        self.window[...] = mask
        self.rel_taps[...] = self.small[22 : 22 + WINDOW * WINDOW, :] * mask

    def place(self, rows_ref, first, r0, size):
        count = rows_ref.shape[0]
        r = r0 + lax.broadcasted_iota(jnp.int32, (size, 1), 0)
        cell, slot = r >> 3, r & 7
        want = first + slot * CELLS + cell
        want = jnp.where((slot < self.cls.shape[1]) & (cell < CELLS), want, -1)
        col = lax.broadcasted_iota(jnp.int32, (size, count), 1)
        pick = jnp.where(col == want, 1.0, 0.0).astype(BF16)
        return dot(pick, rows_ref[...])

    def unplace(self, src_ref, out_ref):
        count = out_ref.shape[0]
        own = self.cls.shape[1] * CELLS
        lead = lax.rem(lax.axis_index(HEAD) * own, 16)
        r = lax.broadcasted_iota(jnp.int32, (1, ROWS), 1)
        cell, slot = r >> 3, r & 7
        target = lead + slot * CELLS + cell
        target = jnp.where((slot < self.cls.shape[1]) & (cell < CELLS), target, -1)
        t = lax.broadcasted_iota(jnp.int32, (count, ROWS), 0)
        pick = jnp.where(t == target, 1.0, 0.0).astype(BF16)
        out_ref[...] = dot(pick, src_ref[...]).astype(BF16)

    def read_tokens(self):
        first = lax.axis_index(HEAD) * (self.cls.shape[1] * CELLS)
        size = 80

        def body(r0, _):
            live = wide(self.live[pl.ds(r0, size), :])
            x = self.place(self.tokens, first, r0, size)
            self.first[pl.ds(r0, size), :] = x
            c0 = r0 // SLOTS
            self.pos_src[pl.ds(GRID + c0, size // SLOTS)] = (x * live).reshape(-1, SLOTS, D)
            return 0

        rows_loop(ROWS, size, body, 0)

    def read_cotangent(self):
        first = lax.axis_index(HEAD) * (self.cls.shape[1] * CELLS)
        size = 80

        def body(r0, _):
            live = wide(self.live[pl.ds(r0, size), :])
            c = self.place(self.cot, first, r0, size)
            self.go[pl.ds(r0, size), :] = (c * live).astype(BF16)
            return 0

        rows_loop(ROWS, size, body, 0)
        self.go_t[...] = self.go[...].T
        self.back[...] = jnp.zeros((ROWS, D), F32)

    def norm_one(self):
        for c in range(D // LANES):
            lanes = slice(c * LANES, (c + 1) * LANES)

            def put(cell, value):
                rows = pl.ds(pl.multiple_of(cell * SLOTS, SLOTS), SLOTS)
                self.first[rows, lanes] = self.first[rows, lanes] + value + self.small[8:9, lanes]

            def tap(a, b):
                t = 13 + (a + 1) * 3 + b + 1
                return self.small[t : t + 1, lanes]

            conv(self.pos_src, 1, tap, 1, lanes, put)

        def body(r0, _):
            rows = pl.ds(r0, 16)
            n, u, inv = norm_rows(self.first[rows, :], self.row(0), self.row(1))
            self.n1[rows, :] = n.astype(BF16)
            self.u1[rows, :] = u
            self.inv1[rows, :] = jnp.broadcast_to(inv, (16, LANES))
            return 0

        rows_loop(ROWS, 16, body, 0, unroll=5)
        self.n1_t[...] = self.n1[...].T

    def project(self, k):
        low = (self.q, self.k, self.v)[k]
        for b in range(2):
            cols = lane_block(b)
            p = self.times(self.n1[...], k, b)
            if k != 1:
                p = p + self.small[2 + k // 2 : 3 + k // 2, cols]
            low[:, cols] = p.astype(BF16)

    def image_sum(self, x):
        total = jnp.zeros((SLOTS, D), F32)
        for i in range(IMG_GROUP):
            im = wide(self.im8[i])
            total = total + im * jnp.sum(im * x, axis=0, keepdims=True)
        return total

    def softmax(self):
        def top(r0, best):
            live = wide(self.live[pl.ds(r0, 16), :])
            keys = jnp.where(live > 0, self.k[pl.ds(r0, 16), :].astype(F32), NEG_LARGE)
            return jnp.maximum(best, jnp.max(keys.reshape(2, SLOTS, D), axis=0))

        best = rows_loop(ROWS, 16, top, jnp.full((SLOTS, D), NEG_LARGE, F32), unroll=5)
        shift = jnp.zeros((SLOTS, D), F32)
        for i in range(IMG_GROUP):
            im = wide(self.im8[i])
            most = jnp.max(jnp.where(im > 0, best, NEG_LARGE), axis=0, keepdims=True)
            shift = jnp.where(im > 0, most, shift)
        shift2 = jnp.concatenate([shift, shift], axis=0)

        def raise_(r0, total):
            rows = pl.ds(r0, 16)
            live = wide(self.live[rows, :])
            keys = self.k[rows, :].astype(F32)
            e = jnp.where(live > 0, jnp.exp(jnp.where(live > 0, keys - shift2, 0.0)), 0.0)
            self.soft[rows, :] = e
            return total + fold(e)

        total = self.image_sum(
            rows_loop(ROWS, 16, raise_, jnp.zeros((SLOTS, D), F32), unroll=5)
        )
        scale = 1.0 / jnp.where(total > 0, total, 1.0)
        scale2 = jnp.concatenate([scale, scale], axis=0)

        def divide(r0, _):
            rows = pl.ds(r0, 16)
            soft = self.soft[rows, :] * scale2
            self.soft[rows, :] = soft
            self.soft_low[rows, :] = soft.astype(BF16)
            return 0

        rows_loop(ROWS, 16, divide, 0, unroll=5)

    def by_image(self, x):
        tiles = x.reshape(ROWS // 16, 16, WIDE)
        parts = []
        for i in range(IMG_GROUP):
            im = jnp.concatenate([self.im16[i]] * (WIDE // LANES), axis=1)
            parts.append((tiles * im[None]).reshape(ROWS, WIDE))
        return jnp.concatenate(parts, axis=1)

    def head_blocks(self, x):
        r = lax.broadcasted_iota(jnp.int32, x.shape, 0) // HEAD_DIM
        c = (lax.broadcasted_iota(jnp.int32, x.shape, 1) % WIDE) // HEAD_DIM
        return jnp.where(r == c, x, 0.0).astype(BF16)

    def stacked(self, x):
        return jnp.concatenate([x[:, lane_block(i)] for i in range(IMG_GROUP)], axis=0)

    def contexts(self):
        for b in range(2):
            cols = lane_block(b)
            ctx = dot(self.soft_low[:, cols], self.by_image(self.v[:, cols]), TN)
            ctx = self.head_blocks(ctx)
            self.ctx[b] = ctx
            self.factor[:, cols] = dot(self.by_image(self.q[:, cols]), self.stacked(ctx))

    def fill_window(self):
        def fill(r0, _):
            rows = pl.ds(r0, 16)
            v = self.v[rows, :].astype(F32) * wide(self.live[rows, :])
            c0 = r0 // SLOTS
            self.rel_src[pl.ds(HALO * GRID + c0, 2)] = v.reshape(2, SLOTS, D)
            return 0

        rows_loop(ROWS, 16, fill, 0, unroll=5)
        self.rel[CELLS * SLOTS :, :] = jnp.zeros((SLOTS, D), F32)

    def window_sum(self, c):
        lanes = slice(c * LANES, (c + 1) * LANES)

        def put(cell, value):
            rows = pl.ds(pl.multiple_of(cell * SLOTS, SLOTS), SLOTS)
            self.rel[rows, lanes] = value

        def tap(a, b):
            t = (a + HALO) * WINDOW + b + HALO
            return self.rel_taps[t : t + 1, lanes]

        conv(self.rel_src, HALO, tap, REACHES[c], lanes, put)

    def mix(self):
        def mix(r0, _):
            rows = pl.ds(r0, 16)
            m = self.factor[rows, :] * INV_SCALE + self.q[rows, :].astype(F32) * self.rel[rows, :]
            self.mixed[rows, :] = (m * wide(self.live[rows, :])).astype(BF16)
            return 0

        rows_loop(ROWS, 16, mix, 0, unroll=5)

    def norm_two(self):
        for b in range(2):
            cols = lane_block(b)
            p = self.times_t(self.mixed[...], 3, b)
            self.second[:, cols] = self.first[:, cols] + p + self.small[4:5, cols]

        def body(r0, _):
            rows = pl.ds(r0, 16)
            n, u, inv = norm_rows(self.second[rows, :], self.row(5), self.row(6))
            self.n2[rows, :] = n.astype(BF16)
            self.u2[rows, :] = u
            self.inv2[rows, :] = jnp.broadcast_to(inv, (16, LANES))
            return 0

        rows_loop(ROWS, 16, body, 0, unroll=5)
        self.n2_t[...] = self.n2[...].T

    def hidden_block(self, r):
        up, down = 4 + 2 * r, 5 + 2 * r
        for b in range(2):
            cols = lane_block(b)
            h = self.times(self.n2[...], up, b) + self.small[pl.ds(9 + r, 1), cols]
            self.hidden[:, cols] = h
            self.factor[:, cols] = self.times(self.go[...], down, b)

        def body(r0, total):
            rows = pl.ds(r0, 16)
            act, slope = erf_parts(self.hidden[rows, :])
            g = self.factor[rows, :] * slope
            self.active[rows, :] = act.astype(BF16)
            self.low[rows, :] = g.astype(BF16)
            return total + fold(g)

        total = rows_loop(ROWS, 16, body, jnp.zeros((SLOTS, D), F32), unroll=5)
        self.sums[pl.ds(9 + r, 1), :] = jnp.sum(total, axis=0, keepdims=True)

    def hidden_grads(self, r):
        up, down = 4 + 2 * r, 5 + 2 * r
        self.put_grad(down, self.go_t[...], self.active)
        self.put_grad(up, self.n2_t[...], self.low)
        for b in range(2):
            cols = lane_block(b)
            self.second[:, cols] += self.times_t(self.active[...], down, b)
            self.back[:, cols] += self.times_t(self.low[...], up, b)

    def finish_out(self):
        def body(r0, _):
            rows = pl.ds(r0, 16)
            self.out_low[rows, :] = (self.second[rows, :] + self.row(7)).astype(BF16)
            return 0

        rows_loop(ROWS, 16, body, 0, unroll=5)
        self.unplace(self.out_low, self.out_own)

    def back_two(self):
        zero = jnp.zeros((SLOTS, D), F32)

        def body(r0, sums):
            rows = pl.ds(r0, 16)
            back, u = self.back[rows, :], self.u2[rows, :]
            go = self.go[rows, :].astype(F32)
            gs = go + norm_back(back, u, wide(self.inv2[rows, :]), self.row(5))
            self.gs[rows, :] = gs
            self.gs_low[rows, :] = gs.astype(BF16)
            new = (gs, back * u, back, go)
            return tuple(s + fold(n) for s, n in zip(sums, new, strict=True))

        sums = rows_loop(ROWS, 16, body, (zero,) * 4, unroll=5)
        for j, s in zip((4, 5, 6, 7), sums, strict=True):
            self.sums[j : j + 1, :] = jnp.sum(s, axis=0, keepdims=True)

    def grad_proj(self):
        self.put_grad(3, self.gs_low[...].T, self.mixed)

    def back_heads(self):
        for b in range(2):
            cols = lane_block(b)
            self.d[:, cols] = self.times(self.gs_low[...], 3, b)

        def fill(r0, _):
            rows = pl.ds(r0, 16)
            d = self.d[rows, :] * wide(self.live[rows, :])
            self.d[rows, :] = d
            self.f[rows, :] = (d * INV_SCALE).astype(BF16)
            c0 = r0 // SLOTS
            dq = d * self.q[rows, :].astype(F32)
            self.dq_src[pl.ds(HALO * GRID + c0, 2)] = dq.reshape(2, SLOTS, D)
            return 0

        rows_loop(ROWS, 16, fill, 0, unroll=5)
        for b in range(2):
            cols = lane_block(b)
            f3 = self.by_image(self.f[:, cols])
            g = self.head_blocks(dot(self.q[:, cols], f3, TN))
            self.gq[:, cols] = dot(f3, self.ctx[b], NT)
            self.gk[:, cols] = dot(self.by_image(self.v[:, cols]), g, NT)
            self.gv[:, cols] = dot(self.by_image(self.soft_low[:, cols]), self.stacked(g))

    def back_window(self, c):
        lanes = slice(c * LANES, (c + 1) * LANES)

        def put(cell, value):
            rows = pl.ds(pl.multiple_of(cell * SLOTS, SLOTS), SLOTS)
            self.gv[rows, lanes] = self.gv[rows, lanes] + value * self.live[rows, :]

        def tap(a, b):
            t = (HALO - a) * WINDOW + HALO - b
            return self.rel_taps[t : t + 1, lanes]

        conv(self.dq_src, HALO, tap, REACHES[c], lanes, put)

    def window_taps(self, c):
        lanes = slice(c * LANES, (c + 1) * LANES)

        def up(cell):
            return self.dq_src[HALO * GRID + cell, :, lanes]

        def put_tap(a, b, value):
            t = (a + HALO) * WINDOW + b + HALO
            keep = self.window[t : t + 1, lanes]
            self.sums[22 + t : 23 + t, lanes] = value * keep

        tap_sums(up, self.rel_src, HALO, REACHES[c], lanes, put_tap)

    def back_query_key(self):
        zero = jnp.zeros((SLOTS, D), F32)

        def inner(r0, total):
            rows = pl.ds(r0, 16)
            return total + fold(self.soft[rows, :] * self.gk[rows, :])

        shared = self.image_sum(rows_loop(ROWS, 16, inner, zero, unroll=5))
        shared2 = jnp.concatenate([shared, shared], axis=0)

        def low(r0, total):
            rows = pl.ds(r0, 16)
            gq = self.gq[rows, :] + self.d[rows, :] * self.rel[rows, :]
            gk = self.soft[rows, :] * (self.gk[rows, :] - shared2)
            self.gl[0, rows, :] = gq.astype(BF16)
            self.gl[1, rows, :] = gk.astype(BF16)
            return total + fold(gq)

        total = rows_loop(ROWS, 16, low, zero, unroll=5)
        self.sums[2:3, :] = jnp.sum(total, axis=0, keepdims=True)

    def back_value(self):
        def low(r0, total):
            rows = pl.ds(r0, 16)
            gv = self.gv[rows, :]
            self.gl[2, rows, :] = gv.astype(BF16)
            return total + fold(gv)

        total = rows_loop(ROWS, 16, low, jnp.zeros((SLOTS, D), F32), unroll=5)
        self.sums[3:4, :] = jnp.sum(total, axis=0, keepdims=True)
        self.grad_of(2)

    def grad_of(self, k):
        self.put_grad(k, self.n1_t[...], self.gl.at[k])

    def back_project(self):
        for b in range(2):
            cols = lane_block(b)
            back = self.times_t(self.gl[0], 0, b)
            back = back + self.times_t(self.gl[1], 1, b)
            self.back[:, cols] = back + self.times_t(self.gl[2], 2, b)

    def back_one(self):
        zero = jnp.zeros((SLOTS, D), F32)
        self.pos_up[0:GRID] = jnp.zeros((GRID, SLOTS, D), F32)
        self.pos_up[GRID + CELLS :] = jnp.zeros((GRID, SLOTS, D), F32)

        def body(r0, sums):
            rows = pl.ds(r0, 16)
            back, u = self.back[rows, :], self.u1[rows, :]
            gf = self.gs[rows, :] + norm_back(back, u, wide(self.inv1[rows, :]), self.row(0))
            c0 = r0 // SLOTS
            self.pos_up[pl.ds(GRID + c0, 2)] = gf.reshape(2, SLOTS, D)
            new = (back * u, back, gf)
            return tuple(s + fold(n) for s, n in zip(sums, new, strict=True))

        sums = rows_loop(ROWS, 16, body, (zero,) * 3, unroll=5)
        for j, s in zip((0, 1, 8), sums, strict=True):
            self.sums[j : j + 1, :] = jnp.sum(s, axis=0, keepdims=True)

    def back_position(self):
        for c in range(D // LANES):
            lanes = slice(c * LANES, (c + 1) * LANES)

            def put(cell, value):
                rows = pl.ds(pl.multiple_of(cell * SLOTS, SLOTS), SLOTS)
                gf = self.pos_up[GRID + cell, :, lanes]
                self.first[rows, lanes] = gf + value * self.live[rows, :]

            def tap(a, b):
                t = 13 + (1 - a) * 3 + 1 - b
                return self.small[t : t + 1, lanes]

            conv(self.pos_up, 1, tap, 1, lanes, put)

    def position_taps(self):
        for c in range(D // LANES):
            lanes = slice(c * LANES, (c + 1) * LANES)

            def up(cell):
                return self.pos_up[GRID + cell, :, lanes]

            def put_tap(a, b, value):
                t = 13 + (a + 1) * 3 + b + 1
                self.sums[t : t + 1, lanes] = value

            tap_sums(up, self.pos_src, 1, 1, lanes, put_tap)

    def finish_in(self):
        def down(r0, _):
            rows = pl.ds(r0, 16)
            self.in_low[rows, :] = self.first[rows, :].astype(BF16)
            return 0

        rows_loop(ROWS, 16, down, 0, unroll=5)
        self.unplace(self.in_low, self.in_own)


SLOT_OF = (0, 1, 2, 3, 4, 6, 8, 10, 5, 7, 9, 11)
MATS = len(SLOT_OF)
EARLY = 4
AXES = "xchly"
HEAD_ROWS = 320
SMALL_ROWS = 72
AG_ROUTES = ("lhyxc", "hlxyc", "lhxyc", "hylxc", "hyxlc", "hxylc", "lhxyc", "lhyxc", "hyxlc", "hylxc", "lhxyc", "hxlyc")
RS_ROUTES = ("cxylh", "cyxhl", "cylhx", "cylhx", "clxhy", "cxhyl", "clxyh", "cxyhl", "cylhx", "cylxh", "chxyl", "clxhy")
ORDER = (
    480, 482, 483, 481, 40, 20, 43, 63, 46, 70, 6, 60, 50, 41, 3, 0, 1, 26, 110, 66,
    23, 21, 103, 10, 30, 81, 83, 80, 61, 86, 90, 484, 55, 47, 44, 42, 51, 106, 100, 186,
    166, 101, 121, 163, 120, 123, 221, 161, 190, 181, 210, 130, 150, 226, 126, 485, 15, 75, 62, 71,
    35, 24, 22, 27, 64, 67, 4, 31, 2, 11, 7, 183, 203, 180, 140, 206, 160, 170, 200, 201,
    223, 230, 146, 141, 220, 143, 95, 82, 84, 87, 91, 56, 45, 52, 48, 76, 72, 65, 68, 115,
    104, 111, 102, 107, 135, 122, 127, 124, 131, 36, 32, 25, 28, 96, 92, 88, 85, 16, 5, 8,
    12, 57, 49, 53, 155, 151, 142, 147, 144, 195, 182, 191, 184, 187, 215, 211, 202, 204, 207, 175,
    162, 164, 167, 171, 116, 105, 108, 112, 37, 33, 29, 17, 9, 13, 97, 89, 93, 235, 224, 231,
    227, 222, 77, 69, 73, 58, 54, 136, 128, 125, 132, 196, 185, 188, 192, 176, 168, 165, 172, 156,
    152, 148, 145, 59, 488, 491, 493, 18, 14, 494, 38, 34, 117, 113, 109, 492, 236, 232, 228, 216,
    212, 205, 208, 225, 495, 19, 98, 78, 74, 94, 486, 137, 133, 129, 157, 153, 149, 197, 189, 193,
    39, 487, 489, 490, 79, 118, 114, 99, 177, 169, 173, 217, 209, 213, 496, 237, 229, 233, 497, 138,
    134, 158, 154, 119, 498, 198, 194, 499, 322, 324, 320, 178, 323, 342, 321, 340, 174, 343, 344, 341,
    139, 159, 218, 214, 500, 501, 381, 384, 382, 383, 380, 335, 327, 328, 360, 362, 326, 364, 325, 363,
    361, 199, 238, 234, 355, 348, 347, 345, 346, 179, 502, 395, 386, 387, 385, 388, 219, 503, 400, 401,
    422, 403, 404, 375, 365, 366, 368, 367, 402, 423, 421, 420, 424, 239, 504, 505, 461, 464, 462, 443,
    460, 463, 442, 415, 408, 441, 407, 444, 440, 405, 336, 331, 329, 330, 406, 356, 351, 350, 349, 506,
    376, 370, 369, 371, 527, 435, 425, 426, 428, 427, 507, 475, 467, 468, 465, 396, 391, 389, 455, 446,
    445, 466, 447, 390, 448, 508, 300, 301, 303, 304, 509, 519, 510, 511, 512, 315, 515, 476, 471, 470,
    469, 260, 307, 377, 262, 242, 337, 333, 305, 416, 409, 411, 410, 308, 241, 261, 244, 302, 243, 240,
    516, 397, 392, 393, 264, 263, 332, 372, 306, 521, 275, 265, 266, 268, 267, 513, 357, 352, 520, 456,
    451, 450, 449, 255, 248, 246, 247, 353, 245, 373, 436, 430, 429, 431, 518, 514, 517, 282, 280, 281,
    283, 528, 284, 417, 412, 316, 311, 309, 310, 378, 413, 374, 522, 523, 295, 287, 285, 286, 398, 394,
    288, 477, 473, 472, 276, 269, 270, 271, 525, 457, 452, 453, 533, 529, 358, 338, 334, 437, 433, 354,
    432, 524, 534, 418, 414, 317, 312, 313, 526, 256, 249, 251, 250, 530, 277, 296, 289, 290, 291, 273,
    272, 399, 379, 438, 458, 454, 434, 359, 478, 474, 339, 535, 419, 318, 257, 314, 252, 253, 297, 293,
    292, 479, 459, 536, 278, 274, 258, 254, 439, 542, 298, 294, 279, 531, 537, 319, 259, 299, 543, 544,
    532, 538, 545, 539, 546, 540, 541, 547, 548,
)


def scratch_of():
    f, h, low = (ROWS, D), (ROWS, LANES), pltpu.VMEM((ROWS, D), BF16)
    halo3 = pltpu.VMEM(((GRID + 2 * HALO) * GRID, SLOTS, D), F32)
    halo1 = pltpu.VMEM(((GRID + 2) * GRID, SLOTS, D), F32)
    high, column, turned = pltpu.VMEM(f, F32), pltpu.VMEM(h, F32), pltpu.VMEM((D, ROWS), BF16)
    taps = pltpu.VMEM((WINDOW * WINDOW, D), F32)
    return dict(
        live=column,
        im8=pltpu.VMEM((IMG_GROUP, SLOTS, LANES), F32),
        im16=pltpu.VMEM((IMG_GROUP, 16, LANES), BF16),
        window=taps,
        rel_taps=taps,
        pos_src=halo1,
        pos_up=halo1,
        rel_src=halo3,
        dq_src=halo3,
        first=high,
        u1=high,
        inv1=column,
        second=high,
        u2=high,
        inv2=column,
        n1=low,
        n1_t=turned,
        n2=low,
        n2_t=turned,
        go=low,
        go_t=turned,
        q=low,
        k=low,
        v=low,
        soft=high,
        soft_low=low,
        ctx=pltpu.VMEM((2, WIDE, IMG_GROUP * WIDE), BF16),
        factor=high,
        rel=high,
        mixed=low,
        hidden=high,
        active=low,
        low=low,
        out_low=low,
        back=high,
        gs=high,
        gs_low=low,
        d=high,
        f=low,
        gq=high,
        gk=high,
        gv=high,
        gl=pltpu.VMEM((3, ROWS, D), BF16),
        in_low=low,
    )


class Links:
    def __init__(self):
        dp, head = lax.axis_index(DP), lax.axis_index(HEAD)
        self.far = lax.axis_size(DP) // 4
        self.at = dict(x=head // 2, c=head % 2, h=dp // 4, l=dp // 2 % 2, y=dp % 2)

    def count(self, axis):
        return self.far if axis == "h" else 2

    def peer(self, axis, step):
        return lax.rem(self.at[axis] + step, self.count(axis))

    def device(self, axis, step):
        at = {**self.at, axis: self.peer(axis, step)}
        return (at["h"] * 4 + at["l"] * 2 + at["y"], at["x"] * 2 + at["c"])

    def steps(self, axis, do):
        self.repeat(self.count(axis), do, 8)

    def repeat(self, size, do, most):
        if size <= most:
            for step in range(1, size):
                do(step)
        else:

            def body(step, _):
                do(step)
                return 0

            lax.fori_loop(1, size, body, 0)

    def others(self, name, do):
        dp, head, heads = lax.axis_index(DP), lax.axis_index(HEAD), lax.axis_size(HEAD)

        def one(step):
            if name == ALL:
                i = lax.rem(dp * heads + head + step, lax.axis_size(ALL))
                do((i // heads, lax.rem(i, heads)))
            elif name == DP:
                do((lax.rem(dp + step, lax.axis_size(DP)), head))
            else:
                do((dp, lax.rem(head + step, heads)))

        self.repeat(lax.axis_size(name), one, 32)

    def signal(self):
        def one(device):
            pl.semaphore_signal(
                pltpu.get_barrier_semaphore(),
                inc=1,
                device_id=device,
                device_id_type=pl.DeviceIdType.MESH,
            )

        self.others(ALL, one)

    def meet(self):
        pl.semaphore_wait(pltpu.get_barrier_semaphore(), lax.axis_size(ALL) - 1)

    def copy(self, src, dst, send, recv, device):
        return pltpu.make_async_remote_copy(
            src_ref=src,
            dst_ref=dst,
            send_sem=send,
            recv_sem=recv,
            device_id=device,
            device_id_type=pl.DeviceIdType.MESH,
        )

    def region(self, blocks, slot, whole, **at):
        at = {**self.at, **at}
        place = [slice(None) if axis in whole else at[axis] for axis in AXES]
        return blocks.at[(*place, slot)]


class Gather:
    def __init__(self, links, w, send, recv):
        self.links, self.w, self.sems = links, w, (send, recv)

    def start(self, slot, i, j):
        path, links = AG_ROUTES[slot], self.links

        def along(**at):
            part = links.region(self.w, slot, path[: max(i, 0)], **at)
            sems = [s.at[slot, j] for s in self.sems]
            links.steps(
                path[j],
                lambda step: links.copy(part, part, *sems, links.device(path[j], step)).start(),
            )

        if i < 0:
            along()
        else:
            links.steps(path[i], lambda step: along(**{path[i]: links.peer(path[i], step)}))

    def descriptor(self, slot, j):
        path = AG_ROUTES[slot]
        at = {"h": pl.ds(0, self.links.far - 1)} if path[j] == "h" else {}
        part = self.links.region(self.w, slot, path[:j], **at)
        sems = [s.at[slot, j] for s in self.sems]
        return self.links.copy(part, part, *sems, self.links.device(path[j], 1))

    def arrive(self, slot, j):
        self.descriptor(slot, j).wait_recv()

    def sent(self):
        for slot in range(MATS):
            for j in range(len(AXES)):
                self.descriptor(slot, j).wait_send()

    def steps(self):
        for slot in range(MATS):
            for j in range(len(AXES)):
                for i in range(-1, j):
                    yield functools.partial(self.start, slot, i, j)
            for j in range(len(AXES)):
                yield functools.partial(self.arrive, slot, j)


class Scatter:
    def __init__(self, links, g, boxes, total, send, recv):
        self.links, self.g, self.boxes, self.total = links, g, boxes, total
        self.sems = (send, recv)

    def box(self, slot, j):
        return self.boxes[slot * len(AXES) + j - 1]

    def start(self, slot, i, j):
        path, links = RS_ROUTES[slot], self.links
        first = sum(links.count(a) - 1 for a in path[:i]) - 1
        sems = self.sems[0].at[slot, i], self.sems[1].at[slot, j - 1]

        def go(step):
            at = {path[i]: links.peer(path[i], step)}
            into = self.box(slot, j).at[first + step]
            device = links.device(path[i], step)

            def part(into, **more):
                src = links.region(self.g, slot, path[j + 1 :], **at, **more)
                links.copy(src, into, *sems, device).start()

            if j == len(AXES):
                part(into)
            else:
                links.steps(
                    path[j], lambda n: part(into.at[n - 1], **{path[j]: links.peer(path[j], n)})
                )

        links.steps(path[i], go)

    def add(self, slot, j):
        path, links = RS_ROUTES[slot], self.links
        box = self.box(slot, j)
        self.arrived(slot, j).wait_recv()

        def total(own, pick):
            value = own[...].astype(F32)
            for e in range(box.shape[0]):
                value = value + pick(box.at[e])[...].astype(F32)
            return value

        if j == len(AXES):
            own = links.region(self.g, slot, "")
            self.total[SLOT_OF.index(slot)] = total(own, lambda b: b)
            return

        def one(n):
            own = links.region(self.g, slot, path[j + 1 :], **{path[j]: links.peer(path[j], n)})
            own[...] = total(own, lambda b: b.at[n - 1]).astype(BF16)

        links.steps(path[j], one)

    def arrived(self, slot, j):
        box = self.box(slot, j)
        sems = self.sems[0].at[slot, j - 1], self.sems[1].at[slot, j - 1]
        return self.links.copy(box, box, *sems, self.links.device("c", 1))

    def sent(self):
        for slot in range(MATS):
            path = RS_ROUTES[slot]
            for i in range(len(AXES)):
                at = {"h": pl.ds(0, self.links.far - 1)} if path[i] == "h" else {}
                part = self.links.region(self.g, slot, path[i + 1 :], **at)
                sems = [s.at[slot, i] for s in self.sems]
                self.links.copy(part, part, *sems, self.links.device(path[i], 1)).wait_send()

    def steps(self):
        for slot in range(MATS):
            for i in range(len(AXES)):
                for j in range(i + 1, len(AXES) + 1):
                    yield functools.partial(self.start, slot, i, j)
            for j in range(1, len(AXES) + 1):
                yield functools.partial(self.add, slot, j)


class Small:
    def __init__(self, links, sums, parts, in_c, in_x, in_y, in_h, in_l, full, send, recv):
        self.links, self.sums, self.parts, self.full = links, sums, parts, full
        self.in_c, self.in_x, self.in_y, self.in_h, self.in_l = in_c, in_x, in_y, in_h, in_l
        self.send, self.recv = send, recv

    def go(self, stage, src, dst, axis):
        sems = (self.send.at[stage], self.recv.at[stage])
        self.links.steps(
            axis, lambda step: self.links.copy(src, dst, *sems, self.links.device(axis, step)).start()
        )

    def wait(self, stage):
        x, c = self.links.at["x"], self.links.at["c"]
        ref = (
            self.in_c,
            self.in_x,
            self.in_y,
            self.in_h.at[pl.ds(0, self.links.far - 1)],
            self.in_l,
            self.full.at[c, x],
            self.full.at[c],
        )[stage]
        sems = (self.send.at[stage], self.recv.at[stage])
        return self.links.copy(ref, ref, *sems, self.links.device("cxyhlxc"[stage], 1))

    def tick(self, stage):
        at = self.links.at
        x, c, h = at["x"], at["c"], at["h"]
        mine = self.parts.at[c, x]
        if stage:
            self.wait(stage - 1).wait_recv()
        if stage == 0:
            for b in range(D // LANES):
                self.parts[b // 2, b % 2] = self.sums[:, b * LANES : (b + 1) * LANES]
            self.go(0, self.parts.at[1 - c], self.in_c, "c")
        if stage == 1:
            self.parts[c] = self.parts[c] + self.in_c[...]
            self.go(1, self.parts.at[c, 1 - x], self.in_x, "x")
        if stage == 2:
            mine[...] = mine[...] + self.in_x[...]
            self.go(2, mine, self.in_y, "y")
        if stage == 3:
            self.in_h[h] = mine[...] + self.in_y[...]
            self.go(3, self.in_h.at[h], self.in_h.at[h], "h")
        if stage == 4:
            total = self.in_h[0]
            for i in range(1, self.links.far):
                total = total + self.in_h[i]
            self.sums[:, 0:LANES] = total
            self.go(4, self.sums.at[:, pl.ds(0, LANES)], self.in_l, "l")
        if stage == 5:
            self.full[c, x] = self.sums[:, 0:LANES] + self.in_l[...]
            self.go(5, self.full.at[c, x], self.full.at[c, x], "x")
        if stage == 6:
            self.go(6, self.full.at[c], self.full.at[c], "c")

    def sent(self):
        for stage in range(7):
            self.wait(stage).wait_send()


class Rows:
    def __init__(self, links, blocks, out, own, send, recv):
        self.links, self.blocks, self.out, self.own = links, blocks, out, own
        self.send, self.recv = send, recv

    def hop(self, i):
        x, c = self.links.at["x"], self.links.at["c"]
        x, axis = ((x, "x"), (x, "c"), (1 - x, "c"))[i]
        block = self.blocks.at[2 * x + c]
        return self.links.copy(
            block, block, self.send.at[i], self.recv.at[i], self.links.device(axis, 1)
        )

    def tick(self, stage):
        if stage == 0:
            self.hop(0).start()
            self.hop(1).start()
        if stage == 1:
            self.hop(0).wait_recv()
            self.hop(2).start()
        if stage == 2:
            self.hop(1).wait_recv()
            self.hop(2).wait_recv()
            self.join()

    def sent(self):
        for i in range(3):
            self.hop(i).wait_send()

    def join(self):
        heads, end, own = self.blocks.shape[0], self.out.shape[0], self.own
        for h in range(heads):
            lo, hi = h * own, (h + 1) * own
            base = lo // 16 * 16
            first = base + 16 if lo % 16 else base
            last = hi // 16 * 16 if h + 1 < heads else end
            self.out[first:last, :] = self.blocks[h, first - base : last - base, :]
            if lo % 16:
                before = (lo - own) // 16 * 16
                tail = self.blocks[h - 1, base - before : base - before + 16, :]
                self.out[base : base + 16, :] = tail + self.blocks[h, 0:16, :]


class Exchange:
    def __init__(self, links, name, buffer, send, recv):
        self.links, self.name, self.buffer, self.send, self.recv = links, name, buffer, send, recv

    def start(self, value):
        own = lax.axis_index(self.name)
        self.buffer[own] = value
        mine = self.buffer.at[own]
        self.links.others(
            self.name,
            lambda device: self.links.copy(mine, mine, self.send, self.recv, device).start(),
        )

    def descriptor(self):
        ref = self.buffer.at[pl.ds(0, self.buffer.shape[0] - 1)]
        return self.links.copy(ref, ref, self.send, self.recv, self.links.device("c", 1))

    def total(self):
        self.descriptor().wait_recv()
        return jnp.sum(self.buffer[...], axis=0)

    def sent(self):
        self.descriptor().wait_send()


def exact(a, b, dims):
    return lax.dot_general(
        a, b, dims, precision=lax.Precision.HIGHEST, preferred_element_type=F32
    )


class Adafactor:
    def __init__(self, refs, lo, hi, row_share, col_share, sq_share):
        self.__dict__.update(refs)
        self.lo, self.hi = lo, hi
        self.row_share, self.col_share, self.sq_share = row_share, col_share, sq_share

    def eye(self, count, first):
        r = lax.broadcasted_iota(jnp.int32, (count, LANES), 0)
        c = lax.broadcasted_iota(jnp.int32, (count, LANES), 1)
        return jnp.where(c == r + first, 1.0, 0.0)

    def lane(self, k, value, rest):
        lanes = lax.broadcasted_iota(jnp.int32, rest.shape, 1)
        return jnp.where(lanes == k, value, rest)

    def squares(self):
        rows, count = self.wg.shape[1], self.hi - self.lo
        by_row = jnp.zeros((rows, LANES), F32)
        by_col = []
        for k in range(self.lo, self.hi):
            g = self.wg[k]
            s = g * g + SQUARE_FLOOR
            by_row = self.lane(k, jnp.sum(s, axis=1, keepdims=True), by_row)
            by_col.append(jnp.sum(s, axis=0, keepdims=True))
        rest = jnp.zeros((SLOTS - count, LANES), F32)
        self.col_share.start(jnp.concatenate([*by_col, rest] if count < SLOTS else by_col, axis=0))
        turned = exact(self.eye(SLOTS, self.lo), by_row, NT)
        if rows < LANES:
            turned = jnp.concatenate([turned, jnp.zeros((SLOTS, LANES - rows), F32)], axis=1)
        self.row_share.start(turned)

    def scale(self):
        rows, lo, hi = self.wg.shape[1], self.lo, self.hi
        total = self.row_share.total()[0 : hi - lo, 0:rows]
        new_rows = SECOND_DECAY * self.row_state[lo:hi, :] + (1.0 - SECOND_DECAY) * (
            total * (1.0 / D)
        )
        self.new_rows[lo:hi, :] = new_rows
        row = exact(new_rows, self.eye(hi - lo, lo), TN)
        total = self.col_share.total()[0 : hi - lo]
        cols = SECOND_DECAY * self.col_state[lo:hi, :] + (1.0 - SECOND_DECAY) * (
            total * (1.0 / D)
        )
        self.new_cols[lo:hi, :] = cols
        sums = jnp.zeros((1, LANES), F32)
        for k in range(lo, hi):
            u = self.wg[k] * lax.rsqrt(row[:, k : k + 1] * cols[k - lo : k - lo + 1, :])
            self.upd[k] = u
            s = jnp.sum(jnp.sum(u * u, axis=0, keepdims=True), axis=1, keepdims=True)
            sums = self.lane(k, s, sums)
        mass = jnp.sum(row, axis=0, keepdims=True)
        self.sq_share.start(jnp.concatenate([sums, mass], axis=0))

    def apply(self):
        total = self.sq_share.total()
        mean = total[1:2] * (1.0 / (D * lax.axis_size(HEAD)))
        rms = jnp.sqrt(total[0:1] * mean * (1.0 / (D * D)))
        rate = STEP_RATE * jnp.sqrt(mean) / jnp.maximum(1.0, rms)
        for k in range(self.lo, self.hi):
            new = self.weights[k] - rate[:, k : k + 1] * self.upd[k]
            self.new_weights[k] = new
            self.copy[k] = new.astype(BF16)
            self.new_ema[k] = AVERAGE_KEEP * self.ema[k] + (1.0 - AVERAGE_KEEP) * new
        self.rms[self.lo // 4 : self.lo // 4 + 1, :] = rms


class SmallStep:
    def __init__(self, refs):
        self.__dict__.update(refs)

    def clips(self):
        lanes = lax.broadcasted_iota(jnp.int32, (1, LANES), 1)
        clip = jnp.where(lanes < EARLY, self.rms[0:1, :], self.rms[1:2, :])
        clip = jnp.where(lanes < MATS, clip, self.small_clip[...])
        self.clip[...] = clip[:, 0 : self.clip.shape[1]]

    def small_step(self):
        count, full = self.small.shape[0], self.full
        g = jnp.concatenate([full[b // 2, b % 2, 0:count, :] for b in range(D // LANES)], axis=1)
        self.small_grads[...] = g
        state = SECOND_DECAY * self.small_state[...] + (1.0 - SECOND_DECAY) * (
            g * g + SQUARE_FLOOR
        )
        self.new_small_state[...] = state
        u = g * lax.rsqrt(state)
        rms = jnp.sqrt(jnp.sum(u * u, axis=1, keepdims=True) * (1.0 / D))
        new = self.small[...] - SMALL_RATE * u / jnp.maximum(1.0, rms)
        self.new_small[...] = new
        self.new_small_ema[...] = AVERAGE_KEEP * self.small_ema[...] + (1.0 - AVERAGE_KEEP) * new
        r = lax.broadcasted_iota(jnp.int32, (count, LANES), 0)
        c = lax.broadcasted_iota(jnp.int32, (count, LANES), 1)
        picked = jnp.where(c == r + MATS, rms, 0.0)
        self.small_clip[...] = jnp.sum(picked, axis=0, keepdims=True)


class Inputs(NamedTuple):
    cls: Any
    img: Any
    tokens: Any
    cot: Any
    weights: Any
    row_state: Any
    col_state: Any
    ema: Any
    small: Any
    small_state: Any
    small_ema: Any


class Outputs(NamedTuple):
    out: Any
    grad_in: Any
    wg: Any
    new_rows: Any
    new_cols: Any
    new_weights: Any
    copy: Any
    new_ema: Any
    small_grads: Any
    new_small_state: Any
    new_small: Any
    new_small_ema: Any
    clip: Any


def box_shapes(links, block):
    for path in RS_ROUTES:
        for j in range(1, len(AXES) + 1):
            entries = sum(links.count(a) - 1 for a in path[:j])
            ways = [links.count(path[j]) - 1] if j < len(AXES) else []
            rest = [links.count(a) for a in AXES if a in path[j + 1 :]]
            yield pltpu.VMEM((entries, *ways, *rest, *block), BF16)


def shared_of(weights, parts, heads):
    links, (_, rows, _) = Links(), weights.shape
    block = (rows, LANES)
    every = pltpu.VMEM((2, 2, links.far, 2, 2, MATS, *block), BF16)
    out_rows = pltpu.VMEM((heads, HEAD_ROWS, D), BF16)
    dma = pltpu.SemaphoreType.DMA

    def f(*shape):
        return pltpu.VMEM(shape, F32)

    part = f(SMALL_ROWS, LANES)
    return dict(
        w=every,
        g=every,
        out_rows=out_rows,
        in_rows=out_rows,
        sums=f(SMALL_ROWS, D),
        parts=f(2, 2, SMALL_ROWS, LANES),
        in_c=f(2, SMALL_ROWS, LANES),
        in_x=part,
        in_y=part,
        in_h=f(links.far, SMALL_ROWS, LANES),
        in_l=part,
        full=f(2, 2, SMALL_ROWS, LANES),
        row_box=f(2, heads, SLOTS, LANES),
        col_box=f(2, parts, SLOTS, LANES),
        sq_box=f(2, parts * heads, 2, LANES),
        upd=f(MATS, *block),
        small_clip=f(1, LANES),
        rms=f(2, LANES),
        ag_send=dma((MATS, len(AXES))),
        ag_recv=dma((MATS, len(AXES))),
        rs_send=dma((MATS, len(AXES))),
        rs_recv=dma((MATS, len(AXES))),
        small_send=dma((7,)),
        small_recv=dma((7,)),
        out_send=dma((3,)),
        out_recv=dma((3,)),
        in_send=dma((3,)),
        in_recv=dma((3,)),
        opt_send=dma((2, 3)),
        opt_recv=dma((2, 3)),
        fetched=dma((len(Inputs._fields),)),
        stored=dma((len(Outputs._fields),)),
    )


class Ready:
    def __init__(self, src, dst, sem):
        self.copy = pltpu.make_async_copy(src, dst, sem)
        self.start, self.wait = self.copy.start, self.copy.wait


def then(*steps):
    def run():
        for step in steps:
            step()

    return run


def block_kernel(names, *refs):
    n_in, n_out = len(Inputs._fields), len(Outputs._fields)
    ins, outs, refs = Inputs(*refs[:n_in]), Outputs(*refs[n_in : n_in + n_out]), refs[n_in + n_out :]
    r = types.SimpleNamespace(**dict(zip(names, refs)))
    fetch = Inputs(
        *[
            Ready(ref, getattr(r, name), r.fetched.at[i])
            for i, (name, ref) in enumerate(zip(Inputs._fields, ins))
        ]
    )
    store = Outputs(
        *[
            Ready(getattr(r, name), ref, r.stored.at[i])
            for i, (name, ref) in enumerate(zip(Outputs._fields, outs))
        ]
    )
    boxes = refs[len(names) :]
    links = Links()
    links.signal()
    for one in (fetch.weights, *fetch[0:2], fetch.small, *fetch[2:4], *fetch[5:8], *fetch[9:]):
        one.start()
    r.out_own = r.out_rows.at[lax.axis_index(HEAD)]
    r.in_own = r.in_rows.at[lax.axis_index(HEAD)]
    own = r.cls.shape[1] * CELLS
    blk = Block(vars(r))
    gather = Gather(links, r.w, r.ag_send, r.ag_recv)
    scatter = Scatter(links, r.g, boxes, r.wg, r.rs_send, r.rs_recv)
    small = Small(
        links,
        *(r.sums, r.parts, r.in_c, r.in_x, r.in_y, r.in_h, r.in_l, r.full),
        r.small_send,
        r.small_recv,
    )
    out_rows = Rows(links, r.out_rows, r.out, own, r.out_send, r.out_recv)
    in_rows = Rows(links, r.in_rows, r.grad_in, own, r.in_send, r.in_recv)
    shares, opts = [], []
    for part, (lo, hi) in enumerate(((0, EARLY), (EARLY, MATS))):
        boxes = (HEAD, r.row_box), (DP, r.col_box), (ALL, r.sq_box)
        shares += [
            Exchange(links, axis, box.at[part], r.opt_send.at[part, i], r.opt_recv.at[part, i])
            for i, (axis, box) in enumerate(boxes)
        ]
        opts.append(Adafactor(vars(r), lo, hi, *shares[-3:]))
    step = SmallStep(vars(r))

    def round_weights():
        for k in range(MATS):
            mine = links.region(r.w, SLOT_OF[k], "")
            mine[...] = r.weights[k].astype(BF16)

    ops = [*gather.steps(), *scatter.steps()]
    ops += [then(fetch.weights.wait, round_weights), links.meet]
    ops += [
        then(fetch.small.wait, fetch.cls.wait, fetch.img.wait, blk.setup),
        then(fetch.tokens.wait, blk.read_tokens),
        blk.norm_one,
        then(fetch.cot.wait, blk.read_cotangent),
    ]
    ops += [functools.partial(blk.project, k) for k in range(3)]
    ops += [blk.softmax, blk.contexts, blk.fill_window]
    ops += [functools.partial(blk.window_sum, c) for c in range(D // LANES)]
    ops += [blk.mix, blk.norm_two]
    for i in range(4):
        ops += [functools.partial(blk.hidden_block, i), functools.partial(blk.hidden_grads, i)]
    ops += [blk.finish_out, blk.back_two, blk.grad_proj, blk.back_heads, blk.back_query_key]
    ops += [functools.partial(blk.grad_of, k) for k in range(2)]
    ops += [functools.partial(blk.back_window, c) for c in range(D // LANES)]
    ops += [blk.back_value]
    ops += [functools.partial(blk.window_taps, c) for c in range(D // LANES)]
    ops += [blk.back_project, blk.back_one, blk.back_position, blk.position_taps, blk.finish_in]
    for rows, done in ((out_rows, store.out), (in_rows, store.grad_in)):
        ops += [functools.partial(rows.tick, stage) for stage in range(2)]
        ops += [then(functools.partial(rows.tick, 2), done.start)]
    ops += [functools.partial(small.tick, stage) for stage in range(8)]
    ops += [
        then(
            fetch.small_state.wait,
            fetch.small_ema.wait,
            step.small_step,
            store.small_grads.start,
            store.new_small_state.start,
            store.new_small.start,
            store.new_small_ema.start,
        ),
        opts[1].squares,
        then(store.wg.start, opts[0].squares),
        then(fetch.row_state.wait, fetch.col_state.wait, opts[1].scale),
        then(opts[0].scale, store.new_rows.start, store.new_cols.start),
        then(fetch.ema.wait, opts[1].apply),
        then(
            opts[0].apply, store.new_weights.start, store.copy.start, store.new_ema.start
        ),
        then(step.clips, store.clip.start),
    ]
    for i in ORDER:
        ops[i]()
    for transfer in (gather, scatter, small, out_rows, in_rows, *shares):
        transfer.sent()
    for one in store:
        one.wait()


def finish_kernel(count, *refs):
    ins, outs, held = refs[:count], refs[count : 2 * count], refs[2 * count : 3 * count]
    took, gave = refs[3 * count :]
    come = [pltpu.make_async_copy(a, b, took.at[i]) for i, (a, b) in enumerate(zip(ins, held))]
    leave = [pltpu.make_async_copy(a, b, gave.at[i]) for i, (a, b) in enumerate(zip(held, outs))]
    for one in come:
        one.start()
    for one, other in zip(come, leave):
        one.wait()
        other.start()
    for one in leave:
        one.wait()


def local(
    tokens,
    cotangent,
    crop_image,
    crop_class,
    weights,
    row_state,
    col_state,
    weights_ema,
    small_params,
    small_state,
    small_ema,
):
    parts, heads = lax.axis_size(DP), lax.axis_size(HEAD)
    shared = shared_of(weights, parts, heads)
    own = scratch_of()

    def like(x, dtype=None):
        return jax.ShapeDtypeStruct(x.shape, dtype or x.dtype)

    clips = weights.shape[0] + small_params.shape[0]
    outs = (
        like(tokens),
        like(tokens),
        like(weights),
        like(row_state),
        like(col_state),
        like(weights),
        like(weights, BF16),
        like(weights),
        like(small_params),
        like(small_params),
        like(small_params),
        like(small_params),
        jax.ShapeDtypeStruct((1, clips), F32),
    )
    args = Inputs(
        crop_class,
        crop_image,
        tokens,
        cotangent,
        weights,
        row_state,
        col_state,
        weights_ema,
        small_params,
        small_state,
        small_ema,
    )
    staged = [pltpu.SMEM(x.shape, x.dtype) for x in args[:2]]
    staged += [pltpu.VMEM(x.shape, x.dtype) for x in (*args[2:], *outs)]
    names = (*shared, *own, *Inputs._fields, *Outputs._fields)
    far = pl.BlockSpec(memory_space=pltpu.HBM)
    res = pl.pallas_call(
        functools.partial(block_kernel, names),
        out_shape=outs,
        in_specs=[far] * len(args),
        out_specs=(far,) * len(outs),
        scratch_shapes=[
            *shared.values(),
            *own.values(),
            *staged,
            *box_shapes(Links(), weights.shape[1:]),
        ],
        compiler_params=pltpu.CompilerParams(
            collective_id=0, has_side_effects=True, vmem_limit_bytes=63 << 20
        ),
        name="block",
    )(*args)
    res = pl.pallas_call(
        functools.partial(finish_kernel, len(outs)),
        out_shape=outs,
        in_specs=[far] * len(outs),
        out_specs=(far,) * len(outs),
        scratch_shapes=[
            *[pltpu.VMEM(x.shape, x.dtype) for x in outs],
            pltpu.SemaphoreType.DMA((len(outs),)),
            pltpu.SemaphoreType.DMA((len(outs),)),
        ],
        compiler_params=pltpu.CompilerParams(vmem_limit_bytes=63 << 20),
        name="finish",
    )(*res)
    return (*res[:-1], res[-1].reshape(clips))


def solution(mesh):
    in_specs = (
        P(DP, None),
        P(DP, None),
        P(DP, None),
        P(DP, None),
        P(None, DP, HEAD),
        P(None, DP),
        P(None, HEAD),
        P(None, DP, HEAD),
        P(),
        P(),
        P(),
    )
    out_specs = (
        P(DP, None),
        P(DP, None),
        P(None, DP, HEAD),
        P(None, DP),
        P(None, HEAD),
        P(None, DP, HEAD),
        P(None, DP, HEAD),
        P(None, DP, HEAD),
        P(),
        P(),
        P(),
        P(),
        P(),
    )
    return jax.shard_map(local, mesh=mesh, in_specs=in_specs, out_specs=out_specs, check_vma=False)
```

```python
import functools
import itertools
import math
import types
from typing import Any, NamedTuple

import jax
import jax.numpy as jnp
from jax import lax
from jax.experimental import pallas as pl
from jax.experimental.pallas import tpu as pltpu
from jax.sharding import PartitionSpec as P

DP, HEAD = "dp", "head"
ALL = (DP, HEAD)
D = 512
HEAD_DIM = 64
GRID = 7
SMALL_GRID = 3
WINDOW = 7
IMG_GROUP = 3
CELLS = GRID * GRID
SLOTS = 8
CELL_PAD = CELLS + 1
ROWS = CELL_PAD * SLOTS
PIECES = 5
PIECE = ROWS // PIECES
LANES = 128
WIDE = 256
REACHES = (1, 2, 3, 3)
HALO = WINDOW // 2

NORM_EPS = 1e-06
SQUARE_FLOOR = 1e-30
SECOND_DECAY = 0.999
STEP_RATE = 0.02
SMALL_RATE = 0.05
AVERAGE_KEEP = 0.9
NEG_LARGE = -1e30
ROOT_HALF = 0.7071067811865476
INV_ROOT_TAU = 0.3989422804014327
INV_SCALE = 1.0 / math.sqrt(HEAD_DIM)

F32 = jnp.float32
BF16 = jnp.bfloat16
NN = (((1,), (0,)), ((), ()))
NT = (((1,), (1,)), ((), ()))
TN = (((0,), (0,)), ((), ()))


def dot(a, b, dims=NN):
    return lax.dot_general(a, b, dims, preferred_element_type=F32)


def lane_block(b):
    return slice(b * WIDE, (b + 1) * WIDE)


def wide(col):
    return jnp.concatenate([col] * (D // LANES), axis=1)


def rows_loop(count, size, body, init=None, unroll=1):
    def step(j, carry):
        return body(pl.multiple_of(j * size, size), carry)

    return lax.fori_loop(0, count // size, step, init, unroll=unroll)


def piece_loop(piece, body):
    def step(j, carry):
        body(pl.multiple_of(piece * PIECE + j * 16, 16))
        return carry

    lax.fori_loop(0, PIECE // 16, step, 0, unroll=5)


def conv(src, halo, tap, reach, lanes, put):
    def line(y, _):
        sums = [jnp.zeros((SLOTS, LANES), F32) for _ in range(GRID)]
        for a in range(-reach, reach + 1):
            base = (y + (a + halo)) * GRID
            cells = [src[base + x, :, lanes] for x in range(GRID)]
            for b in range(-reach, reach + 1):
                t = tap(a, b)
                for x in range(GRID):
                    if 0 <= x + b < GRID:
                        sums[x] = sums[x] + t * cells[x + b]
        for x in range(GRID):
            put(y * GRID + x, sums[x])
        return 0

    lax.fori_loop(0, GRID, line, 0)


def tap_sums(up, src, halo, reach, lanes, put):
    for a in range(-reach, reach + 1):

        def line(y, sums):
            sums = list(sums)
            ups = [up(y * GRID + x) for x in range(GRID)]
            base = (y + (a + halo)) * GRID
            cells = [src[base + x, :, lanes] for x in range(GRID)]
            for i, b in enumerate(range(-reach, reach + 1)):
                for x in range(GRID):
                    if 0 <= x + b < GRID:
                        sums[i] = sums[i] + ups[x] * cells[x + b]
            return tuple(sums)

        start = tuple(jnp.zeros((SLOTS, LANES), F32) for _ in range(2 * reach + 1))
        sums = lax.fori_loop(0, GRID, line, start)
        for i, b in enumerate(range(-reach, reach + 1)):
            put(a, b, jnp.sum(sums[i], axis=0, keepdims=True))


def fold(x):
    return jnp.sum(x.reshape(x.shape[0] // SLOTS, SLOTS, x.shape[1]), axis=0)


def erf_parts(h):
    e = lax.erf(h * ROOT_HALF)
    half = 0.5 * (1.0 + e)
    return h * half, half + h * jnp.exp(-0.5 * h * h) * INV_ROOT_TAU


def norm_rows(v, gain, shift):
    centre = jnp.sum(v, axis=1, keepdims=True) * (1.0 / D)
    offset = v - centre
    spread = jnp.sum(offset * offset, axis=1, keepdims=True) * (1.0 / D)
    inverse = lax.rsqrt(spread + NORM_EPS)
    unit = offset * inverse
    return unit * gain + shift, unit, inverse


def norm_back(up, unit, inverse, gain):
    z = up * gain
    mean_z = jnp.sum(z, axis=1, keepdims=True) * (1.0 / D)
    mean_zu = jnp.sum(z * unit, axis=1, keepdims=True) * (1.0 / D)
    return inverse * (z - mean_z - unit * mean_zu)


class Block:
    def __init__(self, refs):
        self.__dict__.update(refs)

    def matrix(self, k, lo, hi):
        parts = []
        for h in range(lo, hi):
            part = self.w[h // 2, h % 2, :, :, :, k]
            if part.shape[-2] % 16:
                part = part.astype(F32).reshape(D, LANES).astype(BF16)
            else:
                part = part.reshape(D, LANES)
            parts.append(part)
        return jnp.concatenate(parts, axis=1)

    def times(self, lhs, k, b):
        return dot(lhs, self.matrix(k, 2 * b, 2 * b + 2))

    def times_t(self, lhs, k, b):
        return dot(lhs, self.matrix(k, 0, 4)[lane_block(b), :], NT)

    def put_grad(self, k, lhs_t, rhs):
        for b in range(2):
            g = dot(lhs_t, rhs[:, lane_block(b)])
            for i in range(2):
                piece = g[:, i * LANES : (i + 1) * LANES]
                place = self.g.shape[2:5]
                piece = piece.reshape(*place, self.g.shape[-2], LANES)
                self.g[b, i, :, :, :, k] = piece.astype(BF16)

    def row(self, j):
        return self.small[j : j + 1, :]

    def setup(self):
        head = lax.axis_index(HEAD)
        slots = self.cls.shape[1]
        self.sums[...] = jnp.zeros(self.sums.shape, F32)
        sub = lax.broadcasted_iota(jnp.int32, (SLOTS, LANES), 0)
        valid = jnp.where(sub < slots, 1.0, 0.0)
        full = jnp.zeros((SLOTS, LANES), F32)
        images = [jnp.zeros((SLOTS, LANES), F32) for _ in range(IMG_GROUP)]
        for s in range(slots):
            full = jnp.where(sub == s, jnp.where(self.cls[head, s] == 0, 1.0, 0.0), full)
            for i in range(IMG_GROUP):
                images[i] = jnp.where(
                    sub == s, jnp.where(self.img[head, s] == i, 1.0, 0.0), images[i]
                )
        for cell in range(CELLS):
            small = cell // GRID < SMALL_GRID and cell % GRID < SMALL_GRID
            self.live[cell * SLOTS : (cell + 1) * SLOTS, :] = valid if small else full
        self.live[CELLS * SLOTS :, :] = jnp.zeros((SLOTS, LANES), F32)
        for i in range(IMG_GROUP):
            self.im8[i] = images[i]
            self.im16[i] = jnp.concatenate([images[i], images[i]], axis=0).astype(BF16)
        self.pos_src[0:GRID] = jnp.zeros((GRID, SLOTS, D), F32)
        self.pos_src[GRID + CELLS :] = jnp.zeros((GRID, SLOTS, D), F32)
        for pad in (self.rel_src, self.dq_src):
            pad[0 : HALO * GRID] = jnp.zeros((HALO * GRID, SLOTS, D), F32)
            pad[HALO * GRID + CELLS :] = jnp.zeros((HALO * GRID, SLOTS, D), F32)
        tap = lax.broadcasted_iota(jnp.int32, (WINDOW * WINDOW, 1), 0)
        row_off = jnp.abs(tap // WINDOW - HALO)
        col_off = jnp.abs(tap % WINDOW - HALO)
        off = jnp.maximum(row_off, col_off)
        heads = lax.broadcasted_iota(jnp.int32, (1, D), 1) // HEAD_DIM
        reach = jnp.where(heads < 2, 1, jnp.where(heads < 5, 2, 3))
        mask = jnp.where(off <= reach, 1.0, 0.0)
        self.window[...] = mask
        self.rel_taps[...] = self.small[22 : 22 + WINDOW * WINDOW, :] * mask

    def place(self, rows_ref, first, r0, size):
        count = rows_ref.shape[0]
        r = r0 + lax.broadcasted_iota(jnp.int32, (size, 1), 0)
        cell, slot = r >> 3, r & 7
        want = first + slot * CELLS + cell
        want = jnp.where((slot < self.cls.shape[1]) & (cell < CELLS), want, -1)
        col = lax.broadcasted_iota(jnp.int32, (size, count), 1)
        pick = jnp.where(col == want, 1.0, 0.0).astype(BF16)
        return dot(pick, rows_ref[...])

    def unplace(self, src_ref, out_ref):
        count = out_ref.shape[0]
        own = self.cls.shape[1] * CELLS
        lead = lax.rem(lax.axis_index(HEAD) * own, 16)
        r = lax.broadcasted_iota(jnp.int32, (1, ROWS), 1)
        cell, slot = r >> 3, r & 7
        target = lead + slot * CELLS + cell
        target = jnp.where((slot < self.cls.shape[1]) & (cell < CELLS), target, -1)
        t = lax.broadcasted_iota(jnp.int32, (count, ROWS), 0)
        pick = jnp.where(t == target, 1.0, 0.0).astype(BF16)
        out_ref[...] = dot(pick, src_ref[...]).astype(BF16)

    def read_tokens(self, piece):
        first = lax.axis_index(HEAD) * (self.cls.shape[1] * CELLS)
        r0 = piece * PIECE
        rows = slice(r0, r0 + PIECE)
        x = self.place(self.tokens, first, r0, PIECE)
        self.first[rows, :] = x
        cells = slice(GRID + r0 // SLOTS, GRID + (r0 + PIECE) // SLOTS)
        self.pos_src[cells] = (x * wide(self.live[rows, :])).reshape(-1, SLOTS, D)

    def read_cotangent(self, piece):
        first = lax.axis_index(HEAD) * (self.cls.shape[1] * CELLS)
        rows = slice(piece * PIECE, (piece + 1) * PIECE)
        c = self.place(self.cot, first, piece * PIECE, PIECE)
        self.go[rows, :] = (c * wide(self.live[rows, :])).astype(BF16)

    def turn_cotangent(self):
        self.go_t[...] = self.go[...].T
        self.back[...] = jnp.zeros((ROWS, D), F32)

    def position(self, c):
        lanes = slice(c * LANES, (c + 1) * LANES)

        def put(cell, value):
            rows = pl.ds(pl.multiple_of(cell * SLOTS, SLOTS), SLOTS)
            self.first[rows, lanes] = self.first[rows, lanes] + value + self.small[8:9, lanes]

        def tap(a, b):
            t = 13 + (a + 1) * 3 + b + 1
            return self.small[t : t + 1, lanes]

        conv(self.pos_src, 1, tap, 1, lanes, put)

    def norm_one(self, piece):
        def body(r0):
            rows = pl.ds(r0, 16)
            n, u, inv = norm_rows(self.first[rows, :], self.row(0), self.row(1))
            self.n1[rows, :] = n.astype(BF16)
            self.u1[rows, :] = u
            self.inv1[rows, :] = jnp.broadcast_to(inv, (16, LANES))

        piece_loop(piece, body)

    def turn_one(self):
        self.n1_t[...] = self.n1[...].T

    def project(self, k, b):
        low, cols = (self.q, self.k, self.v)[k], lane_block(b)
        p = self.times(self.n1[...], k, b)
        if k != 1:
            p = p + self.small[2 + k // 2 : 3 + k // 2, cols]
        low[:, cols] = p.astype(BF16)

    def image_sum(self, x):
        total = jnp.zeros((SLOTS, D), F32)
        for i in range(IMG_GROUP):
            im = wide(self.im8[i])
            total = total + im * jnp.sum(im * x, axis=0, keepdims=True)
        return total

    def key_tops(self):
        def top(r0, best):
            live = wide(self.live[pl.ds(r0, 16), :])
            keys = jnp.where(live > 0, self.k[pl.ds(r0, 16), :].astype(F32), NEG_LARGE)
            return jnp.maximum(best, jnp.max(keys.reshape(2, SLOTS, D), axis=0))

        best = rows_loop(ROWS, 16, top, jnp.full((SLOTS, D), NEG_LARGE, F32), unroll=5)
        shift = jnp.zeros((SLOTS, D), F32)
        for i in range(IMG_GROUP):
            im = wide(self.im8[i])
            most = jnp.max(jnp.where(im > 0, best, NEG_LARGE), axis=0, keepdims=True)
            shift = jnp.where(im > 0, most, shift)
        self.soft_acc[0:SLOTS, :] = shift

    def key_powers(self):
        shift2 = jnp.concatenate([self.soft_acc[0:SLOTS, :]] * 2, axis=0)

        def power(r0, total):
            rows = pl.ds(r0, 16)
            live = wide(self.live[rows, :])
            keys = self.k[rows, :].astype(F32)
            e = jnp.where(live > 0, jnp.exp(jnp.where(live > 0, keys - shift2, 0.0)), 0.0)
            self.soft[rows, :] = e
            return total + fold(e)

        total = rows_loop(ROWS, 16, power, jnp.zeros((SLOTS, D), F32), unroll=5)
        total = self.image_sum(total)
        self.soft_acc[SLOTS : 2 * SLOTS, :] = 1.0 / jnp.where(total > 0, total, 1.0)

    def key_shares(self):
        scale2 = jnp.concatenate([self.soft_acc[SLOTS : 2 * SLOTS, :]] * 2, axis=0)

        def divide(r0, _):
            rows = pl.ds(r0, 16)
            soft = self.soft[rows, :] * scale2
            self.soft[rows, :] = soft
            self.soft_low[rows, :] = soft.astype(BF16)
            return 0

        rows_loop(ROWS, 16, divide, 0, unroll=5)

    def by_image(self, x):
        tiles = x.reshape(ROWS // 16, 16, WIDE)
        parts = []
        for i in range(IMG_GROUP):
            im = jnp.concatenate([self.im16[i]] * (WIDE // LANES), axis=1)
            parts.append((tiles * im[None]).reshape(ROWS, WIDE))
        return jnp.concatenate(parts, axis=1)

    def head_blocks(self, x):
        r = lax.broadcasted_iota(jnp.int32, x.shape, 0) // HEAD_DIM
        c = (lax.broadcasted_iota(jnp.int32, x.shape, 1) % WIDE) // HEAD_DIM
        return jnp.where(r == c, x, 0.0).astype(BF16)

    def stacked(self, x):
        return jnp.concatenate([x[:, lane_block(i)] for i in range(IMG_GROUP)], axis=0)

    def contexts(self, b):
        cols = lane_block(b)
        ctx = dot(self.soft_low[:, cols], self.by_image(self.v[:, cols]), TN)
        ctx = self.head_blocks(ctx)
        self.ctx[b] = ctx
        self.factor[:, cols] = dot(self.by_image(self.q[:, cols]), self.stacked(ctx))

    def fill_window(self):
        def fill(r0, _):
            rows = pl.ds(r0, 16)
            v = self.v[rows, :].astype(F32) * wide(self.live[rows, :])
            c0 = r0 // SLOTS
            self.rel_src[pl.ds(HALO * GRID + c0, 2)] = v.reshape(2, SLOTS, D)
            return 0

        rows_loop(ROWS, 16, fill, 0, unroll=5)
        self.rel[CELLS * SLOTS :, :] = jnp.zeros((SLOTS, D), F32)

    def window_sum(self, c):
        lanes = slice(c * LANES, (c + 1) * LANES)

        def put(cell, value):
            rows = pl.ds(pl.multiple_of(cell * SLOTS, SLOTS), SLOTS)
            self.rel[rows, lanes] = value

        def tap(a, b):
            t = (a + HALO) * WINDOW + b + HALO
            return self.rel_taps[t : t + 1, lanes]

        conv(self.rel_src, HALO, tap, REACHES[c], lanes, put)

    def mix(self):
        def mix(r0, _):
            rows = pl.ds(r0, 16)
            m = self.factor[rows, :] * INV_SCALE + self.q[rows, :].astype(F32) * self.rel[rows, :]
            self.mixed[rows, :] = (m * wide(self.live[rows, :])).astype(BF16)
            return 0

        rows_loop(ROWS, 16, mix, 0, unroll=5)

    def attend(self, b):
        cols = lane_block(b)
        p = self.times_t(self.mixed[...], 3, b)
        self.second[:, cols] = self.first[:, cols] + p + self.small[4:5, cols]

    def norm_two(self, piece):
        def body(r0):
            rows = pl.ds(r0, 16)
            n, u, inv = norm_rows(self.second[rows, :], self.row(5), self.row(6))
            self.n2[rows, :] = n.astype(BF16)
            self.u2[rows, :] = u
            self.inv2[rows, :] = jnp.broadcast_to(inv, (16, LANES))

        piece_loop(piece, body)

    def turn_two(self):
        self.n2_t[...] = self.n2[...].T

    def hidden_in(self, r):
        for b in range(2):
            cols = lane_block(b)
            h = self.times(self.n2[...], 4 + 2 * r, b) + self.small[9 + r : 10 + r, cols]
            self.hidden[:, cols] = h
            self.factor[:, cols] = self.times(self.go[...], 5 + 2 * r, b)

    def hidden_out(self, r):
        def body(r0, total):
            rows = pl.ds(r0, 16)
            act, slope = erf_parts(self.hidden[rows, :])
            g = self.factor[rows, :] * slope
            self.active[rows, :] = act.astype(BF16)
            self.low[rows, :] = g.astype(BF16)
            return total + fold(g)

        total = rows_loop(ROWS, 16, body, jnp.zeros((SLOTS, D), F32), unroll=5)
        self.sums[9 + r : 10 + r, :] = jnp.sum(total, axis=0, keepdims=True)

    def grad_down(self, r):
        self.put_grad(5 + 2 * r, self.go_t[...], self.active)

    def grad_up(self, r):
        self.put_grad(4 + 2 * r, self.n2_t[...], self.low)

    def add_down(self, r):
        for b in range(2):
            self.second[:, lane_block(b)] += self.times_t(self.active[...], 5 + 2 * r, b)

    def add_back(self, r):
        for b in range(2):
            self.back[:, lane_block(b)] += self.times_t(self.low[...], 4 + 2 * r, b)

    def finish_out(self):
        def body(r0, _):
            rows = pl.ds(r0, 16)
            self.out_low[rows, :] = (self.second[rows, :] + self.row(7)).astype(BF16)
            return 0

        rows_loop(ROWS, 16, body, 0, unroll=5)
        self.unplace(self.out_low, self.out_own)

    def back_two(self):
        zero = jnp.zeros((SLOTS, D), F32)

        def body(r0, sums):
            rows = pl.ds(r0, 16)
            back, u = self.back[rows, :], self.u2[rows, :]
            go = self.go[rows, :].astype(F32)
            gs = go + norm_back(back, u, wide(self.inv2[rows, :]), self.row(5))
            self.gs[rows, :] = gs
            self.gs_low[rows, :] = gs.astype(BF16)
            new = (gs, back * u, back, go)
            return tuple(s + fold(n) for s, n in zip(sums, new, strict=True))

        sums = rows_loop(ROWS, 16, body, (zero,) * 4, unroll=5)
        for j, s in zip((4, 5, 6, 7), sums, strict=True):
            self.sums[j : j + 1, :] = jnp.sum(s, axis=0, keepdims=True)

    def grad_proj(self):
        self.put_grad(3, self.gs_low[...].T, self.mixed)

    def back_mixed(self):
        for b in range(2):
            self.d[:, lane_block(b)] = self.times(self.gs_low[...], 3, b)

    def back_fill(self):
        def fill(r0, _):
            rows = pl.ds(r0, 16)
            d = self.d[rows, :] * wide(self.live[rows, :])
            self.d[rows, :] = d
            self.f[rows, :] = (d * INV_SCALE).astype(BF16)
            c0 = r0 // SLOTS
            dq = d * self.q[rows, :].astype(F32)
            self.dq_src[pl.ds(HALO * GRID + c0, 2)] = dq.reshape(2, SLOTS, D)
            return 0

        rows_loop(ROWS, 16, fill, 0, unroll=5)
    def back_heads(self, b):
        cols = lane_block(b)
        f3 = self.by_image(self.f[:, cols])
        g = self.head_blocks(dot(self.q[:, cols], f3, TN))
        self.gq[:, cols] = dot(f3, self.ctx[b], NT)
        self.gk[:, cols] = dot(self.by_image(self.v[:, cols]), g, NT)
        self.gv[:, cols] = dot(self.by_image(self.soft_low[:, cols]), self.stacked(g))

    def back_window(self, c):
        lanes = slice(c * LANES, (c + 1) * LANES)

        def put(cell, value):
            rows = pl.ds(pl.multiple_of(cell * SLOTS, SLOTS), SLOTS)
            self.gv[rows, lanes] = self.gv[rows, lanes] + value * self.live[rows, :]

        def tap(a, b):
            t = (HALO - a) * WINDOW + HALO - b
            return self.rel_taps[t : t + 1, lanes]

        conv(self.dq_src, HALO, tap, REACHES[c], lanes, put)

    def window_taps(self, c):
        lanes = slice(c * LANES, (c + 1) * LANES)

        def up(cell):
            return self.dq_src[HALO * GRID + cell, :, lanes]

        def put_tap(a, b, value):
            t = (a + HALO) * WINDOW + b + HALO
            keep = self.window[t : t + 1, lanes]
            self.sums[22 + t : 23 + t, lanes] = value * keep

        tap_sums(up, self.rel_src, HALO, REACHES[c], lanes, put_tap)

    def back_inner(self):
        def inner(r0, total):
            rows = pl.ds(r0, 16)
            return total + fold(self.soft[rows, :] * self.gk[rows, :])

        total = rows_loop(ROWS, 16, inner, jnp.zeros((SLOTS, D), F32), unroll=5)
        self.soft_acc[0:SLOTS, :] = self.image_sum(total)

    def back_query_key(self):
        zero = jnp.zeros((SLOTS, D), F32)
        shared2 = jnp.concatenate([self.soft_acc[0:SLOTS, :]] * 2, axis=0)

        def low(r0, total):
            rows = pl.ds(r0, 16)
            gq = self.gq[rows, :] + self.d[rows, :] * self.rel[rows, :]
            gk = self.soft[rows, :] * (self.gk[rows, :] - shared2)
            self.gl[0, rows, :] = gq.astype(BF16)
            self.gl[1, rows, :] = gk.astype(BF16)
            return total + fold(gq)

        total = rows_loop(ROWS, 16, low, zero, unroll=5)
        self.sums[2:3, :] = jnp.sum(total, axis=0, keepdims=True)

    def back_value(self):
        def low(r0, total):
            rows = pl.ds(r0, 16)
            gv = self.gv[rows, :]
            self.gl[2, rows, :] = gv.astype(BF16)
            return total + fold(gv)

        total = rows_loop(ROWS, 16, low, jnp.zeros((SLOTS, D), F32), unroll=5)
        self.sums[3:4, :] = jnp.sum(total, axis=0, keepdims=True)

    def grad_of(self, k):
        self.put_grad(k, self.n1_t[...], self.gl.at[k])

    def back_project(self, b):
        back = self.times_t(self.gl[0], 0, b)
        back = back + self.times_t(self.gl[1], 1, b)
        self.back[:, lane_block(b)] = back + self.times_t(self.gl[2], 2, b)

    def back_one(self):
        zero = jnp.zeros((SLOTS, D), F32)
        self.pos_up[0:GRID] = jnp.zeros((GRID, SLOTS, D), F32)
        self.pos_up[GRID + CELLS :] = jnp.zeros((GRID, SLOTS, D), F32)

        def body(r0, sums):
            rows = pl.ds(r0, 16)
            back, u = self.back[rows, :], self.u1[rows, :]
            gf = self.gs[rows, :] + norm_back(back, u, wide(self.inv1[rows, :]), self.row(0))
            c0 = r0 // SLOTS
            self.pos_up[pl.ds(GRID + c0, 2)] = gf.reshape(2, SLOTS, D)
            new = (back * u, back, gf)
            return tuple(s + fold(n) for s, n in zip(sums, new, strict=True))

        sums = rows_loop(ROWS, 16, body, (zero,) * 3, unroll=5)
        for j, s in zip((0, 1, 8), sums, strict=True):
            self.sums[j : j + 1, :] = jnp.sum(s, axis=0, keepdims=True)

    def back_position(self):
        for c in range(D // LANES):
            lanes = slice(c * LANES, (c + 1) * LANES)

            def put(cell, value):
                rows = pl.ds(pl.multiple_of(cell * SLOTS, SLOTS), SLOTS)
                gf = self.pos_up[GRID + cell, :, lanes]
                self.first[rows, lanes] = gf + value * self.live[rows, :]

            def tap(a, b):
                t = 13 + (1 - a) * 3 + 1 - b
                return self.small[t : t + 1, lanes]

            conv(self.pos_up, 1, tap, 1, lanes, put)

    def position_taps(self):
        for c in range(D // LANES):
            lanes = slice(c * LANES, (c + 1) * LANES)

            def up(cell):
                return self.pos_up[GRID + cell, :, lanes]

            def put_tap(a, b, value):
                t = 13 + (a + 1) * 3 + b + 1
                self.sums[t : t + 1, lanes] = value

            tap_sums(up, self.pos_src, 1, 1, lanes, put_tap)

    def finish_in(self):
        def down(r0, _):
            rows = pl.ds(r0, 16)
            self.in_low[rows, :] = self.first[rows, :].astype(BF16)
            return 0

        rows_loop(ROWS, 16, down, 0, unroll=5)
        self.unplace(self.in_low, self.in_own)


SLOT_OF = (0, 1, 2, 3, 4, 6, 8, 10, 5, 7, 9, 11)
MATS = len(SLOT_OF)
EARLY = 4
AXES = "xchly"
WAYS, ENTRIES = 3, 6
HEAD_ROWS = 320
SMALL_ROWS = 72
AG_ROUTES = ("zyxc", "zyxc", "zxyc", "zxyc", "zxyc", "zyxc", "yhxlc", "xylhc", "xhylc", "hlyxc", "hxlyc", "hlyxc")
RS_ROUTES = ("cyxz", "cxyz", "cyxz", "cyxz", "cxhyl", "cyhlx", "cxlhy", "cyhlx", "cylxh", "clyxh", "cyxhl", "chlxy")
ORDER = (
    390, 392, 393, 399, 397, 394, 395, 391, 11, 66, 129, 152, 136, 76, 156, 106, 132, 116, 109, 169,
    396, 22, 69, 87, 96, 398, 403, 401, 72, 400, 147, 412, 0, 414, 172, 411, 127, 81, 77, 70,
    121, 110, 117, 410, 73, 86, 176, 402, 33, 406, 404, 407, 18, 12, 15, 13, 149, 408, 44, 405,
    409, 413, 415, 29, 24, 23, 26, 101, 97, 88, 167, 55, 7, 4, 1, 2, 89, 126, 113, 19,
    16, 14, 67, 40, 37, 35, 90, 108, 112, 30, 27, 25, 34, 68, 102, 98, 51, 48, 91, 46,
    94, 45, 8, 5, 62, 59, 146, 56, 141, 137, 128, 20, 17, 3, 166, 107, 130, 41, 38, 36,
    57, 92, 21, 418, 31, 28, 82, 78, 103, 99, 419, 74, 422, 423, 52, 133, 49, 47, 424, 71,
    95, 142, 138, 32, 420, 421, 161, 157, 427, 148, 9, 6, 150, 131, 430, 63, 60, 58, 153, 181,
    168, 177, 428, 431, 170, 93, 134, 122, 118, 111, 114, 429, 10, 417, 42, 39, 426, 83, 75, 79,
    162, 158, 154, 173, 416, 425, 53, 50, 151, 182, 174, 171, 178, 43, 432, 64, 61, 143, 135, 434,
    139, 433, 437, 436, 435, 54, 104, 438, 123, 119, 115, 100, 439, 65, 441, 84, 80, 445, 449, 252,
    250, 251, 163, 155, 461, 253, 254, 159, 105, 457, 144, 140, 183, 175, 440, 453, 230, 85, 232, 231,
    442, 265, 256, 258, 255, 234, 233, 124, 120, 179, 446, 450, 293, 290, 291, 292, 145, 458, 257, 294,
    245, 237, 235, 454, 270, 271, 274, 272, 462, 273, 164, 160, 125, 443, 305, 297, 296, 298, 295, 236,
    184, 180, 447, 455, 311, 314, 313, 312, 310, 285, 276, 459, 277, 165, 463, 278, 451, 332, 334, 266,
    261, 260, 333, 330, 331, 275, 185, 444, 259, 448, 460, 325, 318, 317, 316, 315, 246, 456, 352, 351,
    353, 350, 345, 335, 238, 465, 338, 354, 492, 452, 336, 373, 306, 372, 464, 370, 466, 337, 301, 374,
    371, 468, 365, 358, 355, 286, 300, 469, 357, 281, 483, 299, 485, 267, 356, 385, 467, 346, 339, 262,
    219, 221, 220, 482, 263, 471, 326, 340, 341, 375, 477, 319, 226, 222, 476, 366, 320, 223, 470, 360,
    268, 264, 376, 474, 475, 347, 342, 343, 307, 302, 303, 478, 361, 378, 481, 208, 210, 209, 359, 279,
    472, 473, 327, 322, 323, 377, 480, 197, 198, 199, 321, 241, 227, 224, 269, 479, 215, 211, 212, 348,
    344, 187, 186, 386, 381, 188, 484, 308, 379, 493, 487, 304, 239, 486, 204, 200, 367, 488, 328, 287,
    362, 193, 189, 380, 490, 201, 324, 190, 498, 494, 216, 363, 309, 228, 213, 282, 489, 349, 387, 283,
    499, 491, 205, 202, 247, 243, 280, 225, 242, 368, 382, 364, 383, 194, 240, 329, 191, 217, 214, 495,
    288, 284, 500, 388, 384, 206, 203, 369, 229, 195, 192, 289, 248, 244, 501, 389, 218, 207, 249, 507,
    196, 508, 502, 496, 503, 509, 510, 497, 504, 505, 506, 511, 512, 513,
)


def scratch_of():
    f, h, low = (ROWS, D), (ROWS, LANES), pltpu.VMEM((ROWS, D), BF16)
    halo3 = pltpu.VMEM(((GRID + 2 * HALO) * GRID, SLOTS, D), F32)
    halo1 = pltpu.VMEM(((GRID + 2) * GRID, SLOTS, D), F32)
    high, column, turned = pltpu.VMEM(f, F32), pltpu.VMEM(h, F32), pltpu.VMEM((D, ROWS), BF16)
    taps = pltpu.VMEM((WINDOW * WINDOW, D), F32)
    return dict(
        live=column,
        im8=pltpu.VMEM((IMG_GROUP, SLOTS, LANES), F32),
        im16=pltpu.VMEM((IMG_GROUP, 16, LANES), BF16),
        window=taps,
        rel_taps=taps,
        pos_src=halo1,
        pos_up=halo1,
        rel_src=halo3,
        dq_src=halo3,
        first=high,
        u1=high,
        inv1=column,
        second=high,
        u2=high,
        inv2=column,
        n1=low,
        n1_t=turned,
        n2=low,
        n2_t=turned,
        go=low,
        go_t=turned,
        q=low,
        k=low,
        v=low,
        soft=high,
        soft_low=low,
        soft_acc=pltpu.VMEM((2 * SLOTS, D), F32),
        ctx=pltpu.VMEM((2, WIDE, IMG_GROUP * WIDE), BF16),
        factor=high,
        rel=high,
        mixed=low,
        hidden=high,
        active=low,
        low=low,
        out_low=low,
        back=high,
        gs=high,
        gs_low=low,
        d=high,
        f=low,
        gq=high,
        gk=high,
        gv=high,
        gl=pltpu.VMEM((3, ROWS, D), BF16),
        in_low=low,
    )


class Links:
    def __init__(self):
        dp, head = lax.axis_index(DP), lax.axis_index(HEAD)
        self.far = lax.axis_size(DP) // 4
        self.at = dict(x=head // 2, c=head % 2, h=dp // 4, l=dp // 2 % 2, y=dp % 2)

    def count(self, axis):
        return dict(h=self.far, z=2 * self.far, d=4).get(axis, 2)

    def peer(self, axis, step):
        if axis in "zd":
            one, two = "hl" if axis == "z" else "xy"
            return {one: self.next(one, step // 2), two: self.next(two, step % 2)}
        return {axis: self.next(axis, step)}

    def next(self, axis, step):
        return lax.rem(self.at[axis] + step, self.count(axis))

    def device(self, axis, step):
        at = {**self.at, **self.peer(axis, step)}
        return (at["h"] * 4 + at["l"] * 2 + at["y"], at["x"] * 2 + at["c"])

    def steps(self, axis, do):
        self.repeat(self.count(axis), do, 8)

    def repeat(self, size, do, most):
        if size <= most:
            for step in range(1, size):
                do(step)
        else:

            def body(step, _):
                do(step)
                return 0

            lax.fori_loop(1, size, body, 0)

    def others(self, name, do):
        dp, head, heads = lax.axis_index(DP), lax.axis_index(HEAD), lax.axis_size(HEAD)

        def one(step):
            if name == ALL:
                i = lax.rem(dp * heads + head + step, lax.axis_size(ALL))
                do((i // heads, lax.rem(i, heads)))
            elif name == DP:
                do((lax.rem(dp + step, lax.axis_size(DP)), head))
            else:
                do((dp, lax.rem(head + step, heads)))

        self.repeat(lax.axis_size(name), one, 32)

    def signal(self):
        def one(device):
            pl.semaphore_signal(
                pltpu.get_barrier_semaphore(),
                inc=1,
                device_id=device,
                device_id_type=pl.DeviceIdType.MESH,
            )

        self.others(ALL, one)

    def meet(self):
        pl.semaphore_wait(pltpu.get_barrier_semaphore(), lax.axis_size(ALL) - 1)

    def copy(self, src, dst, send, recv, device):
        return pltpu.make_async_remote_copy(
            src_ref=src,
            dst_ref=dst,
            send_sem=send,
            recv_sem=recv,
            device_id=device,
            device_id_type=pl.DeviceIdType.MESH,
        )

    def region(self, blocks, slot, whole, **at):
        at = {**self.at, **at}
        whole = whole.replace("z", "hl").replace("d", "xy")
        place = [slice(None) if axis in whole else at[axis] for axis in AXES]
        return blocks.at[(*place, slot)]


class Gather:
    def __init__(self, links, w, send, recv):
        self.links, self.w, self.sems = links, w, (send, recv)

    def start(self, slot, i, j):
        path, links = AG_ROUTES[slot], self.links

        def along(whole, at):
            part = links.region(self.w, slot, whole, **at)

            def go(step):
                sems = [s.at[slot, j, (step - 1) % WAYS] for s in self.sems]
                links.copy(part, part, *sems, links.device(path[j], step)).start()

            links.steps(path[j], go)

        if i < 0:
            along("", {})
        elif path[i] == "z" and i == 0:
            along("z", {})
        else:
            links.steps(path[i], lambda step: along(path[:i], links.peer(path[i], step)))

    def waits(self, slot, j, wait):
        path, links = AG_ROUTES[slot], self.links

        def one(step):
            part = links.region(self.w, slot, path[:j], **links.peer(path[j], step))
            sems = [s.at[slot, j, (step - 1) % WAYS] for s in self.sems]
            wait(links.copy(part, part, *sems, links.device(path[j], step)))

        links.steps(path[j], one)

    def arrive(self, slot, j):
        self.waits(slot, j, lambda copy: copy.wait_recv())

    def sent(self):
        for slot, path in enumerate(AG_ROUTES):
            for j in range(len(path)):
                self.waits(slot, j, lambda copy: copy.wait_send())

    def steps(self):
        for slot, path in enumerate(AG_ROUTES):
            for j in range(len(path)):
                for i in range(-1, j):
                    if path[0] != "z" or j == 0 or i >= 0:
                        yield functools.partial(self.start, slot, i, j)
            for j in range(len(path)):
                yield functools.partial(self.arrive, slot, j)


class Scatter:
    def __init__(self, links, g, boxes, total, send, recv):
        self.links, self.g, self.boxes, self.total = links, g, boxes, total
        self.sems = (send, recv)

    def box(self, slot, j):
        return self.boxes[slot * len(AXES) + j - 1]

    def merged(self, slot, j):
        path = RS_ROUTES[slot]
        return path[-1] == "z" and j == len(path) - 1

    def start(self, slot, i, j):
        path, links = RS_ROUTES[slot], self.links
        first = sum(links.count(a) - 1 for a in path[:i]) - 1
        skip = first + 1 if path[-1] == "z" and j == len(path) else 0

        def go(step):
            entry = first + step - skip
            sems = (
                self.sems[0].at[slot, i, (first + step) % ENTRIES],
                self.sems[1].at[slot, j - 1, entry % ENTRIES],
            )
            into = self.box(slot, j).at[entry]
            device = links.device(path[i], step)

            def part(into, whole, more):
                src = links.region(self.g, slot, whole, **links.peer(path[i], step), **more)
                links.copy(src, into, *sems, device).start()

            if j == len(path) or self.merged(slot, j):
                part(into, path[j:], {})
            else:
                links.steps(
                    path[j], lambda n: part(into.at[n - 1], path[j + 1 :], links.peer(path[j], n))
                )

        links.steps(path[i], go)

    def add(self, slot, j):
        path, links = RS_ROUTES[slot], self.links
        box = self.box(slot, j)
        for e in range(box.shape[0]):
            self.entry(slot, j, e, (0, j - 1), box.at[e]).wait_recv()

        def total(own, pick):
            value = own[...].astype(F32)
            for e in range(box.shape[0]):
                value = value + pick(box.at[e])[...].astype(F32)
            return value

        if j == len(path):
            own = links.region(self.g, slot, "")
            self.total[SLOT_OF.index(slot)] = total(own, lambda b: b)
            return

        def one(n):
            own = links.region(self.g, slot, path[j + 1 :], **links.peer(path[j], n))
            own[...] = total(own, lambda b: b.at[n - 1]).astype(BF16)

        if self.merged(slot, j):
            own = links.region(self.g, slot, "z")
            own[...] = total(own, lambda b: b).astype(BF16)
        else:
            links.steps(path[j], one)

    def entry(self, slot, j, e, places, ref):
        sems = [s.at[slot, n, e % ENTRIES] for s, n in zip(self.sems, places)]
        return self.links.copy(ref, ref, *sems, self.links.device("c", 1))

    def sent(self):
        for slot, path in enumerate(RS_ROUTES):
            for i in range(len(path)):
                first = sum(self.links.count(a) - 1 for a in path[:i]) - 1

                def one(step):
                    part = self.links.region(
                        self.g, slot, path[i + 1 :], **self.links.peer(path[i], step)
                    )
                    self.entry(slot, i, first + step, (i, 0), part).wait_send()

                self.links.steps(path[i], one)

    def steps(self):
        for slot, path in enumerate(RS_ROUTES):
            for i in range(len(path)):
                for j in range(i + 1, len(path) + 1):
                    if not (path[-1] == "z" and j == len(path) and i + 1 < len(path)):
                        yield functools.partial(self.start, slot, i, j)
            for j in range(1, len(path) + 1):
                yield functools.partial(self.add, slot, j)


class Small:
    def __init__(self, links, sums, parts, in_c, in_x, in_y, in_h, in_l, full, send, recv):
        self.links, self.sums, self.parts, self.full = links, sums, parts, full
        self.in_c, self.in_x, self.in_y, self.in_h, self.in_l = in_c, in_x, in_y, in_h, in_l
        self.send, self.recv = send, recv

    def go(self, stage, src, dst, axis):
        sems = (self.send.at[stage], self.recv.at[stage])
        self.links.steps(
            axis, lambda step: self.links.copy(src, dst, *sems, self.links.device(axis, step)).start()
        )

    def wait(self, stage):
        x, c = self.links.at["x"], self.links.at["c"]
        ref = (
            self.in_c,
            self.in_x,
            self.in_y,
            self.in_h.at[pl.ds(0, self.links.far - 1)],
            self.in_l,
            self.full.at[c, x],
            self.full.at[c],
        )[stage]
        sems = (self.send.at[stage], self.recv.at[stage])
        return self.links.copy(ref, ref, *sems, self.links.device("cxyhlxc"[stage], 1))

    def tick(self, stage):
        at = self.links.at
        x, c, h = at["x"], at["c"], at["h"]
        mine = self.parts.at[c, x]
        if stage:
            self.wait(stage - 1).wait_recv()
        if stage == 0:
            for b in range(D // LANES):
                self.parts[b // 2, b % 2] = self.sums[:, b * LANES : (b + 1) * LANES]
            self.go(0, self.parts.at[1 - c], self.in_c, "c")
        if stage == 1:
            self.parts[c] = self.parts[c] + self.in_c[...]
            self.go(1, self.parts.at[c, 1 - x], self.in_x, "x")
        if stage == 2:
            mine[...] = mine[...] + self.in_x[...]
            self.go(2, mine, self.in_y, "y")
        if stage == 3:
            self.in_h[h] = mine[...] + self.in_y[...]
            self.go(3, self.in_h.at[h], self.in_h.at[h], "h")
        if stage == 4:
            total = self.in_h[0]
            for i in range(1, self.links.far):
                total = total + self.in_h[i]
            self.sums[:, 0:LANES] = total
            self.go(4, self.sums.at[:, pl.ds(0, LANES)], self.in_l, "l")
        if stage == 5:
            self.full[c, x] = self.sums[:, 0:LANES] + self.in_l[...]
            self.go(5, self.full.at[c, x], self.full.at[c, x], "x")
        if stage == 6:
            self.go(6, self.full.at[c], self.full.at[c], "c")

    def sent(self):
        for stage in range(7):
            self.wait(stage).wait_send()


class Rows:
    def __init__(self, links, blocks, out, own, send, recv):
        self.links, self.blocks, self.out, self.own = links, blocks, out, own
        self.send, self.recv = send, recv

    def hop(self, i):
        x, c = self.links.at["x"], self.links.at["c"]
        x, axis = ((x, "x"), (x, "c"), (1 - x, "c"))[i]
        block = self.blocks.at[2 * x + c]
        return self.links.copy(
            block, block, self.send.at[i], self.recv.at[i], self.links.device(axis, 1)
        )

    def tick(self, stage):
        if stage == 0:
            self.hop(0).start()
            self.hop(1).start()
        if stage == 1:
            self.hop(0).wait_recv()
            self.hop(2).start()
        if stage == 2:
            self.hop(1).wait_recv()
            self.hop(2).wait_recv()
            self.join()

    def sent(self):
        for i in range(3):
            self.hop(i).wait_send()

    def join(self):
        heads, end, own = self.blocks.shape[0], self.out.shape[0], self.own
        for h in range(heads):
            lo, hi = h * own, (h + 1) * own
            base = lo // 16 * 16
            first = base + 16 if lo % 16 else base
            last = hi // 16 * 16 if h + 1 < heads else end
            self.out[first:last, :] = self.blocks[h, first - base : last - base, :]
            if lo % 16:
                before = (lo - own) // 16 * 16
                tail = self.blocks[h - 1, base - before : base - before + 16, :]
                self.out[base : base + 16, :] = tail + self.blocks[h, 0:16, :]


class Exchange:
    def __init__(self, links, name, buffer, send, recv):
        self.links, self.name, self.buffer, self.send, self.recv = links, name, buffer, send, recv

    def start(self, value):
        own = lax.axis_index(self.name)
        self.buffer[own] = value
        mine = self.buffer.at[own]
        self.links.others(
            self.name,
            lambda device: self.links.copy(mine, mine, self.send, self.recv, device).start(),
        )

    def descriptor(self):
        ref = self.buffer.at[pl.ds(0, self.buffer.shape[0] - 1)]
        return self.links.copy(ref, ref, self.send, self.recv, self.links.device("c", 1))

    def total(self):
        self.descriptor().wait_recv()
        return jnp.sum(self.buffer[...], axis=0)

    def sent(self):
        self.descriptor().wait_send()


def exact(a, b, dims):
    return lax.dot_general(
        a, b, dims, precision=lax.Precision.HIGHEST, preferred_element_type=F32
    )


class Adafactor:
    def __init__(self, refs, lo, hi, row_share, col_share, sq_share):
        self.__dict__.update(refs)
        self.lo, self.hi = lo, hi
        self.row_share, self.col_share, self.sq_share = row_share, col_share, sq_share

    def eye(self, count, first):
        r = lax.broadcasted_iota(jnp.int32, (count, LANES), 0)
        c = lax.broadcasted_iota(jnp.int32, (count, LANES), 1)
        return jnp.where(c == r + first, 1.0, 0.0)

    def lane(self, k, value, rest):
        lanes = lax.broadcasted_iota(jnp.int32, rest.shape, 1)
        return jnp.where(lanes == k, value, rest)

    def squares(self):
        rows, count = self.wg.shape[1], self.hi - self.lo
        by_row = jnp.zeros((rows, LANES), F32)
        by_col = []
        for k in range(self.lo, self.hi):
            g = self.wg[k]
            s = g * g + SQUARE_FLOOR
            by_row = self.lane(k, jnp.sum(s, axis=1, keepdims=True), by_row)
            by_col.append(jnp.sum(s, axis=0, keepdims=True))
        rest = jnp.zeros((SLOTS - count, LANES), F32)
        self.col_share.start(jnp.concatenate([*by_col, rest] if count < SLOTS else by_col, axis=0))
        turned = exact(self.eye(SLOTS, self.lo), by_row, NT)
        if rows < LANES:
            turned = jnp.concatenate([turned, jnp.zeros((SLOTS, LANES - rows), F32)], axis=1)
        self.row_share.start(turned)

    def scale(self):
        rows, lo, hi = self.wg.shape[1], self.lo, self.hi
        total = self.row_share.total()[0 : hi - lo, 0:rows]
        new_rows = SECOND_DECAY * self.row_state[lo:hi, :] + (1.0 - SECOND_DECAY) * (
            total * (1.0 / D)
        )
        self.new_rows[lo:hi, :] = new_rows
        row = exact(new_rows, self.eye(hi - lo, lo), TN)
        total = self.col_share.total()[0 : hi - lo]
        cols = SECOND_DECAY * self.col_state[lo:hi, :] + (1.0 - SECOND_DECAY) * (
            total * (1.0 / D)
        )
        self.new_cols[lo:hi, :] = cols
        sums = jnp.zeros((1, LANES), F32)
        for k in range(lo, hi):
            u = self.wg[k] * lax.rsqrt(row[:, k : k + 1] * cols[k - lo : k - lo + 1, :])
            self.upd[k] = u
            s = jnp.sum(jnp.sum(u * u, axis=0, keepdims=True), axis=1, keepdims=True)
            sums = self.lane(k, s, sums)
        mass = jnp.sum(row, axis=0, keepdims=True)
        self.sq_share.start(jnp.concatenate([sums, mass], axis=0))

    def rates(self):
        total = self.sq_share.total()
        mean = total[1:2] * (1.0 / (D * lax.axis_size(HEAD)))
        rms = jnp.sqrt(total[0:1] * mean * (1.0 / (D * D)))
        rate = STEP_RATE * jnp.sqrt(mean) / jnp.maximum(1.0, rms)
        lanes = lax.broadcasted_iota(jnp.int32, (1, LANES), 1)
        mine = (lanes >= self.lo) & (lanes < self.hi)
        self.clip[0:1, :] = jnp.where(mine, rms, self.clip[0:1, :])
        self.clip[1:2, :] = jnp.where(mine, rate, self.clip[1:2, :])


class SmallStep:
    def __init__(self, refs):
        self.__dict__.update(refs)

    def small_step(self):
        count, full = self.small.shape[0], self.full
        g = jnp.concatenate([full[b // 2, b % 2, 0:count, :] for b in range(D // LANES)], axis=1)
        self.small_grads[...] = g
        state = SECOND_DECAY * self.small_state[...] + (1.0 - SECOND_DECAY) * (
            g * g + SQUARE_FLOOR
        )
        self.new_small_state[...] = state
        u = g * lax.rsqrt(state)
        rms = jnp.sqrt(jnp.sum(u * u, axis=1, keepdims=True) * (1.0 / D))
        new = self.small[...] - SMALL_RATE * u / jnp.maximum(1.0, rms)
        self.new_small[...] = new
        self.new_small_ema[...] = AVERAGE_KEEP * self.small_ema[...] + (1.0 - AVERAGE_KEEP) * new
        r = lax.broadcasted_iota(jnp.int32, (count, LANES), 0)
        c = lax.broadcasted_iota(jnp.int32, (count, LANES), 1)
        picked = jnp.where(c == r + MATS, rms, 0.0)
        small = jnp.sum(picked, axis=0, keepdims=True)
        lanes = lax.broadcasted_iota(jnp.int32, (1, LANES), 1)
        self.clip[0:1, :] = jnp.where(lanes < MATS, self.clip[0:1, :], small)


class Inputs(NamedTuple):
    cls: Any
    img: Any
    tokens: Any
    cot: Any
    weights: Any
    row_state: Any
    col_state: Any
    small: Any
    small_state: Any
    small_ema: Any


class Outputs(NamedTuple):
    out: Any
    grad_in: Any
    wg: Any
    new_rows: Any
    new_cols: Any
    small_grads: Any
    new_small_state: Any
    new_small: Any
    new_small_ema: Any
    upd: Any
    clip: Any


def box_shapes(links, block):
    for path in RS_ROUTES:
        for j in range(1, len(AXES) + 1):
            entries = sum(links.count(a) - 1 for a in path[:j])
            if j > len(path):
                shape = (1, SLOTS, LANES)
            elif j == len(path):
                first = links.count("z") - 1 if path[-1] == "z" else entries
                shape = (first, *block)
            elif path[-1] == "z" and j == len(path) - 1:
                shape = (entries, links.count("h"), links.count("l"), *block)
            else:
                rest = path[j + 1 :].replace("z", "hl").replace("d", "xy")
                rest = [links.count(a) for a in AXES if a in rest]
                shape = (entries, links.count(path[j]) - 1, *rest, *block)
            yield pltpu.VMEM(shape, BF16)


def shared_of(weights, parts, heads):
    links, (_, rows, _) = Links(), weights.shape
    block = (rows, LANES)
    every = pltpu.VMEM((2, 2, links.far, 2, 2, MATS, *block), BF16)
    out_rows = pltpu.VMEM((heads, HEAD_ROWS, D), BF16)
    dma = pltpu.SemaphoreType.DMA

    def f(*shape):
        return pltpu.VMEM(shape, F32)

    part = f(SMALL_ROWS, LANES)
    return dict(
        w=every,
        g=every,
        out_rows=out_rows,
        in_rows=out_rows,
        sums=f(SMALL_ROWS, D),
        parts=f(2, 2, SMALL_ROWS, LANES),
        in_c=f(2, SMALL_ROWS, LANES),
        in_x=part,
        in_y=part,
        in_h=f(links.far, SMALL_ROWS, LANES),
        in_l=part,
        full=f(2, 2, SMALL_ROWS, LANES),
        row_box=f(2, heads, SLOTS, LANES),
        col_box=f(2, parts, SLOTS, LANES),
        sq_box=f(2, parts * heads, 2, LANES),
        ag_send=dma((MATS, len(AXES), WAYS)),
        ag_recv=dma((MATS, len(AXES), WAYS)),
        rs_send=dma((MATS, len(AXES), ENTRIES)),
        rs_recv=dma((MATS, len(AXES), ENTRIES)),
        small_send=dma((7,)),
        small_recv=dma((7,)),
        out_send=dma((3,)),
        out_recv=dma((3,)),
        in_send=dma((3,)),
        in_recv=dma((3,)),
        opt_send=dma((2, 3)),
        opt_recv=dma((2, 3)),
        fetched=dma((len(Inputs._fields),)),
        stored=dma((len(Outputs._fields),)),
    )


class Ready:
    def __init__(self, src, dst, sem):
        self.copy = pltpu.make_async_copy(src, dst, sem)
        self.start, self.wait = self.copy.start, self.copy.wait


def then(*steps):
    def run():
        for step in steps:
            step()

    return run


def block_kernel(names, *refs):
    n_in, n_out = len(Inputs._fields), len(Outputs._fields)
    ins, outs, refs = Inputs(*refs[:n_in]), Outputs(*refs[n_in : n_in + n_out]), refs[n_in + n_out :]
    r = types.SimpleNamespace(**dict(zip(names, refs)))
    fetch = Inputs(
        *[
            Ready(ref, getattr(r, name), r.fetched.at[i])
            for i, (name, ref) in enumerate(zip(Inputs._fields, ins))
        ]
    )
    store = Outputs(
        *[
            Ready(getattr(r, name), ref, r.stored.at[i])
            for i, (name, ref) in enumerate(zip(Outputs._fields, outs))
        ]
    )
    boxes = refs[len(names) :]
    links = Links()
    links.signal()
    for one in (fetch.weights, *fetch[0:2], fetch.small, *fetch[2:4], *fetch[5:7], *fetch[8:]):
        one.start()
    r.out_own = r.out_rows.at[lax.axis_index(HEAD)]
    r.in_own = r.in_rows.at[lax.axis_index(HEAD)]
    own = r.cls.shape[1] * CELLS
    blk = Block(vars(r))
    gather = Gather(links, r.w, r.ag_send, r.ag_recv)
    scatter = Scatter(links, r.g, boxes, r.wg, r.rs_send, r.rs_recv)
    small = Small(
        links,
        *(r.sums, r.parts, r.in_c, r.in_x, r.in_y, r.in_h, r.in_l, r.full),
        r.small_send,
        r.small_recv,
    )
    out_rows = Rows(links, r.out_rows, r.out, own, r.out_send, r.out_recv)
    in_rows = Rows(links, r.in_rows, r.grad_in, own, r.in_send, r.in_recv)
    shares, opts = [], []
    for part, (lo, hi) in enumerate(((0, EARLY), (EARLY, MATS))):
        boxes = (HEAD, r.row_box), (DP, r.col_box), (ALL, r.sq_box)
        shares += [
            Exchange(links, axis, box.at[part], r.opt_send.at[part, i], r.opt_recv.at[part, i])
            for i, (axis, box) in enumerate(boxes)
        ]
        opts.append(Adafactor(vars(r), lo, hi, *shares[-3:]))
    step = SmallStep(vars(r))

    def round_weights():
        r.clip[...] = jnp.zeros(r.clip.shape, F32)
        for k in range(MATS):
            mine = links.region(r.w, SLOT_OF[k], "")
            mine[...] = r.weights[k].astype(BF16)

    ops = [*gather.steps(), *scatter.steps()]
    ops += [then(fetch.weights.wait, round_weights), links.meet]
    ops += [then(fetch.small.wait, fetch.cls.wait, fetch.img.wait, blk.setup)]
    ops += [fetch.tokens.wait, fetch.cot.wait]

    def each(step, *ranges):
        for place in itertools.product(*map(range, ranges)):
            ops.append(functools.partial(step, *place))

    each(blk.read_tokens, PIECES)
    each(blk.position, D // LANES)
    each(blk.norm_one, PIECES)
    ops.append(blk.turn_one)
    each(blk.read_cotangent, PIECES)
    ops.append(blk.turn_cotangent)
    each(blk.project, 3, 2)
    ops += [blk.key_tops, blk.key_powers, blk.key_shares]
    each(blk.contexts, 2)
    ops.append(blk.fill_window)
    each(blk.window_sum, D // LANES)
    ops.append(blk.mix)
    each(blk.attend, 2)
    each(blk.norm_two, PIECES)
    ops.append(blk.turn_two)
    each(blk.hidden_in, 4)
    each(blk.hidden_out, 4)
    each(blk.grad_down, 4)
    each(blk.grad_up, 4)
    each(blk.add_down, 4)
    each(blk.add_back, 4)
    ops += [blk.finish_out, blk.back_two, blk.grad_proj, blk.back_mixed, blk.back_fill]
    each(blk.back_heads, 2)
    ops += [blk.back_inner, blk.back_query_key]
    each(blk.back_window, D // LANES)
    ops.append(blk.back_value)
    each(blk.grad_of, 3)
    each(blk.window_taps, D // LANES)
    each(blk.back_project, 2)
    ops += [blk.back_one, blk.back_position, blk.position_taps, blk.finish_in]
    for rows, done in ((out_rows, store.out), (in_rows, store.grad_in)):
        ops += [functools.partial(rows.tick, stage) for stage in range(2)]
        ops += [then(functools.partial(rows.tick, 2), done.start)]
    ops += [functools.partial(small.tick, stage) for stage in range(8)]
    ops += [
        then(
            fetch.small_state.wait,
            fetch.small_ema.wait,
            step.small_step,
            store.small_grads.start,
            store.new_small_state.start,
            store.new_small.start,
            store.new_small_ema.start,
        ),
        opts[1].squares,
        then(store.wg.start, opts[0].squares),
        then(fetch.row_state.wait, fetch.col_state.wait, opts[1].scale),
        then(opts[0].scale, store.upd.start, store.new_rows.start, store.new_cols.start),
        opts[1].rates,
        opts[0].rates,
        store.clip.start,
    ]
    for i in ORDER:
        ops[i]()
    for transfer in (gather, scatter, small, out_rows, in_rows, *shares):
        transfer.sent()
    for one in store:
        one.wait()


PASSED = 9


def finish_kernel(*refs):
    count = PASSED + 4
    ins, outs, held = refs[:count], refs[count : 2 * count], refs[2 * count : 3 * count]
    new_weights, low, new_ema, clips, took, gave = refs[3 * count :]
    upd, clip, weights, ema = held[PASSED:]
    come = [pltpu.make_async_copy(a, b, took.at[i]) for i, (a, b) in enumerate(zip(ins, held))]
    leave = [*held[:5], new_weights, low, new_ema, *held[5:PASSED], clips]
    leave = [pltpu.make_async_copy(a, b, gave.at[i]) for i, (a, b) in enumerate(zip(leave, outs))]
    for one in come[::-1]:
        one.start()
    for one in come[PASSED:]:
        one.wait()
    for k in range(weights.shape[0]):
        new = weights[k] - clip[1:2, k : k + 1] * upd[k]
        new_weights[k] = new
        low[k] = new.astype(BF16)
        new_ema[k] = AVERAGE_KEEP * ema[k] + (1.0 - AVERAGE_KEEP) * new
    clips[...] = clip[0:1, 0 : clips.shape[1]]
    for i in (5, 6, 7, count - 1):
        leave[i].start()
    for i in range(PASSED):
        come[i].wait()
        leave[i if i < 5 else i + 3].start()
    for one in leave:
        one.wait()


def local(
    tokens,
    cotangent,
    crop_image,
    crop_class,
    weights,
    row_state,
    col_state,
    weights_ema,
    small_params,
    small_state,
    small_ema,
):
    parts, heads = lax.axis_size(DP), lax.axis_size(HEAD)
    shared = shared_of(weights, parts, heads)
    own = scratch_of()

    def like(x, dtype=None):
        return jax.ShapeDtypeStruct(x.shape, dtype or x.dtype)

    clips = weights.shape[0] + small_params.shape[0]
    passed = (
        *[like(x) for x in (tokens, tokens, weights, row_state, col_state)],
        *[like(small_params)] * 4,
    )
    middle = (*passed, like(weights), jax.ShapeDtypeStruct((2, LANES), F32))
    stepped = (like(weights), like(weights, BF16), like(weights))
    last = jax.ShapeDtypeStruct((1, clips), F32)
    outs = (*passed[:5], *stepped, *passed[5:], last)
    args = Inputs(
        crop_class,
        crop_image,
        tokens,
        cotangent,
        weights,
        row_state,
        col_state,
        small_params,
        small_state,
        small_ema,
    )
    staged = [pltpu.SMEM(x.shape, x.dtype) for x in args[:2]]
    staged += [pltpu.VMEM(x.shape, x.dtype) for x in (*args[2:], *middle)]
    names = (*shared, *own, *Inputs._fields, *Outputs._fields)
    far = pl.BlockSpec(memory_space=pltpu.HBM)
    res = pl.pallas_call(
        functools.partial(block_kernel, names),
        out_shape=middle,
        in_specs=[far] * len(args),
        out_specs=(far,) * len(middle),
        scratch_shapes=[
            *shared.values(),
            *own.values(),
            *staged,
            *box_shapes(Links(), weights.shape[1:]),
        ],
        compiler_params=pltpu.CompilerParams(
            collective_id=0, has_side_effects=True, vmem_limit_bytes=63 << 20
        ),
        name="block",
    )(*args)
    ins = (*res, weights, weights_ema)
    kept = [pltpu.VMEM(x.shape, x.dtype) for x in (*middle, weights, weights_ema, *stepped, last)]
    res = pl.pallas_call(
        finish_kernel,
        out_shape=outs,
        in_specs=[far] * len(ins),
        out_specs=(far,) * len(outs),
        scratch_shapes=[*kept, *[pltpu.SemaphoreType.DMA((len(outs),))] * 2],
        compiler_params=pltpu.CompilerParams(vmem_limit_bytes=63 << 20),
        name="finish",
    )(*ins)
    return (*res[:-1], res[-1].reshape(clips))


def solution(mesh):
    in_specs = (
        P(DP, None),
        P(DP, None),
        P(DP, None),
        P(DP, None),
        P(None, DP, HEAD),
        P(None, DP),
        P(None, HEAD),
        P(None, DP, HEAD),
        P(),
        P(),
        P(),
    )
    out_specs = (
        P(DP, None),
        P(DP, None),
        P(None, DP, HEAD),
        P(None, DP),
        P(None, HEAD),
        P(None, DP, HEAD),
        P(None, DP, HEAD),
        P(None, DP, HEAD),
        P(),
        P(),
        P(),
        P(),
        P(),
    )
    return jax.shard_map(local, mesh=mesh, in_specs=in_specs, out_specs=out_specs, check_vma=False)
```

```python
import functools
import itertools
import math
import types
from typing import Any, NamedTuple

import jax
import jax.numpy as jnp
from jax import lax
from jax.experimental import pallas as pl
from jax.experimental.pallas import tpu as pltpu
from jax.sharding import PartitionSpec as P

DP, HEAD = "dp", "head"
ALL = (DP, HEAD)
D = 512
HEAD_DIM = 64
GRID = 7
SMALL_GRID = 3
WINDOW = 7
IMG_GROUP = 3
CELLS = GRID * GRID
SLOTS = 8
CELL_PAD = CELLS + 1
ROWS = CELL_PAD * SLOTS
PIECES = 5
PIECE = ROWS // PIECES
LANES = 128
WIDE = 256
REACHES = (1, 2, 3, 3)
HALO = WINDOW // 2

NORM_EPS = 1e-06
SQUARE_FLOOR = 1e-30
SECOND_DECAY = 0.999
STEP_RATE = 0.02
SMALL_RATE = 0.05
AVERAGE_KEEP = 0.9
NEG_LARGE = -1e30
ROOT_HALF = 0.7071067811865476
INV_ROOT_TAU = 0.3989422804014327
INV_SCALE = 1.0 / math.sqrt(HEAD_DIM)

F32 = jnp.float32
BF16 = jnp.bfloat16
NN = (((1,), (0,)), ((), ()))
NT = (((1,), (1,)), ((), ()))
TN = (((0,), (0,)), ((), ()))


def dot(a, b, dims=NN):
    return lax.dot_general(a, b, dims, preferred_element_type=F32)


def lane_block(b):
    return slice(b * WIDE, (b + 1) * WIDE)


def wide(col):
    return jnp.concatenate([col] * (D // LANES), axis=1)


def rows_loop(count, size, body, init=None, unroll=1):
    def step(j, carry):
        return body(pl.multiple_of(j * size, size), carry)

    return lax.fori_loop(0, count // size, step, init, unroll=unroll)


def piece_loop(piece, body):
    def step(j, carry):
        body(pl.multiple_of(piece * PIECE + j * 16, 16))
        return carry

    lax.fori_loop(0, PIECE // 16, step, 0, unroll=5)


def conv(src, halo, tap, reach, lanes, put):
    def line(y, _):
        sums = [jnp.zeros((SLOTS, LANES), F32) for _ in range(GRID)]
        for a in range(-reach, reach + 1):
            base = (y + (a + halo)) * GRID
            cells = [src[base + x, :, lanes] for x in range(GRID)]
            for b in range(-reach, reach + 1):
                t = tap(a, b)
                for x in range(GRID):
                    if 0 <= x + b < GRID:
                        sums[x] = sums[x] + t * cells[x + b]
        for x in range(GRID):
            put(y * GRID + x, sums[x])
        return 0

    lax.fori_loop(0, GRID, line, 0)


def tap_sums(up, src, halo, reach, lanes, put):
    for a in range(-reach, reach + 1):

        def line(y, sums):
            sums = list(sums)
            ups = [up(y * GRID + x) for x in range(GRID)]
            base = (y + (a + halo)) * GRID
            cells = [src[base + x, :, lanes] for x in range(GRID)]
            for i, b in enumerate(range(-reach, reach + 1)):
                for x in range(GRID):
                    if 0 <= x + b < GRID:
                        sums[i] = sums[i] + ups[x] * cells[x + b]
            return tuple(sums)

        start = tuple(jnp.zeros((SLOTS, LANES), F32) for _ in range(2 * reach + 1))
        sums = lax.fori_loop(0, GRID, line, start)
        for i, b in enumerate(range(-reach, reach + 1)):
            put(a, b, jnp.sum(sums[i], axis=0, keepdims=True))


def fold(x):
    return jnp.sum(x.reshape(x.shape[0] // SLOTS, SLOTS, x.shape[1]), axis=0)


def erf_parts(h):
    e = lax.erf(h * ROOT_HALF)
    half = 0.5 * (1.0 + e)
    return h * half, half + h * jnp.exp(-0.5 * h * h) * INV_ROOT_TAU


def norm_rows(v, gain, shift):
    centre = jnp.sum(v, axis=1, keepdims=True) * (1.0 / D)
    offset = v - centre
    spread = jnp.sum(offset * offset, axis=1, keepdims=True) * (1.0 / D)
    inverse = lax.rsqrt(spread + NORM_EPS)
    unit = offset * inverse
    return unit * gain + shift, unit, inverse


def norm_back(up, unit, inverse, gain):
    z = up * gain
    mean_z = jnp.sum(z, axis=1, keepdims=True) * (1.0 / D)
    mean_zu = jnp.sum(z * unit, axis=1, keepdims=True) * (1.0 / D)
    return inverse * (z - mean_z - unit * mean_zu)


class Block:
    def __init__(self, refs):
        self.__dict__.update(refs)

    def matrix(self, k, lo, hi):
        parts = []
        for h in range(lo, hi):
            part = self.w[h // 2, h % 2, :, :, :, k]
            if part.shape[-2] % 16:
                part = part.astype(F32).reshape(D, LANES).astype(BF16)
            else:
                part = part.reshape(D, LANES)
            parts.append(part)
        return jnp.concatenate(parts, axis=1)

    def times(self, lhs, k, b):
        return dot(lhs, self.matrix(k, 2 * b, 2 * b + 2))

    def times_t(self, lhs, k, b):
        return dot(lhs, self.matrix(k, 0, 4)[lane_block(b), :], NT)

    def put_grad(self, k, lhs_t, rhs):
        for b in range(2):
            g = dot(lhs_t, rhs[:, lane_block(b)])
            for i in range(2):
                piece = g[:, i * LANES : (i + 1) * LANES]
                place = self.g.shape[2:5]
                piece = piece.reshape(*place, self.g.shape[-2], LANES)
                self.g[b, i, :, :, :, k] = piece.astype(BF16)

    def row(self, j):
        return self.small[j : j + 1, :]

    def setup(self):
        head = lax.axis_index(HEAD)
        slots = self.cls.shape[1]
        self.sums[...] = jnp.zeros(self.sums.shape, F32)
        sub = lax.broadcasted_iota(jnp.int32, (SLOTS, LANES), 0)
        valid = jnp.where(sub < slots, 1.0, 0.0)
        full = jnp.zeros((SLOTS, LANES), F32)
        images = [jnp.zeros((SLOTS, LANES), F32) for _ in range(IMG_GROUP)]
        for s in range(slots):
            full = jnp.where(sub == s, jnp.where(self.cls[head, s] == 0, 1.0, 0.0), full)
            for i in range(IMG_GROUP):
                images[i] = jnp.where(
                    sub == s, jnp.where(self.img[head, s] == i, 1.0, 0.0), images[i]
                )
        for cell in range(CELLS):
            small = cell // GRID < SMALL_GRID and cell % GRID < SMALL_GRID
            self.live[cell * SLOTS : (cell + 1) * SLOTS, :] = valid if small else full
        self.live[CELLS * SLOTS :, :] = jnp.zeros((SLOTS, LANES), F32)
        for i in range(IMG_GROUP):
            self.im8[i] = images[i]
            self.im16[i] = jnp.concatenate([images[i], images[i]], axis=0).astype(BF16)
        self.pos_src[0:GRID] = jnp.zeros((GRID, SLOTS, D), F32)
        self.pos_src[GRID + CELLS :] = jnp.zeros((GRID, SLOTS, D), F32)
        for pad in (self.rel_src, self.dq_src):
            pad[0 : HALO * GRID] = jnp.zeros((HALO * GRID, SLOTS, D), F32)
            pad[HALO * GRID + CELLS :] = jnp.zeros((HALO * GRID, SLOTS, D), F32)
        tap = lax.broadcasted_iota(jnp.int32, (WINDOW * WINDOW, 1), 0)
        row_off = jnp.abs(tap // WINDOW - HALO)
        col_off = jnp.abs(tap % WINDOW - HALO)
        off = jnp.maximum(row_off, col_off)
        heads = lax.broadcasted_iota(jnp.int32, (1, D), 1) // HEAD_DIM
        reach = jnp.where(heads < 2, 1, jnp.where(heads < 5, 2, 3))
        mask = jnp.where(off <= reach, 1.0, 0.0)
        self.window[...] = mask
        self.rel_taps[...] = self.small[22 : 22 + WINDOW * WINDOW, :] * mask

    def place(self, rows_ref, first, r0, size):
        count = rows_ref.shape[0]
        r = r0 + lax.broadcasted_iota(jnp.int32, (size, 1), 0)
        cell, slot = r >> 3, r & 7
        want = first + slot * CELLS + cell
        want = jnp.where((slot < self.cls.shape[1]) & (cell < CELLS), want, -1)
        col = lax.broadcasted_iota(jnp.int32, (size, count), 1)
        pick = jnp.where(col == want, 1.0, 0.0).astype(BF16)
        return dot(pick, rows_ref[...])

    def unplace(self, src_ref, out_ref):
        count = out_ref.shape[0]
        own = self.cls.shape[1] * CELLS
        lead = lax.rem(lax.axis_index(HEAD) * own, 16)
        r = lax.broadcasted_iota(jnp.int32, (1, ROWS), 1)
        cell, slot = r >> 3, r & 7
        target = lead + slot * CELLS + cell
        target = jnp.where((slot < self.cls.shape[1]) & (cell < CELLS), target, -1)
        t = lax.broadcasted_iota(jnp.int32, (count, ROWS), 0)
        pick = jnp.where(t == target, 1.0, 0.0).astype(BF16)
        out_ref[...] = dot(pick, src_ref[...]).astype(BF16)

    def read_tokens(self, piece):
        first = lax.axis_index(HEAD) * (self.cls.shape[1] * CELLS)
        r0 = piece * PIECE
        rows = slice(r0, r0 + PIECE)
        x = self.place(self.tokens, first, r0, PIECE)
        self.first[rows, :] = x
        cells = slice(GRID + r0 // SLOTS, GRID + (r0 + PIECE) // SLOTS)
        self.pos_src[cells] = (x * wide(self.live[rows, :])).reshape(-1, SLOTS, D)

    def read_cotangent(self, piece):
        first = lax.axis_index(HEAD) * (self.cls.shape[1] * CELLS)
        rows = slice(piece * PIECE, (piece + 1) * PIECE)
        c = self.place(self.cot, first, piece * PIECE, PIECE)
        self.go[rows, :] = (c * wide(self.live[rows, :])).astype(BF16)

    def turn_cotangent(self):
        self.go_t[...] = self.go[...].T
        self.back[...] = jnp.zeros((ROWS, D), F32)

    def position(self, c):
        lanes = slice(c * LANES, (c + 1) * LANES)

        def put(cell, value):
            rows = pl.ds(pl.multiple_of(cell * SLOTS, SLOTS), SLOTS)
            self.first[rows, lanes] = self.first[rows, lanes] + value + self.small[8:9, lanes]

        def tap(a, b):
            t = 13 + (a + 1) * 3 + b + 1
            return self.small[t : t + 1, lanes]

        conv(self.pos_src, 1, tap, 1, lanes, put)

    def norm_one(self, piece):
        def body(r0):
            rows = pl.ds(r0, 16)
            n, u, inv = norm_rows(self.first[rows, :], self.row(0), self.row(1))
            self.n1[rows, :] = n.astype(BF16)
            self.u1[rows, :] = u
            self.inv1[rows, :] = jnp.broadcast_to(inv, (16, LANES))

        piece_loop(piece, body)

    def turn_one(self):
        self.n1_t[...] = self.n1[...].T

    def project(self, k, b):
        low, cols = (self.q, self.k, self.v)[k], lane_block(b)
        p = self.times(self.n1[...], k, b)
        if k != 1:
            p = p + self.small[2 + k // 2 : 3 + k // 2, cols]
        low[:, cols] = p.astype(BF16)

    def image_sum(self, x):
        total = jnp.zeros((SLOTS, D), F32)
        for i in range(IMG_GROUP):
            im = wide(self.im8[i])
            total = total + im * jnp.sum(im * x, axis=0, keepdims=True)
        return total

    def key_tops(self):
        def top(r0, best):
            live = wide(self.live[pl.ds(r0, 16), :])
            keys = jnp.where(live > 0, self.k[pl.ds(r0, 16), :].astype(F32), NEG_LARGE)
            return jnp.maximum(best, jnp.max(keys.reshape(2, SLOTS, D), axis=0))

        best = rows_loop(ROWS, 16, top, jnp.full((SLOTS, D), NEG_LARGE, F32), unroll=5)
        shift = jnp.zeros((SLOTS, D), F32)
        for i in range(IMG_GROUP):
            im = wide(self.im8[i])
            most = jnp.max(jnp.where(im > 0, best, NEG_LARGE), axis=0, keepdims=True)
            shift = jnp.where(im > 0, most, shift)
        self.soft_acc[0:SLOTS, :] = shift

    def key_powers(self):
        shift2 = jnp.concatenate([self.soft_acc[0:SLOTS, :]] * 2, axis=0)

        def power(r0, total):
            rows = pl.ds(r0, 16)
            live = wide(self.live[rows, :])
            keys = self.k[rows, :].astype(F32)
            e = jnp.where(live > 0, jnp.exp(jnp.where(live > 0, keys - shift2, 0.0)), 0.0)
            self.soft[rows, :] = e
            return total + fold(e)

        total = rows_loop(ROWS, 16, power, jnp.zeros((SLOTS, D), F32), unroll=5)
        total = self.image_sum(total)
        self.soft_acc[SLOTS : 2 * SLOTS, :] = 1.0 / jnp.where(total > 0, total, 1.0)

    def key_shares(self):
        scale2 = jnp.concatenate([self.soft_acc[SLOTS : 2 * SLOTS, :]] * 2, axis=0)

        def divide(r0, _):
            rows = pl.ds(r0, 16)
            soft = self.soft[rows, :] * scale2
            self.soft[rows, :] = soft
            self.soft_low[rows, :] = soft.astype(BF16)
            return 0

        rows_loop(ROWS, 16, divide, 0, unroll=5)

    def by_image(self, x):
        tiles = x.reshape(ROWS // 16, 16, WIDE)
        parts = []
        for i in range(IMG_GROUP):
            im = jnp.concatenate([self.im16[i]] * (WIDE // LANES), axis=1)
            parts.append((tiles * im[None]).reshape(ROWS, WIDE))
        return jnp.concatenate(parts, axis=1)

    def head_blocks(self, x):
        r = lax.broadcasted_iota(jnp.int32, x.shape, 0) // HEAD_DIM
        c = (lax.broadcasted_iota(jnp.int32, x.shape, 1) % WIDE) // HEAD_DIM
        return jnp.where(r == c, x, 0.0).astype(BF16)

    def stacked(self, x):
        return jnp.concatenate([x[:, lane_block(i)] for i in range(IMG_GROUP)], axis=0)

    def contexts(self, b):
        cols = lane_block(b)
        ctx = dot(self.soft_low[:, cols], self.by_image(self.v[:, cols]), TN)
        ctx = self.head_blocks(ctx)
        self.ctx[b] = ctx
        self.factor[:, cols] = dot(self.by_image(self.q[:, cols]), self.stacked(ctx))

    def fill_window(self):
        def fill(r0, _):
            rows = pl.ds(r0, 16)
            v = self.v[rows, :].astype(F32) * wide(self.live[rows, :])
            c0 = r0 // SLOTS
            self.rel_src[pl.ds(HALO * GRID + c0, 2)] = v.reshape(2, SLOTS, D)
            return 0

        rows_loop(ROWS, 16, fill, 0, unroll=5)
        self.rel[CELLS * SLOTS :, :] = jnp.zeros((SLOTS, D), F32)

    def window_sum(self, c):
        lanes = slice(c * LANES, (c + 1) * LANES)

        def put(cell, value):
            rows = pl.ds(pl.multiple_of(cell * SLOTS, SLOTS), SLOTS)
            self.rel[rows, lanes] = value

        def tap(a, b):
            t = (a + HALO) * WINDOW + b + HALO
            return self.rel_taps[t : t + 1, lanes]

        conv(self.rel_src, HALO, tap, REACHES[c], lanes, put)

    def mix(self):
        def mix(r0, _):
            rows = pl.ds(r0, 16)
            m = self.factor[rows, :] * INV_SCALE + self.q[rows, :].astype(F32) * self.rel[rows, :]
            self.mixed[rows, :] = (m * wide(self.live[rows, :])).astype(BF16)
            return 0

        rows_loop(ROWS, 16, mix, 0, unroll=5)

    def attend(self, b):
        cols = lane_block(b)
        p = self.times_t(self.mixed[...], 3, b)
        self.second[:, cols] = self.first[:, cols] + p + self.small[4:5, cols]

    def norm_two(self, piece):
        def body(r0):
            rows = pl.ds(r0, 16)
            n, u, inv = norm_rows(self.second[rows, :], self.row(5), self.row(6))
            self.n2[rows, :] = n.astype(BF16)
            self.u2[rows, :] = u
            self.inv2[rows, :] = jnp.broadcast_to(inv, (16, LANES))

        piece_loop(piece, body)

    def turn_two(self):
        self.n2_t[...] = self.n2[...].T

    def hidden_in(self, r):
        for b in range(2):
            cols = lane_block(b)
            h = self.times(self.n2[...], 4 + 2 * r, b) + self.small[9 + r : 10 + r, cols]
            self.hidden[:, cols] = h
            self.factor[:, cols] = self.times(self.go[...], 5 + 2 * r, b)

    def hidden_out(self, r):
        def body(r0, total):
            rows = pl.ds(r0, 16)
            act, slope = erf_parts(self.hidden[rows, :])
            g = self.factor[rows, :] * slope
            self.active[rows, :] = act.astype(BF16)
            self.low[rows, :] = g.astype(BF16)
            return total + fold(g)

        total = rows_loop(ROWS, 16, body, jnp.zeros((SLOTS, D), F32), unroll=5)
        self.sums[9 + r : 10 + r, :] = jnp.sum(total, axis=0, keepdims=True)

    def grad_down(self, r):
        self.put_grad(5 + 2 * r, self.go_t[...], self.active)

    def grad_up(self, r):
        self.put_grad(4 + 2 * r, self.n2_t[...], self.low)

    def add_down(self, r):
        for b in range(2):
            self.second[:, lane_block(b)] += self.times_t(self.active[...], 5 + 2 * r, b)

    def add_back(self, r):
        for b in range(2):
            self.back[:, lane_block(b)] += self.times_t(self.low[...], 4 + 2 * r, b)

    def finish_out(self):
        def body(r0, _):
            rows = pl.ds(r0, 16)
            self.out_low[rows, :] = (self.second[rows, :] + self.row(7)).astype(BF16)
            return 0

        rows_loop(ROWS, 16, body, 0, unroll=5)
        self.unplace(self.out_low, self.out_own)

    def back_two(self):
        zero = jnp.zeros((SLOTS, D), F32)

        def body(r0, sums):
            rows = pl.ds(r0, 16)
            back, u = self.back[rows, :], self.u2[rows, :]
            go = self.go[rows, :].astype(F32)
            gs = go + norm_back(back, u, wide(self.inv2[rows, :]), self.row(5))
            self.gs[rows, :] = gs
            self.gs_low[rows, :] = gs.astype(BF16)
            new = (gs, back * u, back, go)
            return tuple(s + fold(n) for s, n in zip(sums, new, strict=True))

        sums = rows_loop(ROWS, 16, body, (zero,) * 4, unroll=5)
        for j, s in zip((4, 5, 6, 7), sums, strict=True):
            self.sums[j : j + 1, :] = jnp.sum(s, axis=0, keepdims=True)

    def grad_proj(self):
        self.put_grad(3, self.gs_low[...].T, self.mixed)

    def back_mixed(self):
        for b in range(2):
            self.d[:, lane_block(b)] = self.times(self.gs_low[...], 3, b)

    def back_fill(self):
        def fill(r0, _):
            rows = pl.ds(r0, 16)
            d = self.d[rows, :] * wide(self.live[rows, :])
            self.d[rows, :] = d
            self.f[rows, :] = (d * INV_SCALE).astype(BF16)
            c0 = r0 // SLOTS
            dq = d * self.q[rows, :].astype(F32)
            self.dq_src[pl.ds(HALO * GRID + c0, 2)] = dq.reshape(2, SLOTS, D)
            return 0

        rows_loop(ROWS, 16, fill, 0, unroll=5)
    def back_heads(self, b):
        cols = lane_block(b)
        f3 = self.by_image(self.f[:, cols])
        g = self.head_blocks(dot(self.q[:, cols], f3, TN))
        self.gq[:, cols] = dot(f3, self.ctx[b], NT)
        self.gk[:, cols] = dot(self.by_image(self.v[:, cols]), g, NT)
        self.gv[:, cols] = dot(self.by_image(self.soft_low[:, cols]), self.stacked(g))

    def back_window(self, c):
        lanes = slice(c * LANES, (c + 1) * LANES)

        def put(cell, value):
            rows = pl.ds(pl.multiple_of(cell * SLOTS, SLOTS), SLOTS)
            self.gv[rows, lanes] = self.gv[rows, lanes] + value * self.live[rows, :]

        def tap(a, b):
            t = (HALO - a) * WINDOW + HALO - b
            return self.rel_taps[t : t + 1, lanes]

        conv(self.dq_src, HALO, tap, REACHES[c], lanes, put)

    def window_taps(self, c):
        lanes = slice(c * LANES, (c + 1) * LANES)

        def up(cell):
            return self.dq_src[HALO * GRID + cell, :, lanes]

        def put_tap(a, b, value):
            t = (a + HALO) * WINDOW + b + HALO
            keep = self.window[t : t + 1, lanes]
            self.sums[22 + t : 23 + t, lanes] = value * keep

        tap_sums(up, self.rel_src, HALO, REACHES[c], lanes, put_tap)

    def back_inner(self):
        def inner(r0, total):
            rows = pl.ds(r0, 16)
            return total + fold(self.soft[rows, :] * self.gk[rows, :])

        total = rows_loop(ROWS, 16, inner, jnp.zeros((SLOTS, D), F32), unroll=5)
        self.soft_acc[0:SLOTS, :] = self.image_sum(total)

    def back_query_key(self):
        zero = jnp.zeros((SLOTS, D), F32)
        shared2 = jnp.concatenate([self.soft_acc[0:SLOTS, :]] * 2, axis=0)

        def low(r0, total):
            rows = pl.ds(r0, 16)
            gq = self.gq[rows, :] + self.d[rows, :] * self.rel[rows, :]
            gk = self.soft[rows, :] * (self.gk[rows, :] - shared2)
            self.gl[0, rows, :] = gq.astype(BF16)
            self.gl[1, rows, :] = gk.astype(BF16)
            return total + fold(gq)

        total = rows_loop(ROWS, 16, low, zero, unroll=5)
        self.sums[2:3, :] = jnp.sum(total, axis=0, keepdims=True)

    def back_value(self):
        def low(r0, total):
            rows = pl.ds(r0, 16)
            gv = self.gv[rows, :]
            self.gl[2, rows, :] = gv.astype(BF16)
            return total + fold(gv)

        total = rows_loop(ROWS, 16, low, jnp.zeros((SLOTS, D), F32), unroll=5)
        self.sums[3:4, :] = jnp.sum(total, axis=0, keepdims=True)

    def grad_of(self, k):
        self.put_grad(k, self.n1_t[...], self.gl.at[k])

    def back_project(self, b):
        back = self.times_t(self.gl[0], 0, b)
        back = back + self.times_t(self.gl[1], 1, b)
        self.back[:, lane_block(b)] = back + self.times_t(self.gl[2], 2, b)

    def back_one(self):
        zero = jnp.zeros((SLOTS, D), F32)
        self.pos_up[0:GRID] = jnp.zeros((GRID, SLOTS, D), F32)
        self.pos_up[GRID + CELLS :] = jnp.zeros((GRID, SLOTS, D), F32)

        def body(r0, sums):
            rows = pl.ds(r0, 16)
            back, u = self.back[rows, :], self.u1[rows, :]
            gf = self.gs[rows, :] + norm_back(back, u, wide(self.inv1[rows, :]), self.row(0))
            c0 = r0 // SLOTS
            self.pos_up[pl.ds(GRID + c0, 2)] = gf.reshape(2, SLOTS, D)
            new = (back * u, back, gf)
            return tuple(s + fold(n) for s, n in zip(sums, new, strict=True))

        sums = rows_loop(ROWS, 16, body, (zero,) * 3, unroll=5)
        for j, s in zip((0, 1, 8), sums, strict=True):
            self.sums[j : j + 1, :] = jnp.sum(s, axis=0, keepdims=True)

    def back_position(self):
        for c in range(D // LANES):
            lanes = slice(c * LANES, (c + 1) * LANES)

            def put(cell, value):
                rows = pl.ds(pl.multiple_of(cell * SLOTS, SLOTS), SLOTS)
                gf = self.pos_up[GRID + cell, :, lanes]
                self.first[rows, lanes] = gf + value * self.live[rows, :]

            def tap(a, b):
                t = 13 + (1 - a) * 3 + 1 - b
                return self.small[t : t + 1, lanes]

            conv(self.pos_up, 1, tap, 1, lanes, put)

    def position_taps(self):
        for c in range(D // LANES):
            lanes = slice(c * LANES, (c + 1) * LANES)

            def up(cell):
                return self.pos_up[GRID + cell, :, lanes]

            def put_tap(a, b, value):
                t = 13 + (a + 1) * 3 + b + 1
                self.sums[t : t + 1, lanes] = value

            tap_sums(up, self.pos_src, 1, 1, lanes, put_tap)

    def finish_in(self):
        def down(r0, _):
            rows = pl.ds(r0, 16)
            self.in_low[rows, :] = self.first[rows, :].astype(BF16)
            return 0

        rows_loop(ROWS, 16, down, 0, unroll=5)
        self.unplace(self.in_low, self.in_own)


SLOT_OF = (0, 1, 2, 3, 4, 6, 8, 10, 5, 7, 9, 11)
MATS = len(SLOT_OF)
EARLY = 4
AXES = "xchly"
HEAD_ROWS = 320
SMALL_ROWS = 72
AG_ROUTES = ("zxyc", "zxyc", "zyxc", "zyxc", "zxyc", "zyxc", "yhxlc", "yxhlc", "hlxyc", "lhyxc", "hxlyc", "lyhxc")
RS_ROUTES = ("clyhx", "cxlyh", "cyhlx", "cyxlh", "clxhy", "cxhyl", "cylhx", "clyhx", "cxylh", "cylxh", "clxyh", "cylhx")
ORDER = (
    426, 428, 429, 435, 431, 434, 427, 22, 69, 76, 66, 86, 116, 109, 129, 96, 132, 87, 136, 176,
    167, 432, 112, 172, 430, 152, 156, 147, 450, 11, 446, 448, 447, 72, 92, 433, 0, 439, 81, 77,
    70, 436, 437, 101, 97, 88, 438, 440, 33, 442, 441, 29, 24, 23, 26, 444, 73, 443, 55, 445,
    449, 451, 18, 12, 15, 13, 102, 98, 94, 44, 7, 4, 2, 1, 107, 67, 30, 27, 25, 93,
    40, 37, 35, 34, 68, 126, 90, 19, 14, 16, 149, 62, 57, 56, 59, 106, 166, 91, 8, 5,
    3, 51, 45, 48, 46, 141, 130, 128, 137, 31, 28, 41, 38, 82, 78, 36, 74, 89, 181, 177,
    168, 146, 20, 17, 32, 456, 71, 121, 117, 113, 457, 463, 108, 127, 466, 63, 60, 58, 169, 464,
    21, 454, 170, 465, 467, 9, 6, 52, 110, 133, 47, 49, 455, 103, 99, 95, 458, 122, 118, 111,
    459, 161, 148, 42, 39, 157, 114, 460, 150, 173, 153, 142, 138, 131, 134, 10, 452, 83, 75, 79,
    453, 182, 178, 462, 174, 461, 64, 61, 43, 171, 468, 104, 100, 53, 50, 470, 469, 472, 473, 123,
    119, 115, 475, 65, 162, 151, 158, 154, 471, 143, 139, 135, 474, 105, 84, 80, 476, 54, 477, 481,
    489, 266, 267, 268, 485, 289, 288, 287, 286, 85, 290, 269, 270, 183, 175, 179, 497, 163, 155, 159,
    493, 124, 120, 478, 281, 271, 144, 140, 482, 494, 486, 328, 327, 326, 329, 330, 272, 301, 293, 292,
    294, 291, 490, 306, 307, 309, 308, 310, 125, 498, 273, 145, 479, 184, 164, 160, 274, 180, 483, 341,
    334, 333, 491, 348, 347, 349, 346, 282, 331, 350, 275, 321, 314, 312, 313, 276, 311, 277, 499, 495,
    165, 487, 368, 370, 369, 366, 367, 185, 480, 332, 484, 361, 352, 353, 354, 351, 496, 302, 296, 492,
    297, 390, 389, 386, 388, 387, 381, 374, 372, 373, 371, 488, 406, 408, 283, 407, 278, 409, 410, 501,
    342, 336, 337, 335, 528, 279, 500, 502, 322, 315, 401, 503, 421, 411, 412, 247, 249, 248, 250, 246,
    393, 413, 414, 504, 317, 505, 316, 519, 391, 521, 518, 506, 261, 254, 362, 356, 357, 355, 252, 284,
    253, 323, 251, 318, 382, 375, 511, 319, 280, 507, 343, 338, 513, 339, 377, 512, 422, 415, 402, 397,
    295, 508, 324, 320, 383, 378, 379, 509, 417, 516, 209, 208, 206, 207, 210, 416, 515, 344, 340, 187,
    186, 188, 376, 190, 189, 392, 396, 395, 510, 514, 517, 423, 418, 363, 226, 228, 419, 230, 227, 229,
    520, 221, 211, 529, 522, 213, 212, 358, 325, 523, 359, 201, 192, 303, 298, 299, 524, 345, 214, 384,
    191, 241, 231, 262, 255, 526, 256, 285, 534, 257, 403, 398, 233, 530, 424, 364, 360, 420, 193, 232,
    399, 234, 525, 222, 215, 304, 535, 380, 527, 216, 531, 217, 242, 235, 202, 195, 196, 197, 404, 263,
    236, 365, 259, 400, 425, 223, 218, 219, 258, 237, 385, 536, 300, 203, 198, 194, 199, 243, 238, 224,
    220, 394, 264, 260, 537, 305, 239, 204, 200, 244, 240, 405, 543, 225, 265, 532, 205, 245, 544, 538,
    533, 545, 539, 546, 540, 547, 541, 542, 548, 549,
)


def scratch_of():
    f, h, low = (ROWS, D), (ROWS, LANES), pltpu.VMEM((ROWS, D), BF16)
    halo3 = pltpu.VMEM(((GRID + 2 * HALO) * GRID, SLOTS, D), F32)
    halo1 = pltpu.VMEM(((GRID + 2) * GRID, SLOTS, D), F32)
    high, column, turned = pltpu.VMEM(f, F32), pltpu.VMEM(h, F32), pltpu.VMEM((D, ROWS), BF16)
    taps = pltpu.VMEM((WINDOW * WINDOW, D), F32)
    return dict(
        live=column,
        im8=pltpu.VMEM((IMG_GROUP, SLOTS, LANES), F32),
        im16=pltpu.VMEM((IMG_GROUP, 16, LANES), BF16),
        window=taps,
        rel_taps=taps,
        pos_src=halo1,
        pos_up=halo1,
        rel_src=halo3,
        dq_src=halo3,
        first=high,
        u1=high,
        inv1=column,
        second=high,
        u2=high,
        inv2=column,
        n1=low,
        n1_t=turned,
        n2=low,
        n2_t=turned,
        go=low,
        go_t=turned,
        q=low,
        k=low,
        v=low,
        soft=high,
        soft_low=low,
        soft_acc=pltpu.VMEM((2 * SLOTS, D), F32),
        ctx=pltpu.VMEM((2, WIDE, IMG_GROUP * WIDE), BF16),
        factor=high,
        rel=high,
        mixed=low,
        hidden=high,
        active=low,
        low=low,
        out_low=low,
        back=high,
        gs=high,
        gs_low=low,
        d=high,
        f=low,
        gq=high,
        gk=high,
        gv=high,
        gl=pltpu.VMEM((3, ROWS, D), BF16),
        in_low=low,
    )


class Links:
    def __init__(self):
        dp, head = lax.axis_index(DP), lax.axis_index(HEAD)
        self.far = lax.axis_size(DP) // 4
        self.at = dict(x=head // 2, c=head % 2, h=dp // 4, l=dp // 2 % 2, y=dp % 2)

    def count(self, axis):
        return dict(h=self.far, z=2 * self.far, d=4).get(axis, 2)

    def peer(self, axis, step):
        if axis in "zd":
            one, two = "hl" if axis == "z" else "xy"
            return {one: self.next(one, step // 2), two: self.next(two, step % 2)}
        return {axis: self.next(axis, step)}

    def other(self):
        return self.device("c", 1)

    def next(self, axis, step):
        return lax.rem(self.at[axis] + step, self.count(axis))

    def device(self, axis, step):
        at = {**self.at, **self.peer(axis, step)}
        return (at["h"] * 4 + at["l"] * 2 + at["y"], at["x"] * 2 + at["c"])

    def steps(self, axis, do):
        self.repeat(self.count(axis), do, 8)

    def repeat(self, size, do, most):
        if size <= most:
            for step in range(1, size):
                do(step)
        else:

            def body(step, _):
                do(step)
                return 0

            lax.fori_loop(1, size, body, 0)

    def others(self, name, do):
        dp, head, heads = lax.axis_index(DP), lax.axis_index(HEAD), lax.axis_size(HEAD)

        def one(step):
            if name == ALL:
                i = lax.rem(dp * heads + head + step, lax.axis_size(ALL))
                do((i // heads, lax.rem(i, heads)))
            elif name == DP:
                do((lax.rem(dp + step, lax.axis_size(DP)), head))
            else:
                do((dp, lax.rem(head + step, heads)))

        self.repeat(lax.axis_size(name), one, 32)

    def signal(self):
        def one(device):
            pl.semaphore_signal(
                pltpu.get_barrier_semaphore(),
                inc=1,
                device_id=device,
                device_id_type=pl.DeviceIdType.MESH,
            )

        self.others(ALL, one)

    def meet(self):
        pl.semaphore_wait(pltpu.get_barrier_semaphore(), lax.axis_size(ALL) - 1)

    def copy(self, src, dst, send, recv, device):
        return pltpu.make_async_remote_copy(
            src_ref=src,
            dst_ref=dst,
            send_sem=send,
            recv_sem=recv,
            device_id=device,
            device_id_type=pl.DeviceIdType.MESH,
        )

    def region(self, blocks, slot, whole, **at):
        at = {**self.at, **at}
        whole = whole.replace("z", "hl").replace("d", "xy")
        place = [slice(None) if axis in whole else at[axis] for axis in AXES]
        return blocks.at[(*place, slot)]


class Gather:
    def __init__(self, links, w, sizes, send, recv):
        self.links, self.w, self.sizes, self.send, self.recv = links, w, sizes, send, recv

    def start(self, slot, i, j):
        path, links = AG_ROUTES[slot], self.links

        def along(whole, at):
            part = links.region(self.w, slot, whole, **at)

            def go(step):
                sems = self.send.at[slot], self.recv.at[slot, j]
                links.copy(part, part, *sems, links.device(path[j], step)).start()

            links.steps(path[j], go)

        if i < 0:
            along("", {})
        elif path[i] == "z" and i == 0:
            along("z", {})
        else:
            links.steps(path[i], lambda step: along(path[:i], links.peer(path[i], step)))

    def arrive(self, slot, j):
        path, links = AG_ROUTES[slot], self.links
        blocks = (links.count(path[j]) - 1) * math.prod(links.count(a) for a in path[:j])
        size = self.sizes.at[pl.ds(0, blocks)]
        links.copy(size, size, self.send.at[slot], self.recv.at[slot, j], links.other()).wait_recv()

    def sent(self):
        for slot in range(MATS):
            sems = self.send.at[slot], self.recv.at[slot, 0]
            self.links.copy(self.sizes, self.sizes, *sems, self.links.other()).wait_send()

    def steps(self):
        for slot, path in enumerate(AG_ROUTES):
            for j in range(len(path)):
                for i in range(-1, j):
                    if path[0] != "z" or j == 0 or i >= 0:
                        yield functools.partial(self.start, slot, i, j)
            for j in range(len(path)):
                yield functools.partial(self.arrive, slot, j)


class Scatter:
    def __init__(self, links, g, boxes, total, sizes, send, recv):
        self.links, self.g, self.boxes, self.total = links, g, boxes, total
        self.sizes, self.send, self.recv = sizes, send, recv

    def box(self, slot, j):
        return self.boxes[slot * len(AXES) + j - 1]

    def merged(self, slot, j):
        path = RS_ROUTES[slot]
        return path[-1] == "z" and j == len(path) - 1

    def start(self, slot, i, j):
        path, links = RS_ROUTES[slot], self.links
        first = sum(links.count(a) - 1 for a in path[:i]) - 1
        skip = first + 1 if path[-1] == "z" and j == len(path) else 0

        def go(step):
            entry = first + step - skip
            sems = self.send.at[slot], self.recv.at[slot, j - 1]
            into = self.box(slot, j).at[entry]
            device = links.device(path[i], step)

            def part(into, whole, more):
                src = links.region(self.g, slot, whole, **links.peer(path[i], step), **more)
                links.copy(src, into, *sems, device).start()

            if j == len(path) or self.merged(slot, j):
                part(into, path[j:], {})
            else:
                links.steps(
                    path[j], lambda n: part(into.at[n - 1], path[j + 1 :], links.peer(path[j], n))
                )

        links.steps(path[i], go)

    def add(self, slot, j):
        path, links = RS_ROUTES[slot], self.links
        box = self.box(slot, j)
        sems = self.send.at[slot], self.recv.at[slot, j - 1]
        links.copy(box, box, *sems, links.other()).wait_recv()

        def total(own, pick):
            value = own[...].astype(F32)
            for e in range(box.shape[0]):
                value = value + pick(box.at[e])[...].astype(F32)
            return value

        if j == len(path):
            own = links.region(self.g, slot, "")
            self.total[SLOT_OF.index(slot)] = total(own, lambda b: b)
            return

        def one(n):
            own = links.region(self.g, slot, path[j + 1 :], **links.peer(path[j], n))
            own[...] = total(own, lambda b: b.at[n - 1]).astype(BF16)

        if self.merged(slot, j):
            own = links.region(self.g, slot, "z")
            own[...] = total(own, lambda b: b).astype(BF16)
        else:
            links.steps(path[j], one)

    def sent(self):
        for slot in range(MATS):
            sems = self.send.at[slot], self.recv.at[slot, 0]
            self.links.copy(self.sizes, self.sizes, *sems, self.links.other()).wait_send()

    def steps(self):
        for slot, path in enumerate(RS_ROUTES):
            for i in range(len(path)):
                for j in range(i + 1, len(path) + 1):
                    if not (path[-1] == "z" and j == len(path) and i + 1 < len(path)):
                        yield functools.partial(self.start, slot, i, j)
            for j in range(1, len(path) + 1):
                yield functools.partial(self.add, slot, j)


class Small:
    def __init__(self, links, sums, parts, in_c, in_x, in_y, in_h, in_l, full, send, recv):
        self.links, self.sums, self.parts, self.full = links, sums, parts, full
        self.in_c, self.in_x, self.in_y, self.in_h, self.in_l = in_c, in_x, in_y, in_h, in_l
        self.send, self.recv = send, recv

    def go(self, stage, src, dst, axis):
        sems = (self.send.at[stage], self.recv.at[stage])
        self.links.steps(
            axis, lambda step: self.links.copy(src, dst, *sems, self.links.device(axis, step)).start()
        )

    def wait(self, stage):
        x, c = self.links.at["x"], self.links.at["c"]
        ref = (
            self.in_c,
            self.in_x,
            self.in_y,
            self.in_h.at[pl.ds(0, self.links.far - 1)],
            self.in_l,
            self.full.at[c, x],
            self.full.at[c],
        )[stage]
        sems = (self.send.at[stage], self.recv.at[stage])
        return self.links.copy(ref, ref, *sems, self.links.device("cxyhlxc"[stage], 1))

    def tick(self, stage):
        at = self.links.at
        x, c, h = at["x"], at["c"], at["h"]
        mine = self.parts.at[c, x]
        if stage:
            self.wait(stage - 1).wait_recv()
        if stage == 0:
            for b in range(D // LANES):
                self.parts[b // 2, b % 2] = self.sums[:, b * LANES : (b + 1) * LANES]
            self.go(0, self.parts.at[1 - c], self.in_c, "c")
        if stage == 1:
            self.parts[c] = self.parts[c] + self.in_c[...]
            self.go(1, self.parts.at[c, 1 - x], self.in_x, "x")
        if stage == 2:
            mine[...] = mine[...] + self.in_x[...]
            self.go(2, mine, self.in_y, "y")
        if stage == 3:
            self.in_h[h] = mine[...] + self.in_y[...]
            self.go(3, self.in_h.at[h], self.in_h.at[h], "h")
        if stage == 4:
            total = self.in_h[0]
            for i in range(1, self.links.far):
                total = total + self.in_h[i]
            self.sums[:, 0:LANES] = total
            self.go(4, self.sums.at[:, pl.ds(0, LANES)], self.in_l, "l")
        if stage == 5:
            self.full[c, x] = self.sums[:, 0:LANES] + self.in_l[...]
            self.go(5, self.full.at[c, x], self.full.at[c, x], "x")
        if stage == 6:
            self.go(6, self.full.at[c], self.full.at[c], "c")

    def sent(self):
        for stage in range(7):
            self.wait(stage).wait_send()


class Rows:
    def __init__(self, links, blocks, out, own, send, recv):
        self.links, self.blocks, self.out, self.own = links, blocks, out, own
        self.send, self.recv = send, recv

    def hop(self, i):
        x, c = self.links.at["x"], self.links.at["c"]
        x, axis = ((x, "x"), (x, "c"), (1 - x, "c"))[i]
        block = self.blocks.at[2 * x + c]
        return self.links.copy(
            block, block, self.send.at[i], self.recv.at[i], self.links.device(axis, 1)
        )

    def tick(self, stage):
        if stage == 0:
            self.hop(0).start()
            self.hop(1).start()
        if stage == 1:
            self.hop(0).wait_recv()
            self.hop(2).start()
        if stage == 2:
            self.hop(1).wait_recv()
            self.hop(2).wait_recv()
            self.join()

    def sent(self):
        for i in range(3):
            self.hop(i).wait_send()

    def join(self):
        heads, end, own = self.blocks.shape[0], self.out.shape[0], self.own
        for h in range(heads):
            lo, hi = h * own, (h + 1) * own
            base = lo // 16 * 16
            first = base + 16 if lo % 16 else base
            last = hi // 16 * 16 if h + 1 < heads else end
            self.out[first:last, :] = self.blocks[h, first - base : last - base, :]
            if lo % 16:
                before = (lo - own) // 16 * 16
                tail = self.blocks[h - 1, base - before : base - before + 16, :]
                self.out[base : base + 16, :] = tail + self.blocks[h, 0:16, :]


class Exchange:
    def __init__(self, links, name, buffer, send, recv):
        self.links, self.name, self.buffer, self.send, self.recv = links, name, buffer, send, recv

    def start(self, value):
        own = lax.axis_index(self.name)
        self.buffer[own] = value
        mine = self.buffer.at[own]
        self.links.others(
            self.name,
            lambda device: self.links.copy(mine, mine, self.send, self.recv, device).start(),
        )

    def descriptor(self):
        ref = self.buffer.at[pl.ds(0, self.buffer.shape[0] - 1)]
        return self.links.copy(ref, ref, self.send, self.recv, self.links.device("c", 1))

    def total(self):
        self.descriptor().wait_recv()
        return jnp.sum(self.buffer[...], axis=0)

    def sent(self):
        self.descriptor().wait_send()


def exact(a, b, dims):
    return lax.dot_general(
        a, b, dims, precision=lax.Precision.HIGHEST, preferred_element_type=F32
    )


class Adafactor:
    def __init__(self, refs, lo, hi, row_share, col_share, sq_share):
        self.__dict__.update(refs)
        self.lo, self.hi = lo, hi
        self.row_share, self.col_share, self.sq_share = row_share, col_share, sq_share

    def eye(self, count, first):
        r = lax.broadcasted_iota(jnp.int32, (count, LANES), 0)
        c = lax.broadcasted_iota(jnp.int32, (count, LANES), 1)
        return jnp.where(c == r + first, 1.0, 0.0)

    def lane(self, k, value, rest):
        lanes = lax.broadcasted_iota(jnp.int32, rest.shape, 1)
        return jnp.where(lanes == k, value, rest)

    def squares(self):
        rows, count = self.wg.shape[1], self.hi - self.lo
        by_row = jnp.zeros((rows, LANES), F32)
        by_col = []
        for k in range(self.lo, self.hi):
            g = self.wg[k]
            s = g * g + SQUARE_FLOOR
            by_row = self.lane(k, jnp.sum(s, axis=1, keepdims=True), by_row)
            by_col.append(jnp.sum(s, axis=0, keepdims=True))
        rest = jnp.zeros((SLOTS - count, LANES), F32)
        self.col_share.start(jnp.concatenate([*by_col, rest] if count < SLOTS else by_col, axis=0))
        turned = exact(self.eye(SLOTS, self.lo), by_row, NT)
        if rows < LANES:
            turned = jnp.concatenate([turned, jnp.zeros((SLOTS, LANES - rows), F32)], axis=1)
        self.row_share.start(turned)

    def scale(self):
        rows, lo, hi = self.wg.shape[1], self.lo, self.hi
        total = self.row_share.total()[0 : hi - lo, 0:rows]
        new_rows = SECOND_DECAY * self.row_state[lo:hi, :] + (1.0 - SECOND_DECAY) * (
            total * (1.0 / D)
        )
        self.new_rows[lo:hi, :] = new_rows
        row = exact(new_rows, self.eye(hi - lo, lo), TN)
        total = self.col_share.total()[0 : hi - lo]
        cols = SECOND_DECAY * self.col_state[lo:hi, :] + (1.0 - SECOND_DECAY) * (
            total * (1.0 / D)
        )
        self.new_cols[lo:hi, :] = cols
        sums = jnp.zeros((1, LANES), F32)
        for k in range(lo, hi):
            u = self.wg[k] * lax.rsqrt(row[:, k : k + 1] * cols[k - lo : k - lo + 1, :])
            self.upd[k] = u
            s = jnp.sum(jnp.sum(u * u, axis=0, keepdims=True), axis=1, keepdims=True)
            sums = self.lane(k, s, sums)
        mass = jnp.sum(row, axis=0, keepdims=True)
        self.sq_share.start(jnp.concatenate([sums, mass], axis=0))

    def apply(self):
        total = self.sq_share.total()
        mean = total[1:2] * (1.0 / (D * lax.axis_size(HEAD)))
        rms = jnp.sqrt(total[0:1] * mean * (1.0 / (D * D)))
        rate = STEP_RATE * jnp.sqrt(mean) / jnp.maximum(1.0, rms)
        for k in range(self.lo, self.hi):
            new = self.weights[k] - rate[:, k : k + 1] * self.upd[k]
            self.new_weights[k] = new
            self.copy[k] = new.astype(BF16)
            self.new_ema[k] = AVERAGE_KEEP * self.ema[k] + (1.0 - AVERAGE_KEEP) * new
        self.rms[self.lo // 4 : self.lo // 4 + 1, :] = rms


class SmallStep:
    def __init__(self, refs):
        self.__dict__.update(refs)

    def clips(self):
        lanes = lax.broadcasted_iota(jnp.int32, (1, LANES), 1)
        clip = jnp.where(lanes < EARLY, self.rms[0:1, :], self.rms[1:2, :])
        clip = jnp.where(lanes < MATS, clip, self.small_clip[...])
        self.clip[...] = clip[:, 0 : self.clip.shape[1]]

    def small_step(self):
        count, full = self.small.shape[0], self.full
        g = jnp.concatenate([full[b // 2, b % 2, 0:count, :] for b in range(D // LANES)], axis=1)
        self.small_grads[...] = g
        state = SECOND_DECAY * self.small_state[...] + (1.0 - SECOND_DECAY) * (
            g * g + SQUARE_FLOOR
        )
        self.new_small_state[...] = state
        u = g * lax.rsqrt(state)
        rms = jnp.sqrt(jnp.sum(u * u, axis=1, keepdims=True) * (1.0 / D))
        new = self.small[...] - SMALL_RATE * u / jnp.maximum(1.0, rms)
        self.new_small[...] = new
        self.new_small_ema[...] = AVERAGE_KEEP * self.small_ema[...] + (1.0 - AVERAGE_KEEP) * new
        r = lax.broadcasted_iota(jnp.int32, (count, LANES), 0)
        c = lax.broadcasted_iota(jnp.int32, (count, LANES), 1)
        picked = jnp.where(c == r + MATS, rms, 0.0)
        self.small_clip[...] = jnp.sum(picked, axis=0, keepdims=True)


class Inputs(NamedTuple):
    cls: Any
    img: Any
    tokens: Any
    cot: Any
    weights: Any
    row_state: Any
    col_state: Any
    ema: Any
    small: Any
    small_state: Any
    small_ema: Any


class Outputs(NamedTuple):
    out: Any
    grad_in: Any
    wg: Any
    new_rows: Any
    new_cols: Any
    new_weights: Any
    copy: Any
    new_ema: Any
    small_grads: Any
    new_small_state: Any
    new_small: Any
    new_small_ema: Any
    clip: Any


def box_shapes(links, block):
    for path in RS_ROUTES:
        for j in range(1, len(AXES) + 1):
            entries = sum(links.count(a) - 1 for a in path[:j])
            if j > len(path):
                shape = (1, SLOTS, LANES)
            elif j == len(path):
                first = links.count("z") - 1 if path[-1] == "z" else entries
                shape = (first, *block)
            elif path[-1] == "z" and j == len(path) - 1:
                shape = (entries, links.count("h"), links.count("l"), *block)
            else:
                rest = path[j + 1 :].replace("z", "hl").replace("d", "xy")
                rest = [links.count(a) for a in AXES if a in rest]
                shape = (entries, links.count(path[j]) - 1, *rest, *block)
            yield pltpu.VMEM(shape, BF16)


def shared_of(weights, parts, heads):
    links, (_, rows, _) = Links(), weights.shape
    block = (rows, LANES)
    every = pltpu.VMEM((2, 2, links.far, 2, 2, MATS, *block), BF16)
    out_rows = pltpu.VMEM((heads, HEAD_ROWS, D), BF16)
    dma = pltpu.SemaphoreType.DMA

    def f(*shape):
        return pltpu.VMEM(shape, F32)

    part = f(SMALL_ROWS, LANES)
    return dict(
        w=every,
        g=every,
        out_rows=out_rows,
        in_rows=out_rows,
        sums=f(SMALL_ROWS, D),
        parts=f(2, 2, SMALL_ROWS, LANES),
        in_c=f(2, SMALL_ROWS, LANES),
        in_x=part,
        in_y=part,
        in_h=f(links.far, SMALL_ROWS, LANES),
        in_l=part,
        full=f(2, 2, SMALL_ROWS, LANES),
        row_box=f(2, heads, SLOTS, LANES),
        col_box=f(2, parts, SLOTS, LANES),
        sq_box=f(2, parts * heads, 2, LANES),
        upd=f(MATS, *block),
        small_clip=f(1, LANES),
        rms=f(2, LANES),
        sizes=pltpu.VMEM((parts * heads - 1, *block), BF16),
        ag_send=dma((MATS,)),
        ag_recv=dma((MATS, len(AXES))),
        rs_send=dma((MATS,)),
        rs_recv=dma((MATS, len(AXES))),
        small_send=dma((7,)),
        small_recv=dma((7,)),
        out_send=dma((3,)),
        out_recv=dma((3,)),
        in_send=dma((3,)),
        in_recv=dma((3,)),
        opt_send=dma((2, 3)),
        opt_recv=dma((2, 3)),
        fetched=dma((len(Inputs._fields),)),
        stored=dma((len(Outputs._fields),)),
    )


class Ready:
    def __init__(self, src, dst, sem):
        self.copy = pltpu.make_async_copy(src, dst, sem)
        self.start, self.wait = self.copy.start, self.copy.wait


def then(*steps):
    def run():
        for step in steps:
            step()

    return run


def block_kernel(names, *refs):
    n_in, n_out = len(Inputs._fields), len(Outputs._fields)
    ins, outs, refs = Inputs(*refs[:n_in]), Outputs(*refs[n_in : n_in + n_out]), refs[n_in + n_out :]
    r = types.SimpleNamespace(**dict(zip(names, refs)))
    fetch = Inputs(
        *[
            Ready(ref, getattr(r, name), r.fetched.at[i])
            for i, (name, ref) in enumerate(zip(Inputs._fields, ins))
        ]
    )
    store = Outputs(
        *[
            Ready(getattr(r, name), ref, r.stored.at[i])
            for i, (name, ref) in enumerate(zip(Outputs._fields, outs))
        ]
    )
    boxes = refs[len(names) :]
    links = Links()
    links.signal()
    for one in (fetch.weights, *fetch[0:2], fetch.small, *fetch[2:4], *fetch[5:8], *fetch[9:]):
        one.start()
    r.out_own = r.out_rows.at[lax.axis_index(HEAD)]
    r.in_own = r.in_rows.at[lax.axis_index(HEAD)]
    own = r.cls.shape[1] * CELLS
    blk = Block(vars(r))
    gather = Gather(links, r.w, r.sizes, r.ag_send, r.ag_recv)
    scatter = Scatter(links, r.g, boxes, r.wg, r.sizes, r.rs_send, r.rs_recv)
    small = Small(
        links,
        *(r.sums, r.parts, r.in_c, r.in_x, r.in_y, r.in_h, r.in_l, r.full),
        r.small_send,
        r.small_recv,
    )
    out_rows = Rows(links, r.out_rows, r.out, own, r.out_send, r.out_recv)
    in_rows = Rows(links, r.in_rows, r.grad_in, own, r.in_send, r.in_recv)
    shares, opts = [], []
    for part, (lo, hi) in enumerate(((0, EARLY), (EARLY, MATS))):
        boxes = (HEAD, r.row_box), (DP, r.col_box), (ALL, r.sq_box)
        shares += [
            Exchange(links, axis, box.at[part], r.opt_send.at[part, i], r.opt_recv.at[part, i])
            for i, (axis, box) in enumerate(boxes)
        ]
        opts.append(Adafactor(vars(r), lo, hi, *shares[-3:]))
    step = SmallStep(vars(r))

    def round_weights():
        for k in range(MATS):
            mine = links.region(r.w, SLOT_OF[k], "")
            mine[...] = r.weights[k].astype(BF16)

    ops = [*gather.steps(), *scatter.steps()]
    ops += [then(fetch.weights.wait, round_weights), links.meet]
    ops += [then(fetch.small.wait, fetch.cls.wait, fetch.img.wait, blk.setup)]
    ops += [fetch.tokens.wait, fetch.cot.wait]

    def each(step, *ranges):
        for place in itertools.product(*map(range, ranges)):
            ops.append(functools.partial(step, *place))

    each(blk.read_tokens, PIECES)
    each(blk.position, D // LANES)
    each(blk.norm_one, PIECES)
    ops.append(blk.turn_one)
    each(blk.read_cotangent, PIECES)
    ops.append(blk.turn_cotangent)
    each(blk.project, 3, 2)
    ops += [blk.key_tops, blk.key_powers, blk.key_shares]
    each(blk.contexts, 2)
    ops.append(blk.fill_window)
    each(blk.window_sum, D // LANES)
    ops.append(blk.mix)
    each(blk.attend, 2)
    each(blk.norm_two, PIECES)
    ops.append(blk.turn_two)
    each(blk.hidden_in, 4)
    each(blk.hidden_out, 4)
    each(blk.grad_down, 4)
    each(blk.grad_up, 4)
    each(blk.add_down, 4)
    each(blk.add_back, 4)
    ops += [blk.finish_out, blk.back_two, blk.grad_proj, blk.back_mixed, blk.back_fill]
    each(blk.back_heads, 2)
    ops += [blk.back_inner, blk.back_query_key]
    each(blk.back_window, D // LANES)
    ops.append(blk.back_value)
    each(blk.grad_of, 3)
    each(blk.window_taps, D // LANES)
    each(blk.back_project, 2)
    ops += [blk.back_one, blk.back_position, blk.position_taps, blk.finish_in]
    for rows, done in ((out_rows, store.out), (in_rows, store.grad_in)):
        ops += [functools.partial(rows.tick, stage) for stage in range(2)]
        ops += [then(functools.partial(rows.tick, 2), done.start)]
    ops += [functools.partial(small.tick, stage) for stage in range(8)]
    ops += [
        then(
            fetch.small_state.wait,
            fetch.small_ema.wait,
            step.small_step,
            store.small_grads.start,
            store.new_small_state.start,
            store.new_small.start,
            store.new_small_ema.start,
        ),
        opts[1].squares,
        then(store.wg.start, opts[0].squares),
        then(fetch.row_state.wait, fetch.col_state.wait, opts[1].scale),
        then(opts[0].scale, store.new_rows.start, store.new_cols.start),
        then(fetch.ema.wait, opts[1].apply),
        then(
            opts[0].apply, store.new_weights.start, store.copy.start, store.new_ema.start
        ),
        then(step.clips, store.clip.start),
    ]
    for i in ORDER:
        ops[i]()
    for transfer in (gather, scatter, small, out_rows, in_rows, *shares):
        transfer.sent()
    for one in store:
        one.wait()


def finish_kernel(count, *refs):
    ins, outs, held = refs[:count], refs[count : 2 * count], refs[2 * count : 3 * count]
    took, gave = refs[3 * count :]
    come = [pltpu.make_async_copy(a, b, took.at[i]) for i, (a, b) in enumerate(zip(ins, held))]
    leave = [pltpu.make_async_copy(a, b, gave.at[i]) for i, (a, b) in enumerate(zip(held, outs))]
    for one in come:
        one.start()
    for one, other in zip(come, leave):
        one.wait()
        other.start()
    for one in leave:
        one.wait()


def local(
    tokens,
    cotangent,
    crop_image,
    crop_class,
    weights,
    row_state,
    col_state,
    weights_ema,
    small_params,
    small_state,
    small_ema,
):
    parts, heads = lax.axis_size(DP), lax.axis_size(HEAD)
    shared = shared_of(weights, parts, heads)
    own = scratch_of()

    def like(x, dtype=None):
        return jax.ShapeDtypeStruct(x.shape, dtype or x.dtype)

    clips = weights.shape[0] + small_params.shape[0]
    outs = (
        like(tokens),
        like(tokens),
        like(weights),
        like(row_state),
        like(col_state),
        like(weights),
        like(weights, BF16),
        like(weights),
        like(small_params),
        like(small_params),
        like(small_params),
        like(small_params),
        jax.ShapeDtypeStruct((1, clips), F32),
    )
    args = Inputs(
        crop_class,
        crop_image,
        tokens,
        cotangent,
        weights,
        row_state,
        col_state,
        weights_ema,
        small_params,
        small_state,
        small_ema,
    )
    staged = [pltpu.SMEM(x.shape, x.dtype) for x in args[:2]]
    staged += [pltpu.VMEM(x.shape, x.dtype) for x in (*args[2:], *outs)]
    names = (*shared, *own, *Inputs._fields, *Outputs._fields)
    far = pl.BlockSpec(memory_space=pltpu.HBM)
    res = pl.pallas_call(
        functools.partial(block_kernel, names),
        out_shape=outs,
        in_specs=[far] * len(args),
        out_specs=(far,) * len(outs),
        scratch_shapes=[
            *shared.values(),
            *own.values(),
            *staged,
            *box_shapes(Links(), weights.shape[1:]),
        ],
        compiler_params=pltpu.CompilerParams(
            collective_id=0, has_side_effects=True, vmem_limit_bytes=63 << 20
        ),
        name="block",
    )(*args)
    res = pl.pallas_call(
        functools.partial(finish_kernel, len(outs)),
        out_shape=outs,
        in_specs=[far] * len(outs),
        out_specs=(far,) * len(outs),
        scratch_shapes=[
            *[pltpu.VMEM(x.shape, x.dtype) for x in outs],
            pltpu.SemaphoreType.DMA((len(outs),)),
            pltpu.SemaphoreType.DMA((len(outs),)),
        ],
        compiler_params=pltpu.CompilerParams(vmem_limit_bytes=63 << 20),
        name="finish",
    )(*res)
    return (*res[:-1], res[-1].reshape(clips))


def solution(mesh):
    in_specs = (
        P(DP, None),
        P(DP, None),
        P(DP, None),
        P(DP, None),
        P(None, DP, HEAD),
        P(None, DP),
        P(None, HEAD),
        P(None, DP, HEAD),
        P(),
        P(),
        P(),
    )
    out_specs = (
        P(DP, None),
        P(DP, None),
        P(None, DP, HEAD),
        P(None, DP),
        P(None, HEAD),
        P(None, DP, HEAD),
        P(None, DP, HEAD),
        P(None, DP, HEAD),
        P(),
        P(),
        P(),
        P(),
        P(),
    )
    return jax.shard_map(local, mesh=mesh, in_specs=in_specs, out_specs=out_specs, check_vma=False)
```

```python
import functools
import itertools
import math
import types
from typing import Any, NamedTuple

import jax
import jax.numpy as jnp
from jax import lax
from jax.experimental import pallas as pl
from jax.experimental.pallas import tpu as pltpu
from jax.sharding import PartitionSpec as P

DP, HEAD = "dp", "head"
ALL = (DP, HEAD)
D = 512
HEAD_DIM = 64
GRID = 7
SMALL_GRID = 3
WINDOW = 7
IMG_GROUP = 3
CELLS = GRID * GRID
SLOTS = 8
CELL_PAD = CELLS + 1
ROWS = CELL_PAD * SLOTS
PIECES = 5
PIECE = ROWS // PIECES
LANES = 128
WIDE = 256
REACHES = (1, 2, 3, 3)
HALO = WINDOW // 2

NORM_EPS = 1e-06
SQUARE_FLOOR = 1e-30
SECOND_DECAY = 0.999
STEP_RATE = 0.02
SMALL_RATE = 0.05
AVERAGE_KEEP = 0.9
NEG_LARGE = -1e30
ROOT_HALF = 0.7071067811865476
INV_ROOT_TAU = 0.3989422804014327
INV_SCALE = 1.0 / math.sqrt(HEAD_DIM)

F32 = jnp.float32
BF16 = jnp.bfloat16
NN = (((1,), (0,)), ((), ()))
NT = (((1,), (1,)), ((), ()))
TN = (((0,), (0,)), ((), ()))


def dot(a, b, dims=NN):
    return lax.dot_general(a, b, dims, preferred_element_type=F32)


def lane_block(b):
    return slice(b * WIDE, (b + 1) * WIDE)


def wide(col):
    return jnp.concatenate([col] * (D // LANES), axis=1)


def rows_loop(count, size, body, init=None, unroll=1):
    def step(j, carry):
        return body(pl.multiple_of(j * size, size), carry)

    return lax.fori_loop(0, count // size, step, init, unroll=unroll)


def piece_loop(piece, body):
    def step(j, carry):
        body(pl.multiple_of(piece * PIECE + j * 16, 16))
        return carry

    lax.fori_loop(0, PIECE // 16, step, 0, unroll=5)


def conv(src, halo, tap, reach, lanes, put):
    def line(y, _):
        sums = [jnp.zeros((SLOTS, LANES), F32) for _ in range(GRID)]
        for a in range(-reach, reach + 1):
            base = (y + (a + halo)) * GRID
            cells = [src[base + x, :, lanes] for x in range(GRID)]
            for b in range(-reach, reach + 1):
                t = tap(a, b)
                for x in range(GRID):
                    if 0 <= x + b < GRID:
                        sums[x] = sums[x] + t * cells[x + b]
        for x in range(GRID):
            put(y * GRID + x, sums[x])
        return 0

    lax.fori_loop(0, GRID, line, 0)


def tap_sums(up, src, halo, reach, lanes, put):
    for a in range(-reach, reach + 1):

        def line(y, sums):
            sums = list(sums)
            ups = [up(y * GRID + x) for x in range(GRID)]
            base = (y + (a + halo)) * GRID
            cells = [src[base + x, :, lanes] for x in range(GRID)]
            for i, b in enumerate(range(-reach, reach + 1)):
                for x in range(GRID):
                    if 0 <= x + b < GRID:
                        sums[i] = sums[i] + ups[x] * cells[x + b]
            return tuple(sums)

        start = tuple(jnp.zeros((SLOTS, LANES), F32) for _ in range(2 * reach + 1))
        sums = lax.fori_loop(0, GRID, line, start)
        for i, b in enumerate(range(-reach, reach + 1)):
            put(a, b, jnp.sum(sums[i], axis=0, keepdims=True))


def fold(x):
    return jnp.sum(x.reshape(x.shape[0] // SLOTS, SLOTS, x.shape[1]), axis=0)


def erf_parts(h):
    e = lax.erf(h * ROOT_HALF)
    half = 0.5 * (1.0 + e)
    return h * half, half + h * jnp.exp(-0.5 * h * h) * INV_ROOT_TAU


def norm_rows(v, gain, shift):
    centre = jnp.sum(v, axis=1, keepdims=True) * (1.0 / D)
    offset = v - centre
    spread = jnp.sum(offset * offset, axis=1, keepdims=True) * (1.0 / D)
    inverse = lax.rsqrt(spread + NORM_EPS)
    unit = offset * inverse
    return unit * gain + shift, unit, inverse


def norm_back(up, unit, inverse, gain):
    z = up * gain
    mean_z = jnp.sum(z, axis=1, keepdims=True) * (1.0 / D)
    mean_zu = jnp.sum(z * unit, axis=1, keepdims=True) * (1.0 / D)
    return inverse * (z - mean_z - unit * mean_zu)


class Block:
    def __init__(self, refs):
        self.__dict__.update(refs)

    def matrix(self, k, lo, hi):
        parts = []
        for h in range(lo, hi):
            part = self.w[h // 2, h % 2, :, :, :, k]
            if part.shape[-2] % 16:
                part = part.astype(F32).reshape(D, LANES).astype(BF16)
            else:
                part = part.reshape(D, LANES)
            parts.append(part)
        return jnp.concatenate(parts, axis=1)

    def times(self, lhs, k, b):
        return dot(lhs, self.matrix(k, 2 * b, 2 * b + 2))

    def times_t(self, lhs, k, b):
        return dot(lhs, self.matrix(k, 0, 4)[lane_block(b), :], NT)

    def put_grad(self, k, lhs_t, rhs):
        for b in range(2):
            g = dot(lhs_t, rhs[:, lane_block(b)])
            for i in range(2):
                piece = g[:, i * LANES : (i + 1) * LANES]
                place = self.g.shape[2:5]
                piece = piece.reshape(*place, self.g.shape[-2], LANES)
                self.g[b, i, :, :, :, k] = piece.astype(BF16)

    def row(self, j):
        return self.small[j : j + 1, :]

    def setup(self):
        head = lax.axis_index(HEAD)
        slots = self.cls.shape[1]
        self.sums[...] = jnp.zeros(self.sums.shape, F32)
        sub = lax.broadcasted_iota(jnp.int32, (SLOTS, LANES), 0)
        valid = jnp.where(sub < slots, 1.0, 0.0)
        full = jnp.zeros((SLOTS, LANES), F32)
        images = [jnp.zeros((SLOTS, LANES), F32) for _ in range(IMG_GROUP)]
        for s in range(slots):
            full = jnp.where(sub == s, jnp.where(self.cls[head, s] == 0, 1.0, 0.0), full)
            for i in range(IMG_GROUP):
                images[i] = jnp.where(
                    sub == s, jnp.where(self.img[head, s] == i, 1.0, 0.0), images[i]
                )
        for cell in range(CELLS):
            small = cell // GRID < SMALL_GRID and cell % GRID < SMALL_GRID
            self.live[cell * SLOTS : (cell + 1) * SLOTS, :] = valid if small else full
        self.live[CELLS * SLOTS :, :] = jnp.zeros((SLOTS, LANES), F32)
        for i in range(IMG_GROUP):
            self.im8[i] = images[i]
            self.im16[i] = jnp.concatenate([images[i], images[i]], axis=0).astype(BF16)
        self.pos_src[0:GRID] = jnp.zeros((GRID, SLOTS, D), F32)
        self.pos_src[GRID + CELLS :] = jnp.zeros((GRID, SLOTS, D), F32)
        for pad in (self.rel_src, self.dq_src):
            pad[0 : HALO * GRID] = jnp.zeros((HALO * GRID, SLOTS, D), F32)
            pad[HALO * GRID + CELLS :] = jnp.zeros((HALO * GRID, SLOTS, D), F32)
        tap = lax.broadcasted_iota(jnp.int32, (WINDOW * WINDOW, 1), 0)
        row_off = jnp.abs(tap // WINDOW - HALO)
        col_off = jnp.abs(tap % WINDOW - HALO)
        off = jnp.maximum(row_off, col_off)
        heads = lax.broadcasted_iota(jnp.int32, (1, D), 1) // HEAD_DIM
        reach = jnp.where(heads < 2, 1, jnp.where(heads < 5, 2, 3))
        mask = jnp.where(off <= reach, 1.0, 0.0)
        self.window[...] = mask
        self.rel_taps[...] = self.small[22 : 22 + WINDOW * WINDOW, :] * mask

    def place(self, rows_ref, first, r0, size):
        count = rows_ref.shape[0]
        r = r0 + lax.broadcasted_iota(jnp.int32, (size, 1), 0)
        cell, slot = r >> 3, r & 7
        want = first + slot * CELLS + cell
        want = jnp.where((slot < self.cls.shape[1]) & (cell < CELLS), want, -1)
        col = lax.broadcasted_iota(jnp.int32, (size, count), 1)
        pick = jnp.where(col == want, 1.0, 0.0).astype(BF16)
        return dot(pick, rows_ref[...])

    def unplace(self, src_ref, out_ref):
        count = out_ref.shape[0]
        own = self.cls.shape[1] * CELLS
        lead = lax.rem(lax.axis_index(HEAD) * own, 16)
        r = lax.broadcasted_iota(jnp.int32, (1, ROWS), 1)
        cell, slot = r >> 3, r & 7
        target = lead + slot * CELLS + cell
        target = jnp.where((slot < self.cls.shape[1]) & (cell < CELLS), target, -1)
        t = lax.broadcasted_iota(jnp.int32, (count, ROWS), 0)
        pick = jnp.where(t == target, 1.0, 0.0).astype(BF16)
        out_ref[...] = dot(pick, src_ref[...]).astype(BF16)

    def read_tokens(self, piece):
        first = lax.axis_index(HEAD) * (self.cls.shape[1] * CELLS)
        r0 = piece * PIECE
        rows = slice(r0, r0 + PIECE)
        x = self.place(self.tokens, first, r0, PIECE)
        self.first[rows, :] = x
        cells = slice(GRID + r0 // SLOTS, GRID + (r0 + PIECE) // SLOTS)
        self.pos_src[cells] = (x * wide(self.live[rows, :])).reshape(-1, SLOTS, D)

    def read_cotangent(self, piece):
        first = lax.axis_index(HEAD) * (self.cls.shape[1] * CELLS)
        rows = slice(piece * PIECE, (piece + 1) * PIECE)
        c = self.place(self.cot, first, piece * PIECE, PIECE)
        self.go[rows, :] = (c * wide(self.live[rows, :])).astype(BF16)

    def turn_cotangent(self):
        self.go_t[...] = self.go[...].T
        self.back[...] = jnp.zeros((ROWS, D), F32)

    def position(self, c):
        lanes = slice(c * LANES, (c + 1) * LANES)

        def put(cell, value):
            rows = pl.ds(pl.multiple_of(cell * SLOTS, SLOTS), SLOTS)
            self.first[rows, lanes] = self.first[rows, lanes] + value + self.small[8:9, lanes]

        def tap(a, b):
            t = 13 + (a + 1) * 3 + b + 1
            return self.small[t : t + 1, lanes]

        conv(self.pos_src, 1, tap, 1, lanes, put)

    def norm_one(self, piece):
        def body(r0):
            rows = pl.ds(r0, 16)
            n, u, inv = norm_rows(self.first[rows, :], self.row(0), self.row(1))
            self.n1[rows, :] = n.astype(BF16)
            self.u1[rows, :] = u
            self.inv1[rows, :] = jnp.broadcast_to(inv, (16, LANES))

        piece_loop(piece, body)

    def turn_one(self):
        self.n1_t[...] = self.n1[...].T

    def project(self, k, b):
        low, cols = (self.q, self.k, self.v)[k], lane_block(b)
        p = self.times(self.n1[...], k, b)
        if k != 1:
            p = p + self.small[2 + k // 2 : 3 + k // 2, cols]
        low[:, cols] = p.astype(BF16)

    def image_sum(self, x):
        total = jnp.zeros((SLOTS, D), F32)
        for i in range(IMG_GROUP):
            im = wide(self.im8[i])
            total = total + im * jnp.sum(im * x, axis=0, keepdims=True)
        return total

    def key_tops(self):
        def top(r0, best):
            live = wide(self.live[pl.ds(r0, 16), :])
            keys = jnp.where(live > 0, self.k[pl.ds(r0, 16), :].astype(F32), NEG_LARGE)
            return jnp.maximum(best, jnp.max(keys.reshape(2, SLOTS, D), axis=0))

        best = rows_loop(ROWS, 16, top, jnp.full((SLOTS, D), NEG_LARGE, F32), unroll=5)
        shift = jnp.zeros((SLOTS, D), F32)
        for i in range(IMG_GROUP):
            im = wide(self.im8[i])
            most = jnp.max(jnp.where(im > 0, best, NEG_LARGE), axis=0, keepdims=True)
            shift = jnp.where(im > 0, most, shift)
        self.soft_acc[0:SLOTS, :] = shift

    def key_powers(self):
        shift2 = jnp.concatenate([self.soft_acc[0:SLOTS, :]] * 2, axis=0)

        def power(r0, total):
            rows = pl.ds(r0, 16)
            live = wide(self.live[rows, :])
            keys = self.k[rows, :].astype(F32)
            e = jnp.where(live > 0, jnp.exp(jnp.where(live > 0, keys - shift2, 0.0)), 0.0)
            self.soft[rows, :] = e
            return total + fold(e)

        total = rows_loop(ROWS, 16, power, jnp.zeros((SLOTS, D), F32), unroll=5)
        total = self.image_sum(total)
        self.soft_acc[SLOTS : 2 * SLOTS, :] = 1.0 / jnp.where(total > 0, total, 1.0)

    def key_shares(self):
        scale2 = jnp.concatenate([self.soft_acc[SLOTS : 2 * SLOTS, :]] * 2, axis=0)

        def divide(r0, _):
            rows = pl.ds(r0, 16)
            soft = self.soft[rows, :] * scale2
            self.soft[rows, :] = soft
            self.soft_low[rows, :] = soft.astype(BF16)
            return 0

        rows_loop(ROWS, 16, divide, 0, unroll=5)

    def by_image(self, x):
        tiles = x.reshape(ROWS // 16, 16, WIDE)
        parts = []
        for i in range(IMG_GROUP):
            im = jnp.concatenate([self.im16[i]] * (WIDE // LANES), axis=1)
            parts.append((tiles * im[None]).reshape(ROWS, WIDE))
        return jnp.concatenate(parts, axis=1)

    def head_blocks(self, x):
        r = lax.broadcasted_iota(jnp.int32, x.shape, 0) // HEAD_DIM
        c = (lax.broadcasted_iota(jnp.int32, x.shape, 1) % WIDE) // HEAD_DIM
        return jnp.where(r == c, x, 0.0).astype(BF16)

    def stacked(self, x):
        return jnp.concatenate([x[:, lane_block(i)] for i in range(IMG_GROUP)], axis=0)

    def contexts(self, b):
        cols = lane_block(b)
        ctx = dot(self.soft_low[:, cols], self.by_image(self.v[:, cols]), TN)
        ctx = self.head_blocks(ctx)
        self.ctx[b] = ctx
        self.factor[:, cols] = dot(self.by_image(self.q[:, cols]), self.stacked(ctx))

    def fill_window(self):
        def fill(r0, _):
            rows = pl.ds(r0, 16)
            v = self.v[rows, :].astype(F32) * wide(self.live[rows, :])
            c0 = r0 // SLOTS
            self.rel_src[pl.ds(HALO * GRID + c0, 2)] = v.reshape(2, SLOTS, D)
            return 0

        rows_loop(ROWS, 16, fill, 0, unroll=5)
        self.rel[CELLS * SLOTS :, :] = jnp.zeros((SLOTS, D), F32)

    def window_sum(self, c):
        lanes = slice(c * LANES, (c + 1) * LANES)

        def put(cell, value):
            rows = pl.ds(pl.multiple_of(cell * SLOTS, SLOTS), SLOTS)
            self.rel[rows, lanes] = value

        def tap(a, b):
            t = (a + HALO) * WINDOW + b + HALO
            return self.rel_taps[t : t + 1, lanes]

        conv(self.rel_src, HALO, tap, REACHES[c], lanes, put)

    def mix(self):
        def mix(r0, _):
            rows = pl.ds(r0, 16)
            m = self.factor[rows, :] * INV_SCALE + self.q[rows, :].astype(F32) * self.rel[rows, :]
            self.mixed[rows, :] = (m * wide(self.live[rows, :])).astype(BF16)
            return 0

        rows_loop(ROWS, 16, mix, 0, unroll=5)

    def attend(self, b):
        cols = lane_block(b)
        p = self.times_t(self.mixed[...], 3, b)
        self.second[:, cols] = self.first[:, cols] + p + self.small[4:5, cols]

    def norm_two(self, piece):
        def body(r0):
            rows = pl.ds(r0, 16)
            n, u, inv = norm_rows(self.second[rows, :], self.row(5), self.row(6))
            self.n2[rows, :] = n.astype(BF16)
            self.u2[rows, :] = u
            self.inv2[rows, :] = jnp.broadcast_to(inv, (16, LANES))

        piece_loop(piece, body)

    def turn_two(self):
        self.n2_t[...] = self.n2[...].T

    def hidden_in(self, r):
        for b in range(2):
            cols = lane_block(b)
            h = self.times(self.n2[...], 4 + 2 * r, b) + self.small[9 + r : 10 + r, cols]
            self.hidden[:, cols] = h
            self.factor[:, cols] = self.times(self.go[...], 5 + 2 * r, b)

    def hidden_out(self, r):
        def body(r0, total):
            rows = pl.ds(r0, 16)
            act, slope = erf_parts(self.hidden[rows, :])
            g = self.factor[rows, :] * slope
            self.active[rows, :] = act.astype(BF16)
            self.low[rows, :] = g.astype(BF16)
            return total + fold(g)

        total = rows_loop(ROWS, 16, body, jnp.zeros((SLOTS, D), F32), unroll=5)
        self.sums[9 + r : 10 + r, :] = jnp.sum(total, axis=0, keepdims=True)

    def grad_down(self, r):
        self.put_grad(5 + 2 * r, self.go_t[...], self.active)

    def grad_up(self, r):
        self.put_grad(4 + 2 * r, self.n2_t[...], self.low)

    def add_down(self, r):
        for b in range(2):
            self.second[:, lane_block(b)] += self.times_t(self.active[...], 5 + 2 * r, b)

    def add_back(self, r):
        for b in range(2):
            self.back[:, lane_block(b)] += self.times_t(self.low[...], 4 + 2 * r, b)

    def finish_out(self):
        def body(r0, _):
            rows = pl.ds(r0, 16)
            self.out_low[rows, :] = (self.second[rows, :] + self.row(7)).astype(BF16)
            return 0

        rows_loop(ROWS, 16, body, 0, unroll=5)
        self.unplace(self.out_low, self.out_own)

    def back_two(self):
        zero = jnp.zeros((SLOTS, D), F32)

        def body(r0, sums):
            rows = pl.ds(r0, 16)
            back, u = self.back[rows, :], self.u2[rows, :]
            go = self.go[rows, :].astype(F32)
            gs = go + norm_back(back, u, wide(self.inv2[rows, :]), self.row(5))
            self.gs[rows, :] = gs
            self.gs_low[rows, :] = gs.astype(BF16)
            new = (gs, back * u, back, go)
            return tuple(s + fold(n) for s, n in zip(sums, new, strict=True))

        sums = rows_loop(ROWS, 16, body, (zero,) * 4, unroll=5)
        for j, s in zip((4, 5, 6, 7), sums, strict=True):
            self.sums[j : j + 1, :] = jnp.sum(s, axis=0, keepdims=True)

    def grad_proj(self):
        self.put_grad(3, self.gs_low[...].T, self.mixed)

    def back_mixed(self):
        for b in range(2):
            self.d[:, lane_block(b)] = self.times(self.gs_low[...], 3, b)

    def back_fill(self):
        def fill(r0, _):
            rows = pl.ds(r0, 16)
            d = self.d[rows, :] * wide(self.live[rows, :])
            self.d[rows, :] = d
            self.f[rows, :] = (d * INV_SCALE).astype(BF16)
            c0 = r0 // SLOTS
            dq = d * self.q[rows, :].astype(F32)
            self.dq_src[pl.ds(HALO * GRID + c0, 2)] = dq.reshape(2, SLOTS, D)
            return 0

        rows_loop(ROWS, 16, fill, 0, unroll=5)
    def back_heads(self, b):
        cols = lane_block(b)
        f3 = self.by_image(self.f[:, cols])
        g = self.head_blocks(dot(self.q[:, cols], f3, TN))
        self.gq[:, cols] = dot(f3, self.ctx[b], NT)
        self.gk[:, cols] = dot(self.by_image(self.v[:, cols]), g, NT)
        self.gv[:, cols] = dot(self.by_image(self.soft_low[:, cols]), self.stacked(g))

    def back_window(self, c):
        lanes = slice(c * LANES, (c + 1) * LANES)

        def put(cell, value):
            rows = pl.ds(pl.multiple_of(cell * SLOTS, SLOTS), SLOTS)
            self.gv[rows, lanes] = self.gv[rows, lanes] + value * self.live[rows, :]

        def tap(a, b):
            t = (HALO - a) * WINDOW + HALO - b
            return self.rel_taps[t : t + 1, lanes]

        conv(self.dq_src, HALO, tap, REACHES[c], lanes, put)

    def window_taps(self, c):
        lanes = slice(c * LANES, (c + 1) * LANES)

        def up(cell):
            return self.dq_src[HALO * GRID + cell, :, lanes]

        def put_tap(a, b, value):
            t = (a + HALO) * WINDOW + b + HALO
            keep = self.window[t : t + 1, lanes]
            self.sums[22 + t : 23 + t, lanes] = value * keep

        tap_sums(up, self.rel_src, HALO, REACHES[c], lanes, put_tap)

    def back_inner(self):
        def inner(r0, total):
            rows = pl.ds(r0, 16)
            return total + fold(self.soft[rows, :] * self.gk[rows, :])

        total = rows_loop(ROWS, 16, inner, jnp.zeros((SLOTS, D), F32), unroll=5)
        self.soft_acc[0:SLOTS, :] = self.image_sum(total)

    def back_query_key(self):
        zero = jnp.zeros((SLOTS, D), F32)
        shared2 = jnp.concatenate([self.soft_acc[0:SLOTS, :]] * 2, axis=0)

        def low(r0, total):
            rows = pl.ds(r0, 16)
            gq = self.gq[rows, :] + self.d[rows, :] * self.rel[rows, :]
            gk = self.soft[rows, :] * (self.gk[rows, :] - shared2)
            self.gl[0, rows, :] = gq.astype(BF16)
            self.gl[1, rows, :] = gk.astype(BF16)
            return total + fold(gq)

        total = rows_loop(ROWS, 16, low, zero, unroll=5)
        self.sums[2:3, :] = jnp.sum(total, axis=0, keepdims=True)

    def back_value(self):
        def low(r0, total):
            rows = pl.ds(r0, 16)
            gv = self.gv[rows, :]
            self.gl[2, rows, :] = gv.astype(BF16)
            return total + fold(gv)

        total = rows_loop(ROWS, 16, low, jnp.zeros((SLOTS, D), F32), unroll=5)
        self.sums[3:4, :] = jnp.sum(total, axis=0, keepdims=True)

    def grad_of(self, k):
        self.put_grad(k, self.n1_t[...], self.gl.at[k])

    def back_project(self, b):
        back = self.times_t(self.gl[0], 0, b)
        back = back + self.times_t(self.gl[1], 1, b)
        self.back[:, lane_block(b)] = back + self.times_t(self.gl[2], 2, b)

    def back_one(self):
        zero = jnp.zeros((SLOTS, D), F32)
        self.pos_up[0:GRID] = jnp.zeros((GRID, SLOTS, D), F32)
        self.pos_up[GRID + CELLS :] = jnp.zeros((GRID, SLOTS, D), F32)

        def body(r0, sums):
            rows = pl.ds(r0, 16)
            back, u = self.back[rows, :], self.u1[rows, :]
            gf = self.gs[rows, :] + norm_back(back, u, wide(self.inv1[rows, :]), self.row(0))
            c0 = r0 // SLOTS
            self.pos_up[pl.ds(GRID + c0, 2)] = gf.reshape(2, SLOTS, D)
            new = (back * u, back, gf)
            return tuple(s + fold(n) for s, n in zip(sums, new, strict=True))

        sums = rows_loop(ROWS, 16, body, (zero,) * 3, unroll=5)
        for j, s in zip((0, 1, 8), sums, strict=True):
            self.sums[j : j + 1, :] = jnp.sum(s, axis=0, keepdims=True)

    def back_position(self):
        for c in range(D // LANES):
            lanes = slice(c * LANES, (c + 1) * LANES)

            def put(cell, value):
                rows = pl.ds(pl.multiple_of(cell * SLOTS, SLOTS), SLOTS)
                gf = self.pos_up[GRID + cell, :, lanes]
                self.first[rows, lanes] = gf + value * self.live[rows, :]

            def tap(a, b):
                t = 13 + (1 - a) * 3 + 1 - b
                return self.small[t : t + 1, lanes]

            conv(self.pos_up, 1, tap, 1, lanes, put)

    def position_taps(self):
        for c in range(D // LANES):
            lanes = slice(c * LANES, (c + 1) * LANES)

            def up(cell):
                return self.pos_up[GRID + cell, :, lanes]

            def put_tap(a, b, value):
                t = 13 + (a + 1) * 3 + b + 1
                self.sums[t : t + 1, lanes] = value

            tap_sums(up, self.pos_src, 1, 1, lanes, put_tap)

    def finish_in(self):
        def down(r0, _):
            rows = pl.ds(r0, 16)
            self.in_low[rows, :] = self.first[rows, :].astype(BF16)
            return 0

        rows_loop(ROWS, 16, down, 0, unroll=5)
        self.unplace(self.in_low, self.in_own)


SLOT_OF = (0, 1, 2, 3, 4, 6, 8, 10, 5, 7, 9, 11)
MATS = len(SLOT_OF)
EARLY = 4
AXES = "xchly"
HEAD_ROWS = 320
SMALL_ROWS = 72
AG_ROUTES = ("zyxc", "zyxc", "zxyc", "zxyc", "zyxc", "zxyc", "xhlyc", "xyhlc", "xylhc", "hyxlc", "lhxyc", "hlyxc")
RS_ROUTES = ("cylhx", "cxylh", "clyhx", "cyxhl", "cxylh", "cyhxl", "cylhx", "cxyhl", "cxhyl", "clyxh", "clyxh", "cylhx")
ORDER = (
    426, 428, 429, 431, 432, 430, 435, 427, 22, 72, 66, 76, 87, 156, 149, 116, 169, 96, 152, 106,
    127, 434, 11, 136, 86, 107, 446, 129, 450, 172, 176, 448, 69, 433, 0, 439, 436, 437, 81, 73,
    77, 438, 70, 440, 92, 442, 33, 121, 117, 108, 444, 101, 97, 88, 443, 29, 23, 24, 26, 441,
    93, 445, 68, 447, 449, 55, 451, 18, 15, 12, 13, 122, 118, 132, 102, 98, 109, 44, 7, 4,
    1, 2, 30, 25, 27, 110, 147, 40, 34, 37, 35, 111, 126, 19, 14, 16, 67, 146, 91, 62,
    57, 56, 59, 8, 3, 5, 167, 94, 51, 48, 46, 45, 89, 31, 28, 41, 36, 38, 123, 119,
    166, 90, 141, 130, 137, 128, 161, 157, 150, 153, 20, 17, 133, 32, 456, 82, 78, 74, 148, 457,
    463, 71, 464, 466, 21, 63, 60, 454, 58, 113, 115, 465, 455, 458, 52, 47, 9, 6, 459, 49,
    181, 168, 177, 173, 460, 103, 95, 170, 99, 467, 42, 39, 83, 79, 75, 162, 158, 154, 142, 131,
    151, 138, 10, 452, 461, 134, 453, 114, 462, 43, 468, 53, 50, 182, 174, 171, 178, 470, 64, 61,
    112, 469, 472, 143, 139, 135, 473, 471, 104, 100, 474, 163, 155, 159, 475, 84, 80, 54, 476, 65,
    477, 481, 489, 85, 183, 175, 266, 485, 287, 286, 288, 105, 493, 290, 289, 179, 144, 124, 497, 140,
    478, 164, 160, 281, 274, 272, 267, 120, 273, 482, 486, 328, 327, 326, 301, 330, 291, 292, 494, 329,
    294, 293, 490, 308, 310, 269, 145, 165, 306, 309, 270, 271, 498, 184, 180, 268, 125, 479, 341, 334,
    333, 332, 331, 483, 491, 348, 347, 349, 346, 321, 314, 313, 312, 311, 185, 480, 350, 302, 295, 307,
    495, 487, 369, 296, 368, 282, 275, 367, 366, 276, 277, 499, 484, 361, 352, 353, 354, 351, 496, 492,
    387, 389, 388, 390, 386, 297, 488, 409, 408, 406, 381, 373, 372, 501, 410, 407, 528, 371, 500, 342,
    336, 337, 335, 502, 303, 322, 401, 503, 421, 413, 394, 411, 412, 414, 392, 246, 248, 250, 247, 283,
    504, 298, 299, 505, 393, 249, 518, 391, 519, 521, 506, 343, 362, 356, 357, 261, 251, 253, 252, 254,
    382, 376, 511, 315, 377, 370, 520, 507, 355, 422, 513, 417, 416, 338, 508, 402, 415, 395, 396, 397,
    509, 339, 516, 209, 208, 206, 210, 207, 262, 255, 256, 257, 317, 512, 323, 318, 319, 375, 515, 186,
    188, 187, 278, 510, 190, 189, 514, 363, 359, 221, 211, 213, 212, 214, 358, 517, 226, 227, 228, 316,
    374, 279, 522, 423, 344, 418, 419, 403, 201, 191, 192, 399, 398, 304, 529, 193, 194, 523, 340, 229,
    524, 241, 231, 263, 526, 534, 364, 258, 324, 284, 383, 378, 379, 230, 320, 525, 360, 222, 217, 215,
    216, 259, 530, 424, 420, 202, 195, 345, 535, 280, 527, 232, 531, 404, 400, 242, 235, 237, 236, 384,
    380, 197, 365, 264, 325, 196, 223, 425, 219, 218, 203, 198, 536, 199, 285, 260, 243, 238, 233, 239,
    405, 300, 385, 234, 224, 220, 537, 204, 200, 265, 244, 240, 305, 543, 225, 532, 205, 245, 544, 538,
    533, 545, 539, 546, 540, 547, 541, 542, 548, 549,
)


def scratch_of():
    f, h, low = (ROWS, D), (ROWS, LANES), pltpu.VMEM((ROWS, D), BF16)
    halo3 = pltpu.VMEM(((GRID + 2 * HALO) * GRID, SLOTS, D), F32)
    halo1 = pltpu.VMEM(((GRID + 2) * GRID, SLOTS, D), F32)
    high, column, turned = pltpu.VMEM(f, F32), pltpu.VMEM(h, F32), pltpu.VMEM((D, ROWS), BF16)
    taps = pltpu.VMEM((WINDOW * WINDOW, D), F32)
    return dict(
        live=column,
        im8=pltpu.VMEM((IMG_GROUP, SLOTS, LANES), F32),
        im16=pltpu.VMEM((IMG_GROUP, 16, LANES), BF16),
        window=taps,
        rel_taps=taps,
        pos_src=halo1,
        pos_up=halo1,
        rel_src=halo3,
        dq_src=halo3,
        first=high,
        u1=high,
        inv1=column,
        second=high,
        u2=high,
        inv2=column,
        n1=low,
        n1_t=turned,
        n2=low,
        n2_t=turned,
        go=low,
        go_t=turned,
        q=low,
        k=low,
        v=low,
        soft=high,
        soft_low=low,
        soft_acc=pltpu.VMEM((2 * SLOTS, D), F32),
        ctx=pltpu.VMEM((2, WIDE, IMG_GROUP * WIDE), BF16),
        factor=high,
        rel=high,
        mixed=low,
        hidden=high,
        active=low,
        low=low,
        out_low=low,
        back=high,
        gs=high,
        gs_low=low,
        d=high,
        f=low,
        gq=high,
        gk=high,
        gv=high,
        gl=pltpu.VMEM((3, ROWS, D), BF16),
        in_low=low,
    )


class Links:
    def __init__(self):
        dp, head = lax.axis_index(DP), lax.axis_index(HEAD)
        self.far = lax.axis_size(DP) // 4
        self.at = dict(x=head // 2, c=head % 2, h=dp // 4, l=dp // 2 % 2, y=dp % 2)

    def count(self, axis):
        return dict(h=self.far, z=2 * self.far, d=4).get(axis, 2)

    def peer(self, axis, step):
        if axis in "zd":
            one, two = "hl" if axis == "z" else "xy"
            return {one: self.next(one, step // 2), two: self.next(two, step % 2)}
        return {axis: self.next(axis, step)}

    def other(self):
        return self.device("c", 1)

    def next(self, axis, step):
        return lax.rem(self.at[axis] + step, self.count(axis))

    def device(self, axis, step):
        at = {**self.at, **self.peer(axis, step)}
        return (at["h"] * 4 + at["l"] * 2 + at["y"], at["x"] * 2 + at["c"])

    def steps(self, axis, do):
        self.repeat(self.count(axis), do, 8)

    def repeat(self, size, do, most):
        if size <= most:
            for step in range(1, size):
                do(step)
        else:

            def body(step, _):
                do(step)
                return 0

            lax.fori_loop(1, size, body, 0)

    def others(self, name, do):
        dp, head, heads = lax.axis_index(DP), lax.axis_index(HEAD), lax.axis_size(HEAD)

        def one(step):
            if name == ALL:
                i = lax.rem(dp * heads + head + step, lax.axis_size(ALL))
                do((i // heads, lax.rem(i, heads)))
            elif name == DP:
                do((lax.rem(dp + step, lax.axis_size(DP)), head))
            else:
                do((dp, lax.rem(head + step, heads)))

        self.repeat(lax.axis_size(name), one, 32)

    def signal(self):
        def one(device):
            pl.semaphore_signal(
                pltpu.get_barrier_semaphore(),
                inc=1,
                device_id=device,
                device_id_type=pl.DeviceIdType.MESH,
            )

        self.others(DP, one)
        self.others(HEAD, one)

    def meet(self):
        count = lax.axis_size(DP) + lax.axis_size(HEAD) - 2
        pl.semaphore_wait(pltpu.get_barrier_semaphore(), count)

    def copy(self, src, dst, send, recv, device):
        return pltpu.make_async_remote_copy(
            src_ref=src,
            dst_ref=dst,
            send_sem=send,
            recv_sem=recv,
            device_id=device,
            device_id_type=pl.DeviceIdType.MESH,
        )

    def region(self, blocks, slot, whole, **at):
        at = {**self.at, **at}
        whole = whole.replace("z", "hl").replace("d", "xy")
        place = [slice(None) if axis in whole else at[axis] for axis in AXES]
        return blocks.at[(*place, slot)]


class Gather:
    def __init__(self, links, w, sizes, send, recv):
        self.links, self.w, self.sizes, self.send, self.recv = links, w, sizes, send, recv

    def start(self, slot, i, j):
        path, links = AG_ROUTES[slot], self.links

        def along(whole, at):
            part = links.region(self.w, slot, whole, **at)

            def go(step):
                sems = self.send.at[slot], self.recv.at[slot, j]
                links.copy(part, part, *sems, links.device(path[j], step)).start()

            links.steps(path[j], go)

        if i < 0:
            along("", {})
        elif path[i] == "z" and i == 0:
            along("z", {})
        else:
            links.steps(path[i], lambda step: along(path[:i], links.peer(path[i], step)))

    def arrive(self, slot, j):
        path, links = AG_ROUTES[slot], self.links
        blocks = (links.count(path[j]) - 1) * math.prod(links.count(a) for a in path[:j])
        size = self.sizes.at[pl.ds(0, blocks)]
        links.copy(size, size, self.send.at[slot], self.recv.at[slot, j], links.other()).wait_recv()

    def sent(self):
        for slot in range(MATS):
            sems = self.send.at[slot], self.recv.at[slot, 0]
            self.links.copy(self.sizes, self.sizes, *sems, self.links.other()).wait_send()

    def steps(self):
        for slot, path in enumerate(AG_ROUTES):
            for j in range(len(path)):
                for i in range(-1, j):
                    if path[0] != "z" or j == 0 or i >= 0:
                        yield functools.partial(self.start, slot, i, j)
            for j in range(len(path)):
                yield functools.partial(self.arrive, slot, j)


class Scatter:
    def __init__(self, links, g, boxes, total, sizes, send, recv):
        self.links, self.g, self.boxes, self.total = links, g, boxes, total
        self.sizes, self.send, self.recv = sizes, send, recv

    def box(self, slot, j):
        return self.boxes[slot * len(AXES) + j - 1]

    def merged(self, slot, j):
        path = RS_ROUTES[slot]
        return path[-1] == "z" and j == len(path) - 1

    def start(self, slot, i, j):
        path, links = RS_ROUTES[slot], self.links
        first = sum(links.count(a) - 1 for a in path[:i]) - 1
        skip = first + 1 if path[-1] == "z" and j == len(path) else 0

        def go(step):
            entry = first + step - skip
            sems = self.send.at[slot], self.recv.at[slot, j - 1]
            into = self.box(slot, j).at[entry]
            device = links.device(path[i], step)

            def part(into, whole, more):
                src = links.region(self.g, slot, whole, **links.peer(path[i], step), **more)
                links.copy(src, into, *sems, device).start()

            if j == len(path) or self.merged(slot, j):
                part(into, path[j:], {})
            else:
                links.steps(
                    path[j], lambda n: part(into.at[n - 1], path[j + 1 :], links.peer(path[j], n))
                )

        links.steps(path[i], go)

    def add(self, slot, j):
        path, links = RS_ROUTES[slot], self.links
        box = self.box(slot, j)
        sems = self.send.at[slot], self.recv.at[slot, j - 1]
        links.copy(box, box, *sems, links.other()).wait_recv()

        def total(own, pick):
            value = own[...].astype(F32)
            for e in range(box.shape[0]):
                value = value + pick(box.at[e])[...].astype(F32)
            return value

        if j == len(path):
            own = links.region(self.g, slot, "")
            self.total[SLOT_OF.index(slot)] = total(own, lambda b: b)
            return

        def one(n):
            own = links.region(self.g, slot, path[j + 1 :], **links.peer(path[j], n))
            own[...] = total(own, lambda b: b.at[n - 1]).astype(BF16)

        if self.merged(slot, j):
            own = links.region(self.g, slot, "z")
            own[...] = total(own, lambda b: b).astype(BF16)
        else:
            links.steps(path[j], one)

    def sent(self):
        for slot in range(MATS):
            sems = self.send.at[slot], self.recv.at[slot, 0]
            self.links.copy(self.sizes, self.sizes, *sems, self.links.other()).wait_send()

    def steps(self):
        for slot, path in enumerate(RS_ROUTES):
            for i in range(len(path)):
                for j in range(i + 1, len(path) + 1):
                    if not (path[-1] == "z" and j == len(path) and i + 1 < len(path)):
                        yield functools.partial(self.start, slot, i, j)
            for j in range(1, len(path) + 1):
                yield functools.partial(self.add, slot, j)


class Small:
    def __init__(self, links, sums, parts, in_c, in_x, in_y, in_h, in_l, full, send, recv):
        self.links, self.sums, self.parts, self.full = links, sums, parts, full
        self.in_c, self.in_x, self.in_y, self.in_h, self.in_l = in_c, in_x, in_y, in_h, in_l
        self.send, self.recv = send, recv

    def go(self, stage, src, dst, axis):
        sems = (self.send.at[stage], self.recv.at[stage])
        self.links.steps(
            axis, lambda step: self.links.copy(src, dst, *sems, self.links.device(axis, step)).start()
        )

    def wait(self, stage):
        x, c = self.links.at["x"], self.links.at["c"]
        ref = (
            self.in_c,
            self.in_x,
            self.in_y,
            self.in_h.at[pl.ds(0, self.links.far - 1)],
            self.in_l,
            self.full.at[c, x],
            self.full.at[c],
        )[stage]
        sems = (self.send.at[stage], self.recv.at[stage])
        return self.links.copy(ref, ref, *sems, self.links.device("cxyhlxc"[stage], 1))

    def tick(self, stage):
        at = self.links.at
        x, c, h = at["x"], at["c"], at["h"]
        mine = self.parts.at[c, x]
        if stage:
            self.wait(stage - 1).wait_recv()
        if stage == 0:
            for b in range(D // LANES):
                self.parts[b // 2, b % 2] = self.sums[:, b * LANES : (b + 1) * LANES]
            self.go(0, self.parts.at[1 - c], self.in_c, "c")
        if stage == 1:
            self.parts[c] = self.parts[c] + self.in_c[...]
            self.go(1, self.parts.at[c, 1 - x], self.in_x, "x")
        if stage == 2:
            mine[...] = mine[...] + self.in_x[...]
            self.go(2, mine, self.in_y, "y")
        if stage == 3:
            self.in_h[h] = mine[...] + self.in_y[...]
            self.go(3, self.in_h.at[h], self.in_h.at[h], "h")
        if stage == 4:
            total = self.in_h[0]
            for i in range(1, self.links.far):
                total = total + self.in_h[i]
            self.sums[:, 0:LANES] = total
            self.go(4, self.sums.at[:, pl.ds(0, LANES)], self.in_l, "l")
        if stage == 5:
            self.full[c, x] = self.sums[:, 0:LANES] + self.in_l[...]
            self.go(5, self.full.at[c, x], self.full.at[c, x], "x")
        if stage == 6:
            self.go(6, self.full.at[c], self.full.at[c], "c")

    def sent(self):
        for stage in range(7):
            self.wait(stage).wait_send()


class Rows:
    def __init__(self, links, blocks, out, own, send, recv):
        self.links, self.blocks, self.out, self.own = links, blocks, out, own
        self.send, self.recv = send, recv

    def hop(self, i):
        x, c = self.links.at["x"], self.links.at["c"]
        x, axis = ((x, "x"), (x, "c"), (1 - x, "c"))[i]
        block = self.blocks.at[2 * x + c]
        return self.links.copy(
            block, block, self.send.at[i], self.recv.at[i], self.links.device(axis, 1)
        )

    def tick(self, stage):
        if stage == 0:
            self.hop(0).start()
            self.hop(1).start()
        if stage == 1:
            self.hop(0).wait_recv()
            self.hop(2).start()
        if stage == 2:
            self.hop(1).wait_recv()
            self.hop(2).wait_recv()
            self.join()

    def sent(self):
        for i in range(3):
            self.hop(i).wait_send()

    def join(self):
        heads, end, own = self.blocks.shape[0], self.out.shape[0], self.own
        for h in range(heads):
            lo, hi = h * own, (h + 1) * own
            base = lo // 16 * 16
            first = base + 16 if lo % 16 else base
            last = hi // 16 * 16 if h + 1 < heads else end
            self.out[first:last, :] = self.blocks[h, first - base : last - base, :]
            if lo % 16:
                before = (lo - own) // 16 * 16
                tail = self.blocks[h - 1, base - before : base - before + 16, :]
                self.out[base : base + 16, :] = tail + self.blocks[h, 0:16, :]


class Exchange:
    def __init__(self, links, name, buffer, send, recv):
        self.links, self.name, self.buffer, self.send, self.recv = links, name, buffer, send, recv

    def start(self, value):
        own = lax.axis_index(self.name)
        self.buffer[own] = value
        mine = self.buffer.at[own]
        self.links.others(
            self.name,
            lambda device: self.links.copy(mine, mine, self.send, self.recv, device).start(),
        )

    def descriptor(self):
        ref = self.buffer.at[pl.ds(0, self.buffer.shape[0] - 1)]
        return self.links.copy(ref, ref, self.send, self.recv, self.links.device("c", 1))

    def total(self):
        self.descriptor().wait_recv()
        return jnp.sum(self.buffer[...], axis=0)

    def sent(self):
        self.descriptor().wait_send()


def exact(a, b, dims):
    return lax.dot_general(
        a, b, dims, precision=lax.Precision.HIGHEST, preferred_element_type=F32
    )


class Adafactor:
    def __init__(self, refs, lo, hi, row_share, col_share, sq_share):
        self.__dict__.update(refs)
        self.lo, self.hi = lo, hi
        self.row_share, self.col_share, self.sq_share = row_share, col_share, sq_share

    def eye(self, count, first):
        r = lax.broadcasted_iota(jnp.int32, (count, LANES), 0)
        c = lax.broadcasted_iota(jnp.int32, (count, LANES), 1)
        return jnp.where(c == r + first, 1.0, 0.0)

    def lane(self, k, value, rest):
        lanes = lax.broadcasted_iota(jnp.int32, rest.shape, 1)
        return jnp.where(lanes == k, value, rest)

    def squares(self):
        rows, count = self.wg.shape[1], self.hi - self.lo
        by_row = jnp.zeros((rows, LANES), F32)
        by_col = []
        for k in range(self.lo, self.hi):
            g = self.wg[k]
            s = g * g + SQUARE_FLOOR
            by_row = self.lane(k, jnp.sum(s, axis=1, keepdims=True), by_row)
            by_col.append(jnp.sum(s, axis=0, keepdims=True))
        rest = jnp.zeros((SLOTS - count, LANES), F32)
        self.col_share.start(jnp.concatenate([*by_col, rest] if count < SLOTS else by_col, axis=0))
        turned = exact(self.eye(SLOTS, self.lo), by_row, NT)
        if rows < LANES:
            turned = jnp.concatenate([turned, jnp.zeros((SLOTS, LANES - rows), F32)], axis=1)
        self.row_share.start(turned)

    def scale(self):
        rows, lo, hi = self.wg.shape[1], self.lo, self.hi
        total = self.row_share.total()[0 : hi - lo, 0:rows]
        new_rows = SECOND_DECAY * self.row_state[lo:hi, :] + (1.0 - SECOND_DECAY) * (
            total * (1.0 / D)
        )
        self.new_rows[lo:hi, :] = new_rows
        row = exact(new_rows, self.eye(hi - lo, lo), TN)
        total = self.col_share.total()[0 : hi - lo]
        cols = SECOND_DECAY * self.col_state[lo:hi, :] + (1.0 - SECOND_DECAY) * (
            total * (1.0 / D)
        )
        self.new_cols[lo:hi, :] = cols
        sums = jnp.zeros((1, LANES), F32)
        for k in range(lo, hi):
            u = self.wg[k] * lax.rsqrt(row[:, k : k + 1] * cols[k - lo : k - lo + 1, :])
            self.upd[k] = u
            s = jnp.sum(jnp.sum(u * u, axis=0, keepdims=True), axis=1, keepdims=True)
            sums = self.lane(k, s, sums)
        mass = jnp.sum(row, axis=0, keepdims=True)
        self.sq_share.start(jnp.concatenate([sums, mass], axis=0))

    def apply(self):
        total = self.sq_share.total()
        mean = total[1:2] * (1.0 / (D * lax.axis_size(HEAD)))
        rms = jnp.sqrt(total[0:1] * mean * (1.0 / (D * D)))
        rate = STEP_RATE * jnp.sqrt(mean) / jnp.maximum(1.0, rms)
        for k in range(self.lo, self.hi):
            new = self.weights[k] - rate[:, k : k + 1] * self.upd[k]
            self.new_weights[k] = new
            self.copy[k] = new.astype(BF16)
            self.new_ema[k] = AVERAGE_KEEP * self.ema[k] + (1.0 - AVERAGE_KEEP) * new
        self.rms[self.lo // 4 : self.lo // 4 + 1, :] = rms


class SmallStep:
    def __init__(self, refs):
        self.__dict__.update(refs)

    def clips(self):
        lanes = lax.broadcasted_iota(jnp.int32, (1, LANES), 1)
        clip = jnp.where(lanes < EARLY, self.rms[0:1, :], self.rms[1:2, :])
        clip = jnp.where(lanes < MATS, clip, self.small_clip[...])
        self.clip[...] = clip[:, 0 : self.clip.shape[1]]

    def small_step(self):
        count, full = self.small.shape[0], self.full
        g = jnp.concatenate([full[b // 2, b % 2, 0:count, :] for b in range(D // LANES)], axis=1)
        self.small_grads[...] = g
        state = SECOND_DECAY * self.small_state[...] + (1.0 - SECOND_DECAY) * (
            g * g + SQUARE_FLOOR
        )
        self.new_small_state[...] = state
        u = g * lax.rsqrt(state)
        rms = jnp.sqrt(jnp.sum(u * u, axis=1, keepdims=True) * (1.0 / D))
        new = self.small[...] - SMALL_RATE * u / jnp.maximum(1.0, rms)
        self.new_small[...] = new
        self.new_small_ema[...] = AVERAGE_KEEP * self.small_ema[...] + (1.0 - AVERAGE_KEEP) * new
        r = lax.broadcasted_iota(jnp.int32, (count, LANES), 0)
        c = lax.broadcasted_iota(jnp.int32, (count, LANES), 1)
        picked = jnp.where(c == r + MATS, rms, 0.0)
        self.small_clip[...] = jnp.sum(picked, axis=0, keepdims=True)


class Inputs(NamedTuple):
    cls: Any
    img: Any
    tokens: Any
    cot: Any
    weights: Any
    row_state: Any
    col_state: Any
    ema: Any
    small: Any
    small_state: Any
    small_ema: Any


class Outputs(NamedTuple):
    out: Any
    grad_in: Any
    wg: Any
    new_rows: Any
    new_cols: Any
    new_weights: Any
    copy: Any
    new_ema: Any
    small_grads: Any
    new_small_state: Any
    new_small: Any
    new_small_ema: Any
    clip: Any


def box_shapes(links, block):
    for path in RS_ROUTES:
        for j in range(1, len(AXES) + 1):
            entries = sum(links.count(a) - 1 for a in path[:j])
            if j > len(path):
                shape = (1, SLOTS, LANES)
            elif j == len(path):
                first = links.count("z") - 1 if path[-1] == "z" else entries
                shape = (first, *block)
            elif path[-1] == "z" and j == len(path) - 1:
                shape = (entries, links.count("h"), links.count("l"), *block)
            else:
                rest = path[j + 1 :].replace("z", "hl").replace("d", "xy")
                rest = [links.count(a) for a in AXES if a in rest]
                shape = (entries, links.count(path[j]) - 1, *rest, *block)
            yield pltpu.VMEM(shape, BF16)


def shared_of(weights, parts, heads):
    links, (_, rows, _) = Links(), weights.shape
    block = (rows, LANES)
    every = pltpu.VMEM((2, 2, links.far, 2, 2, MATS, *block), BF16)
    out_rows = pltpu.VMEM((heads, HEAD_ROWS, D), BF16)
    dma = pltpu.SemaphoreType.DMA

    def f(*shape):
        return pltpu.VMEM(shape, F32)

    part = f(SMALL_ROWS, LANES)
    return dict(
        w=every,
        g=every,
        out_rows=out_rows,
        in_rows=out_rows,
        sums=f(SMALL_ROWS, D),
        parts=f(2, 2, SMALL_ROWS, LANES),
        in_c=f(2, SMALL_ROWS, LANES),
        in_x=part,
        in_y=part,
        in_h=f(links.far, SMALL_ROWS, LANES),
        in_l=part,
        full=f(2, 2, SMALL_ROWS, LANES),
        row_box=f(2, heads, SLOTS, LANES),
        col_box=f(2, parts, SLOTS, LANES),
        sq_box=f(2, parts * heads, 2, LANES),
        upd=f(MATS, *block),
        small_clip=f(1, LANES),
        rms=f(2, LANES),
        sizes=pltpu.VMEM((parts * heads - 1, *block), BF16),
        ag_send=dma((MATS,)),
        ag_recv=dma((MATS, len(AXES))),
        rs_send=dma((MATS,)),
        rs_recv=dma((MATS, len(AXES))),
        small_send=dma((7,)),
        small_recv=dma((7,)),
        out_send=dma((3,)),
        out_recv=dma((3,)),
        in_send=dma((3,)),
        in_recv=dma((3,)),
        opt_send=dma((2, 3)),
        opt_recv=dma((2, 3)),
        fetched=dma((len(Inputs._fields),)),
        stored=dma((len(Outputs._fields),)),
    )


class Ready:
    def __init__(self, src, dst, sem):
        self.copy = pltpu.make_async_copy(src, dst, sem)
        self.start, self.wait = self.copy.start, self.copy.wait


def then(*steps):
    def run():
        for step in steps:
            step()

    return run


def block_kernel(names, *refs):
    n_in, n_out = len(Inputs._fields), len(Outputs._fields)
    ins, outs, refs = Inputs(*refs[:n_in]), Outputs(*refs[n_in : n_in + n_out]), refs[n_in + n_out :]
    r = types.SimpleNamespace(**dict(zip(names, refs)))
    fetch = Inputs(
        *[
            Ready(ref, getattr(r, name), r.fetched.at[i])
            for i, (name, ref) in enumerate(zip(Inputs._fields, ins))
        ]
    )
    store = Outputs(
        *[
            Ready(getattr(r, name), ref, r.stored.at[i])
            for i, (name, ref) in enumerate(zip(Outputs._fields, outs))
        ]
    )
    boxes = refs[len(names) :]
    links = Links()
    links.signal()
    for one in (fetch.weights, *fetch[0:2], fetch.small, *fetch[2:4], *fetch[5:8], *fetch[9:]):
        one.start()
    r.out_own = r.out_rows.at[lax.axis_index(HEAD)]
    r.in_own = r.in_rows.at[lax.axis_index(HEAD)]
    own = r.cls.shape[1] * CELLS
    blk = Block(vars(r))
    gather = Gather(links, r.w, r.sizes, r.ag_send, r.ag_recv)
    scatter = Scatter(links, r.g, boxes, r.wg, r.sizes, r.rs_send, r.rs_recv)
    small = Small(
        links,
        *(r.sums, r.parts, r.in_c, r.in_x, r.in_y, r.in_h, r.in_l, r.full),
        r.small_send,
        r.small_recv,
    )
    out_rows = Rows(links, r.out_rows, r.out, own, r.out_send, r.out_recv)
    in_rows = Rows(links, r.in_rows, r.grad_in, own, r.in_send, r.in_recv)
    shares, opts = [], []
    for part, (lo, hi) in enumerate(((0, EARLY), (EARLY, MATS))):
        boxes = (HEAD, r.row_box), (DP, r.col_box), (ALL, r.sq_box)
        shares += [
            Exchange(links, axis, box.at[part], r.opt_send.at[part, i], r.opt_recv.at[part, i])
            for i, (axis, box) in enumerate(boxes)
        ]
        opts.append(Adafactor(vars(r), lo, hi, *shares[-3:]))
    step = SmallStep(vars(r))

    def round_weights():
        for k in range(MATS):
            mine = links.region(r.w, SLOT_OF[k], "")
            mine[...] = r.weights[k].astype(BF16)

    ops = [*gather.steps(), *scatter.steps()]
    ops += [then(fetch.weights.wait, round_weights), links.meet]
    ops += [then(fetch.small.wait, fetch.cls.wait, fetch.img.wait, blk.setup)]
    ops += [fetch.tokens.wait, fetch.cot.wait]

    def each(step, *ranges):
        for place in itertools.product(*map(range, ranges)):
            ops.append(functools.partial(step, *place))

    each(blk.read_tokens, PIECES)
    each(blk.position, D // LANES)
    each(blk.norm_one, PIECES)
    ops.append(blk.turn_one)
    each(blk.read_cotangent, PIECES)
    ops.append(blk.turn_cotangent)
    each(blk.project, 3, 2)
    ops += [blk.key_tops, blk.key_powers, blk.key_shares]
    each(blk.contexts, 2)
    ops.append(blk.fill_window)
    each(blk.window_sum, D // LANES)
    ops.append(blk.mix)
    each(blk.attend, 2)
    each(blk.norm_two, PIECES)
    ops.append(blk.turn_two)
    each(blk.hidden_in, 4)
    each(blk.hidden_out, 4)
    each(blk.grad_down, 4)
    each(blk.grad_up, 4)
    each(blk.add_down, 4)
    each(blk.add_back, 4)
    ops += [blk.finish_out, blk.back_two, blk.grad_proj, blk.back_mixed, blk.back_fill]
    each(blk.back_heads, 2)
    ops += [blk.back_inner, blk.back_query_key]
    each(blk.back_window, D // LANES)
    ops.append(blk.back_value)
    each(blk.grad_of, 3)
    each(blk.window_taps, D // LANES)
    each(blk.back_project, 2)
    ops += [blk.back_one, blk.back_position, blk.position_taps, blk.finish_in]
    for rows, done in ((out_rows, store.out), (in_rows, store.grad_in)):
        ops += [functools.partial(rows.tick, stage) for stage in range(2)]
        ops += [then(functools.partial(rows.tick, 2), done.start)]
    ops += [functools.partial(small.tick, stage) for stage in range(8)]
    ops += [
        then(
            fetch.small_state.wait,
            fetch.small_ema.wait,
            step.small_step,
            store.small_grads.start,
            store.new_small_state.start,
            store.new_small.start,
            store.new_small_ema.start,
        ),
        opts[1].squares,
        then(store.wg.start, opts[0].squares),
        then(fetch.row_state.wait, fetch.col_state.wait, opts[1].scale),
        then(opts[0].scale, store.new_rows.start, store.new_cols.start),
        then(fetch.ema.wait, opts[1].apply),
        then(
            opts[0].apply, store.new_weights.start, store.copy.start, store.new_ema.start
        ),
        then(step.clips, store.clip.start),
    ]
    for i in ORDER:
        ops[i]()
    for transfer in (gather, scatter, small, out_rows, in_rows, *shares):
        transfer.sent()
    for one in store:
        one.wait()


def finish_kernel(count, *refs):
    ins, outs, held = refs[:count], refs[count : 2 * count], refs[2 * count : 3 * count]
    took, gave = refs[3 * count :]
    come = [pltpu.make_async_copy(a, b, took.at[i]) for i, (a, b) in enumerate(zip(ins, held))]
    leave = [pltpu.make_async_copy(a, b, gave.at[i]) for i, (a, b) in enumerate(zip(held, outs))]
    for one in come:
        one.start()
    for one, other in zip(come, leave):
        one.wait()
        other.start()
    for one in leave:
        one.wait()


def local(
    tokens,
    cotangent,
    crop_image,
    crop_class,
    weights,
    row_state,
    col_state,
    weights_ema,
    small_params,
    small_state,
    small_ema,
):
    parts, heads = lax.axis_size(DP), lax.axis_size(HEAD)
    shared = shared_of(weights, parts, heads)
    own = scratch_of()

    def like(x, dtype=None):
        return jax.ShapeDtypeStruct(x.shape, dtype or x.dtype)

    clips = weights.shape[0] + small_params.shape[0]
    outs = (
        like(tokens),
        like(tokens),
        like(weights),
        like(row_state),
        like(col_state),
        like(weights),
        like(weights, BF16),
        like(weights),
        like(small_params),
        like(small_params),
        like(small_params),
        like(small_params),
        jax.ShapeDtypeStruct((1, clips), F32),
    )
    args = Inputs(
        crop_class,
        crop_image,
        tokens,
        cotangent,
        weights,
        row_state,
        col_state,
        weights_ema,
        small_params,
        small_state,
        small_ema,
    )
    staged = [pltpu.SMEM(x.shape, x.dtype) for x in args[:2]]
    staged += [pltpu.VMEM(x.shape, x.dtype) for x in (*args[2:], *outs)]
    names = (*shared, *own, *Inputs._fields, *Outputs._fields)
    far = pl.BlockSpec(memory_space=pltpu.HBM)
    res = pl.pallas_call(
        functools.partial(block_kernel, names),
        out_shape=outs,
        in_specs=[far] * len(args),
        out_specs=(far,) * len(outs),
        scratch_shapes=[
            *shared.values(),
            *own.values(),
            *staged,
            *box_shapes(Links(), weights.shape[1:]),
        ],
        compiler_params=pltpu.CompilerParams(
            collective_id=0, has_side_effects=True, vmem_limit_bytes=63 << 20
        ),
        name="block",
    )(*args)
    res = pl.pallas_call(
        functools.partial(finish_kernel, len(outs)),
        out_shape=outs,
        in_specs=[far] * len(outs),
        out_specs=(far,) * len(outs),
        scratch_shapes=[
            *[pltpu.VMEM(x.shape, x.dtype) for x in outs],
            pltpu.SemaphoreType.DMA((len(outs),)),
            pltpu.SemaphoreType.DMA((len(outs),)),
        ],
        compiler_params=pltpu.CompilerParams(vmem_limit_bytes=63 << 20),
        name="finish",
    )(*res)
    return (*res[:-1], res[-1].reshape(clips))


def solution(mesh):
    in_specs = (
        P(DP, None),
        P(DP, None),
        P(DP, None),
        P(DP, None),
        P(None, DP, HEAD),
        P(None, DP),
        P(None, HEAD),
        P(None, DP, HEAD),
        P(),
        P(),
        P(),
    )
    out_specs = (
        P(DP, None),
        P(DP, None),
        P(None, DP, HEAD),
        P(None, DP),
        P(None, HEAD),
        P(None, DP, HEAD),
        P(None, DP, HEAD),
        P(None, DP, HEAD),
        P(),
        P(),
        P(),
        P(),
        P(),
    )
    return jax.shard_map(local, mesh=mesh, in_specs=in_specs, out_specs=out_specs, check_vma=False)
```

```python
import functools
import itertools
import math
import types
from typing import Any, NamedTuple

import jax
import jax.numpy as jnp
from jax import lax
from jax.experimental import pallas as pl
from jax.experimental.pallas import tpu as pltpu
from jax.sharding import PartitionSpec as P

DP, HEAD = "dp", "head"
ALL = (DP, HEAD)
D = 512
HEAD_DIM = 64
GRID = 7
SMALL_GRID = 3
WINDOW = 7
IMG_GROUP = 3
CELLS = GRID * GRID
SLOTS = 8
CELL_PAD = CELLS + 1
ROWS = CELL_PAD * SLOTS
PIECES = 5
PIECE = ROWS // PIECES
LANES = 128
WIDE = 256
REACHES = (1, 2, 3, 3)
HALO = WINDOW // 2

NORM_EPS = 1e-06
SQUARE_FLOOR = 1e-30
SECOND_DECAY = 0.999
STEP_RATE = 0.02
SMALL_RATE = 0.05
AVERAGE_KEEP = 0.9
NEG_LARGE = -1e30
ROOT_HALF = 0.7071067811865476
INV_ROOT_TAU = 0.3989422804014327
INV_SCALE = 1.0 / math.sqrt(HEAD_DIM)

F32 = jnp.float32
BF16 = jnp.bfloat16
NN = (((1,), (0,)), ((), ()))
NT = (((1,), (1,)), ((), ()))
TN = (((0,), (0,)), ((), ()))


def dot(a, b, dims=NN):
    return lax.dot_general(a, b, dims, preferred_element_type=F32)


def lane_block(b):
    return slice(b * WIDE, (b + 1) * WIDE)


def wide(col):
    return jnp.concatenate([col] * (D // LANES), axis=1)


def rows_loop(count, size, body, init=None, unroll=1):
    def step(j, carry):
        return body(pl.multiple_of(j * size, size), carry)

    return lax.fori_loop(0, count // size, step, init, unroll=unroll)


def piece_loop(piece, body):
    def step(j, carry):
        body(pl.multiple_of(piece * PIECE + j * 16, 16))
        return carry

    lax.fori_loop(0, PIECE // 16, step, 0, unroll=5)


def conv(src, halo, tap, reach, lanes, put):
    def line(y, _):
        sums = [jnp.zeros((SLOTS, LANES), F32) for _ in range(GRID)]
        for a in range(-reach, reach + 1):
            base = (y + (a + halo)) * GRID
            cells = [src[base + x, :, lanes] for x in range(GRID)]
            for b in range(-reach, reach + 1):
                t = tap(a, b)
                for x in range(GRID):
                    if 0 <= x + b < GRID:
                        sums[x] = sums[x] + t * cells[x + b]
        for x in range(GRID):
            put(y * GRID + x, sums[x])
        return 0

    lax.fori_loop(0, GRID, line, 0)


def tap_sums(up, src, halo, reach, lanes, put):
    for a in range(-reach, reach + 1):

        def line(y, sums):
            sums = list(sums)
            ups = [up(y * GRID + x) for x in range(GRID)]
            base = (y + (a + halo)) * GRID
            cells = [src[base + x, :, lanes] for x in range(GRID)]
            for i, b in enumerate(range(-reach, reach + 1)):
                for x in range(GRID):
                    if 0 <= x + b < GRID:
                        sums[i] = sums[i] + ups[x] * cells[x + b]
            return tuple(sums)

        start = tuple(jnp.zeros((SLOTS, LANES), F32) for _ in range(2 * reach + 1))
        sums = lax.fori_loop(0, GRID, line, start)
        for i, b in enumerate(range(-reach, reach + 1)):
            put(a, b, jnp.sum(sums[i], axis=0, keepdims=True))


def fold(x):
    return jnp.sum(x.reshape(x.shape[0] // SLOTS, SLOTS, x.shape[1]), axis=0)


def erf_parts(h):
    e = lax.erf(h * ROOT_HALF)
    half = 0.5 * (1.0 + e)
    return h * half, half + h * jnp.exp(-0.5 * h * h) * INV_ROOT_TAU


def norm_rows(v, gain, shift):
    centre = jnp.sum(v, axis=1, keepdims=True) * (1.0 / D)
    offset = v - centre
    spread = jnp.sum(offset * offset, axis=1, keepdims=True) * (1.0 / D)
    inverse = lax.rsqrt(spread + NORM_EPS)
    unit = offset * inverse
    return unit * gain + shift, unit, inverse


def norm_back(up, unit, inverse, gain):
    z = up * gain
    mean_z = jnp.sum(z, axis=1, keepdims=True) * (1.0 / D)
    mean_zu = jnp.sum(z * unit, axis=1, keepdims=True) * (1.0 / D)
    return inverse * (z - mean_z - unit * mean_zu)


class Block:
    def __init__(self, refs):
        self.__dict__.update(refs)

    def matrix(self, k, lo, hi):
        parts = []
        for h in range(lo, hi):
            part = self.w[h // 2, h % 2, :, :, :, k]
            if part.shape[-2] % 16:
                part = part.astype(F32).reshape(D, LANES).astype(BF16)
            else:
                part = part.reshape(D, LANES)
            parts.append(part)
        return jnp.concatenate(parts, axis=1)

    def times(self, lhs, k, b):
        return dot(lhs, self.matrix(k, 2 * b, 2 * b + 2))

    def times_t(self, lhs, k, b):
        return dot(lhs, self.matrix(k, 0, 4)[lane_block(b), :], NT)

    def put_grad(self, k, lhs_t, rhs):
        for b in range(2):
            g = dot(lhs_t, rhs[:, lane_block(b)])
            for i in range(2):
                piece = g[:, i * LANES : (i + 1) * LANES]
                place = self.g.shape[2:5]
                piece = piece.reshape(*place, self.g.shape[-2], LANES)
                self.g[b, i, :, :, :, k] = piece.astype(BF16)

    def row(self, j):
        return self.small[j : j + 1, :]

    def setup(self):
        head = lax.axis_index(HEAD)
        slots = self.cls.shape[1]
        self.sums[...] = jnp.zeros(self.sums.shape, F32)
        sub = lax.broadcasted_iota(jnp.int32, (SLOTS, LANES), 0)
        valid = jnp.where(sub < slots, 1.0, 0.0)
        full = jnp.zeros((SLOTS, LANES), F32)
        images = [jnp.zeros((SLOTS, LANES), F32) for _ in range(IMG_GROUP)]
        for s in range(slots):
            full = jnp.where(sub == s, jnp.where(self.cls[head, s] == 0, 1.0, 0.0), full)
            for i in range(IMG_GROUP):
                images[i] = jnp.where(
                    sub == s, jnp.where(self.img[head, s] == i, 1.0, 0.0), images[i]
                )
        for cell in range(CELLS):
            small = cell // GRID < SMALL_GRID and cell % GRID < SMALL_GRID
            self.live[cell * SLOTS : (cell + 1) * SLOTS, :] = valid if small else full
        self.live[CELLS * SLOTS :, :] = jnp.zeros((SLOTS, LANES), F32)
        for i in range(IMG_GROUP):
            self.im8[i] = images[i]
            self.im16[i] = jnp.concatenate([images[i], images[i]], axis=0).astype(BF16)
        self.pos_src[0:GRID] = jnp.zeros((GRID, SLOTS, D), F32)
        self.pos_src[GRID + CELLS :] = jnp.zeros((GRID, SLOTS, D), F32)
        for pad in (self.rel_src, self.dq_src):
            pad[0 : HALO * GRID] = jnp.zeros((HALO * GRID, SLOTS, D), F32)
            pad[HALO * GRID + CELLS :] = jnp.zeros((HALO * GRID, SLOTS, D), F32)
        tap = lax.broadcasted_iota(jnp.int32, (WINDOW * WINDOW, 1), 0)
        row_off = jnp.abs(tap // WINDOW - HALO)
        col_off = jnp.abs(tap % WINDOW - HALO)
        off = jnp.maximum(row_off, col_off)
        heads = lax.broadcasted_iota(jnp.int32, (1, D), 1) // HEAD_DIM
        reach = jnp.where(heads < 2, 1, jnp.where(heads < 5, 2, 3))
        mask = jnp.where(off <= reach, 1.0, 0.0)
        self.window[...] = mask
        self.rel_taps[...] = self.small[22 : 22 + WINDOW * WINDOW, :] * mask

    def place(self, rows_ref, first, r0, size):
        base = pl.multiple_of(first // 16 * 16, 16)
        r = r0 + lax.broadcasted_iota(jnp.int32, (size, 1), 0)
        cell, slot = r >> 3, r & 7
        want = first - base + slot * CELLS + cell
        want = jnp.where((slot < self.cls.shape[1]) & (cell < CELLS), want, -1)
        col = lax.broadcasted_iota(jnp.int32, (size, HEAD_ROWS), 1)
        pick = jnp.where(col == want, 1.0, 0.0).astype(BF16)
        return dot(pick, rows_ref[pl.ds(base, HEAD_ROWS), :])

    def unplace(self, src_ref, out_ref):
        count = out_ref.shape[0]
        own = self.cls.shape[1] * CELLS
        lead = lax.rem(lax.axis_index(HEAD) * own, 16)
        r = lax.broadcasted_iota(jnp.int32, (1, ROWS), 1)
        cell, slot = r >> 3, r & 7
        target = lead + slot * CELLS + cell
        target = jnp.where((slot < self.cls.shape[1]) & (cell < CELLS), target, -1)
        t = lax.broadcasted_iota(jnp.int32, (count, ROWS), 0)
        pick = jnp.where(t == target, 1.0, 0.0).astype(BF16)
        out_ref[...] = dot(pick, src_ref[...]).astype(BF16)

    def read_tokens(self, piece):
        first = lax.axis_index(HEAD) * (self.cls.shape[1] * CELLS)
        r0 = piece * PIECE
        rows = slice(r0, r0 + PIECE)
        x = self.place(self.tokens, first, r0, PIECE)
        self.first[rows, :] = x
        cells = slice(GRID + r0 // SLOTS, GRID + (r0 + PIECE) // SLOTS)
        self.pos_src[cells] = (x * wide(self.live[rows, :])).reshape(-1, SLOTS, D)

    def read_cotangent(self, piece):
        first = lax.axis_index(HEAD) * (self.cls.shape[1] * CELLS)
        rows = slice(piece * PIECE, (piece + 1) * PIECE)
        c = self.place(self.cot, first, piece * PIECE, PIECE)
        self.go[rows, :] = (c * wide(self.live[rows, :])).astype(BF16)

    def turn_cotangent(self):
        self.go_t[...] = self.go[...].T
        self.back[...] = jnp.zeros((ROWS, D), F32)

    def position(self, c):
        lanes = slice(c * LANES, (c + 1) * LANES)

        def put(cell, value):
            rows = pl.ds(pl.multiple_of(cell * SLOTS, SLOTS), SLOTS)
            self.first[rows, lanes] = self.first[rows, lanes] + value + self.small[8:9, lanes]

        def tap(a, b):
            t = 13 + (a + 1) * 3 + b + 1
            return self.small[t : t + 1, lanes]

        conv(self.pos_src, 1, tap, 1, lanes, put)

    def norm_one(self, piece):
        def body(r0):
            rows = pl.ds(r0, 16)
            n, u, inv = norm_rows(self.first[rows, :], self.row(0), self.row(1))
            self.n1[rows, :] = n.astype(BF16)
            self.u1[rows, :] = u
            self.inv1[rows, :] = jnp.broadcast_to(inv, (16, LANES))

        piece_loop(piece, body)

    def turn_one(self):
        self.n1_t[...] = self.n1[...].T

    def project(self, k, b):
        low, cols = (self.q, self.k, self.v)[k], lane_block(b)
        p = self.times(self.n1[...], k, b)
        if k != 1:
            p = p + self.small[2 + k // 2 : 3 + k // 2, cols]
        low[:, cols] = p.astype(BF16)

    def image_sum(self, x):
        total = jnp.zeros((SLOTS, D), F32)
        for i in range(IMG_GROUP):
            im = wide(self.im8[i])
            total = total + im * jnp.sum(im * x, axis=0, keepdims=True)
        return total

    def key_tops(self):
        def top(r0, best):
            live = wide(self.live[pl.ds(r0, 16), :])
            keys = jnp.where(live > 0, self.k[pl.ds(r0, 16), :].astype(F32), NEG_LARGE)
            return jnp.maximum(best, jnp.max(keys.reshape(2, SLOTS, D), axis=0))

        best = rows_loop(ROWS, 16, top, jnp.full((SLOTS, D), NEG_LARGE, F32), unroll=5)
        shift = jnp.zeros((SLOTS, D), F32)
        for i in range(IMG_GROUP):
            im = wide(self.im8[i])
            most = jnp.max(jnp.where(im > 0, best, NEG_LARGE), axis=0, keepdims=True)
            shift = jnp.where(im > 0, most, shift)
        self.soft_acc[0:SLOTS, :] = shift

    def key_powers(self):
        shift2 = jnp.concatenate([self.soft_acc[0:SLOTS, :]] * 2, axis=0)

        def power(r0, total):
            rows = pl.ds(r0, 16)
            live = wide(self.live[rows, :])
            keys = self.k[rows, :].astype(F32)
            e = jnp.where(live > 0, jnp.exp(jnp.where(live > 0, keys - shift2, 0.0)), 0.0)
            self.soft[rows, :] = e
            return total + fold(e)

        total = rows_loop(ROWS, 16, power, jnp.zeros((SLOTS, D), F32), unroll=5)
        total = self.image_sum(total)
        self.soft_acc[SLOTS : 2 * SLOTS, :] = 1.0 / jnp.where(total > 0, total, 1.0)

    def key_shares(self):
        scale2 = jnp.concatenate([self.soft_acc[SLOTS : 2 * SLOTS, :]] * 2, axis=0)

        def divide(r0, _):
            rows = pl.ds(r0, 16)
            soft = self.soft[rows, :] * scale2
            self.soft[rows, :] = soft
            self.soft_low[rows, :] = soft.astype(BF16)
            return 0

        rows_loop(ROWS, 16, divide, 0, unroll=5)

    def by_image(self, x):
        tiles = x.reshape(ROWS // 16, 16, WIDE)
        parts = []
        for i in range(IMG_GROUP):
            im = jnp.concatenate([self.im16[i]] * (WIDE // LANES), axis=1)
            parts.append((tiles * im[None]).reshape(ROWS, WIDE))
        return jnp.concatenate(parts, axis=1)

    def head_blocks(self, x):
        r = lax.broadcasted_iota(jnp.int32, x.shape, 0) // HEAD_DIM
        c = (lax.broadcasted_iota(jnp.int32, x.shape, 1) % WIDE) // HEAD_DIM
        return jnp.where(r == c, x, 0.0).astype(BF16)

    def stacked(self, x):
        return jnp.concatenate([x[:, lane_block(i)] for i in range(IMG_GROUP)], axis=0)

    def contexts(self, b):
        cols = lane_block(b)
        ctx = dot(self.soft_low[:, cols], self.by_image(self.v[:, cols]), TN)
        ctx = self.head_blocks(ctx)
        self.ctx[b] = ctx
        self.factor[:, cols] = dot(self.by_image(self.q[:, cols]), self.stacked(ctx))

    def fill_window(self):
        def fill(r0, _):
            rows = pl.ds(r0, 16)
            v = self.v[rows, :].astype(F32) * wide(self.live[rows, :])
            c0 = r0 // SLOTS
            self.rel_src[pl.ds(HALO * GRID + c0, 2)] = v.reshape(2, SLOTS, D)
            return 0

        rows_loop(ROWS, 16, fill, 0, unroll=5)
        self.rel[CELLS * SLOTS :, :] = jnp.zeros((SLOTS, D), F32)

    def window_sum(self, c):
        lanes = slice(c * LANES, (c + 1) * LANES)

        def put(cell, value):
            rows = pl.ds(pl.multiple_of(cell * SLOTS, SLOTS), SLOTS)
            self.rel[rows, lanes] = value

        def tap(a, b):
            t = (a + HALO) * WINDOW + b + HALO
            return self.rel_taps[t : t + 1, lanes]

        conv(self.rel_src, HALO, tap, REACHES[c], lanes, put)

    def mix(self):
        def mix(r0, _):
            rows = pl.ds(r0, 16)
            m = self.factor[rows, :] * INV_SCALE + self.q[rows, :].astype(F32) * self.rel[rows, :]
            self.mixed[rows, :] = (m * wide(self.live[rows, :])).astype(BF16)
            return 0

        rows_loop(ROWS, 16, mix, 0, unroll=5)

    def attend(self, b):
        cols = lane_block(b)
        p = self.times_t(self.mixed[...], 3, b)
        self.second[:, cols] = self.first[:, cols] + p + self.small[4:5, cols]

    def norm_two(self, piece):
        def body(r0):
            rows = pl.ds(r0, 16)
            n, u, inv = norm_rows(self.second[rows, :], self.row(5), self.row(6))
            self.n2[rows, :] = n.astype(BF16)
            self.u2[rows, :] = u
            self.inv2[rows, :] = jnp.broadcast_to(inv, (16, LANES))

        piece_loop(piece, body)

    def turn_two(self):
        self.n2_t[...] = self.n2[...].T

    def hidden_in(self, r):
        for b in range(2):
            cols = lane_block(b)
            h = self.times(self.n2[...], 4 + 2 * r, b) + self.small[9 + r : 10 + r, cols]
            self.hidden[:, cols] = h
            self.factor[:, cols] = self.times(self.go[...], 5 + 2 * r, b)

    def hidden_out(self, r):
        def body(r0, total):
            rows = pl.ds(r0, 16)
            act, slope = erf_parts(self.hidden[rows, :])
            g = self.factor[rows, :] * slope
            self.active[rows, :] = act.astype(BF16)
            self.low[rows, :] = g.astype(BF16)
            return total + fold(g)

        total = rows_loop(ROWS, 16, body, jnp.zeros((SLOTS, D), F32), unroll=5)
        self.sums[9 + r : 10 + r, :] = jnp.sum(total, axis=0, keepdims=True)

    def grad_down(self, r):
        self.put_grad(5 + 2 * r, self.go_t[...], self.active)

    def grad_up(self, r):
        self.put_grad(4 + 2 * r, self.n2_t[...], self.low)

    def add_down(self, r):
        for b in range(2):
            self.second[:, lane_block(b)] += self.times_t(self.active[...], 5 + 2 * r, b)

    def add_back(self, r):
        for b in range(2):
            self.back[:, lane_block(b)] += self.times_t(self.low[...], 4 + 2 * r, b)

    def finish_out(self):
        def body(r0, _):
            rows = pl.ds(r0, 16)
            self.out_low[rows, :] = (self.second[rows, :] + self.row(7)).astype(BF16)
            return 0

        rows_loop(ROWS, 16, body, 0, unroll=5)
        self.unplace(self.out_low, self.out_own)

    def back_two(self):
        zero = jnp.zeros((SLOTS, D), F32)

        def body(r0, sums):
            rows = pl.ds(r0, 16)
            back, u = self.back[rows, :], self.u2[rows, :]
            go = self.go[rows, :].astype(F32)
            gs = go + norm_back(back, u, wide(self.inv2[rows, :]), self.row(5))
            self.gs[rows, :] = gs
            self.gs_low[rows, :] = gs.astype(BF16)
            new = (gs, back * u, back, go)
            return tuple(s + fold(n) for s, n in zip(sums, new, strict=True))

        sums = rows_loop(ROWS, 16, body, (zero,) * 4, unroll=5)
        for j, s in zip((4, 5, 6, 7), sums, strict=True):
            self.sums[j : j + 1, :] = jnp.sum(s, axis=0, keepdims=True)

    def grad_proj(self):
        self.put_grad(3, self.gs_low[...].T, self.mixed)

    def back_mixed(self):
        for b in range(2):
            self.d[:, lane_block(b)] = self.times(self.gs_low[...], 3, b)

    def back_fill(self):
        def fill(r0, _):
            rows = pl.ds(r0, 16)
            d = self.d[rows, :] * wide(self.live[rows, :])
            self.d[rows, :] = d
            self.f[rows, :] = (d * INV_SCALE).astype(BF16)
            c0 = r0 // SLOTS
            dq = d * self.q[rows, :].astype(F32)
            self.dq_src[pl.ds(HALO * GRID + c0, 2)] = dq.reshape(2, SLOTS, D)
            return 0

        rows_loop(ROWS, 16, fill, 0, unroll=5)
    def back_heads(self, b):
        cols = lane_block(b)
        f3 = self.by_image(self.f[:, cols])
        g = self.head_blocks(dot(self.q[:, cols], f3, TN))
        self.gq[:, cols] = dot(f3, self.ctx[b], NT)
        self.gk[:, cols] = dot(self.by_image(self.v[:, cols]), g, NT)
        self.gv[:, cols] = dot(self.by_image(self.soft_low[:, cols]), self.stacked(g))

    def back_window(self, c):
        lanes = slice(c * LANES, (c + 1) * LANES)

        def put(cell, value):
            rows = pl.ds(pl.multiple_of(cell * SLOTS, SLOTS), SLOTS)
            self.gv[rows, lanes] = self.gv[rows, lanes] + value * self.live[rows, :]

        def tap(a, b):
            t = (HALO - a) * WINDOW + HALO - b
            return self.rel_taps[t : t + 1, lanes]

        conv(self.dq_src, HALO, tap, REACHES[c], lanes, put)

    def window_taps(self, c):
        lanes = slice(c * LANES, (c + 1) * LANES)

        def up(cell):
            return self.dq_src[HALO * GRID + cell, :, lanes]

        def put_tap(a, b, value):
            t = (a + HALO) * WINDOW + b + HALO
            keep = self.window[t : t + 1, lanes]
            self.sums[22 + t : 23 + t, lanes] = value * keep

        tap_sums(up, self.rel_src, HALO, REACHES[c], lanes, put_tap)

    def back_inner(self):
        def inner(r0, total):
            rows = pl.ds(r0, 16)
            return total + fold(self.soft[rows, :] * self.gk[rows, :])

        total = rows_loop(ROWS, 16, inner, jnp.zeros((SLOTS, D), F32), unroll=5)
        self.soft_acc[0:SLOTS, :] = self.image_sum(total)

    def back_query_key(self):
        zero = jnp.zeros((SLOTS, D), F32)
        shared2 = jnp.concatenate([self.soft_acc[0:SLOTS, :]] * 2, axis=0)

        def low(r0, total):
            rows = pl.ds(r0, 16)
            gq = self.gq[rows, :] + self.d[rows, :] * self.rel[rows, :]
            gk = self.soft[rows, :] * (self.gk[rows, :] - shared2)
            self.gl[0, rows, :] = gq.astype(BF16)
            self.gl[1, rows, :] = gk.astype(BF16)
            return total + fold(gq)

        total = rows_loop(ROWS, 16, low, zero, unroll=5)
        self.sums[2:3, :] = jnp.sum(total, axis=0, keepdims=True)

    def back_value(self):
        def low(r0, total):
            rows = pl.ds(r0, 16)
            gv = self.gv[rows, :]
            self.gl[2, rows, :] = gv.astype(BF16)
            return total + fold(gv)

        total = rows_loop(ROWS, 16, low, jnp.zeros((SLOTS, D), F32), unroll=5)
        self.sums[3:4, :] = jnp.sum(total, axis=0, keepdims=True)

    def grad_of(self, k):
        self.put_grad(k, self.n1_t[...], self.gl.at[k])

    def back_project(self, b):
        back = self.times_t(self.gl[0], 0, b)
        back = back + self.times_t(self.gl[1], 1, b)
        self.back[:, lane_block(b)] = back + self.times_t(self.gl[2], 2, b)

    def back_one(self):
        zero = jnp.zeros((SLOTS, D), F32)
        self.pos_up[0:GRID] = jnp.zeros((GRID, SLOTS, D), F32)
        self.pos_up[GRID + CELLS :] = jnp.zeros((GRID, SLOTS, D), F32)

        def body(r0, sums):
            rows = pl.ds(r0, 16)
            back, u = self.back[rows, :], self.u1[rows, :]
            gf = self.gs[rows, :] + norm_back(back, u, wide(self.inv1[rows, :]), self.row(0))
            c0 = r0 // SLOTS
            self.pos_up[pl.ds(GRID + c0, 2)] = gf.reshape(2, SLOTS, D)
            new = (back * u, back, gf)
            return tuple(s + fold(n) for s, n in zip(sums, new, strict=True))

        sums = rows_loop(ROWS, 16, body, (zero,) * 3, unroll=5)
        for j, s in zip((0, 1, 8), sums, strict=True):
            self.sums[j : j + 1, :] = jnp.sum(s, axis=0, keepdims=True)

    def back_position(self):
        for c in range(D // LANES):
            lanes = slice(c * LANES, (c + 1) * LANES)

            def put(cell, value):
                rows = pl.ds(pl.multiple_of(cell * SLOTS, SLOTS), SLOTS)
                gf = self.pos_up[GRID + cell, :, lanes]
                self.first[rows, lanes] = gf + value * self.live[rows, :]

            def tap(a, b):
                t = 13 + (1 - a) * 3 + 1 - b
                return self.small[t : t + 1, lanes]

            conv(self.pos_up, 1, tap, 1, lanes, put)

    def position_taps(self):
        for c in range(D // LANES):
            lanes = slice(c * LANES, (c + 1) * LANES)

            def up(cell):
                return self.pos_up[GRID + cell, :, lanes]

            def put_tap(a, b, value):
                t = 13 + (a + 1) * 3 + b + 1
                self.sums[t : t + 1, lanes] = value

            tap_sums(up, self.pos_src, 1, 1, lanes, put_tap)

    def finish_in(self):
        def down(r0, _):
            rows = pl.ds(r0, 16)
            self.in_low[rows, :] = self.first[rows, :].astype(BF16)
            return 0

        rows_loop(ROWS, 16, down, 0, unroll=5)
        self.unplace(self.in_low, self.in_own)


SLOT_OF = (0, 1, 2, 3, 4, 6, 8, 10, 5, 7, 9, 11)
MATS = len(SLOT_OF)
EARLY = 4
AXES = "xchly"
HEAD_ROWS = 320
SMALL_ROWS = 72
AG_ROUTES = ("zyxc", "zyxc", "zxyc", "zxyc", "zyxc", "zxyc", "xhlyc", "xyhlc", "xylhc", "hyxlc", "lhxyc", "hlyxc")
RS_ROUTES = ("cylhx", "cxylh", "clyhx", "cyxhl", "cxylh", "cyhxl", "cylhx", "cxyhl", "cxhyl", "clyxh", "clyxh", "cylhx")
ORDER = (
    426, 428, 429, 431, 432, 430, 435, 427, 22, 72, 66, 76, 87, 156, 149, 116, 169, 96, 152, 106,
    127, 434, 11, 136, 86, 107, 446, 129, 450, 172, 176, 448, 69, 433, 0, 439, 436, 437, 81, 73,
    77, 438, 70, 440, 92, 442, 33, 121, 117, 108, 444, 101, 97, 88, 443, 29, 23, 24, 26, 441,
    93, 445, 68, 447, 449, 55, 451, 18, 15, 12, 13, 122, 118, 132, 102, 98, 109, 44, 7, 4,
    1, 2, 30, 25, 27, 110, 147, 40, 34, 37, 35, 111, 126, 19, 14, 16, 67, 146, 91, 62,
    57, 56, 59, 8, 3, 5, 167, 94, 51, 48, 46, 45, 89, 31, 28, 41, 36, 38, 123, 119,
    166, 90, 141, 130, 137, 128, 161, 157, 150, 153, 20, 17, 133, 32, 456, 82, 78, 74, 148, 457,
    463, 71, 464, 466, 21, 63, 60, 454, 58, 113, 115, 465, 455, 458, 52, 47, 9, 6, 459, 49,
    181, 168, 177, 173, 460, 103, 95, 170, 99, 467, 42, 39, 83, 79, 75, 162, 158, 154, 142, 131,
    151, 138, 10, 452, 461, 134, 453, 114, 462, 43, 468, 53, 50, 182, 174, 171, 178, 470, 64, 61,
    112, 469, 472, 143, 139, 135, 473, 471, 104, 100, 474, 163, 155, 159, 475, 84, 80, 54, 476, 65,
    477, 481, 489, 85, 183, 175, 266, 485, 287, 286, 288, 105, 493, 290, 289, 179, 144, 124, 497, 140,
    478, 164, 160, 281, 274, 272, 267, 120, 273, 482, 486, 328, 327, 326, 301, 330, 291, 292, 494, 329,
    294, 293, 490, 308, 310, 269, 145, 165, 306, 309, 270, 271, 498, 184, 180, 268, 125, 479, 341, 334,
    333, 332, 331, 483, 491, 348, 347, 349, 346, 321, 314, 313, 312, 311, 185, 480, 350, 302, 295, 307,
    495, 487, 369, 296, 368, 282, 275, 367, 366, 276, 277, 499, 484, 361, 352, 353, 354, 351, 496, 492,
    387, 389, 388, 390, 386, 297, 488, 409, 408, 406, 381, 373, 372, 501, 410, 407, 528, 371, 500, 342,
    336, 337, 335, 502, 303, 322, 401, 503, 421, 413, 394, 411, 412, 414, 392, 246, 248, 250, 247, 283,
    504, 298, 299, 505, 393, 249, 518, 391, 519, 521, 506, 343, 362, 356, 357, 261, 251, 253, 252, 254,
    382, 376, 511, 315, 377, 370, 520, 507, 355, 422, 513, 417, 416, 338, 508, 402, 415, 395, 396, 397,
    509, 339, 516, 209, 208, 206, 210, 207, 262, 255, 256, 257, 317, 512, 323, 318, 319, 375, 515, 186,
    188, 187, 278, 510, 190, 189, 514, 363, 359, 221, 211, 213, 212, 214, 358, 517, 226, 227, 228, 316,
    374, 279, 522, 423, 344, 418, 419, 403, 201, 191, 192, 399, 398, 304, 529, 193, 194, 523, 340, 229,
    524, 241, 231, 263, 526, 534, 364, 258, 324, 284, 383, 378, 379, 230, 320, 525, 360, 222, 217, 215,
    216, 259, 530, 424, 420, 202, 195, 345, 535, 280, 527, 232, 531, 404, 400, 242, 235, 237, 236, 384,
    380, 197, 365, 264, 325, 196, 223, 425, 219, 218, 203, 198, 536, 199, 285, 260, 243, 238, 233, 239,
    405, 300, 385, 234, 224, 220, 537, 204, 200, 265, 244, 240, 305, 543, 225, 532, 205, 245, 544, 538,
    533, 545, 539, 546, 540, 547, 541, 542, 548, 549,
)


def scratch_of():
    f, h, low = (ROWS, D), (ROWS, LANES), pltpu.VMEM((ROWS, D), BF16)
    halo3 = pltpu.VMEM(((GRID + 2 * HALO) * GRID, SLOTS, D), F32)
    halo1 = pltpu.VMEM(((GRID + 2) * GRID, SLOTS, D), F32)
    high, column, turned = pltpu.VMEM(f, F32), pltpu.VMEM(h, F32), pltpu.VMEM((D, ROWS), BF16)
    taps = pltpu.VMEM((WINDOW * WINDOW, D), F32)
    return dict(
        live=column,
        im8=pltpu.VMEM((IMG_GROUP, SLOTS, LANES), F32),
        im16=pltpu.VMEM((IMG_GROUP, 16, LANES), BF16),
        window=taps,
        rel_taps=taps,
        pos_src=halo1,
        pos_up=halo1,
        rel_src=halo3,
        dq_src=halo3,
        first=high,
        u1=high,
        inv1=column,
        second=high,
        u2=high,
        inv2=column,
        n1=low,
        n1_t=turned,
        n2=low,
        n2_t=turned,
        go=low,
        go_t=turned,
        q=low,
        k=low,
        v=low,
        soft=high,
        soft_low=low,
        soft_acc=pltpu.VMEM((2 * SLOTS, D), F32),
        ctx=pltpu.VMEM((2, WIDE, IMG_GROUP * WIDE), BF16),
        factor=high,
        rel=high,
        mixed=low,
        hidden=high,
        active=low,
        low=low,
        out_low=low,
        back=high,
        gs=high,
        gs_low=low,
        d=high,
        f=low,
        gq=high,
        gk=high,
        gv=high,
        gl=pltpu.VMEM((3, ROWS, D), BF16),
        in_low=low,
    )


class Links:
    def __init__(self):
        dp, head = lax.axis_index(DP), lax.axis_index(HEAD)
        self.far = lax.axis_size(DP) // 4
        self.at = dict(x=head // 2, c=head % 2, h=dp // 4, l=dp // 2 % 2, y=dp % 2)

    def count(self, axis):
        return dict(h=self.far, z=2 * self.far, d=4).get(axis, 2)

    def peer(self, axis, step):
        if axis in "zd":
            one, two = "hl" if axis == "z" else "xy"
            return {one: self.next(one, step // 2), two: self.next(two, step % 2)}
        return {axis: self.next(axis, step)}

    def other(self):
        return self.device("c", 1)

    def next(self, axis, step):
        return lax.rem(self.at[axis] + step, self.count(axis))

    def device(self, axis, step):
        at = {**self.at, **self.peer(axis, step)}
        return (at["h"] * 4 + at["l"] * 2 + at["y"], at["x"] * 2 + at["c"])

    def steps(self, axis, do):
        self.repeat(self.count(axis), do, 8)

    def repeat(self, size, do, most):
        if size <= most:
            for step in range(1, size):
                do(step)
        else:

            def body(step, _):
                do(step)
                return 0

            lax.fori_loop(1, size, body, 0)

    def others(self, name, do):
        dp, head, heads = lax.axis_index(DP), lax.axis_index(HEAD), lax.axis_size(HEAD)

        def one(step):
            if name == ALL:
                i = lax.rem(dp * heads + head + step, lax.axis_size(ALL))
                do((i // heads, lax.rem(i, heads)))
            elif name == DP:
                do((lax.rem(dp + step, lax.axis_size(DP)), head))
            else:
                do((dp, lax.rem(head + step, heads)))

        self.repeat(lax.axis_size(name), one, 32)

    def signal(self):
        def one(device):
            pl.semaphore_signal(
                pltpu.get_barrier_semaphore(),
                inc=1,
                device_id=device,
                device_id_type=pl.DeviceIdType.MESH,
            )

        self.others(DP, one)
        self.others(HEAD, one)

    def meet(self):
        count = lax.axis_size(DP) + lax.axis_size(HEAD) - 2
        pl.semaphore_wait(pltpu.get_barrier_semaphore(), count)

    def copy(self, src, dst, send, recv, device):
        return pltpu.make_async_remote_copy(
            src_ref=src,
            dst_ref=dst,
            send_sem=send,
            recv_sem=recv,
            device_id=device,
            device_id_type=pl.DeviceIdType.MESH,
        )

    def region(self, blocks, slot, whole, **at):
        at = {**self.at, **at}
        whole = whole.replace("z", "hl").replace("d", "xy")
        place = [slice(None) if axis in whole else at[axis] for axis in AXES]
        return blocks.at[(*place, slot)]


class Gather:
    def __init__(self, links, w, sizes, send, recv):
        self.links, self.w, self.sizes, self.send, self.recv = links, w, sizes, send, recv

    def start(self, slot, i, j):
        path, links = AG_ROUTES[slot], self.links

        def along(whole, at):
            part = links.region(self.w, slot, whole, **at)

            def go(step):
                sems = self.send.at[slot], self.recv.at[slot, j]
                links.copy(part, part, *sems, links.device(path[j], step)).start()

            links.steps(path[j], go)

        if i < 0:
            along("", {})
        elif path[i] == "z" and i == 0:
            along("z", {})
        else:
            links.steps(path[i], lambda step: along(path[:i], links.peer(path[i], step)))

    def arrive(self, slot, j):
        path, links = AG_ROUTES[slot], self.links
        blocks = (links.count(path[j]) - 1) * math.prod(links.count(a) for a in path[:j])
        size = self.sizes.at[pl.ds(0, blocks)]
        links.copy(size, size, self.send.at[slot], self.recv.at[slot, j], links.other()).wait_recv()

    def sent(self):
        for slot in range(MATS):
            sems = self.send.at[slot], self.recv.at[slot, 0]
            self.links.copy(self.sizes, self.sizes, *sems, self.links.other()).wait_send()

    def steps(self):
        for slot, path in enumerate(AG_ROUTES):
            for j in range(len(path)):
                for i in range(-1, j):
                    if path[0] != "z" or j == 0 or i >= 0:
                        yield functools.partial(self.start, slot, i, j)
            for j in range(len(path)):
                yield functools.partial(self.arrive, slot, j)


class Scatter:
    def __init__(self, links, g, boxes, total, sizes, send, recv):
        self.links, self.g, self.boxes, self.total = links, g, boxes, total
        self.sizes, self.send, self.recv = sizes, send, recv

    def box(self, slot, j):
        return self.boxes[slot * len(AXES) + j - 1]

    def merged(self, slot, j):
        path = RS_ROUTES[slot]
        return path[-1] == "z" and j == len(path) - 1

    def start(self, slot, i, j):
        path, links = RS_ROUTES[slot], self.links
        first = sum(links.count(a) - 1 for a in path[:i]) - 1
        skip = first + 1 if path[-1] == "z" and j == len(path) else 0

        def go(step):
            entry = first + step - skip
            sems = self.send.at[slot], self.recv.at[slot, j - 1]
            into = self.box(slot, j).at[entry]
            device = links.device(path[i], step)

            def part(into, whole, more):
                src = links.region(self.g, slot, whole, **links.peer(path[i], step), **more)
                links.copy(src, into, *sems, device).start()

            if j == len(path) or self.merged(slot, j):
                part(into, path[j:], {})
            else:
                links.steps(
                    path[j], lambda n: part(into.at[n - 1], path[j + 1 :], links.peer(path[j], n))
                )

        links.steps(path[i], go)

    def add(self, slot, j):
        path, links = RS_ROUTES[slot], self.links
        box = self.box(slot, j)
        sems = self.send.at[slot], self.recv.at[slot, j - 1]
        links.copy(box, box, *sems, links.other()).wait_recv()

        def total(own, pick):
            value = own[...].astype(F32)
            for e in range(box.shape[0]):
                value = value + pick(box.at[e])[...].astype(F32)
            return value

        if j == len(path):
            own = links.region(self.g, slot, "")
            self.total[SLOT_OF.index(slot)] = total(own, lambda b: b)
            return

        def one(n):
            own = links.region(self.g, slot, path[j + 1 :], **links.peer(path[j], n))
            own[...] = total(own, lambda b: b.at[n - 1]).astype(BF16)

        if self.merged(slot, j):
            own = links.region(self.g, slot, "z")
            own[...] = total(own, lambda b: b).astype(BF16)
        else:
            links.steps(path[j], one)

    def sent(self):
        for slot in range(MATS):
            sems = self.send.at[slot], self.recv.at[slot, 0]
            self.links.copy(self.sizes, self.sizes, *sems, self.links.other()).wait_send()

    def steps(self):
        for slot, path in enumerate(RS_ROUTES):
            for i in range(len(path)):
                for j in range(i + 1, len(path) + 1):
                    if not (path[-1] == "z" and j == len(path) and i + 1 < len(path)):
                        yield functools.partial(self.start, slot, i, j)
            for j in range(1, len(path) + 1):
                yield functools.partial(self.add, slot, j)


class Small:
    def __init__(self, links, sums, parts, in_c, in_x, in_y, in_h, in_l, full, send, recv):
        self.links, self.sums, self.parts, self.full = links, sums, parts, full
        self.in_c, self.in_x, self.in_y, self.in_h, self.in_l = in_c, in_x, in_y, in_h, in_l
        self.send, self.recv = send, recv

    def go(self, stage, src, dst, axis):
        sems = (self.send.at[stage], self.recv.at[stage])
        self.links.steps(
            axis, lambda step: self.links.copy(src, dst, *sems, self.links.device(axis, step)).start()
        )

    def wait(self, stage):
        x, c = self.links.at["x"], self.links.at["c"]
        ref = (
            self.in_c,
            self.in_x,
            self.in_y,
            self.in_h.at[pl.ds(0, self.links.far - 1)],
            self.in_l,
            self.full.at[c, x],
            self.full.at[c],
        )[stage]
        sems = (self.send.at[stage], self.recv.at[stage])
        return self.links.copy(ref, ref, *sems, self.links.device("cxyhlxc"[stage], 1))

    def tick(self, stage):
        at = self.links.at
        x, c, h = at["x"], at["c"], at["h"]
        mine = self.parts.at[c, x]
        if stage:
            self.wait(stage - 1).wait_recv()
        if stage == 0:
            for b in range(D // LANES):
                self.parts[b // 2, b % 2] = self.sums[:, b * LANES : (b + 1) * LANES]
            self.go(0, self.parts.at[1 - c], self.in_c, "c")
        if stage == 1:
            self.parts[c] = self.parts[c] + self.in_c[...]
            self.go(1, self.parts.at[c, 1 - x], self.in_x, "x")
        if stage == 2:
            mine[...] = mine[...] + self.in_x[...]
            self.go(2, mine, self.in_y, "y")
        if stage == 3:
            self.in_h[h] = mine[...] + self.in_y[...]
            self.go(3, self.in_h.at[h], self.in_h.at[h], "h")
        if stage == 4:
            total = self.in_h[0]
            for i in range(1, self.links.far):
                total = total + self.in_h[i]
            self.sums[:, 0:LANES] = total
            self.go(4, self.sums.at[:, pl.ds(0, LANES)], self.in_l, "l")
        if stage == 5:
            self.full[c, x] = self.sums[:, 0:LANES] + self.in_l[...]
            self.go(5, self.full.at[c, x], self.full.at[c, x], "x")
        if stage == 6:
            self.go(6, self.full.at[c], self.full.at[c], "c")

    def sent(self):
        for stage in range(7):
            self.wait(stage).wait_send()


class Rows:
    def __init__(self, links, blocks, out, own, send, recv):
        self.links, self.blocks, self.out, self.own = links, blocks, out, own
        self.send, self.recv = send, recv

    def hop(self, i):
        x, c = self.links.at["x"], self.links.at["c"]
        x, axis = ((x, "x"), (x, "c"), (1 - x, "c"))[i]
        block = self.blocks.at[2 * x + c]
        return self.links.copy(
            block, block, self.send.at[i], self.recv.at[i], self.links.device(axis, 1)
        )

    def tick(self, stage):
        if stage == 0:
            self.hop(0).start()
            self.hop(1).start()
        if stage == 1:
            self.hop(0).wait_recv()
            self.hop(2).start()
        if stage == 2:
            self.hop(1).wait_recv()
            self.hop(2).wait_recv()
            self.join()

    def sent(self):
        for i in range(3):
            self.hop(i).wait_send()

    def join(self):
        heads, end, own = self.blocks.shape[0], self.out.shape[0], self.own
        for h in range(heads):
            lo, hi = h * own, (h + 1) * own
            base = lo // 16 * 16
            first = base + 16 if lo % 16 else base
            last = hi // 16 * 16 if h + 1 < heads else end
            self.out[first:last, :] = self.blocks[h, first - base : last - base, :]
            if lo % 16:
                before = (lo - own) // 16 * 16
                tail = self.blocks[h - 1, base - before : base - before + 16, :]
                self.out[base : base + 16, :] = tail + self.blocks[h, 0:16, :]


class Exchange:
    def __init__(self, links, name, buffer, send, recv):
        self.links, self.name, self.buffer, self.send, self.recv = links, name, buffer, send, recv

    def start(self, value):
        own = lax.axis_index(self.name)
        self.buffer[own] = value
        mine = self.buffer.at[own]
        self.links.others(
            self.name,
            lambda device: self.links.copy(mine, mine, self.send, self.recv, device).start(),
        )

    def descriptor(self):
        ref = self.buffer.at[pl.ds(0, self.buffer.shape[0] - 1)]
        return self.links.copy(ref, ref, self.send, self.recv, self.links.device("c", 1))

    def total(self):
        self.descriptor().wait_recv()
        return jnp.sum(self.buffer[...], axis=0)

    def sent(self):
        self.descriptor().wait_send()


def exact(a, b, dims):
    return lax.dot_general(
        a, b, dims, precision=lax.Precision.HIGHEST, preferred_element_type=F32
    )


class Adafactor:
    def __init__(self, refs, lo, hi, row_share, col_share, sq_share):
        self.__dict__.update(refs)
        self.lo, self.hi = lo, hi
        self.row_share, self.col_share, self.sq_share = row_share, col_share, sq_share

    def eye(self, count, first):
        r = lax.broadcasted_iota(jnp.int32, (count, LANES), 0)
        c = lax.broadcasted_iota(jnp.int32, (count, LANES), 1)
        return jnp.where(c == r + first, 1.0, 0.0)

    def lane(self, k, value, rest):
        lanes = lax.broadcasted_iota(jnp.int32, rest.shape, 1)
        return jnp.where(lanes == k, value, rest)

    def squares(self):
        rows, count = self.wg.shape[1], self.hi - self.lo
        by_row = jnp.zeros((rows, LANES), F32)
        by_col = []
        for k in range(self.lo, self.hi):
            g = self.wg[k]
            s = g * g + SQUARE_FLOOR
            by_row = self.lane(k, jnp.sum(s, axis=1, keepdims=True), by_row)
            by_col.append(jnp.sum(s, axis=0, keepdims=True))
        rest = jnp.zeros((SLOTS - count, LANES), F32)
        self.col_share.start(jnp.concatenate([*by_col, rest] if count < SLOTS else by_col, axis=0))
        turned = exact(self.eye(SLOTS, self.lo), by_row, NT)
        if rows < LANES:
            turned = jnp.concatenate([turned, jnp.zeros((SLOTS, LANES - rows), F32)], axis=1)
        self.row_share.start(turned)

    def scale(self):
        rows, lo, hi = self.wg.shape[1], self.lo, self.hi
        total = self.row_share.total()[0 : hi - lo, 0:rows]
        new_rows = SECOND_DECAY * self.row_state[lo:hi, :] + (1.0 - SECOND_DECAY) * (
            total * (1.0 / D)
        )
        self.new_rows[lo:hi, :] = new_rows
        row = exact(new_rows, self.eye(hi - lo, lo), TN)
        total = self.col_share.total()[0 : hi - lo]
        cols = SECOND_DECAY * self.col_state[lo:hi, :] + (1.0 - SECOND_DECAY) * (
            total * (1.0 / D)
        )
        self.new_cols[lo:hi, :] = cols
        sums = jnp.zeros((1, LANES), F32)
        for k in range(lo, hi):
            u = self.wg[k] * lax.rsqrt(row[:, k : k + 1] * cols[k - lo : k - lo + 1, :])
            self.upd[k] = u
            s = jnp.sum(jnp.sum(u * u, axis=0, keepdims=True), axis=1, keepdims=True)
            sums = self.lane(k, s, sums)
        mass = jnp.sum(row, axis=0, keepdims=True)
        self.sq_share.start(jnp.concatenate([sums, mass], axis=0))

    def apply(self):
        total = self.sq_share.total()
        mean = total[1:2] * (1.0 / (D * lax.axis_size(HEAD)))
        rms = jnp.sqrt(total[0:1] * mean * (1.0 / (D * D)))
        rate = STEP_RATE * jnp.sqrt(mean) / jnp.maximum(1.0, rms)
        for k in range(self.lo, self.hi):
            new = self.weights[k] - rate[:, k : k + 1] * self.upd[k]
            self.new_weights[k] = new
            self.copy[k] = new.astype(BF16)
            self.new_ema[k] = AVERAGE_KEEP * self.ema[k] + (1.0 - AVERAGE_KEEP) * new
        self.rms[self.lo // 4 : self.lo // 4 + 1, :] = rms


class SmallStep:
    def __init__(self, refs):
        self.__dict__.update(refs)

    def clips(self):
        lanes = lax.broadcasted_iota(jnp.int32, (1, LANES), 1)
        clip = jnp.where(lanes < EARLY, self.rms[0:1, :], self.rms[1:2, :])
        clip = jnp.where(lanes < MATS, clip, self.small_clip[...])
        self.clip[...] = clip[:, 0 : self.clip.shape[1]]

    def small_step(self):
        count, full = self.small.shape[0], self.full
        g = jnp.concatenate([full[b // 2, b % 2, 0:count, :] for b in range(D // LANES)], axis=1)
        self.small_grads[...] = g
        state = SECOND_DECAY * self.small_state[...] + (1.0 - SECOND_DECAY) * (
            g * g + SQUARE_FLOOR
        )
        self.new_small_state[...] = state
        u = g * lax.rsqrt(state)
        rms = jnp.sqrt(jnp.sum(u * u, axis=1, keepdims=True) * (1.0 / D))
        new = self.small[...] - SMALL_RATE * u / jnp.maximum(1.0, rms)
        self.new_small[...] = new
        self.new_small_ema[...] = AVERAGE_KEEP * self.small_ema[...] + (1.0 - AVERAGE_KEEP) * new
        r = lax.broadcasted_iota(jnp.int32, (count, LANES), 0)
        c = lax.broadcasted_iota(jnp.int32, (count, LANES), 1)
        picked = jnp.where(c == r + MATS, rms, 0.0)
        self.small_clip[...] = jnp.sum(picked, axis=0, keepdims=True)


class Inputs(NamedTuple):
    cls: Any
    img: Any
    tokens: Any
    cot: Any
    weights: Any
    row_state: Any
    col_state: Any
    ema: Any
    small: Any
    small_state: Any
    small_ema: Any


class Outputs(NamedTuple):
    out: Any
    grad_in: Any
    wg: Any
    new_rows: Any
    new_cols: Any
    new_weights: Any
    copy: Any
    new_ema: Any
    small_grads: Any
    new_small_state: Any
    new_small: Any
    new_small_ema: Any
    clip: Any


def box_shapes(links, block):
    for path in RS_ROUTES:
        for j in range(1, len(AXES) + 1):
            entries = sum(links.count(a) - 1 for a in path[:j])
            if j > len(path):
                shape = (1, SLOTS, LANES)
            elif j == len(path):
                first = links.count("z") - 1 if path[-1] == "z" else entries
                shape = (first, *block)
            elif path[-1] == "z" and j == len(path) - 1:
                shape = (entries, links.count("h"), links.count("l"), *block)
            else:
                rest = path[j + 1 :].replace("z", "hl").replace("d", "xy")
                rest = [links.count(a) for a in AXES if a in rest]
                shape = (entries, links.count(path[j]) - 1, *rest, *block)
            yield pltpu.VMEM(shape, BF16)


def shared_of(weights, parts, heads):
    links, (_, rows, _) = Links(), weights.shape
    block = (rows, LANES)
    every = pltpu.VMEM((2, 2, links.far, 2, 2, MATS, *block), BF16)
    out_rows = pltpu.VMEM((heads, HEAD_ROWS, D), BF16)
    dma = pltpu.SemaphoreType.DMA

    def f(*shape):
        return pltpu.VMEM(shape, F32)

    part = f(SMALL_ROWS, LANES)
    return dict(
        w=every,
        g=every,
        out_rows=out_rows,
        in_rows=out_rows,
        sums=f(SMALL_ROWS, D),
        parts=f(2, 2, SMALL_ROWS, LANES),
        in_c=f(2, SMALL_ROWS, LANES),
        in_x=part,
        in_y=part,
        in_h=f(links.far, SMALL_ROWS, LANES),
        in_l=part,
        full=f(2, 2, SMALL_ROWS, LANES),
        row_box=f(2, heads, SLOTS, LANES),
        col_box=f(2, parts, SLOTS, LANES),
        sq_box=f(2, parts * heads, 2, LANES),
        upd=f(MATS, *block),
        small_clip=f(1, LANES),
        rms=f(2, LANES),
        sizes=pltpu.VMEM((parts * heads - 1, *block), BF16),
        ag_send=dma((MATS,)),
        ag_recv=dma((MATS, len(AXES))),
        rs_send=dma((MATS,)),
        rs_recv=dma((MATS, len(AXES))),
        small_send=dma((7,)),
        small_recv=dma((7,)),
        out_send=dma((3,)),
        out_recv=dma((3,)),
        in_send=dma((3,)),
        in_recv=dma((3,)),
        opt_send=dma((2, 3)),
        opt_recv=dma((2, 3)),
        fetched=dma((len(Inputs._fields),)),
        stored=dma((len(Outputs._fields),)),
    )


class Ready:
    def __init__(self, src, dst, sem):
        self.copy = pltpu.make_async_copy(src, dst, sem)
        self.start, self.wait = self.copy.start, self.copy.wait


def then(*steps):
    def run():
        for step in steps:
            step()

    return run


def block_kernel(names, *refs):
    n_in, n_out = len(Inputs._fields), len(Outputs._fields)
    ins, outs, refs = Inputs(*refs[:n_in]), Outputs(*refs[n_in : n_in + n_out]), refs[n_in + n_out :]
    r = types.SimpleNamespace(**dict(zip(names, refs)))
    for rows in (r.tokens, r.cot):
        rows[rows.shape[0] - 32 :, :] = jnp.zeros((32, D), BF16)

    def near(ref, scratch):
        if ref.shape == scratch.shape:
            return scratch
        return scratch.at[pl.ds(0, ref.shape[0])]

    fetch = Inputs(
        *[
            Ready(ref, near(ref, getattr(r, name)), r.fetched.at[i])
            for i, (name, ref) in enumerate(zip(Inputs._fields, ins))
        ]
    )
    store = Outputs(
        *[
            Ready(getattr(r, name), ref, r.stored.at[i])
            for i, (name, ref) in enumerate(zip(Outputs._fields, outs))
        ]
    )
    boxes = refs[len(names) :]
    links = Links()
    links.signal()
    for one in (fetch.weights, *fetch[0:2], fetch.small, *fetch[2:4], *fetch[5:8], *fetch[9:]):
        one.start()
    r.out_own = r.out_rows.at[lax.axis_index(HEAD)]
    r.in_own = r.in_rows.at[lax.axis_index(HEAD)]
    own = r.cls.shape[1] * CELLS
    blk = Block(vars(r))
    gather = Gather(links, r.w, r.sizes, r.ag_send, r.ag_recv)
    scatter = Scatter(links, r.g, boxes, r.wg, r.sizes, r.rs_send, r.rs_recv)
    small = Small(
        links,
        *(r.sums, r.parts, r.in_c, r.in_x, r.in_y, r.in_h, r.in_l, r.full),
        r.small_send,
        r.small_recv,
    )
    out_rows = Rows(links, r.out_rows, r.out, own, r.out_send, r.out_recv)
    in_rows = Rows(links, r.in_rows, r.grad_in, own, r.in_send, r.in_recv)
    shares, opts = [], []
    for part, (lo, hi) in enumerate(((0, EARLY), (EARLY, MATS))):
        boxes = (HEAD, r.row_box), (DP, r.col_box), (ALL, r.sq_box)
        shares += [
            Exchange(links, axis, box.at[part], r.opt_send.at[part, i], r.opt_recv.at[part, i])
            for i, (axis, box) in enumerate(boxes)
        ]
        opts.append(Adafactor(vars(r), lo, hi, *shares[-3:]))
    step = SmallStep(vars(r))

    def round_weights():
        for k in range(MATS):
            mine = links.region(r.w, SLOT_OF[k], "")
            mine[...] = r.weights[k].astype(BF16)

    ops = [*gather.steps(), *scatter.steps()]
    ops += [then(fetch.weights.wait, round_weights), links.meet]
    ops += [then(fetch.small.wait, fetch.cls.wait, fetch.img.wait, blk.setup)]
    ops += [fetch.tokens.wait, fetch.cot.wait]

    def each(step, *ranges):
        for place in itertools.product(*map(range, ranges)):
            ops.append(functools.partial(step, *place))

    each(blk.read_tokens, PIECES)
    each(blk.position, D // LANES)
    each(blk.norm_one, PIECES)
    ops.append(blk.turn_one)
    each(blk.read_cotangent, PIECES)
    ops.append(blk.turn_cotangent)
    each(blk.project, 3, 2)
    ops += [blk.key_tops, blk.key_powers, blk.key_shares]
    each(blk.contexts, 2)
    ops.append(blk.fill_window)
    each(blk.window_sum, D // LANES)
    ops.append(blk.mix)
    each(blk.attend, 2)
    each(blk.norm_two, PIECES)
    ops.append(blk.turn_two)
    each(blk.hidden_in, 4)
    each(blk.hidden_out, 4)
    each(blk.grad_down, 4)
    each(blk.grad_up, 4)
    each(blk.add_down, 4)
    each(blk.add_back, 4)
    ops += [blk.finish_out, blk.back_two, blk.grad_proj, blk.back_mixed, blk.back_fill]
    each(blk.back_heads, 2)
    ops += [blk.back_inner, blk.back_query_key]
    each(blk.back_window, D // LANES)
    ops.append(blk.back_value)
    each(blk.grad_of, 3)
    each(blk.window_taps, D // LANES)
    each(blk.back_project, 2)
    ops += [blk.back_one, blk.back_position, blk.position_taps, blk.finish_in]
    for rows, done in ((out_rows, store.out), (in_rows, store.grad_in)):
        ops += [functools.partial(rows.tick, stage) for stage in range(2)]
        ops += [then(functools.partial(rows.tick, 2), done.start)]
    ops += [functools.partial(small.tick, stage) for stage in range(8)]
    ops += [
        then(
            fetch.small_state.wait,
            fetch.small_ema.wait,
            step.small_step,
            store.small_grads.start,
            store.new_small_state.start,
            store.new_small.start,
            store.new_small_ema.start,
        ),
        opts[1].squares,
        then(store.wg.start, opts[0].squares),
        then(fetch.row_state.wait, fetch.col_state.wait, opts[1].scale),
        then(opts[0].scale, store.new_rows.start, store.new_cols.start),
        then(fetch.ema.wait, opts[1].apply),
        then(
            opts[0].apply, store.new_weights.start, store.copy.start, store.new_ema.start
        ),
        then(step.clips, store.clip.start),
    ]
    for i in ORDER:
        ops[i]()
    for transfer in (gather, scatter, small, out_rows, in_rows, *shares):
        transfer.sent()
    for one in store:
        one.wait()


def finish_kernel(count, *refs):
    ins, outs, held = refs[:count], refs[count : 2 * count], refs[2 * count : 3 * count]
    took, gave = refs[3 * count :]
    come = [pltpu.make_async_copy(a, b, took.at[i]) for i, (a, b) in enumerate(zip(ins, held))]
    leave = [pltpu.make_async_copy(a, b, gave.at[i]) for i, (a, b) in enumerate(zip(held, outs))]
    for one in come:
        one.start()
    for one, other in zip(come, leave):
        one.wait()
        other.start()
    for one in leave:
        one.wait()


def local(
    tokens,
    cotangent,
    crop_image,
    crop_class,
    weights,
    row_state,
    col_state,
    weights_ema,
    small_params,
    small_state,
    small_ema,
):
    parts, heads = lax.axis_size(DP), lax.axis_size(HEAD)
    shared = shared_of(weights, parts, heads)
    own = scratch_of()

    def like(x, dtype=None):
        return jax.ShapeDtypeStruct(x.shape, dtype or x.dtype)

    clips = weights.shape[0] + small_params.shape[0]
    outs = (
        like(tokens),
        like(tokens),
        like(weights),
        like(row_state),
        like(col_state),
        like(weights),
        like(weights, BF16),
        like(weights),
        like(small_params),
        like(small_params),
        like(small_params),
        like(small_params),
        jax.ShapeDtypeStruct((1, clips), F32),
    )
    args = Inputs(
        crop_class,
        crop_image,
        tokens,
        cotangent,
        weights,
        row_state,
        col_state,
        weights_ema,
        small_params,
        small_state,
        small_ema,
    )
    staged = [pltpu.SMEM(x.shape, x.dtype) for x in args[:2]]
    last_rows = tokens.shape[0] // heads * (heads - 1) // 16 * 16
    staged += [pltpu.VMEM((last_rows + HEAD_ROWS, D), BF16)] * 2
    staged += [pltpu.VMEM(x.shape, x.dtype) for x in (*args[4:], *outs)]
    names = (*shared, *own, *Inputs._fields, *Outputs._fields)
    far = pl.BlockSpec(memory_space=pltpu.HBM)
    res = pl.pallas_call(
        functools.partial(block_kernel, names),
        out_shape=outs,
        in_specs=[far] * len(args),
        out_specs=(far,) * len(outs),
        scratch_shapes=[
            *shared.values(),
            *own.values(),
            *staged,
            *box_shapes(Links(), weights.shape[1:]),
        ],
        compiler_params=pltpu.CompilerParams(
            collective_id=0, has_side_effects=True, vmem_limit_bytes=63 << 20
        ),
        name="block",
    )(*args)
    res = pl.pallas_call(
        functools.partial(finish_kernel, len(outs)),
        out_shape=outs,
        in_specs=[far] * len(outs),
        out_specs=(far,) * len(outs),
        scratch_shapes=[
            *[pltpu.VMEM(x.shape, x.dtype) for x in outs],
            pltpu.SemaphoreType.DMA((len(outs),)),
            pltpu.SemaphoreType.DMA((len(outs),)),
        ],
        compiler_params=pltpu.CompilerParams(vmem_limit_bytes=63 << 20),
        name="finish",
    )(*res)
    return (*res[:-1], res[-1].reshape(clips))


def solution(mesh):
    in_specs = (
        P(DP, None),
        P(DP, None),
        P(DP, None),
        P(DP, None),
        P(None, DP, HEAD),
        P(None, DP),
        P(None, HEAD),
        P(None, DP, HEAD),
        P(),
        P(),
        P(),
    )
    out_specs = (
        P(DP, None),
        P(DP, None),
        P(None, DP, HEAD),
        P(None, DP),
        P(None, HEAD),
        P(None, DP, HEAD),
        P(None, DP, HEAD),
        P(None, DP, HEAD),
        P(),
        P(),
        P(),
        P(),
        P(),
    )
    return jax.shard_map(local, mesh=mesh, in_specs=in_specs, out_specs=out_specs, check_vma=False)
```
